32 devices in a mesh: dp: 8 (over z, y), mp: 4 (over x, core).
Axes of the slice: x: 2, y: 2, z: 4, core: 2. Of those that a mesh axis runs over, the one named last changes fastest.
Arguments:
- hidden: bfloat16 [24576, 1024], P('dp', 'mp'), may hold values from -6 to 6
- first_gain: float32 [1024], replicated, may hold values from 0.25 to 1.75
- first_bias: float32 [1024], replicated, may hold values from -1.5 to 1.5
- second_gain: float32 [1024], replicated, may hold values from 0.25 to 1.75
- second_bias: float32 [1024], replicated, may hold values from -1.5 to 1.5
- joined_frozen_weight: bfloat16 [1024, 3072], P(None, 'mp'), may hold values from -0.1875 to 0.1875
- output_frozen_weight: bfloat16 [1024, 1024], P(None, 'mp'), may hold values from -1.5 to 1.5
- expand_frozen_weight: bfloat16 [1024, 4096], P(None, 'mp'), may hold values from -0.1875 to 0.1875
- shrink_frozen_weight: bfloat16 [4096, 1024], P(None, 'mp'), may hold values from -0.09375 to 0.09375
- joined_a: bfloat16 [1024, 128], replicated, may hold values from -0.1875 to 0.1875
- joined_up_factor: bfloat16 [128, 3072], replicated, may hold values from -0.5 to 0.5
- output_a: bfloat16 [1024, 128], replicated, may hold values from -0.1875 to 0.1875
- output_up_factor: bfloat16 [128, 1024], replicated, may hold values from -2 to 2
- expand_a: bfloat16 [1024, 128], replicated, may hold values from -0.1875 to 0.1875
- expand_up_factor: bfloat16 [128, 4096], replicated, may hold values from -0.5 to 0.5
- shrink_a: bfloat16 [4096, 128], replicated, may hold values from -0.09375 to 0.09375
- shrink_up_factor: bfloat16 [128, 1024], replicated, may hold values from -0.5 to 0.5
- cotangent: bfloat16 [24576, 1024], P('dp', 'mp'), may hold values from -6 to 6
Outputs:
- result: bfloat16 [24576, 1024], P('dp', 'mp')
- hidden_grad: float32 [24576, 1024], P('dp', 'mp')
- first_gain_grad: float32 [1024], replicated
- first_bias_grad: float32 [1024], replicated
- second_gain_grad: float32 [1024], replicated
- second_bias_grad: float32 [1024], replicated
- joined_a_grad: float32 [1024, 128], replicated
- joined_b_grad: float32 [128, 3072], replicated
- output_a_grad: float32 [1024, 128], replicated
- output_b_grad: float32 [128, 1024], replicated
- expand_a_grad: float32 [1024, 128], replicated
- expand_b_grad: float32 [128, 4096], replicated
- shrink_a_grad: float32 [4096, 128], replicated
- shrink_b_grad: float32 [128, 1024], replicated
The draws below stay inside these ranges and needn't reach their ends.
All inputs are finite; a program needn't handle non-finite values.
Results may differ from the reference program's by a relative error of at most 0.0045.
The reference program's roundings to bfloat16 on the way count: a program that leaves them out, or rounds other values in their place, can miss the bound.
Values may be sent and summed in bfloat16 or wider, within the bound.
No kernel may reach another device: no remote copies, remote signals or barrier semaphores. Data moves between devices by JAX's collectives and lax.ppermute only.
A program may use at most 384 MiB of HBM per device.

```python
import jax
import jax.numpy as jnp
from jax import lax

D = 1024
HEADS = 16
FF = 4096
ROTARY = 16
RANK = 128
SEQ_LEN = 1024
HEAD_DIM = 64
TOKENS = 24576


def levels(own_key, dims, pieces, low, largest):
    level = 1.0
    for dim, shards_of in pieces:
        draws = jax.random.uniform(jax.random.fold_in(jax.random.fold_in(own_key, 6), dim), (shards_of,), jnp.float32, low / len(pieces), largest / len(pieces))
        level = level * jnp.repeat(jnp.exp(draws), dims[dim] // shards_of).reshape((-1,) + (1,) * (len(dims) - 1 - dim))
    return level


def normal_values(own_key, shape, width, reach, pieces=(), held_as=jnp.bfloat16):
    result = jax.random.normal(own_key, shape, jnp.float32) * width
    if len(pieces) > 0:
        result = levels(own_key, shape, pieces, -0.22, 0.18) * result
    return jnp.clip(result, min=-reach, max=reach).astype(held_as)


def setup_inputs(seed: int = 0) -> dict:
    key_of = jax.random.split(jax.random.key(seed), 19)
    return {
        "hidden": normal_values(key_of[0], (TOKENS, D), 1.0, 6.0, ((0, 8), (1, 4))),
        "first_gain": jnp.clip(1.0 + 0.15 * jax.random.normal(key_of[1], (D,), jnp.float32), 0.25, 1.75),
        "first_bias": normal_values(key_of[2], (D,), 0.3, 1.5, (), jnp.float32),
        "second_gain": jnp.clip(1.0 + 0.15 * jax.random.normal(key_of[3], (D,), jnp.float32), 0.25, 1.75),
        "second_bias": normal_values(key_of[4], (D,), 0.3, 1.5, (), jnp.float32),
        "joined_frozen_weight": normal_values(key_of[5], (D, 3 * D), D ** -0.5, 0.1875, ((1, 4),)),
        "output_frozen_weight": normal_values(key_of[6], (D, D), (D // 64) ** -0.5, 1.5, ((1, 4),)),
        "expand_frozen_weight": normal_values(key_of[7], (D, FF), D ** -0.5, 0.1875, ((1, 4),)),
        "shrink_frozen_weight": normal_values(key_of[8], (FF, D), FF ** -0.5, 0.09375, ((1, 4),)),
        "joined_a": normal_values(key_of[9], (D, RANK), D ** -0.5, 0.1875),
        "joined_up_factor": normal_values(key_of[10], (RANK, 3 * D), RANK ** -0.5, 0.5),
        "output_a": normal_values(key_of[11], (D, RANK), D ** -0.5, 0.1875),
        "output_up_factor": normal_values(key_of[12], (RANK, D), (RANK // 16) ** -0.5, 2.0),
        "expand_a": normal_values(key_of[13], (D, RANK), D ** -0.5, 0.1875),
        "expand_up_factor": normal_values(key_of[14], (RANK, FF), RANK ** -0.5, 0.5),
        "shrink_a": normal_values(key_of[15], (FF, RANK), FF ** -0.5, 0.09375),
        "shrink_up_factor": normal_values(key_of[16], (RANK, D), RANK ** -0.5, 0.5),
        "cotangent": normal_values(key_of[17], (TOKENS, D), 1.0, 6.0, ((0, 8), (1, 4))),
    }


ADAPTER_SCALE = 0.25
EPS = 1e-05
HIGH = lax.Precision.HIGHEST

@jax.custom_vjp
def low(v):
    return lax.optimization_barrier(v.astype(jnp.bfloat16)).astype(jnp.float32)

@jax.custom_vjp
def adapter_backward(v):
    return v

def low_keep(v):
    return (low(v), None)

def low_pass(kept, grad):
    return (grad,)

def back_keep(v):
    return (v, None)

def back_low(kept, grad):
    return (low(grad),)
low.defvjp(low_keep, low_pass)
adapter_backward.defvjp(back_keep, back_low)

def matrix_product(left, right):
    return jnp.dot(left, right, precision=HIGH)

def normalize(full, gain, bias):
    center = full - lax.optimization_barrier(jnp.mean(full, -1, keepdims=True))
    factor = lax.rsqrt(lax.optimization_barrier(jnp.mean(center * center, -1, keepdims=True)) + EPS)
    return center * factor * gain + bias

def tables():
    position = jnp.arange(SEQ_LEN, dtype=jnp.float32)[:, None]
    frequency = 10000.0 ** (-(jnp.arange(ROTARY // 2, dtype=jnp.float32) * 2.0) / ROTARY)
    angles = position * frequency[None, :]
    cosine = jnp.concatenate([jnp.cos(angles), jnp.cos(angles)], -1)[:, None, :]
    sine = jnp.concatenate([jnp.sin(angles), jnp.sin(angles)], -1)[:, None, :]
    return (cosine, sine)

def rotate(block, cosine, sine):
    half = ROTARY // 2
    part = block[..., :ROTARY]
    turned = jnp.concatenate([-part[..., half:], part[..., :half]], -1)
    return jnp.concatenate([part * cosine + turned * sine, block[..., ROTARY:]], -1)

def attend(block):
    query, keys, values = block
    causal = jnp.arange(SEQ_LEN)[:, None] >= jnp.arange(SEQ_LEN)[None, :]
    scores = jnp.einsum('qhe,khe->hqk', query, keys, precision=HIGH) * HEAD_DIM ** (-0.5)
    scores = jnp.where(causal, adapter_backward(scores), -1e+30)
    peak = lax.optimization_barrier(jnp.max(scores, -1, keepdims=True))
    weights = jnp.exp(scores - peak)
    probs = weights / lax.optimization_barrier(jnp.sum(weights, -1, keepdims=True))
    return jnp.einsum('hqk,khe->qhe', low(probs), values, precision=HIGH)

def layer(params, frozen):
    hidden, first_gain, first_bias, second_gain, second_bias, joined_a, joined_up_factor, output_a, output_up_factor, expand_a, expand_up_factor, shrink_a, shrink_up_factor = params
    joined_frozen_weight, output_frozen_weight, expand_frozen_weight, shrink_frozen_weight = frozen
    tokens = hidden.shape[0]
    count = tokens // SEQ_LEN
    first_norm_output = low(normalize(hidden, first_gain, first_bias))
    second_norm_output = low(normalize(hidden, second_gain, second_bias))
    adapter_joined_hidden = low(adapter_backward(matrix_product(first_norm_output, joined_a)))
    mixed_state = adapter_backward(matrix_product(first_norm_output, joined_frozen_weight) + ADAPTER_SCALE * matrix_product(adapter_joined_hidden, joined_up_factor))
    mixed_state = mixed_state.reshape(count, SEQ_LEN, HEADS, 3, HEAD_DIM)
    cosine, sine = tables()
    query = low(rotate(mixed_state[:, :, :, 0], cosine, sine))
    keys = low(rotate(mixed_state[:, :, :, 1], cosine, sine))
    values = low(mixed_state[:, :, :, 2])
    attended_context = lax.map(jax.checkpoint(attend), (query, keys, values))
    attended_context = low(adapter_backward(attended_context.reshape(tokens, HEADS * HEAD_DIM)))
    adapter_output_hidden = low(adapter_backward(matrix_product(attended_context, output_a)))
    attention_branch = matrix_product(attended_context, output_frozen_weight) + ADAPTER_SCALE * matrix_product(adapter_output_hidden, output_up_factor)
    adapter_expand_hidden = low(adapter_backward(matrix_product(second_norm_output, expand_a)))
    upper_hidden = adapter_backward(matrix_product(second_norm_output, expand_frozen_weight) + ADAPTER_SCALE * matrix_product(adapter_expand_hidden, expand_up_factor))
    active_hidden = low(jax.nn.gelu(upper_hidden, approximate=False))
    adapter_shrink_hidden = low(adapter_backward(matrix_product(active_hidden, shrink_a)))
    feedforward_branch = matrix_product(active_hidden, shrink_frozen_weight) + ADAPTER_SCALE * matrix_product(adapter_shrink_hidden, shrink_up_factor)
    return hidden + attention_branch + feedforward_branch

def reference(hidden, first_gain, first_bias, second_gain, second_bias, joined_frozen_weight, output_frozen_weight, expand_frozen_weight, shrink_frozen_weight, joined_a, joined_up_factor, output_a, output_up_factor, expand_a, expand_up_factor, shrink_a, shrink_up_factor, cotangent):
    frozen = (joined_frozen_weight.astype(jnp.float32), output_frozen_weight.astype(jnp.float32), expand_frozen_weight.astype(jnp.float32), shrink_frozen_weight.astype(jnp.float32))
    trained = (hidden.astype(jnp.float32), first_gain.astype(jnp.float32), first_bias.astype(jnp.float32), second_gain.astype(jnp.float32), second_bias.astype(jnp.float32), joined_a.astype(jnp.float32), joined_up_factor.astype(jnp.float32), output_a.astype(jnp.float32), output_up_factor.astype(jnp.float32), expand_a.astype(jnp.float32), expand_up_factor.astype(jnp.float32), shrink_a.astype(jnp.float32), shrink_up_factor.astype(jnp.float32))

    def forward(*params):
        return layer(params, frozen)
    output, pull = jax.vjp(forward, *trained)
    grads = pull(cotangent.astype(jnp.float32))
    return (output.astype(jnp.bfloat16), grads[0], grads[1], grads[2], grads[3], grads[4], grads[5], grads[6], grads[7], grads[8], grads[9], grads[10], grads[11], grads[12])
```

```python
from functools import partial, reduce

import jax
import jax.numpy as jnp
from jax import lax
from jax.experimental import pallas as pl
from jax.experimental.pallas import tpu as pltpu
from jax.sharding import PartitionSpec as P

ROTARY = 16
SEQ_LEN = 1024
HEAD_DIM = 64


ADAPTER_SCALE = 0.25
EPS = 1e-05


def matrix_product(left, right):
    return jnp.dot(left, right, preferred_element_type=jnp.float32)


def matrix_product_transposed_left(left, right):
    return lax.dot_general(
        left, right, (((0,), (0,)), ((), ())), preferred_element_type=jnp.float32
    )


def matrix_product_transposed_right(left, right):
    return lax.dot_general(
        left, right, (((1,), (1,)), ((), ())), preferred_element_type=jnp.float32
    )


def normalize(full, gain, bias):
    center = full - jnp.mean(full, -1, keepdims=True)
    factor = lax.rsqrt(jnp.mean(center * center, -1, keepdims=True) + EPS)
    unit = center * factor
    return (unit, factor, unit * gain + bias)


def tables():
    position = jnp.arange(SEQ_LEN, dtype=jnp.float32)[:, None]
    frequency = 10000.0 ** (-(jnp.arange(ROTARY // 2, dtype=jnp.float32) * 2.0) / ROTARY)
    angles = position * frequency[None, :]
    cosine = jnp.concatenate([jnp.cos(angles), jnp.cos(angles)], -1)[:, None, :]
    sine = jnp.concatenate([jnp.sin(angles), jnp.sin(angles)], -1)[:, None, :]
    return (cosine, sine)


def rotate(block, cosine, sine):
    half = ROTARY // 2
    part = block[..., :ROTARY]
    turned = jnp.concatenate([-part[..., half:], part[..., :half]], -1)
    return jnp.concatenate([part * cosine + turned * sine, block[..., ROTARY:]], -1)


def unrotate(grad, cosine, sine):
    half = ROTARY // 2
    part = grad[..., :ROTARY]
    scaled = part * sine
    untied = jnp.concatenate([scaled[..., half:], -scaled[..., :half]], -1)
    return jnp.concatenate([part * cosine + untied, grad[..., ROTARY:]], -1)


def attend(causal, block):
    query, keys, values = block
    scores = jnp.einsum(
        "qhe,khe->hqk", query, keys, preferred_element_type=jnp.float32
    ) * HEAD_DIM ** (-0.5)
    scores = jnp.where(causal, scores, -1e30)
    peak = jnp.max(scores, -1, keepdims=True)
    weights = jnp.exp(scores - peak)
    total = jnp.sum(weights, -1, keepdims=True)
    probs = (weights / total).astype(jnp.bfloat16)
    attended_context = jnp.einsum("hqk,khe->qhe", probs, values, preferred_element_type=jnp.float32)
    return (attended_context.astype(jnp.bfloat16), (peak + jnp.log(total))[..., 0])


def attend_back(causal, block):
    query, keys, values, grad_context, logsum = block
    scores = jnp.einsum(
        "qhe,khe->hqk", query, keys, preferred_element_type=jnp.float32
    ) * HEAD_DIM ** (-0.5)
    scores = jnp.where(causal, scores, -1e30)
    probs = jnp.exp(scores - logsum[..., None])
    grad_probs = jnp.einsum(
        "qhe,khe->hqk", grad_context, values, preferred_element_type=jnp.float32
    )
    inner = jnp.sum(probs * grad_probs, -1, keepdims=True)
    grad_scores = (probs * (grad_probs - inner)).astype(jnp.bfloat16)
    grad_query = jnp.einsum(
        "hqk,khe->qhe", grad_scores, keys, preferred_element_type=jnp.float32
    ) * HEAD_DIM ** (-0.5)
    grad_keys = jnp.einsum(
        "hqk,qhe->khe", grad_scores, query, preferred_element_type=jnp.float32
    ) * HEAD_DIM ** (-0.5)
    grad_values = jnp.einsum(
        "hqk,qhe->khe", probs.astype(jnp.bfloat16), grad_context, preferred_element_type=jnp.float32
    )
    return (grad_query, grad_keys, grad_values)


def fold_with(weight, adapter_a, carry, piece):
    span = piece.shape[1]
    weight_rows = lax.slice_in_dim(weight, 0, span, axis=0)
    adapter_rows = lax.slice_in_dim(adapter_a, 0, span, axis=0)
    return (
        carry[0] + matrix_product(piece, weight_rows),
        carry[1] + matrix_product(piece, adapter_rows),
    )


def finish(summed_result, low_sum, columns_up_factor):
    adapter_values = low_sum.astype(jnp.bfloat16)
    return (
        summed_result + ADAPTER_SCALE * matrix_product(adapter_values, columns_up_factor),
        adapter_values,
    )


def on_device(
    hidden,
    first_gain,
    first_bias,
    second_gain,
    second_bias,
    joined_frozen_weight,
    output_frozen_weight,
    expand_frozen_weight,
    shrink_frozen_weight,
    joined_a,
    joined_up_factor,
    output_a,
    output_up_factor,
    expand_a,
    expand_up_factor,
    shrink_a,
    shrink_up_factor,
    cotangent,
):
    rank = lax.axis_index("mp")
    rows = hidden.shape[0]
    cols = hidden.shape[1]
    width = cols * lax.axis_size("mp")
    count = rows // SEQ_LEN
    joined_cols = joined_frozen_weight.shape[1]
    expand_cols = expand_frozen_weight.shape[1]
    heads_here = joined_cols // (3 * HEAD_DIM)
    inner_out = joined_cols // 3
    full = lax.all_gather(hidden, "mp", axis=1, tiled=True).astype(jnp.float32)
    unit_one, factor_one, first_norm_output = normalize(full, first_gain, first_bias)
    unit_two, factor_two, second_norm_output = normalize(full, second_gain, second_bias)
    first_norm_output = first_norm_output.astype(jnp.bfloat16)
    second_norm_output = second_norm_output.astype(jnp.bfloat16)
    adapter_joined_hidden = matrix_product(first_norm_output, joined_a).astype(jnp.bfloat16)
    joined_weight_local = lax.dynamic_slice_in_dim(
        joined_up_factor, rank * joined_cols, joined_cols, 1
    )
    mixed_state = matrix_product(
        first_norm_output, joined_frozen_weight
    ) + ADAPTER_SCALE * matrix_product(adapter_joined_hidden, joined_weight_local)
    mixed_state = mixed_state.reshape(count, SEQ_LEN, heads_here, 3, HEAD_DIM)
    cosine, sine = tables()
    query = rotate(mixed_state[:, :, :, 0], cosine, sine).astype(jnp.bfloat16)
    keys = rotate(mixed_state[:, :, :, 1], cosine, sine).astype(jnp.bfloat16)
    values = mixed_state[:, :, :, 2].astype(jnp.bfloat16)
    causal = jnp.arange(SEQ_LEN)[:, None] >= jnp.arange(SEQ_LEN)[None, :]
    attended_context, logsum = lax.map(partial(attend, causal), (query, keys, values))
    attended_context = attended_context.reshape(rows, inner_out)
    adapter_expand_hidden = matrix_product(second_norm_output, expand_a).astype(jnp.bfloat16)
    expand_weight_local = lax.dynamic_slice_in_dim(
        expand_up_factor, rank * expand_cols, expand_cols, 1
    )
    upper_hidden = matrix_product(
        second_norm_output, expand_frozen_weight
    ) + ADAPTER_SCALE * matrix_product(adapter_expand_hidden, expand_weight_local)
    gelu_exact = partial(jax.nn.gelu, approximate=False)
    active_f, gelu_pull = jax.vjp(gelu_exact, upper_hidden)
    active_hidden = active_f.astype(jnp.bfloat16)
    out_rows_a = lax.dynamic_slice_in_dim(output_a, rank * inner_out, inner_out, 0)
    output_columns_up_factor = lax.dynamic_slice_in_dim(output_up_factor, rank * cols, cols, 1)
    shrink_rows_a = lax.dynamic_slice_in_dim(shrink_a, rank * expand_cols, expand_cols, 0)
    shrink_columns_up_factor = lax.dynamic_slice_in_dim(shrink_up_factor, rank * cols, cols, 1)
    zero_pair = (
        jnp.zeros((rows, cols), jnp.float32),
        jnp.zeros((rows, output_a.shape[1]), jnp.float32),
    )
    attn_summed, attn_low = fold_with(
        output_frozen_weight,
        output_a,
        zero_pair,
        lax.all_gather(attended_context, "mp", axis=1, tiled=True),
    )
    mlp_summed, mlp_low = fold_with(
        shrink_frozen_weight,
        shrink_a,
        zero_pair,
        jax.tree.map(lambda a: lax.all_gather(a, "mp", axis=1, tiled=True), active_hidden),
    )
    attention_branch, adapter_output_hidden = finish(
        attn_summed, attn_low, output_columns_up_factor
    )
    feedforward_branch, adapter_shrink_hidden = finish(
        mlp_summed, mlp_low, shrink_columns_up_factor
    )
    result = (hidden.astype(jnp.float32) + attention_branch + feedforward_branch).astype(
        jnp.bfloat16
    )
    back_out, back_shrink = (
        lax.psum_scatter(
            matrix_product_transposed_right(cotangent, output_frozen_weight),
            "mp",
            scatter_dimension=1,
            tiled=True,
        ),
        lax.psum_scatter(
            matrix_product_transposed_right(cotangent, shrink_frozen_weight),
            "mp",
            scatter_dimension=1,
            tiled=True,
        ),
    )
    rank_out, rank_shrink = lax.psum(
        (
            ADAPTER_SCALE * matrix_product_transposed_right(cotangent, output_columns_up_factor),
            ADAPTER_SCALE * matrix_product_transposed_right(cotangent, shrink_columns_up_factor),
        ),
        "mp",
    )
    low_out_grad = rank_out.astype(jnp.bfloat16)
    low_shrink_grad = rank_shrink.astype(jnp.bfloat16)
    output_up_factor_piece = ADAPTER_SCALE * matrix_product_transposed_left(
        adapter_output_hidden, cotangent
    )
    shrink_up_factor_piece = ADAPTER_SCALE * matrix_product_transposed_left(
        adapter_shrink_hidden, cotangent
    )
    grad_context = (back_out + matrix_product_transposed_right(low_out_grad, out_rows_a)).astype(
        jnp.bfloat16
    )
    output_a_piece = matrix_product_transposed_left(attended_context, low_out_grad)
    shrink_a_piece = matrix_product_transposed_left(active_hidden, low_shrink_grad)
    grad_active = back_shrink + matrix_product_transposed_right(low_shrink_grad, shrink_rows_a)
    upper_gradient = gelu_pull(grad_active)[0].astype(jnp.bfloat16)
    grad_context = grad_context.reshape(count, SEQ_LEN, heads_here, HEAD_DIM)
    grad_query, grad_keys, grad_values = lax.map(
        partial(attend_back, causal), (query, keys, values, grad_context, logsum)
    )
    mixed_gradient = jnp.stack(
        [unrotate(grad_query, cosine, sine), unrotate(grad_keys, cosine, sine), grad_values], 3
    )
    mixed_gradient = mixed_gradient.reshape(rows, joined_cols).astype(jnp.bfloat16)
    rank_joined, rank_expand = lax.psum(
        (
            ADAPTER_SCALE * matrix_product_transposed_right(mixed_gradient, joined_weight_local),
            ADAPTER_SCALE * matrix_product_transposed_right(upper_gradient, expand_weight_local),
        ),
        "mp",
    )
    low_joined_grad = rank_joined.astype(jnp.bfloat16)
    low_expand_grad = rank_expand.astype(jnp.bfloat16)
    joined_up_factor_piece = ADAPTER_SCALE * matrix_product_transposed_left(
        adapter_joined_hidden, mixed_gradient
    )
    expand_up_factor_piece = ADAPTER_SCALE * matrix_product_transposed_left(
        adapter_expand_hidden, upper_gradient
    )
    norm_one_cols = lax.dynamic_slice_in_dim(first_norm_output, rank * cols, cols, 1)
    norm_two_cols = lax.dynamic_slice_in_dim(second_norm_output, rank * cols, cols, 1)
    joined_a_piece = matrix_product_transposed_left(norm_one_cols, low_joined_grad)
    expand_a_piece = matrix_product_transposed_left(norm_two_cols, low_expand_grad)
    grad_one, grad_two = (
        lax.psum_scatter(
            matrix_product_transposed_right(mixed_gradient, joined_frozen_weight),
            "mp",
            scatter_dimension=1,
            tiled=True,
        ),
        lax.psum_scatter(
            matrix_product_transposed_right(upper_gradient, expand_frozen_weight),
            "mp",
            scatter_dimension=1,
            tiled=True,
        ),
    )
    joined_rows_a = lax.dynamic_slice_in_dim(joined_a, rank * cols, cols, 0)
    expand_rows_a = lax.dynamic_slice_in_dim(expand_a, rank * cols, cols, 0)
    grad_one = grad_one + matrix_product_transposed_right(low_joined_grad, joined_rows_a)
    grad_two = grad_two + matrix_product_transposed_right(low_expand_grad, expand_rows_a)
    unit_one_cols = lax.dynamic_slice_in_dim(unit_one, rank * cols, cols, 1)
    unit_two_cols = lax.dynamic_slice_in_dim(unit_two, rank * cols, cols, 1)
    gain_one_cols = lax.dynamic_slice_in_dim(first_gain, rank * cols, cols, 0)
    gain_two_cols = lax.dynamic_slice_in_dim(second_gain, rank * cols, cols, 0)
    first_gain_piece = jnp.sum(grad_one * unit_one_cols, 0)
    first_bias_piece = jnp.sum(grad_one, 0)
    second_gain_piece = jnp.sum(grad_two * unit_two_cols, 0)
    second_bias_piece = jnp.sum(grad_two, 0)
    scaled_one = grad_one * gain_one_cols
    scaled_two = grad_two * gain_two_cols
    plain_one, along_one, plain_two, along_two = (
        lax.psum(jnp.sum(scaled_one, -1).astype(jnp.bfloat16), "mp").astype(jnp.float32),
        lax.psum(jnp.sum(scaled_one * unit_one_cols, -1).astype(jnp.bfloat16), "mp").astype(
            jnp.float32
        ),
        lax.psum(jnp.sum(scaled_two, -1).astype(jnp.bfloat16), "mp").astype(jnp.float32),
        lax.psum(jnp.sum(scaled_two * unit_two_cols, -1).astype(jnp.bfloat16), "mp").astype(
            jnp.float32
        ),
    )
    back_one = factor_one * (
        scaled_one - plain_one[:, None] / width - unit_one_cols * along_one[:, None] / width
    )
    back_two = factor_two * (
        scaled_two - plain_two[:, None] / width - unit_two_cols * along_two[:, None] / width
    )
    hidden_grad = cotangent.astype(jnp.float32) + back_one + back_two
    pieces = (
        first_gain_piece,
        first_bias_piece,
        second_gain_piece,
        second_bias_piece,
        joined_a_piece,
        joined_up_factor_piece,
        output_a_piece,
        output_up_factor_piece,
        expand_a_piece,
        expand_up_factor_piece,
        shrink_a_piece,
        shrink_up_factor_piece,
    )
    shapes = (
        first_gain.shape,
        first_bias.shape,
        second_gain.shape,
        second_bias.shape,
        joined_a.shape,
        joined_up_factor.shape,
        output_a.shape,
        output_up_factor.shape,
        expand_a.shape,
        expand_up_factor.shape,
        shrink_a.shape,
        shrink_up_factor.shape,
    )
    along = (0, 0, 0, 0, 0, 1, 0, 1, 0, 1, 0, 1)
    padded = [
        lax.dynamic_update_slice_in_dim(
            jnp.zeros(shape, jnp.float32), piece, rank * piece.shape[axis_dim], axis_dim
        )
        for piece, shape, axis_dim in zip(pieces, shapes, along)
    ]
    grads = lax.psum(
        (
            padded[0],
            padded[1],
            padded[2],
            padded[3],
            padded[4],
            padded[5],
            padded[6],
            padded[7],
            padded[8],
            padded[9],
            padded[10],
            padded[11],
        ),
        ("dp", "mp"),
    )
    return (
        result,
        hidden_grad,
        grads[0],
        grads[1],
        grads[2],
        grads[3],
        grads[4],
        grads[5],
        grads[6],
        grads[7],
        grads[8],
        grads[9],
        grads[10],
        grads[11],
    )


BF = jnp.bfloat16
F32 = jnp.float32
BLOCK = 256
VMEM_LIMIT = 62 << 20


def nn(left, right):
    return lax.dot_general(left, right, (((1,), (0,)), ((), ())), preferred_element_type=F32)


def nt(left, right):
    return lax.dot_general(left, right, (((1,), (1,)), ((), ())), preferred_element_type=F32)


def span(start, size, unit=128):
    return pl.ds(pl.multiple_of(start, unit), size)


def quarter_block(pieces, k, j, blocks):
    if k < 3:
        return pieces[k], j * BLOCK
    half = blocks // 2
    return (pieces[3], j * BLOCK) if j < half else (pieces[4], (j - half) * BLOCK)


def layer_norm(rows_f32):
    center = rows_f32 - jnp.mean(rows_f32, 1, keepdims=True)
    factor = lax.rsqrt(jnp.mean(center * center, 1, keepdims=True) + EPS)
    return center * factor, factor


def attention_kernel(slot, shared, n_w, ids, *refs):
    h_refs, g_refs = refs[0:4], refs[4:8]
    w_refs = refs[8 : 8 + n_w]
    o_own, o_mate = refs[8 + n_w : 10 + n_w]
    o_foreign, o_diag = refs[10 + n_w : 15 + n_w], refs[15 + n_w : 20 + n_w]
    rest = refs[20 + n_w :]
    gain, bias, up, ja, oa, ou, cos_ref, sin_ref = rest[:8]
    rest = rest[8:]
    n_out = 4 if shared else 2
    outs = rest[:n_out]
    (h_v, g_v, w_v, o_v, w_t, q_t, k_t, v_t, k_n, v_n, do_t, dm_t, ctx_t, dk, dv, both, tok_sem, w_sem) = rest[n_out:]
    f, q = ids[0], ids[1]
    seq = h_v.shape[0]
    steps = seq // BLOCK
    heads = q_t.shape[0] // HEAD_DIM
    width = h_v.shape[1]
    piece = width // 4
    for t in range(steps):
        rows = slice(t * BLOCK, (t + 1) * BLOCK)
        for s in range(4):
            cols = slice(s * piece, (s + 1) * piece)
            pltpu.make_async_copy(h_refs[s].at[rows, :], h_v.at[rows, cols], tok_sem.at[0, t]).start()
            pltpu.make_async_copy(g_refs[s].at[rows, :], g_v.at[rows, cols], tok_sem.at[1, t]).start()
    if n_w == 1:
        for s in range(4):
            pltpu.make_async_copy(
                w_refs[0].at[span(lax.bitwise_xor(f, s) * piece, piece), :],
                w_v.at[s * piece : (s + 1) * piece, :],
                w_sem.at[0],
            ).start()
    else:
        for k in range(4):
            row = lax.bitwise_xor(lax.bitwise_xor(q, k), f) * piece
            for j in range(3):
                ref, at = quarter_block(w_refs, k, j, 4)
                pltpu.make_async_copy(
                    ref.at[at : at + BLOCK, :],
                    w_v.at[span(row, piece), j * BLOCK : (j + 1) * BLOCK],
                    w_sem.at[0],
                ).start()
    head_block = lax.bitwise_xor(f, slot)
    for s, ref in ((0, o_own), (1, o_mate)):
        pltpu.make_async_copy(
            ref.at[span(head_block * BLOCK, BLOCK), :], o_v.at[:, s * piece : (s + 1) * piece], w_sem.at[1]
        ).start()
    for s, pieces in ((2, o_foreign), (3, o_diag)):
        for k in range(4):
            ref, at = quarter_block(pieces, k, 3, 4)

            @pl.when(lax.bitwise_xor(q, k) == head_block)
            def _():
                pltpu.make_async_copy(
                    ref.at[at : at + BLOCK, :], o_v.at[:, s * piece : (s + 1) * piece], w_sem.at[1]
                ).start()

    pltpu.make_async_copy(w_v, w_v, w_sem.at[0]).wait()
    pltpu.make_async_copy(o_v, o_v, w_sem.at[1]).wait()
    w_t[...] = w_v[...].T
    up_t = up[...].T
    o_rows = o_v[...]

    def project(t):
        rows = slice(t * BLOCK, (t + 1) * BLOCK)
        pltpu.make_async_copy(h_v.at[rows, :], h_v.at[rows, :], tok_sem.at[0, t]).wait()
        pltpu.make_async_copy(g_v.at[rows, :], g_v.at[rows, :], tok_sem.at[1, t]).wait()
        unit, _ = layer_norm(h_v[rows, :].astype(F32))
        n = (unit * gain[...] + bias[...]).astype(BF)
        low = (nn(n, ja[...]).astype(BF) * ADAPTER_SCALE).astype(BF)
        mixed = nt(w_t[...], n) + nt(up_t, low)
        cos, sin = cos_ref[:, rows], sin_ref[:, rows]
        half = ROTARY // 2
        for h in range(heads):
            own = slice(h * HEAD_DIM, (h + 1) * HEAD_DIM)
            base = 3 * HEAD_DIM * h
            for part in range(2):
                block = mixed[base + part * HEAD_DIM : base + (part + 1) * HEAD_DIM]
                a, b = block[:half], block[half:ROTARY]
                block = jnp.concatenate([a * cos - b * sin, b * cos + a * sin, block[ROTARY:]], 0).astype(BF)
                if part == 0:
                    q_t[own, rows] = (block * HEAD_DIM ** (-0.5)).astype(BF)
                else:
                    k_t[own, rows] = block
                    k_n[rows, own] = block.T
            block = mixed[base + 2 * HEAD_DIM : base + 3 * HEAD_DIM].astype(BF)
            v_t[own, rows] = block
            v_n[rows, own] = block.T
        g = g_v[rows, :]
        low_grad = (nt(g, ou[...]) * ADAPTER_SCALE).astype(BF)
        do_t[:, rows] = (nt(o_rows, g) + nt(oa[...], low_grad)).astype(BF)

    for t in range(steps):
        project(t)

    later = lax.broadcasted_iota(jnp.int32, (BLOCK, BLOCK), 0) > lax.broadcasted_iota(jnp.int32, (BLOCK, BLOCK), 1)
    state = {}

    def products(h, i):
        own, qs = slice(h * HEAD_DIM, (h + 1) * HEAD_DIM), slice(i * BLOCK, (i + 1) * BLOCK)
        state[h, i] = (
            [nn(k_n[j * BLOCK : (j + 1) * BLOCK, own], q_t[own, qs]) for j in range(i + 1)],
            [nn(v_n[j * BLOCK : (j + 1) * BLOCK, own], do_t[own, qs]) for j in range(i + 1)],
        )

    def soft(h, i):
        scores, d_probs = state[h, i]
        scores[-1] = jnp.where(later, -1e30, scores[-1])
        peak = reduce(jnp.maximum, [jnp.max(s, 0, keepdims=True) for s in scores])
        weights = [jnp.exp(s - peak) for s in scores]
        inverse = 1.0 / reduce(jnp.add, [jnp.sum(w, 0, keepdims=True) for w in weights])
        probs = [w * inverse for w in weights]
        inner = reduce(jnp.add, [jnp.sum(p * d, 0, keepdims=True) for p, d in zip(probs, d_probs)])
        state[h, i] = (
            [p.astype(BF) for p in probs],
            [(p * (d - inner)).astype(BF) for p, d in zip(probs, d_probs)],
        )

    def unturn(block, cos, sin):
        half = ROTARY // 2
        a, b = block[:half], block[half:ROTARY]
        return jnp.concatenate([a * cos + b * sin, b * cos - a * sin, block[ROTARY:]], 0).astype(BF)

    def finish_block(h, i):
        own, qs = slice(h * HEAD_DIM, (h + 1) * HEAD_DIM), slice(i * BLOCK, (i + 1) * BLOCK)
        base = 3 * HEAD_DIM * h
        probs, d_scores = state.pop((h, i))
        keys = slice(0, (i + 1) * BLOCK)
        ctx_t[own, qs] = nn(v_t[own, keys], jnp.concatenate(probs, 0)).astype(BF)
        d_query = nn(k_t[own, keys], jnp.concatenate(d_scores, 0)) * HEAD_DIM ** (-0.5)
        dm_t[base : base + HEAD_DIM, qs] = unturn(d_query, cos_ref[:, qs], sin_ref[:, qs])
        query, d_out = q_t[own, qs], do_t[own, qs]
        for j in range(i + 1):
            js = slice(j * BLOCK, (j + 1) * BLOCK)
            if j == i:
                dk[own, js] = nt(query, d_scores[j])
                dv[own, js] = nt(d_out, probs[j])
            else:
                dk[own, js] += nt(query, d_scores[j])
                dv[own, js] += nt(d_out, probs[j])
        if i == steps - 1:
            dm_t[base + HEAD_DIM : base + 2 * HEAD_DIM, :] = unturn(dk[own, :], cos_ref[...], sin_ref[...])
            dm_t[base + 2 * HEAD_DIM : base + 3 * HEAD_DIM, :] = dv[own, :].astype(BF)

    order = [(h, i) for h in range(heads) for i in range(steps)]
    for at in range(len(order) + 2):
        if at < len(order):
            products(*order[at])
        if at >= 2:
            finish_block(*order[at - 2])
        if 1 <= at <= len(order):
            soft(*order[at - 1])
    both[:, :BLOCK] = ctx_t[...].T
    both[:, BLOCK:] = dm_t[...].T
    if shared:
        for s in range(4):
            outs[s][...] = both[span(lax.bitwise_xor(f, s) * BLOCK, BLOCK), :]
    else:
        c = lax.bitwise_and(f, 1)
        half = seq // 2
        outs[0][...] = both[span(c * half, half), :]
        outs[1][...] = both[span((1 - c) * half, half), :]


def any_spec():
    return pl.BlockSpec(memory_space=pl.ANY)


def vmem_spec():
    return pl.BlockSpec(memory_space=pltpu.VMEM)


def smem_spec():
    return pl.BlockSpec(memory_space=pltpu.SMEM)


def attention(slot, shared, ids, hs, gs, ws, os, gain, bias, up, ja, oa, ou, cos, sin):
    seq, piece = hs[0].shape
    width = 4 * piece
    shard = up.shape[1] // 4
    heads = shard // (3 * HEAD_DIM)
    inner = heads * HEAD_DIM
    rank = ja.shape[1]
    n_w = len(ws)
    if shared:
        out_shape = [jax.ShapeDtypeStruct((BLOCK, inner + shard), BF)] * 4
    else:
        out_shape = [jax.ShapeDtypeStruct((seq // 2, inner + shard), BF)] * 2
    return pl.pallas_call(
        partial(attention_kernel, slot, shared, n_w),
        in_specs=[smem_spec()] + [any_spec()] * (8 + n_w + 12) + [vmem_spec()] * 8,
        out_specs=[vmem_spec()] * len(out_shape),
        out_shape=out_shape,
        scratch_shapes=[
            pltpu.VMEM((seq, width), BF),
            pltpu.VMEM((seq, width), BF),
            pltpu.VMEM((width, shard), BF),
            pltpu.VMEM((inner, width), BF),
            pltpu.VMEM((shard, width), BF),
            pltpu.VMEM((inner, seq), BF),
            pltpu.VMEM((inner, seq), BF),
            pltpu.VMEM((inner, seq), BF),
            pltpu.VMEM((seq, inner), BF),
            pltpu.VMEM((seq, inner), BF),
            pltpu.VMEM((inner, seq), BF),
            pltpu.VMEM((shard, seq), BF),
            pltpu.VMEM((inner, seq), BF),
            pltpu.VMEM((inner, seq), F32),
            pltpu.VMEM((inner, seq), F32),
            pltpu.VMEM((seq, inner + shard), BF),
            pltpu.SemaphoreType.DMA((2, seq // BLOCK)),
            pltpu.SemaphoreType.DMA((2,)),
        ],
        compiler_params=pltpu.CompilerParams(vmem_limit_bytes=VMEM_LIMIT),
        cost_estimate=pl.CostEstimate(flops=22_000_000_000, bytes_accessed=12_000_000, transcendentals=3_000_000),
        name="attention",
    )(
        ids, *hs, *gs, *ws, *os, gain, bias,
        lax.slice_in_dim(up, slot * shard, (slot + 1) * shard, axis=1),
        ja,
        lax.slice_in_dim(oa, slot * inner, (slot + 1) * inner, axis=0),
        ou, cos, sin,
    )


def token_copies(ids, own_refs, shared_refs, dst, sem):
    f = ids[0]
    c = lax.bitwise_and(f, 1)
    half = own_refs[0].shape[0] // 2
    piece = own_refs[0].shape[1]
    for s in range(4):
        cols = slice(s * piece, (s + 1) * piece)
        pltpu.make_async_copy(own_refs[s].at[span(c * half, half), :], dst.at[:half, cols], sem).start()
        pltpu.make_async_copy(
            shared_refs[s].at[span(f * BLOCK, BLOCK), :], dst.at[half : half + BLOCK, cols], sem
        ).start()


def arrived(dst, sem):
    pltpu.make_async_copy(dst, dst, sem).wait()


def finish_kernel(ids, *refs):
    h_own, h_sh, g_own, g_sh = refs[0:4], refs[4:8], refs[8:12], refs[12:16]
    a_own, a_sh = refs[16:20], refs[20:24]
    w_own, w_mate, o_own, o_mate = refs[24:28]
    p_foreign, p_diag = refs[28:33], refs[33:38]
    gain, bias, up, ja, oa, ou = refs[38:44]
    attn, e_one, grads, sums = refs[44:48]
    h_v, g_v, c_v, m_v, w_v, o_v, sem = refs[48:]
    f, q = ids[0], ids[1]
    rows, width = h_v.shape
    piece = width // 4
    half = rows - BLOCK
    shard = m_v.shape[1] // 4
    token_copies(ids, h_own, h_sh, h_v, sem.at[0])
    token_copies(ids, g_own, g_sh, g_v, sem.at[1])
    for s in range(4):
        for src, dst in ((a_own[s], slice(0, half)), (a_sh[s], slice(half, rows))):
            pltpu.make_async_copy(src.at[:, :BLOCK], c_v.at[dst, s * BLOCK : (s + 1) * BLOCK], sem.at[2]).start()
            pltpu.make_async_copy(src.at[:, BLOCK:], m_v.at[dst, s * shard : (s + 1) * shard], sem.at[3]).start()
    for s, o_ref, w_ref in ((0, o_own, w_own), (1, o_mate, w_mate)):
        for t in range(4):
            src, dst = span(lax.bitwise_xor(f, t) * piece, piece), slice(t * piece, (t + 1) * piece)
            pltpu.make_async_copy(o_ref.at[src, :], o_v.at[dst, s * piece : (s + 1) * piece], sem.at[4]).start()
            pltpu.make_async_copy(w_ref.at[src, :], w_v.at[dst, s * shard : (s + 1) * shard], sem.at[5]).start()
    for s, pieces in ((2, p_foreign), (3, p_diag)):
        for k in range(4):
            dst = span(lax.bitwise_xor(lax.bitwise_xor(q, k), f) * piece, piece)
            ref, at = quarter_block(pieces, k, 3, 4)
            pltpu.make_async_copy(
                ref.at[at : at + BLOCK, :], o_v.at[dst, s * piece : (s + 1) * piece], sem.at[4]
            ).start()
            for j in range(3):
                ref, at = quarter_block(pieces, k, j, 4)
                pltpu.make_async_copy(
                    ref.at[at : at + BLOCK, :],
                    w_v.at[dst, s * shard + j * BLOCK : s * shard + (j + 1) * BLOCK],
                    sem.at[5],
                ).start()
    for i, dst in ((0, h_v), (1, g_v), (2, c_v), (4, o_v)):
        arrived(dst, sem.at[i])
    g = g_v[...]
    ctx = c_v[...]
    low_out = nn(ctx, oa[...]).astype(BF)
    low_out = (low_out * ADAPTER_SCALE).astype(BF)
    for t in range(rows // BLOCK):
        ts = slice(t * BLOCK, (t + 1) * BLOCK)
        attn[ts, :] = nn(c_v[ts, :], o_v[...]) + nn(low_out[ts], ou[...])
    low_out_grad = (nt(g, ou[...]) * ADAPTER_SCALE).astype(BF)

    def put(base, size, value):
        for s in range(4):
            grads[:, span(base + lax.bitwise_xor(f, s) * size, size)] = value[:, s * size : (s + 1) * size]

    put(0, piece, nn(low_out.T, g))
    put(width, piece, nn(low_out_grad.T, ctx))
    arrived(m_v, sem.at[3])
    arrived(w_v, sem.at[5])
    unit, _ = layer_norm(h_v[...].astype(F32))
    n = (unit * gain[...] + bias[...]).astype(BF)
    low = (nn(n, ja[...]).astype(BF) * ADAPTER_SCALE).astype(BF)
    low_grad = (nt(m_v[...], up[...]) * ADAPTER_SCALE).astype(BF)
    put(2 * width, shard, nn(low.T, m_v[...]))
    put(2 * width + 4 * shard, piece, nn(low_grad.T, n))
    total = [None, None]
    for t in range(rows // BLOCK):
        ts = slice(t * BLOCK, (t + 1) * BLOCK)
        d_norm = nt(m_v[ts, :], w_v[...]) + nt(low_grad[ts], ja[...])
        part = (jnp.sum(d_norm * unit[ts], 0, keepdims=True), jnp.sum(d_norm, 0, keepdims=True))
        total = [p if o is None else o + p for o, p in zip(total, part)]
        e_one[ts, :] = d_norm * gain[...]
    put_sums(sums, f, total)


def put_sums(sums, f, total):
    piece = sums.shape[1] // 4
    value = jnp.concatenate(list(total) + [jnp.zeros((6, sums.shape[1]), F32)], 0)
    for s in range(4):
        sums[:, span(lax.bitwise_xor(f, s) * piece, piece)] = value[:, s * piece : (s + 1) * piece]


def finish_tokens(ids, hs, hsh, gs, gsh, a_own, a_sh, weights, gain, bias, up, ja, oa, ou):
    seq, piece = hs[0].shape
    width = 4 * piece
    rows = seq // 2 + BLOCK
    shard = up.shape[1] // 4
    rank = ja.shape[1]
    return pl.pallas_call(
        finish_kernel,
        in_specs=[smem_spec()] + [any_spec()] * 38 + [vmem_spec()] * 6,
        out_specs=[vmem_spec()] * 4,
        out_shape=[
            jax.ShapeDtypeStruct((rows, width), F32),
            jax.ShapeDtypeStruct((rows, width), F32),
            jax.ShapeDtypeStruct((rank, 3 * width + 4 * shard), F32),
            jax.ShapeDtypeStruct((8, width), F32),
        ],
        scratch_shapes=[
            pltpu.VMEM((rows, width), BF),
            pltpu.VMEM((rows, width), BF),
            pltpu.VMEM((rows, width), BF),
            pltpu.VMEM((rows, 4 * shard), BF),
            pltpu.VMEM((width, 4 * shard), BF),
            pltpu.VMEM((width, width), BF),
            pltpu.SemaphoreType.DMA((6,)),
        ],
        compiler_params=pltpu.CompilerParams(vmem_limit_bytes=VMEM_LIMIT),
        cost_estimate=pl.CostEstimate(flops=18_000_000_000, bytes_accessed=30_000_000, transcendentals=1000),
        name="finish_attention",
    )(ids, *hs, *hsh, *gs, *gsh, *a_own, *a_sh, *weights, gain, bias, up, ja, oa, ou)


def load_mlp_weights(ids, e_own, e_mate, s_own, s_mate, p_foreign, p_diag, e_v, s_v, e_sem, s_sem, chunk):
    f, q = ids[0], ids[1]
    width, hidden = e_v.shape
    piece, part = width // 4, hidden // 4
    per = part // chunk
    for s, e_ref, s_ref in ((0, e_own, s_own), (1, e_mate, s_mate)):
        for u in range(per):
            for t in range(4):
                pltpu.make_async_copy(
                    e_ref.at[span(lax.bitwise_xor(f, t) * piece, piece), u * chunk : (u + 1) * chunk],
                    e_v.at[t * piece : (t + 1) * piece, s * part + u * chunk : s * part + (u + 1) * chunk],
                    e_sem.at[s * per + u],
                ).start()
        for t in range(4):
            for u in range(per):
                pltpu.make_async_copy(
                    s_ref.at[span(lax.bitwise_xor(f, t) * part + u * chunk, chunk), :],
                    s_v.at[t * part + u * chunk : t * part + (u + 1) * chunk, s * piece : (s + 1) * piece],
                    s_sem.at[t * per + u],
                ).start()
    blocks = 2 * part // BLOCK
    for s, pieces in ((2, p_foreign), (3, p_diag)):
        for k in range(4):
            place = lax.bitwise_xor(lax.bitwise_xor(q, k), f)
            for j in range(part // BLOCK):
                ref, at = quarter_block(pieces, k, j, blocks)
                pltpu.make_async_copy(
                    ref.at[at : at + BLOCK, :],
                    e_v.at[span(place * piece, piece), s * part + j * BLOCK : s * part + (j + 1) * BLOCK],
                    e_sem.at[s * per + j * BLOCK // chunk],
                ).start()
            for u in range(per):
                ref, at = quarter_block(pieces, k, part // BLOCK + u * chunk // BLOCK, blocks)
                pltpu.make_async_copy(
                    ref.at[at : at + chunk, :],
                    s_v.at[span(place * part + u * chunk, chunk), s * piece : (s + 1) * piece],
                    s_sem.at[place * per + u],
                ).start()


CHUNK = 512


def mlp_first_kernel(ids, *refs):
    h_own, h_sh, g_own, g_sh = refs[0:4], refs[4:8], refs[8:12], refs[12:16]
    weights = refs[16:30]
    gain, bias, ea, eu, sa, su = refs[30:36]
    act_out, dup_out, ls_out, dle_out, grads = refs[36:41]
    h_v, g_v, n_v, e_v, s_v, act, dup, sem, e_sem, s_sem, o_sem = refs[41:]
    f = ids[0]
    rows, width = h_v.shape
    hidden = e_v.shape[1]
    token_copies(ids, h_own, h_sh, h_v, sem.at[0])
    token_copies(ids, g_own, g_sh, g_v, sem.at[1])
    load_mlp_weights(
        ids, weights[0], weights[1], weights[2], weights[3], weights[4:9], weights[9:14], e_v, s_v, e_sem, s_sem, CHUNK
    )
    arrived(h_v, sem.at[0])
    unit, _ = layer_norm(h_v[...].astype(F32))
    n_v[...] = (unit * gain[...] + bias[...]).astype(BF)
    low = (nn(n_v[...], ea[...]).astype(BF) * ADAPTER_SCALE).astype(BF)
    arrived(g_v, sem.at[1])
    low_grad = (nt(g_v[...], su[...]) * ADAPTER_SCALE).astype(BF)
    state = {}

    def products(b, t):
        ts, bs = slice(t * BLOCK, (t + 1) * BLOCK), slice(b * CHUNK, (b + 1) * CHUNK)
        if t == 0:
            arrived(e_v.at[:, bs], e_sem.at[b])
            arrived(s_v.at[bs, :], s_sem.at[b])
        state[b, t] = (
            nn(n_v[ts, :], e_v[:, bs]) + nn(low[ts], eu[:, bs]),
            nt(g_v[ts, :], s_v[bs, :]) + nt(low_grad[ts], sa[bs, :]),
        )

    def bend(b, t):
        ts, bs = slice(t * BLOCK, (t + 1) * BLOCK), slice(b * CHUNK, (b + 1) * CHUNK)
        upper, d_active = state.pop((b, t))
        normal = 0.5 * (1.0 + lax.erf(upper * 0.7071067811865476))
        density = jnp.exp(-0.5 * upper * upper) * 0.3989422804014327
        act[ts, bs] = (upper * normal).astype(BF)
        dup[ts, bs] = (d_active * (normal + upper * density)).astype(BF)
        if t == rows // BLOCK - 1:
            pltpu.make_async_copy(act.at[:, bs], act_out.at[:, bs], o_sem.at[0]).start()
            pltpu.make_async_copy(dup.at[:, bs], dup_out.at[:, bs], o_sem.at[1]).start()

    order = [(b, t) for b in range(hidden // CHUNK) for t in range(rows // BLOCK)]
    for at in range(len(order) + 1):
        if at < len(order):
            products(*order[at])
        if at > 0:
            bend(*order[at - 1])

    part, piece = hidden // 4, width // 4

    def put(base, size, value):
        for s in range(4):
            grads[:, span(base + lax.bitwise_xor(f, s) * size, size)] = value[:, s * size : (s + 1) * size]

    put(0, part, nn(low_grad.T, act[...]))
    put(hidden, part, nn(low.T, dup[...]))
    low_shrink = (nn(act[...], sa[...]).astype(BF) * ADAPTER_SCALE).astype(BF)
    low_expand_grad = (nt(dup[...], eu[...]) * ADAPTER_SCALE).astype(BF)
    ls_out[...] = low_shrink
    dle_out[...] = low_expand_grad
    put(2 * hidden, piece, nn(low_shrink.T, g_v[...]))
    put(2 * hidden + width, piece, nn(low_expand_grad.T, n_v[...]))
    arrived(act, o_sem.at[0])
    arrived(dup, o_sem.at[1])


def mlp_first(ids, hs, hsh, gs, gsh, weights, gain, bias, ea, eu, sa, su):
    seq, piece = hs[0].shape
    width = 4 * piece
    rows = seq // 2 + BLOCK
    hidden = eu.shape[1]
    rank = ea.shape[1]
    return pl.pallas_call(
        mlp_first_kernel,
        in_specs=[smem_spec()] + [any_spec()] * 30 + [vmem_spec()] * 6,
        out_specs=[any_spec()] * 2 + [vmem_spec()] * 3,
        out_shape=[
            jax.ShapeDtypeStruct((rows, hidden), BF),
            jax.ShapeDtypeStruct((rows, hidden), BF),
            jax.ShapeDtypeStruct((rows, rank), BF),
            jax.ShapeDtypeStruct((rows, rank), BF),
            jax.ShapeDtypeStruct((rank, 2 * hidden + 2 * width), F32),
        ],
        scratch_shapes=[
            pltpu.VMEM((rows, width), BF),
            pltpu.VMEM((rows, width), BF),
            pltpu.VMEM((rows, width), BF),
            pltpu.VMEM((width, hidden), BF),
            pltpu.VMEM((hidden, width), BF),
            pltpu.VMEM((rows, hidden), BF),
            pltpu.VMEM((rows, hidden), BF),
            pltpu.SemaphoreType.DMA((2,)),
            pltpu.SemaphoreType.DMA((hidden // CHUNK,)),
            pltpu.SemaphoreType.DMA((hidden // CHUNK,)),
            pltpu.SemaphoreType.DMA((2,)),
        ],
        compiler_params=pltpu.CompilerParams(vmem_limit_bytes=VMEM_LIMIT),
        cost_estimate=pl.CostEstimate(flops=28_000_000_000, bytes_accessed=40_000_000, transcendentals=3_000_000),
        name="mlp_first",
    )(ids, *hs, *hsh, *gs, *gsh, *weights, gain, bias, ea, eu, sa, su)


def mlp_second_kernel(ids, *refs):
    h_own, h_sh, g_own, g_sh = refs[0:4], refs[4:8], refs[8:12], refs[12:16]
    weights = refs[16:30]
    act_ref, dup_ref, attn_ref, e_ref = refs[30:34]
    gain, ea, su, ls, dle = refs[34:39]
    r_outs, g_outs, sums = refs[39:43], refs[43:47], refs[47]
    h_v, g_v, e_v, s_v, act, dup, attn, e_one, sem, e_sem, s_sem = refs[48:]
    f = ids[0]
    rows, width = h_v.shape
    hidden = e_v.shape[1]
    piece = width // 4
    pltpu.make_async_copy(act_ref, act, sem.at[2]).start()
    load_mlp_weights(
        ids, weights[0], weights[1], weights[2], weights[3], weights[4:9], weights[9:14], e_v, s_v, e_sem, s_sem, hidden // 4
    )
    pltpu.make_async_copy(dup_ref, dup, sem.at[3]).start()
    token_copies(ids, h_own, h_sh, h_v, sem.at[0])
    pltpu.make_async_copy(attn_ref, attn, sem.at[4]).start()
    token_copies(ids, g_own, g_sh, g_v, sem.at[1])
    pltpu.make_async_copy(e_ref, e_one, sem.at[5]).start()
    part = hidden // 4
    arrived(act, sem.at[2])
    for b in range(4):
        arrived(s_v.at[b * part : (b + 1) * part, :], s_sem.at[b])
    arrived(h_v, sem.at[0])
    arrived(attn, sem.at[4])
    for t in range(rows // BLOCK):
        ts = slice(t * BLOCK, (t + 1) * BLOCK)
        value = nn(act[ts, :], s_v[...]) + nn(ls[ts, :], su[...])
        value = (h_v[ts, :].astype(F32) + attn[ts, :] + value).astype(BF)
        for s in range(4):
            r_outs[s][ts, :] = value[:, s * piece : (s + 1) * piece]
    arrived(dup, sem.at[3])
    for b in range(4):
        arrived(e_v.at[:, b * part : (b + 1) * part], e_sem.at[b])
    arrived(g_v, sem.at[1])
    arrived(e_one, sem.at[5])
    total = [None, None]
    for t in range(rows // BLOCK):
        ts = slice(t * BLOCK, (t + 1) * BLOCK)
        d_norm = nt(dup[ts, :], e_v[...]) + nt(dle[ts, :], ea[...])
        unit, factor = layer_norm(h_v[ts, :].astype(F32))
        sums_here = (jnp.sum(d_norm * unit, 0, keepdims=True), jnp.sum(d_norm, 0, keepdims=True))
        total = [p if o is None else o + p for o, p in zip(total, sums_here)]
        e = d_norm * gain[...] + e_one[ts, :]
        plain = jnp.mean(e, 1, keepdims=True)
        along = jnp.mean(e * unit, 1, keepdims=True)
        value = g_v[ts, :].astype(F32) + factor * (e - plain - unit * along)
        for s in range(4):
            g_outs[s][ts, :] = value[:, s * piece : (s + 1) * piece].astype(g_outs[s].dtype)
    put_sums(sums, f, total)


def mlp_second(ids, hs, hsh, gs, gsh, weights, act, dup, attn, e_one, gain, ea, su, ls, dle):
    seq, piece = hs[0].shape
    width = 4 * piece
    rows = seq // 2 + BLOCK
    hidden = act.shape[1]
    return pl.pallas_call(
        mlp_second_kernel,
        in_specs=[smem_spec()] + [any_spec()] * 34 + [vmem_spec()] * 5,
        out_specs=[vmem_spec()] * 9,
        out_shape=[jax.ShapeDtypeStruct((rows, piece), BF)] * 4
        + [
            jax.ShapeDtypeStruct((rows, piece), F32),
            jax.ShapeDtypeStruct((rows, piece), F32),
            jax.ShapeDtypeStruct((rows, piece), BF),
            jax.ShapeDtypeStruct((rows, piece), BF),
            jax.ShapeDtypeStruct((8, width), F32),
        ],
        scratch_shapes=[
            pltpu.VMEM((rows, width), BF),
            pltpu.VMEM((rows, width), BF),
            pltpu.VMEM((width, hidden), BF),
            pltpu.VMEM((hidden, width), BF),
            pltpu.VMEM((rows, hidden), BF),
            pltpu.VMEM((rows, hidden), BF),
            pltpu.VMEM((rows, width), F32),
            pltpu.VMEM((rows, width), F32),
            pltpu.SemaphoreType.DMA((6,)),
            pltpu.SemaphoreType.DMA((4,)),
            pltpu.SemaphoreType.DMA((4,)),
        ],
        compiler_params=pltpu.CompilerParams(vmem_limit_bytes=VMEM_LIMIT),
        cost_estimate=pl.CostEstimate(flops=20_000_000_000, bytes_accessed=45_000_000, transcendentals=1000),
        name="mlp_second",
    )(ids, *hs, *hsh, *gs, *gsh, *weights, act, dup, attn, e_one, gain, ea, su, ls, dle)


def gather_rows_kernel(widen, ids, *refs):
    parts, out = refs[:4], refs[4]
    scratch = refs[5:]
    f = ids[0]
    sem = scratch[-1]
    rows = parts[0].shape[0]
    half = rows - BLOCK
    seq = 2 * half
    copies = []
    for s in range(4):
        src = parts[s]
        if src.dtype != out.dtype:
            scratch[s - 2][...] = src[...].astype(out.dtype)
            src = scratch[s - 2]
        at = lax.bitwise_xor(f, s)
        copies.append(pltpu.make_async_copy(src.at[:half, :], out.at[span(at * half, half), :], sem.at[2 * s]))
        copies.append(
            pltpu.make_async_copy(src.at[half:, :], out.at[span(2 * seq + at * BLOCK, BLOCK), :], sem.at[2 * s + 1])
        )
        copies[-2].start()
        copies[-1].start()
    for copy in copies:
        copy.wait()


def gather_rows(ids, parts, dtype):
    rows, piece = parts[0].shape
    narrow = [p for p in parts if p.dtype != dtype]
    return pl.pallas_call(
        partial(gather_rows_kernel, dtype),
        in_specs=[smem_spec()] + [vmem_spec()] * 4,
        out_specs=any_spec(),
        out_shape=jax.ShapeDtypeStruct((4 * rows, piece), dtype),
        scratch_shapes=[pltpu.VMEM((rows, piece), dtype)] * len(narrow) + [pltpu.SemaphoreType.DMA((8,))],
        compiler_params=pltpu.CompilerParams(vmem_limit_bytes=VMEM_LIMIT),
        name="gather_rows",
    )(ids, *parts)


def swap(axis, bit):
    def run(value):
        size = lax.axis_size(axis)
        return lax.ppermute(value, axis, [(i, i ^ bit) for i in range(size)])

    return run


def after(value, *others):
    return lax.optimization_barrier((value, *others))[0]


def spread(first, to_y, to_z, to_core):
    half = first.shape[0] // 2
    by_y = to_y(first)
    by_z = to_z(first)
    third = to_y(lax.slice_in_dim(by_z, 0, half, axis=0))
    fourth = to_z(lax.slice_in_dim(by_y, half, 2 * half, axis=0))
    pieces = (first, by_y, by_z, third, fourth)
    return pieces, tuple(to_core(p) for p in pieces)


def all_sum(value, bits, swaps, types):
    for bit, exchange, dtype in zip(bits, swaps, types):
        half = value.shape[0] // 2
        keep = lax.dynamic_slice_in_dim(value, bit * half, half, 0)
        send = lax.dynamic_slice_in_dim(value, (1 - bit) * half, half, 0)
        value = keep + exchange(send.astype(dtype)).astype(F32)
    value = value.astype(BF)
    for bit, exchange in reversed(list(zip(bits, swaps))):
        other = exchange(value)
        value = jnp.where(bit == 0, jnp.concatenate([value, other], 0), jnp.concatenate([other, value], 0))
    return value.astype(F32)


def on_device_by_tokens(
    hidden,
    first_gain,
    first_bias,
    second_gain,
    second_bias,
    joined_frozen_weight,
    output_frozen_weight,
    expand_frozen_weight,
    shrink_frozen_weight,
    joined_a,
    joined_up_factor,
    output_a,
    output_up_factor,
    expand_a,
    expand_up_factor,
    shrink_a,
    shrink_up_factor,
    cotangent,
):
    f = lax.axis_index("mp")
    d = lax.axis_index("dp")
    x, c, q = f // 2, f % 2, d % 4
    seq = SEQ_LEN
    width = 4 * hidden.shape[1]
    hidden_units = 4 * expand_frozen_weight.shape[1]
    ids = jnp.stack([f, q]).astype(jnp.int32)
    to_core, to_x, to_diag = swap("mp", 1), swap("mp", 2), swap("mp", 3)
    to_y, to_z, to_far = swap("dp", 1), swap("dp", 2), swap("dp", 4)

    def rows_of(array, at):
        return lax.dynamic_slice_in_dim(array, at * seq, seq, 0)

    def quarter(w):
        size = w.shape[0] // 4
        return lax.dynamic_slice_in_dim(w, q * size, size, 0)

    def columns(w):
        return [lax.slice_in_dim(w, i, i + BLOCK, axis=1) for i in range(0, w.shape[1], BLOCK)]

    pack_one = jnp.concatenate(columns(quarter(joined_frozen_weight)) + [quarter(output_frozen_weight)], 0)
    pack_two = jnp.concatenate(columns(quarter(expand_frozen_weight)) + [quarter(shrink_frozen_weight)], 0)

    def features(array):
        own, other, shared = rows_of(array, x), rows_of(array, 1 - x), array[2 * seq :]
        return own, other, shared

    h_own, h_other, h_shared = features(hidden)
    g_own, g_other, g_shared = features(cotangent)
    first_one = to_x(pack_one)
    hx_own = to_x(h_other)
    gx_own = to_x(after(g_other, first_one))
    hx_shared = to_x(after(h_shared, hx_own))
    gx_shared = to_x(after(g_shared, gx_own))
    first_two = to_x(after(pack_two, hx_shared))
    hs = (h_own, to_core(h_own), hx_own, to_core(hx_own))
    gs = (g_own, to_core(g_own), gx_own, to_core(gx_own))
    hsh = (h_shared, to_core(h_shared), hx_shared, to_core(hx_shared))
    gsh = (g_shared, to_core(g_shared), gx_shared, to_core(gx_shared))
    foreign_one, diag_one = spread(first_one, to_y, to_z, to_core)
    foreign_two, diag_two = spread(first_two, to_y, to_z, to_core)
    w_mate, o_mate = to_core(joined_frozen_weight), to_core(output_frozen_weight)
    e_mate, s_mate = to_core(expand_frozen_weight), to_core(shrink_frozen_weight)

    def ordered(array, axis):
        size = array.shape[axis] // 4
        return jnp.concatenate(
            [lax.dynamic_slice_in_dim(array, (f ^ s) * size, size, axis) for s in range(4)], axis
        )

    gain_one, bias_one, gain_two, bias_two = (
        ordered(v, 0)[None, :] for v in (first_gain, first_bias, second_gain, second_bias)
    )
    ja, oa, ea, sa = (ordered(v, 0) for v in (joined_a, output_a, expand_a, shrink_a))
    ju, ou, eu, su = (ordered(v, 1) for v in (joined_up_factor, output_up_factor, expand_up_factor, shrink_up_factor))
    position = jnp.arange(seq, dtype=F32)[None, :]
    frequency = 10000.0 ** (-(jnp.arange(ROTARY // 2, dtype=F32) * 2.0) / ROTARY)
    angles = frequency[:, None] * position
    cos, sin = jnp.cos(angles), jnp.sin(angles)

    o_parts = (output_frozen_weight, o_mate) + foreign_one + diag_one
    shared_args = (gain_one, bias_one, ju, ja, oa, ou, cos, sin)
    keep_a, send_a = attention(0, False, ids, hs, gs, (joined_frozen_weight,), o_parts, *shared_args)
    b_parts = attention(0, True, ids, hsh, gsh, (joined_frozen_weight,), o_parts, *shared_args)
    keep_c, send_c = attention(2, False, ids, hs, gs, foreign_one, o_parts, *shared_args)
    a_own = (keep_a, to_core(send_a), keep_c, to_core(send_c))
    a_shared = (b_parts[0], to_core(b_parts[1]), to_x(b_parts[2]), to_diag(b_parts[3]))

    attn, e_one, grads_one, sums_one = finish_tokens(
        ids, hs, hsh, gs, gsh, a_own, a_shared,
        (joined_frozen_weight, w_mate, output_frozen_weight, o_mate) + foreign_one + diag_one,
        gain_one, bias_one, ju, ja, oa, ou,
    )
    mlp_weights = (expand_frozen_weight, e_mate, shrink_frozen_weight, s_mate) + foreign_two + diag_two
    act, dup, ls, dle, grads_two = mlp_first(
        ids, hs, hsh, gs, gsh, mlp_weights, gain_two, bias_two, ea, eu, sa, su
    )
    outs = mlp_second(
        ids, hs, hsh, gs, gsh, mlp_weights, act, dup, attn, e_one, gain_two, ea, su, ls, dle
    )
    r, g, sums_two = outs[0:4], outs[4:8], outs[8]
    result = gather_rows(ids, (r[0], to_core(r[1]), to_x(r[2]), to_diag(r[3])), BF)
    hidden_grad = gather_rows(ids, (g[0], to_core(g[1]), to_x(g[2]), to_diag(g[3])), F32)

    bits = (c, d % 2, (d // 2) % 2, d // 4, x)
    swaps = (to_core, to_y, to_z, to_far, to_x)
    types = (F32, BF, BF, BF, F32)
    grads_one = all_sum(grads_one, bits, swaps, types)
    grads_two = all_sum(grads_two, bits, swaps, types)
    sums = lax.psum(jnp.concatenate([sums_one[:2], sums_two[:2]], 0), ("dp", "mp"))
    shard_total = ju.shape[1]

    def cut(array, at, size):
        return lax.slice_in_dim(array, at, at + size, axis=1)

    return (
        result,
        hidden_grad,
        sums[0],
        sums[1],
        sums[2],
        sums[3],
        cut(grads_one, 2 * width + shard_total, width).T,
        cut(grads_one, 2 * width, shard_total),
        cut(grads_one, width, width).T,
        cut(grads_one, 0, width),
        cut(grads_two, 2 * hidden_units + width, width).T,
        cut(grads_two, hidden_units, hidden_units),
        cut(grads_two, 0, hidden_units).T,
        cut(grads_two, 2 * hidden_units, width),
    )


def solution(mesh):
    by_tokens = mesh.shape["mp"] == 4 and mesh.shape["dp"] == 8
    return jax.shard_map(
        on_device_by_tokens if by_tokens else on_device,
        mesh=mesh,
        in_specs=(
            P("dp", "mp"),
            P(),
            P(),
            P(),
            P(),
            P(None, "mp"),
            P(None, "mp"),
            P(None, "mp"),
            P(None, "mp"),
            P(),
            P(),
            P(),
            P(),
            P(),
            P(),
            P(),
            P(),
            P("dp", "mp"),
        ),
        out_specs=(
            P("dp", "mp"),
            P("dp", "mp"),
            P(),
            P(),
            P(),
            P(),
            P(),
            P(),
            P(),
            P(),
            P(),
            P(),
            P(),
            P(),
        ),
        check_vma=False,
    )
```

```python
from functools import partial, reduce

import jax
import jax.numpy as jnp
from jax import lax
from jax.experimental import pallas as pl
from jax.experimental.pallas import tpu as pltpu
from jax.sharding import Mesh
from jax.sharding import PartitionSpec as P

ROTARY = 16
SEQ_LEN = 1024
HEAD_DIM = 64


ADAPTER_SCALE = 0.25
EPS = 1e-05


def matrix_product(left, right):
    return jnp.dot(left, right, preferred_element_type=jnp.float32)


def matrix_product_transposed_left(left, right):
    return lax.dot_general(
        left, right, (((0,), (0,)), ((), ())), preferred_element_type=jnp.float32
    )


def matrix_product_transposed_right(left, right):
    return lax.dot_general(
        left, right, (((1,), (1,)), ((), ())), preferred_element_type=jnp.float32
    )


def normalize(full, gain, bias):
    center = full - jnp.mean(full, -1, keepdims=True)
    factor = lax.rsqrt(jnp.mean(center * center, -1, keepdims=True) + EPS)
    unit = center * factor
    return (unit, factor, unit * gain + bias)


def tables():
    position = jnp.arange(SEQ_LEN, dtype=jnp.float32)[:, None]
    frequency = 10000.0 ** (-(jnp.arange(ROTARY // 2, dtype=jnp.float32) * 2.0) / ROTARY)
    angles = position * frequency[None, :]
    cosine = jnp.concatenate([jnp.cos(angles), jnp.cos(angles)], -1)[:, None, :]
    sine = jnp.concatenate([jnp.sin(angles), jnp.sin(angles)], -1)[:, None, :]
    return (cosine, sine)


def rotate(block, cosine, sine):
    half = ROTARY // 2
    part = block[..., :ROTARY]
    turned = jnp.concatenate([-part[..., half:], part[..., :half]], -1)
    return jnp.concatenate([part * cosine + turned * sine, block[..., ROTARY:]], -1)


def unrotate(grad, cosine, sine):
    half = ROTARY // 2
    part = grad[..., :ROTARY]
    scaled = part * sine
    untied = jnp.concatenate([scaled[..., half:], -scaled[..., :half]], -1)
    return jnp.concatenate([part * cosine + untied, grad[..., ROTARY:]], -1)


def attend(causal, block):
    query, keys, values = block
    scores = jnp.einsum(
        "qhe,khe->hqk", query, keys, preferred_element_type=jnp.float32
    ) * HEAD_DIM ** (-0.5)
    scores = jnp.where(causal, scores, -1e30)
    peak = jnp.max(scores, -1, keepdims=True)
    weights = jnp.exp(scores - peak)
    total = jnp.sum(weights, -1, keepdims=True)
    probs = (weights / total).astype(jnp.bfloat16)
    attended_context = jnp.einsum("hqk,khe->qhe", probs, values, preferred_element_type=jnp.float32)
    return (attended_context.astype(jnp.bfloat16), (peak + jnp.log(total))[..., 0])


def attend_back(causal, block):
    query, keys, values, grad_context, logsum = block
    scores = jnp.einsum(
        "qhe,khe->hqk", query, keys, preferred_element_type=jnp.float32
    ) * HEAD_DIM ** (-0.5)
    scores = jnp.where(causal, scores, -1e30)
    probs = jnp.exp(scores - logsum[..., None])
    grad_probs = jnp.einsum(
        "qhe,khe->hqk", grad_context, values, preferred_element_type=jnp.float32
    )
    inner = jnp.sum(probs * grad_probs, -1, keepdims=True)
    grad_scores = (probs * (grad_probs - inner)).astype(jnp.bfloat16)
    grad_query = jnp.einsum(
        "hqk,khe->qhe", grad_scores, keys, preferred_element_type=jnp.float32
    ) * HEAD_DIM ** (-0.5)
    grad_keys = jnp.einsum(
        "hqk,qhe->khe", grad_scores, query, preferred_element_type=jnp.float32
    ) * HEAD_DIM ** (-0.5)
    grad_values = jnp.einsum(
        "hqk,qhe->khe", probs.astype(jnp.bfloat16), grad_context, preferred_element_type=jnp.float32
    )
    return (grad_query, grad_keys, grad_values)


def fold_with(weight, adapter_a, carry, piece):
    span = piece.shape[1]
    weight_rows = lax.slice_in_dim(weight, 0, span, axis=0)
    adapter_rows = lax.slice_in_dim(adapter_a, 0, span, axis=0)
    return (
        carry[0] + matrix_product(piece, weight_rows),
        carry[1] + matrix_product(piece, adapter_rows),
    )


def finish(summed_result, low_sum, columns_up_factor):
    adapter_values = low_sum.astype(jnp.bfloat16)
    return (
        summed_result + ADAPTER_SCALE * matrix_product(adapter_values, columns_up_factor),
        adapter_values,
    )


def on_device(
    hidden,
    first_gain,
    first_bias,
    second_gain,
    second_bias,
    joined_frozen_weight,
    output_frozen_weight,
    expand_frozen_weight,
    shrink_frozen_weight,
    joined_a,
    joined_up_factor,
    output_a,
    output_up_factor,
    expand_a,
    expand_up_factor,
    shrink_a,
    shrink_up_factor,
    cotangent,
):
    rank = lax.axis_index("mp")
    rows = hidden.shape[0]
    cols = hidden.shape[1]
    width = cols * lax.axis_size("mp")
    count = rows // SEQ_LEN
    joined_cols = joined_frozen_weight.shape[1]
    expand_cols = expand_frozen_weight.shape[1]
    heads_here = joined_cols // (3 * HEAD_DIM)
    inner_out = joined_cols // 3
    full = lax.all_gather(hidden, "mp", axis=1, tiled=True).astype(jnp.float32)
    unit_one, factor_one, first_norm_output = normalize(full, first_gain, first_bias)
    unit_two, factor_two, second_norm_output = normalize(full, second_gain, second_bias)
    first_norm_output = first_norm_output.astype(jnp.bfloat16)
    second_norm_output = second_norm_output.astype(jnp.bfloat16)
    adapter_joined_hidden = matrix_product(first_norm_output, joined_a).astype(jnp.bfloat16)
    joined_weight_local = lax.dynamic_slice_in_dim(
        joined_up_factor, rank * joined_cols, joined_cols, 1
    )
    mixed_state = matrix_product(
        first_norm_output, joined_frozen_weight
    ) + ADAPTER_SCALE * matrix_product(adapter_joined_hidden, joined_weight_local)
    mixed_state = mixed_state.reshape(count, SEQ_LEN, heads_here, 3, HEAD_DIM)
    cosine, sine = tables()
    query = rotate(mixed_state[:, :, :, 0], cosine, sine).astype(jnp.bfloat16)
    keys = rotate(mixed_state[:, :, :, 1], cosine, sine).astype(jnp.bfloat16)
    values = mixed_state[:, :, :, 2].astype(jnp.bfloat16)
    causal = jnp.arange(SEQ_LEN)[:, None] >= jnp.arange(SEQ_LEN)[None, :]
    attended_context, logsum = lax.map(partial(attend, causal), (query, keys, values))
    attended_context = attended_context.reshape(rows, inner_out)
    adapter_expand_hidden = matrix_product(second_norm_output, expand_a).astype(jnp.bfloat16)
    expand_weight_local = lax.dynamic_slice_in_dim(
        expand_up_factor, rank * expand_cols, expand_cols, 1
    )
    upper_hidden = matrix_product(
        second_norm_output, expand_frozen_weight
    ) + ADAPTER_SCALE * matrix_product(adapter_expand_hidden, expand_weight_local)
    gelu_exact = partial(jax.nn.gelu, approximate=False)
    active_f, gelu_pull = jax.vjp(gelu_exact, upper_hidden)
    active_hidden = active_f.astype(jnp.bfloat16)
    out_rows_a = lax.dynamic_slice_in_dim(output_a, rank * inner_out, inner_out, 0)
    output_columns_up_factor = lax.dynamic_slice_in_dim(output_up_factor, rank * cols, cols, 1)
    shrink_rows_a = lax.dynamic_slice_in_dim(shrink_a, rank * expand_cols, expand_cols, 0)
    shrink_columns_up_factor = lax.dynamic_slice_in_dim(shrink_up_factor, rank * cols, cols, 1)
    zero_pair = (
        jnp.zeros((rows, cols), jnp.float32),
        jnp.zeros((rows, output_a.shape[1]), jnp.float32),
    )
    attn_summed, attn_low = fold_with(
        output_frozen_weight,
        output_a,
        zero_pair,
        lax.all_gather(attended_context, "mp", axis=1, tiled=True),
    )
    mlp_summed, mlp_low = fold_with(
        shrink_frozen_weight,
        shrink_a,
        zero_pair,
        jax.tree.map(lambda a: lax.all_gather(a, "mp", axis=1, tiled=True), active_hidden),
    )
    attention_branch, adapter_output_hidden = finish(
        attn_summed, attn_low, output_columns_up_factor
    )
    feedforward_branch, adapter_shrink_hidden = finish(
        mlp_summed, mlp_low, shrink_columns_up_factor
    )
    result = (hidden.astype(jnp.float32) + attention_branch + feedforward_branch).astype(
        jnp.bfloat16
    )
    back_out, back_shrink = (
        lax.psum_scatter(
            matrix_product_transposed_right(cotangent, output_frozen_weight),
            "mp",
            scatter_dimension=1,
            tiled=True,
        ),
        lax.psum_scatter(
            matrix_product_transposed_right(cotangent, shrink_frozen_weight),
            "mp",
            scatter_dimension=1,
            tiled=True,
        ),
    )
    rank_out, rank_shrink = lax.psum(
        (
            ADAPTER_SCALE * matrix_product_transposed_right(cotangent, output_columns_up_factor),
            ADAPTER_SCALE * matrix_product_transposed_right(cotangent, shrink_columns_up_factor),
        ),
        "mp",
    )
    low_out_grad = rank_out.astype(jnp.bfloat16)
    low_shrink_grad = rank_shrink.astype(jnp.bfloat16)
    output_up_factor_piece = ADAPTER_SCALE * matrix_product_transposed_left(
        adapter_output_hidden, cotangent
    )
    shrink_up_factor_piece = ADAPTER_SCALE * matrix_product_transposed_left(
        adapter_shrink_hidden, cotangent
    )
    grad_context = (back_out + matrix_product_transposed_right(low_out_grad, out_rows_a)).astype(
        jnp.bfloat16
    )
    output_a_piece = matrix_product_transposed_left(attended_context, low_out_grad)
    shrink_a_piece = matrix_product_transposed_left(active_hidden, low_shrink_grad)
    grad_active = back_shrink + matrix_product_transposed_right(low_shrink_grad, shrink_rows_a)
    upper_gradient = gelu_pull(grad_active)[0].astype(jnp.bfloat16)
    grad_context = grad_context.reshape(count, SEQ_LEN, heads_here, HEAD_DIM)
    grad_query, grad_keys, grad_values = lax.map(
        partial(attend_back, causal), (query, keys, values, grad_context, logsum)
    )
    mixed_gradient = jnp.stack(
        [unrotate(grad_query, cosine, sine), unrotate(grad_keys, cosine, sine), grad_values], 3
    )
    mixed_gradient = mixed_gradient.reshape(rows, joined_cols).astype(jnp.bfloat16)
    rank_joined, rank_expand = lax.psum(
        (
            ADAPTER_SCALE * matrix_product_transposed_right(mixed_gradient, joined_weight_local),
            ADAPTER_SCALE * matrix_product_transposed_right(upper_gradient, expand_weight_local),
        ),
        "mp",
    )
    low_joined_grad = rank_joined.astype(jnp.bfloat16)
    low_expand_grad = rank_expand.astype(jnp.bfloat16)
    joined_up_factor_piece = ADAPTER_SCALE * matrix_product_transposed_left(
        adapter_joined_hidden, mixed_gradient
    )
    expand_up_factor_piece = ADAPTER_SCALE * matrix_product_transposed_left(
        adapter_expand_hidden, upper_gradient
    )
    norm_one_cols = lax.dynamic_slice_in_dim(first_norm_output, rank * cols, cols, 1)
    norm_two_cols = lax.dynamic_slice_in_dim(second_norm_output, rank * cols, cols, 1)
    joined_a_piece = matrix_product_transposed_left(norm_one_cols, low_joined_grad)
    expand_a_piece = matrix_product_transposed_left(norm_two_cols, low_expand_grad)
    grad_one, grad_two = (
        lax.psum_scatter(
            matrix_product_transposed_right(mixed_gradient, joined_frozen_weight),
            "mp",
            scatter_dimension=1,
            tiled=True,
        ),
        lax.psum_scatter(
            matrix_product_transposed_right(upper_gradient, expand_frozen_weight),
            "mp",
            scatter_dimension=1,
            tiled=True,
        ),
    )
    joined_rows_a = lax.dynamic_slice_in_dim(joined_a, rank * cols, cols, 0)
    expand_rows_a = lax.dynamic_slice_in_dim(expand_a, rank * cols, cols, 0)
    grad_one = grad_one + matrix_product_transposed_right(low_joined_grad, joined_rows_a)
    grad_two = grad_two + matrix_product_transposed_right(low_expand_grad, expand_rows_a)
    unit_one_cols = lax.dynamic_slice_in_dim(unit_one, rank * cols, cols, 1)
    unit_two_cols = lax.dynamic_slice_in_dim(unit_two, rank * cols, cols, 1)
    gain_one_cols = lax.dynamic_slice_in_dim(first_gain, rank * cols, cols, 0)
    gain_two_cols = lax.dynamic_slice_in_dim(second_gain, rank * cols, cols, 0)
    first_gain_piece = jnp.sum(grad_one * unit_one_cols, 0)
    first_bias_piece = jnp.sum(grad_one, 0)
    second_gain_piece = jnp.sum(grad_two * unit_two_cols, 0)
    second_bias_piece = jnp.sum(grad_two, 0)
    scaled_one = grad_one * gain_one_cols
    scaled_two = grad_two * gain_two_cols
    plain_one, along_one, plain_two, along_two = (
        lax.psum(jnp.sum(scaled_one, -1).astype(jnp.bfloat16), "mp").astype(jnp.float32),
        lax.psum(jnp.sum(scaled_one * unit_one_cols, -1).astype(jnp.bfloat16), "mp").astype(
            jnp.float32
        ),
        lax.psum(jnp.sum(scaled_two, -1).astype(jnp.bfloat16), "mp").astype(jnp.float32),
        lax.psum(jnp.sum(scaled_two * unit_two_cols, -1).astype(jnp.bfloat16), "mp").astype(
            jnp.float32
        ),
    )
    back_one = factor_one * (
        scaled_one - plain_one[:, None] / width - unit_one_cols * along_one[:, None] / width
    )
    back_two = factor_two * (
        scaled_two - plain_two[:, None] / width - unit_two_cols * along_two[:, None] / width
    )
    hidden_grad = cotangent.astype(jnp.float32) + back_one + back_two
    pieces = (
        first_gain_piece,
        first_bias_piece,
        second_gain_piece,
        second_bias_piece,
        joined_a_piece,
        joined_up_factor_piece,
        output_a_piece,
        output_up_factor_piece,
        expand_a_piece,
        expand_up_factor_piece,
        shrink_a_piece,
        shrink_up_factor_piece,
    )
    shapes = (
        first_gain.shape,
        first_bias.shape,
        second_gain.shape,
        second_bias.shape,
        joined_a.shape,
        joined_up_factor.shape,
        output_a.shape,
        output_up_factor.shape,
        expand_a.shape,
        expand_up_factor.shape,
        shrink_a.shape,
        shrink_up_factor.shape,
    )
    along = (0, 0, 0, 0, 0, 1, 0, 1, 0, 1, 0, 1)
    padded = [
        lax.dynamic_update_slice_in_dim(
            jnp.zeros(shape, jnp.float32), piece, rank * piece.shape[axis_dim], axis_dim
        )
        for piece, shape, axis_dim in zip(pieces, shapes, along)
    ]
    grads = lax.psum(
        (
            padded[0],
            padded[1],
            padded[2],
            padded[3],
            padded[4],
            padded[5],
            padded[6],
            padded[7],
            padded[8],
            padded[9],
            padded[10],
            padded[11],
        ),
        ("dp", "mp"),
    )
    return (
        result,
        hidden_grad,
        grads[0],
        grads[1],
        grads[2],
        grads[3],
        grads[4],
        grads[5],
        grads[6],
        grads[7],
        grads[8],
        grads[9],
        grads[10],
        grads[11],
    )


BF = jnp.bfloat16
F32 = jnp.float32
BLOCK = 256
VMEM_LIMIT = 62 << 20


def nn(left, right):
    return lax.dot_general(left, right, (((1,), (0,)), ((), ())), preferred_element_type=F32)


def nt(left, right):
    return lax.dot_general(left, right, (((1,), (1,)), ((), ())), preferred_element_type=F32)


def tn(left, right):
    return lax.dot_general(left, right, (((0,), (0,)), ((), ())), preferred_element_type=F32)


def span(start, size, unit=128):
    return pl.ds(pl.multiple_of(start, unit), size)


def layer_norm(rows_f32):
    center = rows_f32 - jnp.mean(rows_f32, 1, keepdims=True)
    factor = lax.rsqrt(jnp.mean(center * center, 1, keepdims=True) + EPS)
    return center * factor, factor


def attention_kernel(slot, shared, n_w, ids, *refs):
    hg_refs = refs[0:6]
    w_refs = refs[6 : 6 + n_w]
    o_own, o_mate = refs[6 + n_w : 8 + n_w]
    o_foreign, o_diag = refs[8 + n_w : 12 + n_w], refs[12 + n_w : 16 + n_w]
    rest = refs[16 + n_w :]
    gain, bias, up, ja, oa, ou, cos_ref, sin_ref = rest[:8]
    rest = rest[8:]
    n_out = 4 if shared else 2
    outs = rest[:n_out]
    (h_v, g_v, w_v, o_v, w_t, q_t, k_t, v_t, k_n, v_n, do_t, dm_t, ctx_t, dk, dv, both, tok_sem, w_sem) = rest[n_out:]
    f, q = ids[0], ids[1]
    seq = h_v.shape[0]
    steps = seq // BLOCK
    heads = q_t.shape[0] // HEAD_DIM
    width = h_v.shape[1]
    piece = width // 4
    start = 2 * seq if shared else lax.shift_right_logical(f, 1) * seq
    for t in range(steps):
        rows = slice(t * BLOCK, (t + 1) * BLOCK)
        for i, dst in enumerate((h_v, g_v)):
            for s in range(4):
                ref = hg_refs[2 * i + s] if s < 2 else hg_refs[2 + s]
                at = (start if s < 2 else i * seq) + t * BLOCK
                pltpu.make_async_copy(
                    ref.at[span(at, BLOCK), :], dst.at[rows, s * piece : (s + 1) * piece], tok_sem.at[i, t]
                ).start()
    if n_w == 1:
        for s in range(4):
            pltpu.make_async_copy(
                w_refs[0].at[span(lax.bitwise_xor(f, s) * piece, piece), :],
                w_v.at[s * piece : (s + 1) * piece, :],
                w_sem.at[0],
            ).start()
    else:
        for k in range(4):
            row = lax.bitwise_xor(lax.bitwise_xor(q, k), f) * piece
            for j in range(3):
                pltpu.make_async_copy(
                    w_refs[k].at[j * BLOCK : (j + 1) * BLOCK, :],
                    w_v.at[span(row, piece), j * BLOCK : (j + 1) * BLOCK],
                    w_sem.at[0],
                ).start()
    head_block = lax.bitwise_xor(f, slot)
    for s, ref in ((0, o_own), (1, o_mate)):
        pltpu.make_async_copy(
            ref.at[span(head_block * BLOCK, BLOCK), :], o_v.at[:, s * piece : (s + 1) * piece], w_sem.at[1]
        ).start()
    for s, pieces in ((2, o_foreign), (3, o_diag)):
        for k in range(4):

            @pl.when(lax.bitwise_xor(q, k) == head_block)
            def _():
                pltpu.make_async_copy(
                    pieces[k], o_v.at[:, s * piece : (s + 1) * piece], w_sem.at[1]
                ).start()

    pltpu.make_async_copy(w_v, w_v, w_sem.at[0]).wait()
    pltpu.make_async_copy(o_v, o_v, w_sem.at[1]).wait()
    w_t[...] = w_v[...].T
    up_t = up[...].T
    o_rows = o_v[...]

    def project(t):
        rows = slice(t * BLOCK, (t + 1) * BLOCK)
        pltpu.make_async_copy(h_v.at[rows, :], h_v.at[rows, :], tok_sem.at[0, t]).wait()
        pltpu.make_async_copy(g_v.at[rows, :], g_v.at[rows, :], tok_sem.at[1, t]).wait()
        unit, _ = layer_norm(h_v[rows, :].astype(F32))
        n = (unit * gain[...] + bias[...]).astype(BF)
        low = (nn(n, ja[...]).astype(BF) * ADAPTER_SCALE).astype(BF)
        mixed = nt(w_t[...], n) + nt(up_t, low)
        cos, sin = cos_ref[:, rows], sin_ref[:, rows]
        half = ROTARY // 2
        for h in range(heads):
            own = slice(h * HEAD_DIM, (h + 1) * HEAD_DIM)
            base = 3 * HEAD_DIM * h
            for part in range(2):
                block = mixed[base + part * HEAD_DIM : base + (part + 1) * HEAD_DIM]
                a, b = block[:half], block[half:ROTARY]
                block = jnp.concatenate([a * cos - b * sin, b * cos + a * sin, block[ROTARY:]], 0).astype(BF)
                if part == 0:
                    q_t[own, rows] = (block * HEAD_DIM ** (-0.5)).astype(BF)
                else:
                    k_t[own, rows] = block
                    k_n[rows, own] = block.T
            block = mixed[base + 2 * HEAD_DIM : base + 3 * HEAD_DIM].astype(BF)
            v_t[own, rows] = block
            v_n[rows, own] = block.T
        g = g_v[rows, :]
        low_grad = (nt(g, ou[...]) * ADAPTER_SCALE).astype(BF)
        do_t[:, rows] = (nt(o_rows, g) + nt(oa[...], low_grad)).astype(BF)

    for t in range(steps):
        project(t)

    later = lax.broadcasted_iota(jnp.int32, (BLOCK, BLOCK), 0) > lax.broadcasted_iota(jnp.int32, (BLOCK, BLOCK), 1)
    state = {}

    def products(h, i):
        own, qs = slice(h * HEAD_DIM, (h + 1) * HEAD_DIM), slice(i * BLOCK, (i + 1) * BLOCK)
        state[h, i] = (
            [nn(k_n[j * BLOCK : (j + 1) * BLOCK, own], q_t[own, qs]) for j in range(i + 1)],
            [nn(v_n[j * BLOCK : (j + 1) * BLOCK, own], do_t[own, qs]) for j in range(i + 1)],
        )

    def soft(h, i):
        scores, d_probs = state[h, i]
        scores[-1] = jnp.where(later, -1e30, scores[-1])
        peak = reduce(jnp.maximum, [jnp.max(s, 0, keepdims=True) for s in scores])
        weights = [jnp.exp(s - peak) for s in scores]
        inverse = 1.0 / reduce(jnp.add, [jnp.sum(w, 0, keepdims=True) for w in weights])
        probs = [w * inverse for w in weights]
        inner = reduce(jnp.add, [jnp.sum(p * d, 0, keepdims=True) for p, d in zip(probs, d_probs)])
        state[h, i] = (
            [p.astype(BF) for p in probs],
            [(p * (d - inner)).astype(BF) for p, d in zip(probs, d_probs)],
        )

    def unturn(block, cos, sin):
        half = ROTARY // 2
        a, b = block[:half], block[half:ROTARY]
        return jnp.concatenate([a * cos + b * sin, b * cos - a * sin, block[ROTARY:]], 0).astype(BF)

    def finish_block(h, i):
        own, qs = slice(h * HEAD_DIM, (h + 1) * HEAD_DIM), slice(i * BLOCK, (i + 1) * BLOCK)
        base = 3 * HEAD_DIM * h
        probs, d_scores = state.pop((h, i))
        keys = slice(0, (i + 1) * BLOCK)
        ctx_t[own, qs] = nn(v_t[own, keys], jnp.concatenate(probs, 0)).astype(BF)
        d_query = nn(k_t[own, keys], jnp.concatenate(d_scores, 0)) * HEAD_DIM ** (-0.5)
        dm_t[base : base + HEAD_DIM, qs] = unturn(d_query, cos_ref[:, qs], sin_ref[:, qs])
        query, d_out = q_t[own, qs], do_t[own, qs]
        for j in range(i + 1):
            js = slice(j * BLOCK, (j + 1) * BLOCK)
            if j == i:
                dk[own, js] = nt(query, d_scores[j])
                dv[own, js] = nt(d_out, probs[j])
            else:
                dk[own, js] += nt(query, d_scores[j])
                dv[own, js] += nt(d_out, probs[j])
        if i == steps - 1:
            dm_t[base + HEAD_DIM : base + 2 * HEAD_DIM, :] = unturn(dk[own, :], cos_ref[...], sin_ref[...])
            dm_t[base + 2 * HEAD_DIM : base + 3 * HEAD_DIM, :] = dv[own, :].astype(BF)

    order = [(h, i) for h in range(heads) for i in range(steps)]
    for at in range(len(order) + 2):
        if at < len(order):
            products(*order[at])
        if at >= 2:
            finish_block(*order[at - 2])
        if 1 <= at <= len(order):
            soft(*order[at - 1])
    both[:, :BLOCK] = ctx_t[...].T
    both[:, BLOCK:] = dm_t[...].T
    if shared:
        for s in range(4):
            outs[s][...] = both[span(lax.bitwise_xor(f, s) * BLOCK, BLOCK), :]
    else:
        c = lax.bitwise_and(f, 1)
        half = seq // 2
        outs[0][...] = both[span(c * half, half), :]
        outs[1][...] = both[span((1 - c) * half, half), :]


def any_spec():
    return pl.BlockSpec(memory_space=pl.ANY)


def vmem_spec():
    return pl.BlockSpec(memory_space=pltpu.VMEM)


def smem_spec():
    return pl.BlockSpec(memory_space=pltpu.SMEM)


def attention(slot, shared, ids, hg, ws, os, gain, bias, up, ja, oa, ou, cos, sin):
    seq, piece = SEQ_LEN, hg[0].shape[1]
    width = 4 * piece
    shard = up.shape[1] // 4
    heads = shard // (3 * HEAD_DIM)
    inner = heads * HEAD_DIM
    rank = ja.shape[1]
    n_w = len(ws)
    if shared:
        out_shape = [jax.ShapeDtypeStruct((BLOCK, inner + shard), BF)] * 4
    else:
        out_shape = [jax.ShapeDtypeStruct((seq // 2, inner + shard), BF)] * 2
    return pl.pallas_call(
        partial(attention_kernel, slot, shared, n_w),
        in_specs=[smem_spec()] + [any_spec()] * (6 + n_w + 10) + [vmem_spec()] * 8,
        out_specs=[vmem_spec()] * len(out_shape),
        out_shape=out_shape,
        scratch_shapes=[
            pltpu.VMEM((seq, width), BF),
            pltpu.VMEM((seq, width), BF),
            pltpu.VMEM((width, shard), BF),
            pltpu.VMEM((inner, width), BF),
            pltpu.VMEM((shard, width), BF),
            pltpu.VMEM((inner, seq), BF),
            pltpu.VMEM((inner, seq), BF),
            pltpu.VMEM((inner, seq), BF),
            pltpu.VMEM((seq, inner), BF),
            pltpu.VMEM((seq, inner), BF),
            pltpu.VMEM((inner, seq), BF),
            pltpu.VMEM((shard, seq), BF),
            pltpu.VMEM((inner, seq), BF),
            pltpu.VMEM((inner, seq), F32),
            pltpu.VMEM((inner, seq), F32),
            pltpu.VMEM((seq, inner + shard), BF),
            pltpu.SemaphoreType.DMA((2, seq // BLOCK)),
            pltpu.SemaphoreType.DMA((2,)),
        ],
        compiler_params=pltpu.CompilerParams(vmem_limit_bytes=VMEM_LIMIT),
        cost_estimate=pl.CostEstimate(flops=100_000_000_000, bytes_accessed=100_000, transcendentals=0),
        name="attention",
    )(
        ids, *hg, *ws, *os, gain, bias,
        lax.slice_in_dim(up, slot * shard, (slot + 1) * shard, axis=1),
        ja,
        lax.slice_in_dim(oa, slot * inner, (slot + 1) * inner, axis=0),
        ou, cos, sin,
    )


def token_copies(ids, tokens, which, dst, sem):
    f = ids[0]
    x, c = lax.shift_right_logical(f, 1), lax.bitwise_and(f, 1)
    seq = SEQ_LEN
    half = seq // 2
    piece = tokens[0].shape[1]
    for s in range(4):
        cols = slice(s * piece, (s + 1) * piece)
        if s < 2:
            own, shared = tokens[2 * which + s], tokens[2 * which + s]
            own_at, shared_at = x * seq, 2 * seq
        else:
            own, shared = tokens[2 + s], tokens[4 + s]
            own_at, shared_at = which * seq, which * seq
        pltpu.make_async_copy(own.at[span(own_at + c * half, half), :], dst.at[:half, cols], sem).start()
        pltpu.make_async_copy(
            shared.at[span(shared_at + f * BLOCK, BLOCK), :], dst.at[half : half + BLOCK, cols], sem
        ).start()


def attention_copies(own, shared, cols, dst, sem):
    half = dst.shape[0] - BLOCK
    size = dst.shape[1] // 4
    for s in range(4):
        to = slice(s * size, (s + 1) * size)
        pltpu.make_async_copy(own[s].at[:, cols], dst.at[:half, to], sem).start()
        pltpu.make_async_copy(shared[s].at[:, cols], dst.at[half : half + BLOCK, to], sem).start()


def arrived(dst, sem):
    pltpu.make_async_copy(dst, dst, sem).wait()


def grads_kernel(ids, *refs):
    tokens, a_own, a_sh = refs[0:8], refs[8:12], refs[12:16]
    gain, bias, up, ja, oa, ou = refs[16:22]
    low_out_ref, low_grad_ref, keep, send = refs[22:26]
    h_v, g_v, c_v, m_v, sem = refs[26:]
    f = ids[0]
    rows, width = h_v.shape
    piece = width // 4
    shard = m_v.shape[1] // 4
    token_copies(ids, tokens, 1, g_v, sem.at[1])
    attention_copies(a_own, a_sh, slice(0, BLOCK), c_v, sem.at[2])
    token_copies(ids, tokens, 0, h_v, sem.at[0])
    attention_copies(a_own, a_sh, slice(BLOCK, BLOCK + shard), m_v, sem.at[3])
    put = partial(put_blocks, f, keep, send)
    arrived(g_v, sem.at[1])
    arrived(c_v, sem.at[2])
    low_out = (nn(c_v[...], oa[...]).astype(BF) * ADAPTER_SCALE).astype(BF)
    low_out_ref[...] = low_out
    low_out_grad = (nt(g_v[...], ou[...]) * ADAPTER_SCALE).astype(BF)
    put(0, piece, low_out.T, g_v)
    put(width, piece, low_out_grad.T, c_v)
    arrived(h_v, sem.at[0])
    unit, _ = layer_norm(h_v[...].astype(F32))
    n = (unit * gain[...] + bias[...]).astype(BF)
    low = (nn(n, ja[...]).astype(BF) * ADAPTER_SCALE).astype(BF)
    arrived(m_v, sem.at[3])
    low_grad = (nt(m_v[...], up[...]) * ADAPTER_SCALE).astype(BF)
    low_grad_ref[...] = low_grad
    put(2 * width, shard, low.T, m_v)
    put(2 * width + 4 * shard, piece, low_grad.T, n)


def put_blocks(f, keep, send, base, size, left, right):
    half = keep.shape[0]
    for s in range(4):
        value = nn(left, right[:, s * size : (s + 1) * size])
        to = span(base + lax.bitwise_xor(f, s) * size, size)
        keep[:, to] = value[:half]
        send[:, to] = value[half:]


def grads_of_attention(ids, tokens, a_own, a_sh, gain, bias, up, ja, oa, ou):
    piece = tokens[0].shape[1]
    width = 4 * piece
    rows = SEQ_LEN // 2 + BLOCK
    shard = up.shape[1] // 4
    rank = ja.shape[1]
    total = 3 * width + 4 * shard
    return pl.pallas_call(
        grads_kernel,
        in_specs=[smem_spec()] + [any_spec()] * 16 + [vmem_spec()] * 6,
        out_specs=[vmem_spec()] * 4,
        out_shape=[
            jax.ShapeDtypeStruct((rows, rank), BF),
            jax.ShapeDtypeStruct((rows, rank), BF),
            jax.ShapeDtypeStruct((rank // 2, total), F32),
            jax.ShapeDtypeStruct((rank // 2, total), F32),
        ],
        scratch_shapes=[
            pltpu.VMEM((rows, width), BF),
            pltpu.VMEM((rows, width), BF),
            pltpu.VMEM((rows, width), BF),
            pltpu.VMEM((rows, 4 * shard), BF),
            pltpu.SemaphoreType.DMA((4,)),
        ],
        compiler_params=pltpu.CompilerParams(vmem_limit_bytes=VMEM_LIMIT),
        cost_estimate=pl.CostEstimate(flops=100_000_000_000, bytes_accessed=100_000, transcendentals=0),
        name="grads_of_attention",
    )(ids, *tokens, *a_own, *a_sh, gain, bias, up, ja, oa, ou)


def load_mlp_weights(ids, e_own, e_mate, s_own, s_mate, p_foreign, p_diag, e_v, s_v, e_sem, s_sem, chunk):
    f, q = ids[0], ids[1]
    width, hidden = e_v.shape
    piece, part = width // 4, hidden // 4
    per = part // chunk
    for s, e_ref, s_ref in ((0, e_own, s_own), (1, e_mate, s_mate)):
        for u in range(per):
            for t in range(4):
                pltpu.make_async_copy(
                    e_ref.at[span(lax.bitwise_xor(f, t) * piece, piece), u * chunk : (u + 1) * chunk],
                    e_v.at[t * piece : (t + 1) * piece, s * part + u * chunk : s * part + (u + 1) * chunk],
                    e_sem.at[s * per + u],
                ).start()
        for t in range(4):
            for u in range(per):
                pltpu.make_async_copy(
                    s_ref.at[span(lax.bitwise_xor(f, t) * part + u * chunk, chunk), :],
                    s_v.at[t * part + u * chunk : t * part + (u + 1) * chunk, s * piece : (s + 1) * piece],
                    s_sem.at[t * per + u],
                ).start()
    for s, pieces in ((2, p_foreign), (3, p_diag)):
        for k in range(4):
            place = lax.bitwise_xor(lax.bitwise_xor(q, k), f)
            for j in range(part // BLOCK):
                pltpu.make_async_copy(
                    pieces[k].at[j * BLOCK : (j + 1) * BLOCK, :],
                    e_v.at[span(place * piece, piece), s * part + j * BLOCK : s * part + (j + 1) * BLOCK],
                    e_sem.at[s * per + j * BLOCK // chunk],
                ).start()
            for u in range(per):
                pltpu.make_async_copy(
                    pieces[k].at[part + u * chunk : part + (u + 1) * chunk, :],
                    s_v.at[span(place * part + u * chunk, chunk), s * piece : (s + 1) * piece],
                    s_sem.at[place * per + u],
                ).start()


CHUNK = 512


def mlp_first_kernel(ids, *refs):
    tokens, weights = refs[0:8], refs[8:20]
    gain, bias, ea, eu, sa, su = refs[20:26]
    act_out, dup_out, ls_out, dle_out, keep, send = refs[26:32]
    h_v, g_v, n_v, e_v, s_v, act, dup, sem, e_sem, s_sem, o_sem = refs[32:]
    f = ids[0]
    rows, width = h_v.shape
    hidden = e_v.shape[1]
    token_copies(ids, tokens, 0, h_v, sem.at[0])
    token_copies(ids, tokens, 1, g_v, sem.at[1])
    load_mlp_weights(
        ids, weights[0], weights[1], weights[2], weights[3], weights[4:8], weights[8:12], e_v, s_v, e_sem, s_sem, CHUNK
    )
    arrived(h_v, sem.at[0])
    unit, _ = layer_norm(h_v[...].astype(F32))
    n_v[...] = (unit * gain[...] + bias[...]).astype(BF)
    low = (nn(n_v[...], ea[...]).astype(BF) * ADAPTER_SCALE).astype(BF)
    arrived(g_v, sem.at[1])
    low_grad = (nt(g_v[...], su[...]) * ADAPTER_SCALE).astype(BF)
    state = {}

    def products(b, t):
        ts, bs = slice(t * BLOCK, (t + 1) * BLOCK), slice(b * CHUNK, (b + 1) * CHUNK)
        if t == 0:
            arrived(e_v.at[:, bs], e_sem.at[b])
            arrived(s_v.at[bs, :], s_sem.at[b])
        state[b, t] = (
            nn(n_v[ts, :], e_v[:, bs]) + nn(low[ts], eu[:, bs]),
            nt(g_v[ts, :], s_v[bs, :]) + nt(low_grad[ts], sa[bs, :]),
        )

    def bend(b, t):
        ts, bs = slice(t * BLOCK, (t + 1) * BLOCK), slice(b * CHUNK, (b + 1) * CHUNK)
        upper, d_active = state.pop((b, t))
        normal = 0.5 * (1.0 + lax.erf(upper * 0.7071067811865476))
        density = jnp.exp(-0.5 * upper * upper) * 0.3989422804014327
        act[ts, bs] = (upper * normal).astype(BF)
        dup[ts, bs] = (d_active * (normal + upper * density)).astype(BF)
        if t == rows // BLOCK - 1:
            pltpu.make_async_copy(act.at[:, bs], act_out.at[:, bs], o_sem.at[0]).start()
            pltpu.make_async_copy(dup.at[:, bs], dup_out.at[:, bs], o_sem.at[1]).start()

    order = [(b, t) for b in range(hidden // CHUNK) for t in range(rows // BLOCK)]
    for at in range(len(order) + 1):
        if at < len(order):
            products(*order[at])
        if at > 0:
            bend(*order[at - 1])

    part, piece = hidden // 4, width // 4

    put = partial(put_blocks, f, keep, send)
    put(0, part, low_grad.T, act)
    put(hidden, part, low.T, dup)
    low_shrink = (nn(act[...], sa[...]).astype(BF) * ADAPTER_SCALE).astype(BF)
    low_expand_grad = (nt(dup[...], eu[...]) * ADAPTER_SCALE).astype(BF)
    ls_out[...] = low_shrink
    dle_out[...] = low_expand_grad
    put(2 * hidden, piece, low_shrink.T, g_v)
    put(2 * hidden + width, piece, low_expand_grad.T, n_v)
    arrived(act, o_sem.at[0])
    arrived(dup, o_sem.at[1])


def mlp_first(ids, tokens, weights, gain, bias, ea, eu, sa, su):
    piece = tokens[0].shape[1]
    width = 4 * piece
    rows = SEQ_LEN // 2 + BLOCK
    hidden = eu.shape[1]
    rank = ea.shape[1]
    return pl.pallas_call(
        mlp_first_kernel,
        in_specs=[smem_spec()] + [any_spec()] * 20 + [vmem_spec()] * 6,
        out_specs=[any_spec()] * 2 + [vmem_spec()] * 4,
        out_shape=[
            jax.ShapeDtypeStruct((rows, hidden), BF),
            jax.ShapeDtypeStruct((rows, hidden), BF),
            jax.ShapeDtypeStruct((rows, rank), BF),
            jax.ShapeDtypeStruct((rows, rank), BF),
            jax.ShapeDtypeStruct((rank // 2, 2 * hidden + 2 * width), F32),
            jax.ShapeDtypeStruct((rank // 2, 2 * hidden + 2 * width), F32),
        ],
        scratch_shapes=[
            pltpu.VMEM((rows, width), BF),
            pltpu.VMEM((rows, width), BF),
            pltpu.VMEM((rows, width), BF),
            pltpu.VMEM((width, hidden), BF),
            pltpu.VMEM((hidden, width), BF),
            pltpu.VMEM((rows, hidden), BF),
            pltpu.VMEM((rows, hidden), BF),
            pltpu.SemaphoreType.DMA((2,)),
            pltpu.SemaphoreType.DMA((hidden // CHUNK,)),
            pltpu.SemaphoreType.DMA((hidden // CHUNK,)),
            pltpu.SemaphoreType.DMA((2,)),
        ],
        compiler_params=pltpu.CompilerParams(vmem_limit_bytes=VMEM_LIMIT),
        cost_estimate=pl.CostEstimate(flops=100_000_000_000, bytes_accessed=100_000, transcendentals=0),
        name="mlp_first",
    )(ids, *tokens, *weights, gain, bias, ea, eu, sa, su)


def load_rows(ids, own, mate, foreign, diag, at, dst, sem):
    f, q = ids[0], ids[1]
    piece = own.shape[0] // 4
    cols = own.shape[1]
    for s, ref in ((0, own), (1, mate)):
        for t in range(4):
            pltpu.make_async_copy(
                ref.at[span(lax.bitwise_xor(f, t) * piece, piece), :],
                dst.at[t * piece : (t + 1) * piece, s * cols : (s + 1) * cols],
                sem,
            ).start()
    for s, pieces in ((2, foreign), (3, diag)):
        for k in range(4):
            rows = span(lax.bitwise_xor(lax.bitwise_xor(q, k), f) * piece, piece)
            for j in range(cols // BLOCK):
                pltpu.make_async_copy(
                    pieces[k].at[at + j * BLOCK : at + (j + 1) * BLOCK, :],
                    dst.at[rows, s * cols + j * BLOCK : s * cols + (j + 1) * BLOCK],
                    sem,
                ).start()


def load_shrink(ids, own, mate, foreign, diag, at, dst, sem):
    f, q = ids[0], ids[1]
    part, piece = dst.shape[0] // 4, dst.shape[1] // 4
    for s, ref in ((0, own), (1, mate)):
        for t in range(4):
            pltpu.make_async_copy(
                ref.at[span(lax.bitwise_xor(f, t) * part, part), :],
                dst.at[t * part : (t + 1) * part, s * piece : (s + 1) * piece],
                sem,
            ).start()
    for s, pieces in ((2, foreign), (3, diag)):
        for k in range(4):
            rows = span(lax.bitwise_xor(lax.bitwise_xor(q, k), f) * part, part)
            pltpu.make_async_copy(
                pieces[k].at[at : at + part, :], dst.at[rows, s * piece : (s + 1) * piece], sem
            ).start()


def result_kernel(ids, *refs):
    tokens, a_own, a_sh = refs[0:8], refs[8:12], refs[12:16]
    o_own, o_mate, s_own, s_mate = refs[16:20]
    one_f, one_d, two_f, two_d = refs[20:24], refs[24:28], refs[28:32], refs[32:36]
    act_ref = refs[36]
    low_out, ou, low_shrink, su = refs[37:41]
    outs = refs[41:45]
    h_v, c_v, o_v, s_v, act, sem = refs[45:]
    f = ids[0]
    rows, width = h_v.shape
    piece = width // 4
    load_rows(ids, o_own, o_mate, one_f, one_d, 0, o_v, sem.at[0])
    attention_copies(a_own, a_sh, slice(0, BLOCK), c_v, sem.at[1])
    token_copies(ids, tokens, 0, h_v, sem.at[2])
    pltpu.make_async_copy(act_ref, act, sem.at[3]).start()
    load_shrink(ids, s_own, s_mate, two_f, two_d, act.shape[1] // 4, s_v, sem.at[4])
    arrived(o_v, sem.at[0])
    arrived(c_v, sem.at[1])
    arrived(h_v, sem.at[2])
    sums = []
    for t in range(rows // BLOCK):
        ts = slice(t * BLOCK, (t + 1) * BLOCK)
        sums.append(
            h_v[ts, :].astype(F32)
            + (nn(c_v[ts, :], o_v[...]) + nn(low_out[ts, :], ou[...]))
            + nn(low_shrink[ts, :], su[...])
        )
    arrived(act, sem.at[3])
    arrived(s_v, sem.at[4])
    for t in range(rows // BLOCK):
        ts = slice(t * BLOCK, (t + 1) * BLOCK)
        value = (sums[t] + nn(act[ts, :], s_v[...])).astype(BF)
        for s in range(4):
            outs[s][ts, :] = value[:, s * piece : (s + 1) * piece]


def result_parts(ids, tokens, a_own, a_sh, o_parts, s_parts, one, two, act, low_out, ou, low_shrink, su):
    piece = tokens[0].shape[1]
    width = 4 * piece
    rows = SEQ_LEN // 2 + BLOCK
    hidden = act.shape[1]
    return pl.pallas_call(
        result_kernel,
        in_specs=[smem_spec()] + [any_spec()] * 37 + [vmem_spec()] * 4,
        out_specs=[vmem_spec()] * 4,
        out_shape=[jax.ShapeDtypeStruct((rows, piece), BF)] * 4,
        scratch_shapes=[
            pltpu.VMEM((rows, width), BF),
            pltpu.VMEM((rows, width), BF),
            pltpu.VMEM((width, width), BF),
            pltpu.VMEM((hidden, width), BF),
            pltpu.VMEM((rows, hidden), BF),
            pltpu.SemaphoreType.DMA((5,)),
        ],
        compiler_params=pltpu.CompilerParams(vmem_limit_bytes=VMEM_LIMIT),
        cost_estimate=pl.CostEstimate(flops=100_000_000_000, bytes_accessed=100_000, transcendentals=0),
        name="result_parts",
    )(ids, *tokens, *a_own, *a_sh, *o_parts, *s_parts, *one, *two, act, low_out, ou, low_shrink, su)


def input_grad_kernel(ids, *refs):
    tokens, a_own, a_sh = refs[0:8], refs[8:12], refs[12:16]
    w_own, w_mate, e_own, e_mate = refs[16:20]
    one_f, one_d, two_f, two_d = refs[20:24], refs[24:28], refs[28:32], refs[32:36]
    dup_ref = refs[36]
    gain_one, gain_two, ja, ea, low_joined_grad, low_expand_grad = refs[37:43]
    outs, sums = refs[43:47], refs[47]
    h_v, g_v, m_v, w_v, e_v, dup, sem = refs[48:]
    f = ids[0]
    rows, width = h_v.shape
    piece = width // 4
    shard = m_v.shape[1] // 4
    attention_copies(a_own, a_sh, slice(BLOCK, BLOCK + shard), m_v, sem.at[0])
    load_rows(ids, w_own, w_mate, one_f, one_d, 0, w_v, sem.at[1])
    pltpu.make_async_copy(dup_ref, dup, sem.at[2]).start()
    load_rows(ids, e_own, e_mate, two_f, two_d, 0, e_v, sem.at[3])
    token_copies(ids, tokens, 0, h_v, sem.at[4])
    token_copies(ids, tokens, 1, g_v, sem.at[5])
    arrived(m_v, sem.at[0])
    arrived(w_v, sem.at[1])
    steps = rows // BLOCK
    ones = []
    for t in range(steps):
        ts = slice(t * BLOCK, (t + 1) * BLOCK)
        ones.append(nt(m_v[ts, :], w_v[...]) + nt(low_joined_grad[ts, :], ja[...]))
    arrived(dup, sem.at[2])
    arrived(e_v, sem.at[3])
    arrived(h_v, sem.at[4])
    arrived(g_v, sem.at[5])
    total = None
    for t in range(steps):
        ts = slice(t * BLOCK, (t + 1) * BLOCK)
        one = ones[t]
        two = nt(dup[ts, :], e_v[...]) + nt(low_expand_grad[ts, :], ea[...])
        unit, factor = layer_norm(h_v[ts, :].astype(F32))
        here = [jnp.sum(v, 0, keepdims=True) for v in (one * unit, one, two * unit, two)]
        total = here if total is None else [a + b for a, b in zip(total, here)]
        e = one * gain_one[...] + two * gain_two[...]
        plain = jnp.mean(e, 1, keepdims=True)
        along = jnp.mean(e * unit, 1, keepdims=True)
        value = g_v[ts, :].astype(F32) + factor * (e - plain - unit * along)
        for s in range(4):
            outs[s][ts, :] = value[:, s * piece : (s + 1) * piece].astype(outs[s].dtype)
    value = jnp.concatenate(total + [jnp.zeros((4, width), F32)], 0)
    for s in range(4):
        sums[:, span(lax.bitwise_xor(f, s) * piece, piece)] = value[:, s * piece : (s + 1) * piece]


def input_grad_parts(
    ids, tokens, a_own, a_sh, w_parts, e_parts, one, two, dup, gain_one, gain_two, ja, ea, low_joined_grad, low_expand_grad
):
    piece = tokens[0].shape[1]
    width = 4 * piece
    rows = SEQ_LEN // 2 + BLOCK
    hidden = dup.shape[1]
    joined = 4 * w_parts[0].shape[1]
    return pl.pallas_call(
        input_grad_kernel,
        in_specs=[smem_spec()] + [any_spec()] * 37 + [vmem_spec()] * 6,
        out_specs=[vmem_spec()] * 5,
        out_shape=[jax.ShapeDtypeStruct((rows, piece), t) for t in (F32, F32, BF, BF)]
        + [jax.ShapeDtypeStruct((8, width), F32)],
        scratch_shapes=[
            pltpu.VMEM((rows, width), BF),
            pltpu.VMEM((rows, width), BF),
            pltpu.VMEM((rows, joined), BF),
            pltpu.VMEM((width, joined), BF),
            pltpu.VMEM((width, hidden), BF),
            pltpu.VMEM((rows, hidden), BF),
            pltpu.SemaphoreType.DMA((6,)),
        ],
        compiler_params=pltpu.CompilerParams(vmem_limit_bytes=VMEM_LIMIT),
        cost_estimate=pl.CostEstimate(flops=100_000_000_000, bytes_accessed=100_000, transcendentals=0),
        name="input_grad_parts",
    )(
        ids, *tokens, *a_own, *a_sh, *w_parts, *e_parts, *one, *two, dup,
        gain_one, gain_two, ja, ea, low_joined_grad, low_expand_grad,
    )


def gather_rows_kernel(widen, ids, *refs):
    parts, out = refs[:4], refs[4]
    scratch = refs[5:]
    f = ids[0]
    sem = scratch[-1]
    rows = parts[0].shape[0]
    half = rows - BLOCK
    seq = 2 * half
    copies = []
    for s in range(4):
        src = parts[s]
        if src.dtype != out.dtype:
            scratch[s - 2][...] = src[...].astype(out.dtype)
            src = scratch[s - 2]
        at = lax.bitwise_xor(f, s)
        copies.append(pltpu.make_async_copy(src.at[:half, :], out.at[span(at * half, half), :], sem.at[2 * s]))
        copies.append(
            pltpu.make_async_copy(src.at[half:, :], out.at[span(2 * seq + at * BLOCK, BLOCK), :], sem.at[2 * s + 1])
        )
        copies[-2].start()
        copies[-1].start()
    for copy in copies:
        copy.wait()


def gather_rows(ids, parts, dtype):
    rows, piece = parts[0].shape
    narrow = [p for p in parts if p.dtype != dtype]
    return pl.pallas_call(
        partial(gather_rows_kernel, dtype),
        in_specs=[smem_spec()] + [vmem_spec()] * 4,
        out_specs=any_spec(),
        out_shape=jax.ShapeDtypeStruct((4 * rows, piece), dtype),
        scratch_shapes=[pltpu.VMEM((rows, piece), dtype)] * len(narrow) + [pltpu.SemaphoreType.DMA((8,))],
        compiler_params=pltpu.CompilerParams(vmem_limit_bytes=VMEM_LIMIT),
        name="gather_rows",
    )(ids, *parts)


def adapters_kernel(cuts, order_ref, *refs):
    order = order_ref[...]
    pieces, outs = refs[:8], refs[8:]
    for (at, size, turned), out in zip(cuts, outs):
        value = jnp.concatenate([p[:, at : at + size] for p in pieces], 0)
        out[...] = tn(value, order) if turned else tn(order, value)


def adapters_out(order, pieces, cuts):
    rank = order.shape[0]
    return pl.pallas_call(
        partial(adapters_kernel, cuts),
        in_specs=[vmem_spec()] * 9,
        out_specs=[vmem_spec()] * len(cuts),
        out_shape=[
            jax.ShapeDtypeStruct((size, rank) if turned else (rank, size), F32) for at, size, turned in cuts
        ],
        compiler_params=pltpu.CompilerParams(vmem_limit_bytes=VMEM_LIMIT),
        name="adapters_out",
    )(order, *pieces)


def split_rows_kernel(keep, received, own, *outs):
    size = own.shape[0]
    own[...] = keep[:size, :] + received[:size, :]
    for k, out in enumerate(outs):
        rows = slice((k + 1) * size, (k + 2) * size)
        out[...] = (keep[rows, :] + received[rows, :]).astype(BF)


def split_rows(keep, received):
    rows, cols = keep.shape
    return pl.pallas_call(
        split_rows_kernel,
        in_specs=[vmem_spec()] * 2,
        out_specs=[vmem_spec()] * 4,
        out_shape=[jax.ShapeDtypeStruct((rows // 4, cols), t) for t in (F32, BF, BF, BF)],
        compiler_params=pltpu.CompilerParams(vmem_limit_bytes=VMEM_LIMIT),
        name="split_rows",
    )(keep, received)


def split_columns_kernel(ids, own, a, b, c, keep, *outs):
    size = keep.shape[1]
    for k, out in enumerate((keep,) + outs):
        cols = span(lax.bitwise_xor(ids[2], k) * size, size)
        total = own[:, cols] + a[:, cols].astype(F32) + b[:, cols].astype(F32) + c[:, cols].astype(F32)
        out[...] = total.astype(out.dtype)


def split_columns(ids, own, received):
    rows, cols = own.shape
    return pl.pallas_call(
        split_columns_kernel,
        in_specs=[smem_spec()] + [vmem_spec()] * 4,
        out_specs=[vmem_spec()] * 4,
        out_shape=[jax.ShapeDtypeStruct((rows, cols // 4), t) for t in (F32, BF, BF, BF)],
        compiler_params=pltpu.CompilerParams(vmem_limit_bytes=VMEM_LIMIT),
        name="split_columns",
    )(ids, own, *received)


def place_columns_kernel(ids, a, b, c, d, out):
    size = a.shape[1]
    for k, part in enumerate((a, b, c, d)):
        out[:, span(lax.bitwise_xor(ids[2], k) * size, size)] = part[...]


def place_columns(ids, parts):
    rows, cols = parts[0].shape
    return pl.pallas_call(
        place_columns_kernel,
        in_specs=[smem_spec()] + [vmem_spec()] * 4,
        out_specs=vmem_spec(),
        out_shape=jax.ShapeDtypeStruct((rows, 4 * cols), parts[0].dtype),
        compiler_params=pltpu.CompilerParams(vmem_limit_bytes=VMEM_LIMIT),
        name="place_columns",
    )(ids, *parts)


def pack_kernel(plan, ids, *refs):
    n_in = len(refs) - 1 - len(plan)
    srcs, outs, sem = refs[:n_in], refs[n_in:-1], refs[-1]
    for out, blocks in zip(outs, plan):
        at = 0
        for src, which, size, col, cols in blocks:
            rows = span(ids[which] * size, size)
            pltpu.make_async_copy(srcs[src].at[rows, col : col + cols], out.at[at : at + size, :], sem).start()
            at += size
    for out in outs:
        pltpu.make_async_copy(out, out, sem).wait()


def pack(ids, arrays, plan):
    shapes = []
    for blocks in plan:
        shapes.append(jax.ShapeDtypeStruct((sum(b[2] for b in blocks), blocks[0][4]), arrays[0].dtype))
    return pl.pallas_call(
        partial(pack_kernel, plan),
        in_specs=[smem_spec()] + [any_spec()] * len(arrays),
        out_specs=[vmem_spec()] * len(plan),
        out_shape=shapes,
        scratch_shapes=[pltpu.SemaphoreType.DMA],
        compiler_params=pltpu.CompilerParams(vmem_limit_bytes=VMEM_LIMIT),
        name="pack",
    )(ids, *arrays)


def order_kernel(ids, order_ref, *refs):
    n = len(refs) // 2
    f = ids[0]
    order = order_ref[...]
    for src, out in zip(refs[:n], refs[n:]):
        axis = 0 if src.shape[0] > src.shape[1] else 1
        size = src.shape[axis] // 4
        for s in range(4):
            at, to = span(lax.bitwise_xor(f, s) * size, size), slice(s * size, (s + 1) * size)
            if src.dtype == F32:
                out[:, to] = src[:, at]
            elif axis == 0:
                out[to, :] = nt(src[at, :], order).astype(BF)
            else:
                out[:, to] = nn(order, src[:, at]).astype(BF)


def order_params(ids, order, params):
    return pl.pallas_call(
        order_kernel,
        in_specs=[smem_spec()] + [vmem_spec()] * (1 + len(params)),
        out_specs=[vmem_spec()] * len(params),
        out_shape=[jax.ShapeDtypeStruct(p.shape, p.dtype) for p in params],
        compiler_params=pltpu.CompilerParams(vmem_limit_bytes=VMEM_LIMIT),
        name="order_params",
    )(ids, order, *params)


def swap(axes):
    def run(value):
        size = lax.axis_size(axes)
        return lax.ppermute(value, axes, [(i, size - 1 - i) for i in range(size)])

    return run


def after(value, *others):
    return lax.optimization_barrier((value, *others))[0]


def on_device_by_tokens(
    hidden,
    first_gain,
    first_bias,
    second_gain,
    second_bias,
    joined_frozen_weight,
    output_frozen_weight,
    expand_frozen_weight,
    shrink_frozen_weight,
    joined_a,
    joined_up_factor,
    output_a,
    output_up_factor,
    expand_a,
    expand_up_factor,
    shrink_a,
    shrink_up_factor,
    cotangent,
):
    x, c, q = lax.axis_index("x"), lax.axis_index("core"), lax.axis_index(("zn", "y"))
    f, far = 2 * x + c, lax.axis_index(("zf", "x"))
    seq, half = SEQ_LEN, SEQ_LEN // 2
    width = 4 * hidden.shape[1]
    rank = joined_a.shape[1]
    units = 4 * expand_frozen_weight.shape[1]
    ids = jnp.stack([f, q, far, 1 - x, 3 - q, 0 * f + 2]).astype(jnp.int32)
    to_core, to_x, to_diag = swap("core"), swap("x"), swap(("x", "core"))
    near = swap("y"), swap("zn"), swap(("zn", "y"))
    cross = to_x, swap("zf"), swap(("zf", "x"))

    piece = width // 4
    out_quarter = lax.dynamic_slice_in_dim(output_frozen_weight, q * piece, piece, 0)
    o_x = to_x(out_quarter)
    hidden, cotangent = after((hidden, cotangent), out_quarter)
    (own,) = pack(ids, (hidden, cotangent), (((0, 3, seq, 0, piece), (1, 3, seq, 0, piece)),))
    h_mate, g_mate = to_core(hidden), to_core(cotangent)
    own_x = to_x(after(own, o_x))
    o_near = tuple(go(o_x) for go in near)

    def blocks(src, which, array):
        return tuple((src, which, array.shape[0] // 4, at, BLOCK) for at in range(0, array.shape[1], BLOCK))

    joined_pack, shared, two_first, two_last = pack(
        after(ids, own),
        (hidden, cotangent, joined_frozen_weight, expand_frozen_weight, shrink_frozen_weight),
        (
            blocks(2, 1, joined_frozen_weight),
            ((0, 5, seq, 0, piece), (1, 5, seq, 0, piece)),
            blocks(3, 1, expand_frozen_weight) + blocks(4, 1, shrink_frozen_weight),
            blocks(3, 4, expand_frozen_weight) + blocks(4, 4, shrink_frozen_weight),
        ),
    )
    place = lax.broadcasted_iota(jnp.int32, (rank, rank), 0)
    order = (lax.broadcasted_iota(jnp.int32, (rank, rank), 1) == (place ^ (c * 64 + q * 16))).astype(BF)
    gain_one, bias_one, gain_two, bias_two, ja, oa, ea, sa, ju, ou, eu, su = order_params(
        after(ids, own),
        order,
        tuple(v[None, :] for v in (first_gain, first_bias, second_gain, second_bias))
        + (joined_a, output_a, expand_a, shrink_a)
        + (joined_up_factor, output_up_factor, expand_up_factor, shrink_up_factor),
    )
    position = jnp.arange(seq, dtype=F32)[None, :]
    frequency = 10000.0 ** (-(jnp.arange(ROTARY // 2, dtype=F32) * 2.0) / ROTARY)
    angles = frequency[:, None] * position
    cos, sin = jnp.cos(angles), jnp.sin(angles)

    joined_x = to_x(after(joined_pack, own_x))
    o_mate = to_core(output_frozen_weight)
    own_x = after(own_x, o_near)
    own_mate = to_core(own_x)
    o_foreign = (o_x,) + o_near
    o_diag = tuple(to_core(p) for p in o_foreign)
    local = (hidden, h_mate, cotangent, g_mate)
    o_parts = (output_frozen_weight, o_mate) + o_foreign + o_diag
    params = (gain_one, bias_one, ju, ja, oa, ou, cos, sin)
    shared_x = to_x(after(shared, own_x))
    keep_a, send_a = attention(
        0, False, ids, local + (own_x, own_mate), (joined_frozen_weight,), o_parts, *params
    )
    e_mate, s_mate, w_mate = (to_core(w) for w in (expand_frozen_weight, shrink_frozen_weight, joined_frozen_weight))
    joined_x, shared_x, e_mate, s_mate, w_mate = after((joined_x, shared_x, e_mate, s_mate, w_mate), keep_a)
    joined_near = tuple(go(joined_x) for go in near)
    shared_mate = to_core(shared_x)
    two_x = to_x(after(two_first, shared_x))
    b_parts = attention(
        0, True, ids, local + (shared_x, shared_mate), (joined_frozen_weight,), o_parts, *params
    )
    joined_near, two_x = after((joined_near, two_x), b_parts[0])
    joined_foreign = (joined_x,) + joined_near
    joined_diag = tuple(to_core(p) for p in joined_foreign)
    two_y, two_z, two_yz = near[0](two_x), near[1](two_x), to_x(after(two_last, two_x))
    keep_c, send_c = attention(2, False, ids, local + (own_x, own_mate), joined_foreign, o_parts, *params)
    two_y, two_z, two_yz = after((two_y, two_z, two_yz), keep_c)
    foreign_two = (two_x, two_y, two_z, two_yz)
    diag_two = tuple(to_core(p) for p in foreign_two)
    tokens = local + (own_x, own_mate, shared_x, shared_mate)
    mlp_weights = (expand_frozen_weight, e_mate, shrink_frozen_weight, s_mate) + foreign_two + diag_two
    act, dup, ls, dle, keep_two, send_two = mlp_first(
        ids, tokens, mlp_weights, gain_two, bias_two, ea, eu, sa, su
    )
    b_moved = tuple(go(p) for go, p in zip((to_core, to_x, to_diag), b_parts[1:]))
    b_moved, a_mate, c_mate = after((b_moved, to_core(send_a), to_core(send_c)), act)
    a_own, a_shared = (keep_a, a_mate, keep_c, c_mate), (b_parts[0],) + b_moved

    two = to_core(send_two)
    low_out, low_joined_grad, keep_one, send_one = grads_of_attention(
        ids, tokens, a_own, a_shared, gain_one, bias_one, ju, ja, oa, ou
    )
    two = split_rows(keep_two, after(two, low_out))
    dup = after(dup, two, send_one)
    two = (two[0],) + tuple(go(p) for go, p in zip(near, two[1:]))
    one = to_core(send_one)
    hidden_grad = input_grad_parts(
        ids, tokens, a_own, a_shared, (joined_frozen_weight, w_mate), (expand_frozen_weight, e_mate),
        joined_foreign + joined_diag, foreign_two + diag_two, dup, gain_one, gain_two, ja, ea, low_joined_grad, dle,
    )
    two, one = after((two, one), hidden_grad[4])
    two = split_columns(ids, two[0], two[1:])
    one = split_rows(keep_one, one)
    act = after(act, two, one)
    sums = hidden_grad[4]
    hidden_grad = tuple(hidden_grad[:2]) + (to_x(hidden_grad[2]), to_diag(hidden_grad[3]))
    one = (one[0],) + tuple(go(p) for go, p in zip(near, one[1:]))
    result = result_parts(
        ids, tokens, a_own, a_shared, (output_frozen_weight, o_mate), (shrink_frozen_weight, s_mate),
        o_foreign + o_diag, foreign_two + diag_two, act, low_out, ou, ls, su,
    )
    hidden_grad, two, one, sums = after((hidden_grad, two, one, sums), result)
    two = (two[0],) + tuple(go(p) for go, p in zip(cross, two[1:]))
    result = (result[0],) + tuple(go(p) for go, p in zip((to_core, to_x, to_diag), result[1:]))
    one = split_columns(ids, one[0], one[1:])
    one = (one[0],) + tuple(go(p) for go, p in zip(cross, one[1:]))

    def part_sum(parts):
        return reduce(jnp.add, [p.astype(F32) for p in parts]).astype(BF)

    def all_of(part, ways):
        return (part,) + tuple(go(part) for go in ways)

    two = all_of(part_sum(two), cross)
    hidden_grad = (hidden_grad[0], to_core(hidden_grad[1])) + hidden_grad[2:]
    one = all_of(part_sum(one), cross)
    two = all_of(place_columns(ids, two), near)
    one = all_of(place_columns(ids, one), near)
    for go in (to_core, near[0], near[1], cross[0], cross[1]):
        sums = sums + go(sums)
    two = two + tuple(to_core(p) for p in two)
    one = one + tuple(to_core(p) for p in one)
    result = gather_rows(ids, result, BF)
    hidden_grad = gather_rows(ids, hidden_grad, F32)
    joined = ju.shape[1]
    expand_a_grad, expand_b_grad, shrink_a_grad, shrink_b_grad = adapters_out(
        order, two,
        ((2 * units + width, width, True), (units, units, False), (0, units, True), (2 * units, width, False)),
    )
    joined_a_grad, joined_b_grad, output_a_grad, output_b_grad = adapters_out(
        order, one,
        ((2 * width + joined, width, True), (2 * width, joined, False), (width, width, True), (0, width, False)),
    )
    return (
        result,
        hidden_grad,
        sums[0],
        sums[1],
        sums[2],
        sums[3],
        joined_a_grad,
        joined_b_grad,
        output_a_grad,
        output_b_grad,
        expand_a_grad,
        expand_b_grad,
        shrink_a_grad,
        shrink_b_grad,
    )


def solution(mesh):
    step, rows, cols = on_device, "dp", "mp"
    if mesh.shape["dp"] == 8 and mesh.shape["mp"] == 4:
        step, rows, cols = on_device_by_tokens, ("zf", "zn", "y"), ("x", "core")
        mesh = Mesh(mesh.devices.reshape((2,) * 5), rows + cols)
    whole, split, tokens = P(), P(None, cols), P(rows, cols)
    return jax.shard_map(
        step,
        mesh=mesh,
        in_specs=(tokens,) + (whole,) * 4 + (split,) * 4 + (whole,) * 8 + (tokens,),
        out_specs=(tokens, tokens) + (whole,) * 12,
        check_vma=False,
    )
```

```python
from functools import partial, reduce

import jax
import jax.numpy as jnp
import numpy as np
from jax import lax
from jax.experimental import pallas as pl
from jax.experimental.pallas import tpu as pltpu
from jax.sharding import Mesh
from jax.sharding import PartitionSpec as P

ROTARY = 16
SEQ_LEN = 1024
HEAD_DIM = 64


ADAPTER_SCALE = 0.25
EPS = 1e-05


def matrix_product(left, right):
    return jnp.dot(left, right, preferred_element_type=jnp.float32)


def matrix_product_transposed_left(left, right):
    return lax.dot_general(
        left, right, (((0,), (0,)), ((), ())), preferred_element_type=jnp.float32
    )


def matrix_product_transposed_right(left, right):
    return lax.dot_general(
        left, right, (((1,), (1,)), ((), ())), preferred_element_type=jnp.float32
    )


def normalize(full, gain, bias):
    center = full - jnp.mean(full, -1, keepdims=True)
    factor = lax.rsqrt(jnp.mean(center * center, -1, keepdims=True) + EPS)
    unit = center * factor
    return (unit, factor, unit * gain + bias)


def tables():
    position = jnp.arange(SEQ_LEN, dtype=jnp.float32)[:, None]
    frequency = 10000.0 ** (-(jnp.arange(ROTARY // 2, dtype=jnp.float32) * 2.0) / ROTARY)
    angles = position * frequency[None, :]
    cosine = jnp.concatenate([jnp.cos(angles), jnp.cos(angles)], -1)[:, None, :]
    sine = jnp.concatenate([jnp.sin(angles), jnp.sin(angles)], -1)[:, None, :]
    return (cosine, sine)


def rotate(block, cosine, sine):
    half = ROTARY // 2
    part = block[..., :ROTARY]
    turned = jnp.concatenate([-part[..., half:], part[..., :half]], -1)
    return jnp.concatenate([part * cosine + turned * sine, block[..., ROTARY:]], -1)


def unrotate(grad, cosine, sine):
    half = ROTARY // 2
    part = grad[..., :ROTARY]
    scaled = part * sine
    untied = jnp.concatenate([scaled[..., half:], -scaled[..., :half]], -1)
    return jnp.concatenate([part * cosine + untied, grad[..., ROTARY:]], -1)


def attend(causal, block):
    query, keys, values = block
    scores = jnp.einsum(
        "qhe,khe->hqk", query, keys, preferred_element_type=jnp.float32
    ) * HEAD_DIM ** (-0.5)
    scores = jnp.where(causal, scores, -1e30)
    peak = jnp.max(scores, -1, keepdims=True)
    weights = jnp.exp(scores - peak)
    total = jnp.sum(weights, -1, keepdims=True)
    probs = (weights / total).astype(jnp.bfloat16)
    attended_context = jnp.einsum("hqk,khe->qhe", probs, values, preferred_element_type=jnp.float32)
    return (attended_context.astype(jnp.bfloat16), (peak + jnp.log(total))[..., 0])


def attend_back(causal, block):
    query, keys, values, grad_context, logsum = block
    scores = jnp.einsum(
        "qhe,khe->hqk", query, keys, preferred_element_type=jnp.float32
    ) * HEAD_DIM ** (-0.5)
    scores = jnp.where(causal, scores, -1e30)
    probs = jnp.exp(scores - logsum[..., None])
    grad_probs = jnp.einsum(
        "qhe,khe->hqk", grad_context, values, preferred_element_type=jnp.float32
    )
    inner = jnp.sum(probs * grad_probs, -1, keepdims=True)
    grad_scores = (probs * (grad_probs - inner)).astype(jnp.bfloat16)
    grad_query = jnp.einsum(
        "hqk,khe->qhe", grad_scores, keys, preferred_element_type=jnp.float32
    ) * HEAD_DIM ** (-0.5)
    grad_keys = jnp.einsum(
        "hqk,qhe->khe", grad_scores, query, preferred_element_type=jnp.float32
    ) * HEAD_DIM ** (-0.5)
    grad_values = jnp.einsum(
        "hqk,qhe->khe", probs.astype(jnp.bfloat16), grad_context, preferred_element_type=jnp.float32
    )
    return (grad_query, grad_keys, grad_values)


def fold_with(weight, adapter_a, carry, piece):
    span = piece.shape[1]
    weight_rows = lax.slice_in_dim(weight, 0, span, axis=0)
    adapter_rows = lax.slice_in_dim(adapter_a, 0, span, axis=0)
    return (
        carry[0] + matrix_product(piece, weight_rows),
        carry[1] + matrix_product(piece, adapter_rows),
    )


def finish(summed_result, low_sum, columns_up_factor):
    adapter_values = low_sum.astype(jnp.bfloat16)
    return (
        summed_result + ADAPTER_SCALE * matrix_product(adapter_values, columns_up_factor),
        adapter_values,
    )


def on_device(
    hidden,
    first_gain,
    first_bias,
    second_gain,
    second_bias,
    joined_frozen_weight,
    output_frozen_weight,
    expand_frozen_weight,
    shrink_frozen_weight,
    joined_a,
    joined_up_factor,
    output_a,
    output_up_factor,
    expand_a,
    expand_up_factor,
    shrink_a,
    shrink_up_factor,
    cotangent,
):
    rank = lax.axis_index("mp")
    rows = hidden.shape[0]
    cols = hidden.shape[1]
    width = cols * lax.axis_size("mp")
    count = rows // SEQ_LEN
    joined_cols = joined_frozen_weight.shape[1]
    expand_cols = expand_frozen_weight.shape[1]
    heads_here = joined_cols // (3 * HEAD_DIM)
    inner_out = joined_cols // 3
    full = lax.all_gather(hidden, "mp", axis=1, tiled=True).astype(jnp.float32)
    unit_one, factor_one, first_norm_output = normalize(full, first_gain, first_bias)
    unit_two, factor_two, second_norm_output = normalize(full, second_gain, second_bias)
    first_norm_output = first_norm_output.astype(jnp.bfloat16)
    second_norm_output = second_norm_output.astype(jnp.bfloat16)
    adapter_joined_hidden = matrix_product(first_norm_output, joined_a).astype(jnp.bfloat16)
    joined_weight_local = lax.dynamic_slice_in_dim(
        joined_up_factor, rank * joined_cols, joined_cols, 1
    )
    mixed_state = matrix_product(
        first_norm_output, joined_frozen_weight
    ) + ADAPTER_SCALE * matrix_product(adapter_joined_hidden, joined_weight_local)
    mixed_state = mixed_state.reshape(count, SEQ_LEN, heads_here, 3, HEAD_DIM)
    cosine, sine = tables()
    query = rotate(mixed_state[:, :, :, 0], cosine, sine).astype(jnp.bfloat16)
    keys = rotate(mixed_state[:, :, :, 1], cosine, sine).astype(jnp.bfloat16)
    values = mixed_state[:, :, :, 2].astype(jnp.bfloat16)
    causal = jnp.arange(SEQ_LEN)[:, None] >= jnp.arange(SEQ_LEN)[None, :]
    attended_context, logsum = lax.map(partial(attend, causal), (query, keys, values))
    attended_context = attended_context.reshape(rows, inner_out)
    adapter_expand_hidden = matrix_product(second_norm_output, expand_a).astype(jnp.bfloat16)
    expand_weight_local = lax.dynamic_slice_in_dim(
        expand_up_factor, rank * expand_cols, expand_cols, 1
    )
    upper_hidden = matrix_product(
        second_norm_output, expand_frozen_weight
    ) + ADAPTER_SCALE * matrix_product(adapter_expand_hidden, expand_weight_local)
    gelu_exact = partial(jax.nn.gelu, approximate=False)
    active_f, gelu_pull = jax.vjp(gelu_exact, upper_hidden)
    active_hidden = active_f.astype(jnp.bfloat16)
    out_rows_a = lax.dynamic_slice_in_dim(output_a, rank * inner_out, inner_out, 0)
    output_columns_up_factor = lax.dynamic_slice_in_dim(output_up_factor, rank * cols, cols, 1)
    shrink_rows_a = lax.dynamic_slice_in_dim(shrink_a, rank * expand_cols, expand_cols, 0)
    shrink_columns_up_factor = lax.dynamic_slice_in_dim(shrink_up_factor, rank * cols, cols, 1)
    zero_pair = (
        jnp.zeros((rows, cols), jnp.float32),
        jnp.zeros((rows, output_a.shape[1]), jnp.float32),
    )
    attn_summed, attn_low = fold_with(
        output_frozen_weight,
        output_a,
        zero_pair,
        lax.all_gather(attended_context, "mp", axis=1, tiled=True),
    )
    mlp_summed, mlp_low = fold_with(
        shrink_frozen_weight,
        shrink_a,
        zero_pair,
        jax.tree.map(lambda a: lax.all_gather(a, "mp", axis=1, tiled=True), active_hidden),
    )
    attention_branch, adapter_output_hidden = finish(
        attn_summed, attn_low, output_columns_up_factor
    )
    feedforward_branch, adapter_shrink_hidden = finish(
        mlp_summed, mlp_low, shrink_columns_up_factor
    )
    result = (hidden.astype(jnp.float32) + attention_branch + feedforward_branch).astype(
        jnp.bfloat16
    )
    back_out, back_shrink = (
        lax.psum_scatter(
            matrix_product_transposed_right(cotangent, output_frozen_weight),
            "mp",
            scatter_dimension=1,
            tiled=True,
        ),
        lax.psum_scatter(
            matrix_product_transposed_right(cotangent, shrink_frozen_weight),
            "mp",
            scatter_dimension=1,
            tiled=True,
        ),
    )
    rank_out, rank_shrink = lax.psum(
        (
            ADAPTER_SCALE * matrix_product_transposed_right(cotangent, output_columns_up_factor),
            ADAPTER_SCALE * matrix_product_transposed_right(cotangent, shrink_columns_up_factor),
        ),
        "mp",
    )
    low_out_grad = rank_out.astype(jnp.bfloat16)
    low_shrink_grad = rank_shrink.astype(jnp.bfloat16)
    output_up_factor_piece = ADAPTER_SCALE * matrix_product_transposed_left(
        adapter_output_hidden, cotangent
    )
    shrink_up_factor_piece = ADAPTER_SCALE * matrix_product_transposed_left(
        adapter_shrink_hidden, cotangent
    )
    grad_context = (back_out + matrix_product_transposed_right(low_out_grad, out_rows_a)).astype(
        jnp.bfloat16
    )
    output_a_piece = matrix_product_transposed_left(attended_context, low_out_grad)
    shrink_a_piece = matrix_product_transposed_left(active_hidden, low_shrink_grad)
    grad_active = back_shrink + matrix_product_transposed_right(low_shrink_grad, shrink_rows_a)
    upper_gradient = gelu_pull(grad_active)[0].astype(jnp.bfloat16)
    grad_context = grad_context.reshape(count, SEQ_LEN, heads_here, HEAD_DIM)
    grad_query, grad_keys, grad_values = lax.map(
        partial(attend_back, causal), (query, keys, values, grad_context, logsum)
    )
    mixed_gradient = jnp.stack(
        [unrotate(grad_query, cosine, sine), unrotate(grad_keys, cosine, sine), grad_values], 3
    )
    mixed_gradient = mixed_gradient.reshape(rows, joined_cols).astype(jnp.bfloat16)
    rank_joined, rank_expand = lax.psum(
        (
            ADAPTER_SCALE * matrix_product_transposed_right(mixed_gradient, joined_weight_local),
            ADAPTER_SCALE * matrix_product_transposed_right(upper_gradient, expand_weight_local),
        ),
        "mp",
    )
    low_joined_grad = rank_joined.astype(jnp.bfloat16)
    low_expand_grad = rank_expand.astype(jnp.bfloat16)
    joined_up_factor_piece = ADAPTER_SCALE * matrix_product_transposed_left(
        adapter_joined_hidden, mixed_gradient
    )
    expand_up_factor_piece = ADAPTER_SCALE * matrix_product_transposed_left(
        adapter_expand_hidden, upper_gradient
    )
    norm_one_cols = lax.dynamic_slice_in_dim(first_norm_output, rank * cols, cols, 1)
    norm_two_cols = lax.dynamic_slice_in_dim(second_norm_output, rank * cols, cols, 1)
    joined_a_piece = matrix_product_transposed_left(norm_one_cols, low_joined_grad)
    expand_a_piece = matrix_product_transposed_left(norm_two_cols, low_expand_grad)
    grad_one, grad_two = (
        lax.psum_scatter(
            matrix_product_transposed_right(mixed_gradient, joined_frozen_weight),
            "mp",
            scatter_dimension=1,
            tiled=True,
        ),
        lax.psum_scatter(
            matrix_product_transposed_right(upper_gradient, expand_frozen_weight),
            "mp",
            scatter_dimension=1,
            tiled=True,
        ),
    )
    joined_rows_a = lax.dynamic_slice_in_dim(joined_a, rank * cols, cols, 0)
    expand_rows_a = lax.dynamic_slice_in_dim(expand_a, rank * cols, cols, 0)
    grad_one = grad_one + matrix_product_transposed_right(low_joined_grad, joined_rows_a)
    grad_two = grad_two + matrix_product_transposed_right(low_expand_grad, expand_rows_a)
    unit_one_cols = lax.dynamic_slice_in_dim(unit_one, rank * cols, cols, 1)
    unit_two_cols = lax.dynamic_slice_in_dim(unit_two, rank * cols, cols, 1)
    gain_one_cols = lax.dynamic_slice_in_dim(first_gain, rank * cols, cols, 0)
    gain_two_cols = lax.dynamic_slice_in_dim(second_gain, rank * cols, cols, 0)
    first_gain_piece = jnp.sum(grad_one * unit_one_cols, 0)
    first_bias_piece = jnp.sum(grad_one, 0)
    second_gain_piece = jnp.sum(grad_two * unit_two_cols, 0)
    second_bias_piece = jnp.sum(grad_two, 0)
    scaled_one = grad_one * gain_one_cols
    scaled_two = grad_two * gain_two_cols
    plain_one, along_one, plain_two, along_two = (
        lax.psum(jnp.sum(scaled_one, -1).astype(jnp.bfloat16), "mp").astype(jnp.float32),
        lax.psum(jnp.sum(scaled_one * unit_one_cols, -1).astype(jnp.bfloat16), "mp").astype(
            jnp.float32
        ),
        lax.psum(jnp.sum(scaled_two, -1).astype(jnp.bfloat16), "mp").astype(jnp.float32),
        lax.psum(jnp.sum(scaled_two * unit_two_cols, -1).astype(jnp.bfloat16), "mp").astype(
            jnp.float32
        ),
    )
    back_one = factor_one * (
        scaled_one - plain_one[:, None] / width - unit_one_cols * along_one[:, None] / width
    )
    back_two = factor_two * (
        scaled_two - plain_two[:, None] / width - unit_two_cols * along_two[:, None] / width
    )
    hidden_grad = cotangent.astype(jnp.float32) + back_one + back_two
    pieces = (
        first_gain_piece,
        first_bias_piece,
        second_gain_piece,
        second_bias_piece,
        joined_a_piece,
        joined_up_factor_piece,
        output_a_piece,
        output_up_factor_piece,
        expand_a_piece,
        expand_up_factor_piece,
        shrink_a_piece,
        shrink_up_factor_piece,
    )
    shapes = (
        first_gain.shape,
        first_bias.shape,
        second_gain.shape,
        second_bias.shape,
        joined_a.shape,
        joined_up_factor.shape,
        output_a.shape,
        output_up_factor.shape,
        expand_a.shape,
        expand_up_factor.shape,
        shrink_a.shape,
        shrink_up_factor.shape,
    )
    along = (0, 0, 0, 0, 0, 1, 0, 1, 0, 1, 0, 1)
    padded = [
        lax.dynamic_update_slice_in_dim(
            jnp.zeros(shape, jnp.float32), piece, rank * piece.shape[axis_dim], axis_dim
        )
        for piece, shape, axis_dim in zip(pieces, shapes, along)
    ]
    grads = lax.psum(
        (
            padded[0],
            padded[1],
            padded[2],
            padded[3],
            padded[4],
            padded[5],
            padded[6],
            padded[7],
            padded[8],
            padded[9],
            padded[10],
            padded[11],
        ),
        ("dp", "mp"),
    )
    return (
        result,
        hidden_grad,
        grads[0],
        grads[1],
        grads[2],
        grads[3],
        grads[4],
        grads[5],
        grads[6],
        grads[7],
        grads[8],
        grads[9],
        grads[10],
        grads[11],
    )


BF = jnp.bfloat16
F32 = jnp.float32
BLOCK = 256
VMEM_LIMIT = 62 << 20


def nn(left, right):
    return lax.dot_general(left, right, (((1,), (0,)), ((), ())), preferred_element_type=F32)


def nt(left, right):
    return lax.dot_general(left, right, (((1,), (1,)), ((), ())), preferred_element_type=F32)


def tn(left, right):
    return lax.dot_general(left, right, (((0,), (0,)), ((), ())), preferred_element_type=F32)


def span(start, size, unit=128):
    return pl.ds(pl.multiple_of(start, unit), size)


def layer_norm(rows_f32):
    center = rows_f32 - jnp.mean(rows_f32, 1, keepdims=True)
    factor = lax.rsqrt(jnp.mean(center * center, 1, keepdims=True) + EPS)
    return center * factor, factor


def attention_kernel(slots, shared, ids, *refs):
    hg_refs, w_own = refs[0:6], refs[6]
    o_own, o_mate = refs[7:9]
    foreign, diag = refs[9:13], refs[13:17]
    gain, bias, up, ja, oa, ou, cos_ref, sin_ref = refs[17:25]
    n_out = 4 if shared else 2
    outs = refs[25 : 25 + n_out]
    (h_v, g_v, w_v, o_v, w_t, q_t, k_t, v_t, k_n, v_n, do_t, dm_t, ctx_t, dk, dv, both, tok_sem, w_sem) = refs[25 + n_out :]
    f, q = ids[0], ids[1]
    seq = h_v.shape[0]
    steps = seq // BLOCK
    heads = q_t.shape[0] // HEAD_DIM
    width = h_v.shape[1]
    piece = width // 4
    shard = w_v.shape[1] // len(slots)
    for i, slot in enumerate(slots):
        if slot == 0:
            for s in range(4):
                pltpu.make_async_copy(
                    w_own.at[span(lax.bitwise_xor(f, s) * piece, piece), :],
                    w_v.at[s * piece : (s + 1) * piece, i * shard : (i + 1) * shard],
                    w_sem.at[0],
                ).start()
        else:
            for k in range(4):
                row = lax.bitwise_xor(lax.bitwise_xor(q, k), f) * piece
                pltpu.make_async_copy(
                    foreign[k].at[:, :shard], w_v.at[span(row, piece), i * shard : (i + 1) * shard], w_sem.at[0]
                ).start()
        head_block = lax.bitwise_xor(f, slot)
        rows = slice(i * BLOCK, (i + 1) * BLOCK)
        for s, ref in ((0, o_own), (1, o_mate)):
            pltpu.make_async_copy(
                ref.at[span(head_block * BLOCK, BLOCK), :], o_v.at[rows, s * piece : (s + 1) * piece], w_sem.at[1]
            ).start()
        for s, pieces in ((2, foreign), (3, diag)):
            for k in range(4):

                @pl.when(lax.bitwise_xor(q, k) == head_block)
                def _():
                    pltpu.make_async_copy(
                        pieces[k].at[:, shard : shard + BLOCK], o_v.at[rows, s * piece : (s + 1) * piece], w_sem.at[1]
                    ).start()

    start = 2 * seq if shared else lax.shift_right_logical(f, 1) * seq
    for i, dst in enumerate((h_v, g_v)):
        for s in range(4):
            ref = hg_refs[2 * i + s] if s < 2 else hg_refs[2 + s]
            at = start if s < 2 else i * seq
            pltpu.make_async_copy(
                ref.at[span(at, seq), :], dst.at[:, s * piece : (s + 1) * piece], tok_sem.at[i]
            ).start()

    pltpu.make_async_copy(w_v, w_v, w_sem.at[0]).wait()
    w_t[...] = w_v[...].T
    pltpu.make_async_copy(o_v, o_v, w_sem.at[1]).wait()
    up_t = jnp.concatenate([up[:, s * shard : (s + 1) * shard] for s in slots], 1).T
    oa_rows = jnp.concatenate([oa[s * BLOCK : (s + 1) * BLOCK, :] for s in slots], 0)
    o_rows = o_v[...]

    def project(t):
        rows = slice(t * BLOCK, (t + 1) * BLOCK)
        unit, _ = layer_norm(h_v[rows, :].astype(F32))
        n = (unit * gain[...] + bias[...]).astype(BF)
        low = (nn(n, ja[...]).astype(BF) * ADAPTER_SCALE).astype(BF)
        mixed = nt(w_t[...], n) + nt(up_t, low)
        cos, sin = cos_ref[:, rows], sin_ref[:, rows]
        half = ROTARY // 2
        for h in range(heads):
            own = slice(h * HEAD_DIM, (h + 1) * HEAD_DIM)
            base = 3 * HEAD_DIM * h
            for part in range(2):
                block = mixed[base + part * HEAD_DIM : base + (part + 1) * HEAD_DIM]
                a, b = block[:half], block[half:ROTARY]
                block = jnp.concatenate([a * cos - b * sin, b * cos + a * sin, block[ROTARY:]], 0).astype(BF)
                if part == 0:
                    q_t[own, rows] = (block * HEAD_DIM ** (-0.5)).astype(BF)
                else:
                    k_t[own, rows] = block
                    k_n[rows, own] = block.T
            block = mixed[base + 2 * HEAD_DIM : base + 3 * HEAD_DIM].astype(BF)
            v_t[own, rows] = block
            v_n[rows, own] = block.T
        g = g_v[rows, :]
        low_grad = (nt(g, ou[...]) * ADAPTER_SCALE).astype(BF)
        do_t[:, rows] = (nt(o_rows, g) + nt(oa_rows, low_grad)).astype(BF)

    for i, dst in enumerate((h_v, g_v)):
        pltpu.make_async_copy(dst, dst, tok_sem.at[i]).wait()
    for t in range(steps):
        project(t)

    later = lax.broadcasted_iota(jnp.int32, (BLOCK, BLOCK), 0) > lax.broadcasted_iota(jnp.int32, (BLOCK, BLOCK), 1)
    state = {}

    def products(h, i):
        own, qs = slice(h * HEAD_DIM, (h + 1) * HEAD_DIM), slice(i * BLOCK, (i + 1) * BLOCK)
        state[h, i] = (
            [nn(k_n[j * BLOCK : (j + 1) * BLOCK, own], q_t[own, qs]) for j in range(i + 1)],
            [nn(v_n[j * BLOCK : (j + 1) * BLOCK, own], do_t[own, qs]) for j in range(i + 1)],
        )

    def soft(h, i):
        scores, d_probs = state[h, i]
        scores[-1] = jnp.where(later, -1e30, scores[-1])
        peak = reduce(jnp.maximum, [jnp.max(s, 0, keepdims=True) for s in scores])
        weights = [jnp.exp(s - peak) for s in scores]
        inverse = 1.0 / reduce(jnp.add, [jnp.sum(w, 0, keepdims=True) for w in weights])
        probs = [w * inverse for w in weights]
        inner = reduce(jnp.add, [jnp.sum(p * d, 0, keepdims=True) for p, d in zip(probs, d_probs)])
        state[h, i] = (
            [p.astype(BF) for p in probs],
            [(p * (d - inner)).astype(BF) for p, d in zip(probs, d_probs)],
        )

    def unturn(block, cos, sin):
        half = ROTARY // 2
        a, b = block[:half], block[half:ROTARY]
        return jnp.concatenate([a * cos + b * sin, b * cos - a * sin, block[ROTARY:]], 0).astype(BF)

    def finish_block(h, i):
        own, qs = slice(h * HEAD_DIM, (h + 1) * HEAD_DIM), slice(i * BLOCK, (i + 1) * BLOCK)
        base = 3 * HEAD_DIM * h
        probs, d_scores = state.pop((h, i))
        keys = slice(0, (i + 1) * BLOCK)
        ctx_t[own, qs] = nn(v_t[own, keys], jnp.concatenate(probs, 0)).astype(BF)
        d_query = nn(k_t[own, keys], jnp.concatenate(d_scores, 0)) * HEAD_DIM ** (-0.5)
        dm_t[base : base + HEAD_DIM, qs] = unturn(d_query, cos_ref[:, qs], sin_ref[:, qs])
        query, d_out = q_t[own, qs], do_t[own, qs]
        for j in range(i + 1):
            js = slice(j * BLOCK, (j + 1) * BLOCK)
            if j == i:
                dk[own, js] = nt(query, d_scores[j])
                dv[own, js] = nt(d_out, probs[j])
            else:
                dk[own, js] += nt(query, d_scores[j])
                dv[own, js] += nt(d_out, probs[j])
        if i == steps - 1:
            dm_t[base + HEAD_DIM : base + 2 * HEAD_DIM, :] = unturn(dk[own, :], cos_ref[...], sin_ref[...])
            dm_t[base + 2 * HEAD_DIM : base + 3 * HEAD_DIM, :] = dv[own, :].astype(BF)

    order = [(h, i) for h in range(heads) for i in range(steps)]
    for at in range(len(order) + 2):
        if at < len(order):
            products(*order[at])
        if at >= 2:
            finish_block(*order[at - 2])
        if 1 <= at <= len(order):
            soft(*order[at - 1])
    for i in range(len(slots)):
        at = i * (BLOCK + shard)
        both[:, at : at + BLOCK] = ctx_t[i * BLOCK : (i + 1) * BLOCK, :].T
        both[:, at + BLOCK : at + BLOCK + shard] = dm_t[i * shard : (i + 1) * shard, :].T
    if shared:
        for s in range(4):
            outs[s][...] = both[span(lax.bitwise_xor(f, s) * BLOCK, BLOCK), :]
    else:
        c = lax.bitwise_and(f, 1)
        half = seq // 2
        outs[0][...] = both[span(c * half, half), :]
        outs[1][...] = both[span((1 - c) * half, half), :]


def any_spec():
    return pl.BlockSpec(memory_space=pl.ANY)


def vmem_spec():
    return pl.BlockSpec(memory_space=pltpu.VMEM)


def smem_spec():
    return pl.BlockSpec(memory_space=pltpu.SMEM)


def attention(slots, shared, ids, hg, w_own, os, gain, bias, up, ja, oa, ou, cos, sin):
    seq, piece = SEQ_LEN, hg[0].shape[1]
    width = 4 * piece
    shard, own = up.shape[1] // 4, oa.shape[0] // 4
    joined, inner = shard * len(slots), own * len(slots)
    out_shape = [jax.ShapeDtypeStruct((BLOCK if shared else seq // 2, inner + joined), BF)] * (4 if shared else 2)

    return pl.pallas_call(
        partial(attention_kernel, slots, shared),
        in_specs=[smem_spec()] + [any_spec()] * 17 + [vmem_spec()] * 8,
        out_specs=[vmem_spec()] * len(out_shape),
        out_shape=out_shape,
        scratch_shapes=[
            pltpu.VMEM((seq, width), BF),
            pltpu.VMEM((seq, width), BF),
            pltpu.VMEM((width, joined), BF),
            pltpu.VMEM((inner, width), BF),
            pltpu.VMEM((joined, width), BF),
            pltpu.VMEM((inner, seq), BF),
            pltpu.VMEM((inner, seq), BF),
            pltpu.VMEM((inner, seq), BF),
            pltpu.VMEM((seq, inner), BF),
            pltpu.VMEM((seq, inner), BF),
            pltpu.VMEM((inner, seq), BF),
            pltpu.VMEM((joined, seq), BF),
            pltpu.VMEM((inner, seq), BF),
            pltpu.VMEM((inner, seq), F32),
            pltpu.VMEM((inner, seq), F32),
            pltpu.VMEM((seq, inner + joined), BF),
            pltpu.SemaphoreType.DMA((2,)),
            pltpu.SemaphoreType.DMA((2,)),
        ],
        compiler_params=pltpu.CompilerParams(vmem_limit_bytes=VMEM_LIMIT),
        cost_estimate=pl.CostEstimate(flops=100_000_000_000, bytes_accessed=100_000, transcendentals=0),
        name="attention",
    )(ids, *hg, w_own, *os, gain, bias, up, ja, oa, ou, cos, sin)


def token_copies(ids, tokens, which, dst, sem):
    f = ids[0]
    x, c = lax.shift_right_logical(f, 1), lax.bitwise_and(f, 1)
    seq = SEQ_LEN
    half = seq // 2
    piece = tokens[0].shape[1]
    for s in range(4):
        cols = slice(s * piece, (s + 1) * piece)
        if s < 2:
            own, shared = tokens[2 * which + s], tokens[2 * which + s]
            own_at, shared_at = x * seq, 2 * seq
        else:
            own, shared = tokens[2 + s], tokens[4 + s]
            own_at, shared_at = which * seq, which * seq
        pltpu.make_async_copy(own.at[span(own_at + c * half, half), :], dst.at[:half, cols], sem).start()
        pltpu.make_async_copy(
            shared.at[span(shared_at + f * BLOCK, BLOCK), :], dst.at[half : half + BLOCK, cols], sem
        ).start()


def attention_copies(own, shared, at, dst, sem):
    half = dst.shape[0] - BLOCK
    size = dst.shape[1] // 4
    pitch = shared[0].shape[1]
    for s in range(4):
        to = slice(s * size, (s + 1) * size)
        col = (s // 2) * pitch + at
        pltpu.make_async_copy(own[s % 2].at[:, col : col + size], dst.at[:half, to], sem).start()
        pltpu.make_async_copy(shared[s].at[:, at : at + size], dst.at[half : half + BLOCK, to], sem).start()


def arrived(dst, sem):
    pltpu.make_async_copy(dst, dst, sem).wait()


def grads_kernel(ids, *refs):
    tokens, a_own, a_sh = refs[0:8], refs[8:10], refs[10:14]
    gain, bias, up, ja, oa, ou = refs[14:20]
    low_out_ref, low_grad_ref, keep, send = refs[20:24]
    h_v, g_v, c_v, m_v, sem = refs[24:]
    f = ids[0]
    rows, width = h_v.shape
    piece = width // 4
    shard = m_v.shape[1] // 4
    token_copies(ids, tokens, 1, g_v, sem.at[1])
    attention_copies(a_own, a_sh, 0, c_v, sem.at[2])
    token_copies(ids, tokens, 0, h_v, sem.at[0])
    attention_copies(a_own, a_sh, BLOCK, m_v, sem.at[3])
    put = partial(put_blocks, f, keep, send)
    arrived(g_v, sem.at[1])
    arrived(c_v, sem.at[2])
    low_out = (nn(c_v[...], oa[...]).astype(BF) * ADAPTER_SCALE).astype(BF)
    low_out_ref[...] = low_out
    low_out_grad = (nt(g_v[...], ou[...]) * ADAPTER_SCALE).astype(BF)
    put(0, piece, low_out.T, g_v)
    put(width, piece, low_out_grad.T, c_v)
    arrived(h_v, sem.at[0])
    unit, _ = layer_norm(h_v[...].astype(F32))
    n = (unit * gain[...] + bias[...]).astype(BF)
    low = (nn(n, ja[...]).astype(BF) * ADAPTER_SCALE).astype(BF)
    arrived(m_v, sem.at[3])
    low_grad = (nt(m_v[...], up[...]) * ADAPTER_SCALE).astype(BF)
    low_grad_ref[...] = low_grad
    put(2 * width, shard, low.T, m_v)
    put(2 * width + 4 * shard, piece, low_grad.T, n)


def put_blocks(f, keep, send, base, size, left, right):
    half = keep.shape[0]
    for s in range(4):
        value = nn(left, right[:, s * size : (s + 1) * size])
        to = span(base + lax.bitwise_xor(f, s) * size, size)
        keep[:, to] = value[:half]
        send[:, to] = value[half:]


def grads_of_attention(ids, tokens, a_own, a_sh, gain, bias, up, ja, oa, ou):
    piece = tokens[0].shape[1]
    width = 4 * piece
    rows = SEQ_LEN // 2 + BLOCK
    shard = up.shape[1] // 4
    rank = ja.shape[1]
    total = 3 * width + 4 * shard
    return pl.pallas_call(
        grads_kernel,
        in_specs=[smem_spec()] + [any_spec()] * 14 + [vmem_spec()] * 6,
        out_specs=[vmem_spec()] * 4,
        out_shape=[
            jax.ShapeDtypeStruct((rows, rank), BF),
            jax.ShapeDtypeStruct((rows, rank), BF),
            jax.ShapeDtypeStruct((rank // 2, total), F32),
            jax.ShapeDtypeStruct((rank // 2, total), F32),
        ],
        scratch_shapes=[
            pltpu.VMEM((rows, width), BF),
            pltpu.VMEM((rows, width), BF),
            pltpu.VMEM((rows, width), BF),
            pltpu.VMEM((rows, 4 * shard), BF),
            pltpu.SemaphoreType.DMA((4,)),
        ],
        compiler_params=pltpu.CompilerParams(vmem_limit_bytes=VMEM_LIMIT),
        cost_estimate=pl.CostEstimate(flops=100_000_000_000, bytes_accessed=100_000, transcendentals=0),
        name="grads_of_attention",
    )(ids, *tokens, *a_own, *a_sh, gain, bias, up, ja, oa, ou)


def start_slot(slot, ids, weights, e_v, s_v, e_sem, s_sem):
    f, q = ids[0], ids[1]
    e_own, e_mate, s_own, s_mate = weights[:4]
    foreign, diag = weights[4:8], weights[8:12]
    width, hidden = e_v.shape
    piece, part = width // 4, hidden // 4
    cols = slice(slot * part, (slot + 1) * part)
    if slot < 2:
        for t in range(4):
            pltpu.make_async_copy(
                weights[slot].at[span(lax.bitwise_xor(f, t) * piece, piece), :],
                e_v.at[t * piece : (t + 1) * piece, cols],
                e_sem.at[slot],
            ).start()
    else:
        for k in range(4):
            rows = span(lax.bitwise_xor(lax.bitwise_xor(q, k), f) * piece, piece)
            pltpu.make_async_copy(
                weights[4 * slot - 4 + k].at[:piece, :], e_v.at[rows, cols], e_sem.at[slot]
            ).start()
    for s, ref in ((0, s_own), (1, s_mate)):
        pltpu.make_async_copy(
            ref.at[span(lax.bitwise_xor(f, slot) * part, part), :],
            s_v.at[cols, s * piece : (s + 1) * piece],
            s_sem.at[slot],
        ).start()
    for k in range(4):

        @pl.when(lax.bitwise_xor(lax.bitwise_xor(q, k), f) == slot)
        def _():
            for s, pieces in ((2, foreign), (3, diag)):
                shrink_copies(pieces[k], s_v, slot * part, s * piece, s_sem.at[slot])


def shrink_copies(pack, dst, row, col, sem):
    for u in range(pack.shape[1] // BLOCK):
        pltpu.make_async_copy(
            pack.at[BLOCK:, u * BLOCK : (u + 1) * BLOCK],
            dst.at[span(row + u * BLOCK, BLOCK), col : col + BLOCK],
            sem,
        ).start()


CHUNK = 512


def mlp_first_kernel(ids, *refs):
    tokens, weights = refs[0:8], refs[8:20]
    gain, bias, ea, eu, sa, su = refs[20:26]
    act_out, dup_out, ls_out, dle_out, keep, send = refs[26:32]
    h_v, g_v, n_v, e_v, s_v, act, dup, sem, e_sem, s_sem, o_sem = refs[32:]
    f = ids[0]
    rows, width = h_v.shape
    hidden = e_v.shape[1]
    token_copies(ids, tokens, 0, h_v, sem.at[0])
    token_copies(ids, tokens, 1, g_v, sem.at[1])
    load = lambda slot: start_slot(slot, ids, weights, e_v, s_v, e_sem, s_sem)
    load(0)
    arrived(h_v, sem.at[0])
    unit, _ = layer_norm(h_v[...].astype(F32))
    n_v[...] = (unit * gain[...] + bias[...]).astype(BF)
    low = (nn(n_v[...], ea[...]).astype(BF) * ADAPTER_SCALE).astype(BF)
    arrived(g_v, sem.at[1])
    low_grad = (nt(g_v[...], su[...]) * ADAPTER_SCALE).astype(BF)
    load(1)
    state = {}
    part, piece = hidden // 4, width // 4

    def products(b, t):
        ts, bs = slice(t * BLOCK, (t + 1) * BLOCK), slice(b * CHUNK, (b + 1) * CHUNK)
        if t == 0 and bs.start % part == 0:
            slot = bs.start // part
            whole = slice(slot * part, (slot + 1) * part)
            if 1 <= slot < 3:
                load(slot + 1)
            arrived(e_v.at[:, whole], e_sem.at[slot])
            arrived(s_v.at[whole, :], s_sem.at[slot])
        state[b, t] = (
            nn(n_v[ts, :], e_v[:, bs]) + nn(low[ts], eu[:, bs]),
            nt(g_v[ts, :], s_v[bs, :]) + nt(low_grad[ts], sa[bs, :]),
        )

    def bend(b, t):
        ts, bs = slice(t * BLOCK, (t + 1) * BLOCK), slice(b * CHUNK, (b + 1) * CHUNK)
        upper, d_active = state.pop((b, t))
        normal = 0.5 * (1.0 + lax.erf(upper * 0.7071067811865476))
        density = jnp.exp(-0.5 * upper * upper) * 0.3989422804014327
        act[ts, bs] = (upper * normal).astype(BF)
        dup[ts, bs] = (d_active * (normal + upper * density)).astype(BF)
        if t == rows // BLOCK - 1:
            pltpu.make_async_copy(act.at[:, bs], act_out.at[:, bs], o_sem.at[0]).start()
            pltpu.make_async_copy(dup.at[:, bs], dup_out.at[:, bs], o_sem.at[1]).start()

    order = [(b, t) for b in range(hidden // CHUNK) for t in range(rows // BLOCK)]
    for at in range(len(order) + 1):
        if at < len(order):
            products(*order[at])
        if at > 0:
            bend(*order[at - 1])

    put = partial(put_blocks, f, keep, send)
    put(0, part, low_grad.T, act)
    put(hidden, part, low.T, dup)
    low_shrink = (nn(act[...], sa[...]).astype(BF) * ADAPTER_SCALE).astype(BF)
    low_expand_grad = (nt(dup[...], eu[...]) * ADAPTER_SCALE).astype(BF)
    ls_out[...] = low_shrink
    dle_out[...] = low_expand_grad
    put(2 * hidden, piece, low_shrink.T, g_v)
    put(2 * hidden + width, piece, low_expand_grad.T, n_v)
    arrived(act, o_sem.at[0])
    arrived(dup, o_sem.at[1])


def mlp_first(ids, tokens, weights, gain, bias, ea, eu, sa, su):
    piece = tokens[0].shape[1]
    width = 4 * piece
    rows = SEQ_LEN // 2 + BLOCK
    hidden = eu.shape[1]
    rank = ea.shape[1]
    return pl.pallas_call(
        mlp_first_kernel,
        in_specs=[smem_spec()] + [any_spec()] * 20 + [vmem_spec()] * 6,
        out_specs=[any_spec()] * 2 + [vmem_spec()] * 4,
        out_shape=[
            jax.ShapeDtypeStruct((rows, hidden), BF),
            jax.ShapeDtypeStruct((rows, hidden), BF),
            jax.ShapeDtypeStruct((rows, rank), BF),
            jax.ShapeDtypeStruct((rows, rank), BF),
            jax.ShapeDtypeStruct((rank // 2, 2 * hidden + 2 * width), F32),
            jax.ShapeDtypeStruct((rank // 2, 2 * hidden + 2 * width), F32),
        ],
        scratch_shapes=[
            pltpu.VMEM((rows, width), BF),
            pltpu.VMEM((rows, width), BF),
            pltpu.VMEM((rows, width), BF),
            pltpu.VMEM((width, hidden), BF),
            pltpu.VMEM((hidden, width), BF),
            pltpu.VMEM((rows, hidden), BF),
            pltpu.VMEM((rows, hidden), BF),
            pltpu.SemaphoreType.DMA((2,)),
            pltpu.SemaphoreType.DMA((4,)),
            pltpu.SemaphoreType.DMA((4,)),
            pltpu.SemaphoreType.DMA((2,)),
        ],
        compiler_params=pltpu.CompilerParams(vmem_limit_bytes=VMEM_LIMIT),
        cost_estimate=pl.CostEstimate(flops=100_000_000_000, bytes_accessed=100_000, transcendentals=0),
        name="mlp_first",
    )(ids, *tokens, *weights, gain, bias, ea, eu, sa, su)


def rows_of_slot(s, ids, own, mate, foreign, diag, col, dst, sems):
    f, q = ids[0], ids[1]
    piece = own.shape[0] // 4
    cols = own.shape[1]
    to = slice(s * cols, (s + 1) * cols)
    for t in range(4):
        if s < 2:
            src = (own, mate)[s].at[span(lax.bitwise_xor(f, t) * piece, piece), :]
            place = t
        else:
            src = (foreign, diag)[s - 2][t].at[:piece, col : col + cols]
            place = lax.bitwise_xor(lax.bitwise_xor(q, t), f)
        pltpu.make_async_copy(src, dst.at[span(place * piece, piece), to], sems.at[place]).start()


def shrink_of_slot(s, ids, own, mate, foreign, diag, dst, sem):
    f, q = ids[0], ids[1]
    part, piece = dst.shape[0] // 4, dst.shape[1] // 4
    for t in range(4):
        if s < 2:
            src = (own, mate)[s].at[span(lax.bitwise_xor(f, t) * part, part), :]
            pltpu.make_async_copy(src, dst.at[t * part : (t + 1) * part, s * piece : (s + 1) * piece], sem).start()
        else:
            row = lax.bitwise_xor(lax.bitwise_xor(q, t), f) * part
            shrink_copies((foreign, diag)[s - 2][t], dst, row, s * piece, sem)


def result_kernel(ids, *refs):
    tokens, a_own, a_sh = refs[0:8], refs[8:10], refs[10:14]
    o_own, o_mate, s_own, s_mate = refs[14:18]
    one_f, one_d, two_f, two_d = refs[18:22], refs[22:26], refs[26:30], refs[30:34]
    act_ref = refs[34]
    low_out, ou, low_shrink, su = refs[35:39]
    outs = refs[39:43]
    h_v, c_v, o_v, s_v, act, sem, o_sem, s_sem = refs[43:]
    f = ids[0]
    rows, width = h_v.shape
    piece = width // 4
    attention_copies(a_own, a_sh, 0, c_v, sem.at[1])
    for s in range(4):
        rows_of_slot(s, ids, o_own, o_mate, one_f, one_d, 3 * piece, o_v, o_sem)
    token_copies(ids, tokens, 0, h_v, sem.at[2])
    pltpu.make_async_copy(act_ref, act, sem.at[3]).start()
    arrived(c_v, sem.at[1])
    for t in range(4):
        arrived(o_v.at[t * piece : (t + 1) * piece, :], o_sem.at[t])
    arrived(h_v, sem.at[2])
    for s in range(4):
        shrink_of_slot(s, ids, s_own, s_mate, two_f, two_d, s_v, s_sem.at[s])
    blocks = [slice(t * BLOCK, (t + 1) * BLOCK) for t in range(rows // BLOCK)]
    sums = [
        h_v[ts, :].astype(F32)
        + (nn(c_v[ts, :], o_v[...]) + nn(low_out[ts, :], ou[...]))
        + nn(low_shrink[ts, :], su[...])
        for ts in blocks
    ]
    arrived(act, sem.at[3])
    for s in range(4):
        arrived(s_v.at[:, s * piece : (s + 1) * piece], s_sem.at[s])
    for total, ts in zip(sums, blocks):
        value = (total + nn(act[ts, :], s_v[...])).astype(BF)
        for s in range(4):
            outs[s][ts, :] = value[:, s * piece : (s + 1) * piece]


def result_parts(ids, tokens, a_own, a_sh, o_parts, s_parts, one, two, act, low_out, ou, low_shrink, su):
    piece = tokens[0].shape[1]
    width = 4 * piece
    rows = SEQ_LEN // 2 + BLOCK
    hidden = act.shape[1]
    return pl.pallas_call(
        result_kernel,
        in_specs=[smem_spec()] + [any_spec()] * 35 + [vmem_spec()] * 4,
        out_specs=[vmem_spec()] * 4,
        out_shape=[jax.ShapeDtypeStruct((rows, piece), BF)] * 4,
        scratch_shapes=[
            pltpu.VMEM((rows, width), BF),
            pltpu.VMEM((rows, width), BF),
            pltpu.VMEM((width, width), BF),
            pltpu.VMEM((hidden, width), BF),
            pltpu.VMEM((rows, hidden), BF),
            pltpu.SemaphoreType.DMA((4,)),
            pltpu.SemaphoreType.DMA((4,)),
            pltpu.SemaphoreType.DMA((4,)),
        ],
        compiler_params=pltpu.CompilerParams(vmem_limit_bytes=VMEM_LIMIT),
        cost_estimate=pl.CostEstimate(flops=100_000_000_000, bytes_accessed=100_000, transcendentals=0),
        name="result_parts",
    )(ids, *tokens, *a_own, *a_sh, *o_parts, *s_parts, *one, *two, act, low_out, ou, low_shrink, su)


def input_grad_kernel(ids, *refs):
    tokens, a_own, a_sh = refs[0:8], refs[8:10], refs[10:14]
    w_own, w_mate, e_own, e_mate = refs[14:18]
    one_f, one_d, two_f, two_d = refs[18:22], refs[22:26], refs[26:30], refs[30:34]
    dup_ref = refs[34]
    gain_one, gain_two, ja, ea, low_joined_grad, low_expand_grad = refs[35:41]
    outs, sums = refs[41:45], refs[45]
    h_v, g_v, m_v, w_v, e_v, dup, one_v, sem, w_sem, e_sem = refs[46:]
    f = ids[0]
    rows, width = h_v.shape
    piece = width // 4
    shard = m_v.shape[1] // 4
    attention_copies(a_own, a_sh, BLOCK, m_v, sem.at[0])
    for s in range(4):
        rows_of_slot(s, ids, w_own, w_mate, one_f, one_d, 0, w_v, w_sem)
    arrived(m_v, sem.at[0])
    blocks = [slice(t * BLOCK, (t + 1) * BLOCK) for t in range(rows // BLOCK)]
    for t in range(4):
        arrived(w_v.at[t * piece : (t + 1) * piece, :], w_sem.at[t])
    pltpu.make_async_copy(dup_ref, dup, sem.at[3]).start()
    for s in range(4):
        rows_of_slot(s, ids, e_own, e_mate, two_f, two_d, 0, e_v, e_sem)
    token_copies(ids, tokens, 0, h_v, sem.at[1])
    token_copies(ids, tokens, 1, g_v, sem.at[2])
    for ts in blocks:
        one_v[ts, :] = nt(m_v[ts, :], w_v[...]) + nt(low_joined_grad[ts, :], ja[...])
    arrived(dup, sem.at[3])
    for t in range(4):
        arrived(e_v.at[t * piece : (t + 1) * piece, :], e_sem.at[t])
    arrived(h_v, sem.at[1])
    arrived(g_v, sem.at[2])
    total = None
    for ts in blocks:
        one = one_v[ts, :]
        two = nt(dup[ts, :], e_v[...]) + nt(low_expand_grad[ts, :], ea[...])
        unit, factor = layer_norm(h_v[ts, :].astype(F32))
        here = [jnp.sum(v, 0, keepdims=True) for v in (one * unit, one, two * unit, two)]
        total = here if total is None else [a + b for a, b in zip(total, here)]
        e = one * gain_one[...] + two * gain_two[...]
        plain = jnp.mean(e, 1, keepdims=True)
        along = jnp.mean(e * unit, 1, keepdims=True)
        value = g_v[ts, :].astype(F32) + factor * (e - plain - unit * along)
        for s in range(4):
            outs[s][ts, :] = value[:, s * piece : (s + 1) * piece].astype(outs[s].dtype)
    value = jnp.concatenate(total + [jnp.zeros((4, width), F32)], 0)
    for s in range(4):
        sums[:, span(lax.bitwise_xor(f, s) * piece, piece)] = value[:, s * piece : (s + 1) * piece]


def input_grad_parts(
    ids, tokens, a_own, a_sh, w_parts, e_parts, one, two, dup, gain_one, gain_two, ja, ea, low_joined_grad, low_expand_grad
):
    piece = tokens[0].shape[1]
    width = 4 * piece
    rows = SEQ_LEN // 2 + BLOCK
    hidden = dup.shape[1]
    joined = 4 * w_parts[0].shape[1]
    return pl.pallas_call(
        input_grad_kernel,
        in_specs=[smem_spec()] + [any_spec()] * 35 + [vmem_spec()] * 6,
        out_specs=[vmem_spec()] * 5,
        out_shape=[jax.ShapeDtypeStruct((rows, piece), t) for t in (F32, F32, BF, BF)]
        + [jax.ShapeDtypeStruct((8, width), F32)],
        scratch_shapes=[
            pltpu.VMEM((rows, width), BF),
            pltpu.VMEM((rows, width), BF),
            pltpu.VMEM((rows, joined), BF),
            pltpu.VMEM((width, joined), BF),
            pltpu.VMEM((width, hidden), BF),
            pltpu.VMEM((rows, hidden), BF),
            pltpu.VMEM((rows, width), F32),
            pltpu.SemaphoreType.DMA((4,)),
            pltpu.SemaphoreType.DMA((4,)),
            pltpu.SemaphoreType.DMA((4,)),
        ],
        compiler_params=pltpu.CompilerParams(vmem_limit_bytes=VMEM_LIMIT),
        cost_estimate=pl.CostEstimate(flops=100_000_000_000, bytes_accessed=100_000, transcendentals=0),
        name="input_grad_parts",
    )(
        ids, *tokens, *a_own, *a_sh, *w_parts, *e_parts, *one, *two, dup,
        gain_one, gain_two, ja, ea, low_joined_grad, low_expand_grad,
    )


def gather_rows_kernel(widen, ids, *refs):
    parts, out = refs[:4], refs[4]
    scratch = refs[5:]
    f = ids[0]
    sem = scratch[-1]
    rows = parts[0].shape[0]
    half = rows - BLOCK
    seq = 2 * half
    copies = []
    for s in range(4):
        src = parts[s]
        if src.dtype != out.dtype:
            scratch[s - 2][...] = src[...].astype(out.dtype)
            src = scratch[s - 2]
        at = lax.bitwise_xor(f, s)
        copies.append(pltpu.make_async_copy(src.at[:half, :], out.at[span(at * half, half), :], sem.at[2 * s]))
        copies.append(
            pltpu.make_async_copy(src.at[half:, :], out.at[span(2 * seq + at * BLOCK, BLOCK), :], sem.at[2 * s + 1])
        )
        copies[-2].start()
        copies[-1].start()
    for copy in copies:
        copy.wait()


def gather_rows(ids, parts, dtype):
    rows, piece = parts[0].shape
    narrow = [p for p in parts if p.dtype != dtype]
    return pl.pallas_call(
        partial(gather_rows_kernel, dtype),
        in_specs=[smem_spec()] + [vmem_spec()] * 4,
        out_specs=any_spec(),
        out_shape=jax.ShapeDtypeStruct((4 * rows, piece), dtype),
        scratch_shapes=[pltpu.VMEM((rows, piece), dtype)] * len(narrow) + [pltpu.SemaphoreType.DMA((8,))],
        compiler_params=pltpu.CompilerParams(vmem_limit_bytes=VMEM_LIMIT),
        name="gather_rows",
    )(ids, *parts)


def adapters_kernel(cuts, sums_at, ids, order_ref, *refs):
    order = order_ref[...]
    pieces, outs = refs[:8], refs[8:]
    for (at, size, turned), out in zip(cuts, outs):
        value = jnp.concatenate([p[:, at : at + size] for p in pieces], 0)
        out[...] = tn(value, order) if turned else tn(order, value)
    if sums_at is not None:
        sums, lanes = outs[-2:]
        for k in range(4):
            lanes[span(lax.bitwise_xor(ids[1], k) * 16, 16, 16), :] = pieces[k][:, sums_at : sums_at + 128].astype(F32)
        for i in range(8):
            sums[:, i * 128 : (i + 1) * 128] = lanes[i * 8 : (i + 1) * 8, :]


def adapters_out(ids, order, pieces, cuts, sums_at=None):
    rank = order.shape[0]
    out_shape = [jax.ShapeDtypeStruct((size, rank) if turned else (rank, size), F32) for at, size, turned in cuts]
    scratch = []
    if sums_at is not None:
        out_shape.append(jax.ShapeDtypeStruct((8, 1024), F32))
        scratch.append(pltpu.VMEM((64, 128), F32))
    return pl.pallas_call(
        partial(adapters_kernel, cuts, sums_at),
        in_specs=[smem_spec()] + [vmem_spec()] * 9,
        out_specs=[vmem_spec()] * len(out_shape),
        out_shape=out_shape,
        scratch_shapes=scratch,
        compiler_params=pltpu.CompilerParams(vmem_limit_bytes=VMEM_LIMIT),
        name="adapters_out",
    )(ids, order, *pieces)


def join_rows_kernel(keep, received, sums, other, out):
    cols = keep.shape[1]
    out[:, :cols] = (keep[...] + received[...]).astype(BF)
    total = sums[...] + other[...]
    out[:, cols:] = jnp.concatenate([total[:, i * 128 : (i + 1) * 128] for i in range(8)], 0).astype(BF)


def join_rows(keep, received, sums, other):
    rows, cols = keep.shape
    return pl.pallas_call(
        join_rows_kernel,
        in_specs=[vmem_spec()] * 4,
        out_specs=vmem_spec(),
        out_shape=jax.ShapeDtypeStruct((rows, cols + 128), BF),
        compiler_params=pltpu.CompilerParams(vmem_limit_bytes=VMEM_LIMIT),
        name="join_rows",
    )(keep, received, sums, other)


def split_rows_kernel(keep, received, own, *outs):
    size = own.shape[0]
    own[...] = keep[:size, :] + received[:size, :]
    for k, out in enumerate(outs):
        rows = slice((k + 1) * size, (k + 2) * size)
        out[...] = (keep[rows, :] + received[rows, :]).astype(BF)


def split_rows(keep, received):
    rows, cols = keep.shape
    return pl.pallas_call(
        split_rows_kernel,
        in_specs=[vmem_spec()] * 2,
        out_specs=[vmem_spec()] * 4,
        out_shape=[jax.ShapeDtypeStruct((rows // 4, cols), t) for t in (F32, BF, BF, BF)],
        compiler_params=pltpu.CompilerParams(vmem_limit_bytes=VMEM_LIMIT),
        name="split_rows",
    )(keep, received)


def pack_kernel(plan, ids, *refs):
    n_in = len(refs) - 1 - len(plan)
    srcs, outs, sem = refs[:n_in], refs[n_in:-1], refs[-1]
    for out, (shape, blocks) in zip(outs, plan):
        for src, which, size, sub, rows, to_row, to_col in blocks:
            cols = srcs[src].shape[1]
            pltpu.make_async_copy(
                srcs[src].at[span(ids[which] * size + sub, rows), :],
                out.at[to_row : to_row + rows, to_col : to_col + cols],
                sem,
            ).start()
    for out in outs:
        pltpu.make_async_copy(out, out, sem).wait()


def pack(ids, arrays, plan):
    return pl.pallas_call(
        partial(pack_kernel, plan),
        in_specs=[smem_spec()] + [any_spec()] * len(arrays),
        out_specs=[vmem_spec()] * len(plan),
        out_shape=[jax.ShapeDtypeStruct(shape, arrays[0].dtype) for shape, _ in plan],
        scratch_shapes=[pltpu.SemaphoreType.DMA],
        compiler_params=pltpu.CompilerParams(vmem_limit_bytes=VMEM_LIMIT),
        name="pack",
    )(ids, *arrays)


def order_kernel(late, ids, order_ref, other_ref, *refs):
    n = len(refs) // 2
    f = ids[0]
    for i, (src, out) in enumerate(zip(refs[:n], refs[n:])):
        order = (other_ref if i in late else order_ref)[...]
        axis = 0 if src.shape[0] > src.shape[1] else 1
        size = src.shape[axis] // 4
        for s in range(4):
            at, to = span(lax.bitwise_xor(f, s) * size, size), slice(s * size, (s + 1) * size)
            if src.dtype == F32:
                out[:, to] = src[:, at]
            elif axis == 0:
                out[to, :] = nt(src[at, :], order).astype(BF)
            else:
                out[:, to] = nn(order, src[:, at]).astype(BF)


def order_params(ids, order, other, params, late):
    return pl.pallas_call(
        partial(order_kernel, late),
        in_specs=[smem_spec()] + [vmem_spec()] * (2 + len(params)),
        out_specs=[vmem_spec()] * len(params),
        out_shape=[jax.ShapeDtypeStruct(p.shape, p.dtype) for p in params],
        compiler_params=pltpu.CompilerParams(vmem_limit_bytes=VMEM_LIMIT),
        name="order_params",
    )(ids, order, other, *params)


def swap(axes):
    def run(value):
        size = lax.axis_size(axes)
        return lax.ppermute(value, axes, [(i, size - 1 - i) for i in range(size)])

    return run


def after(value, *others):
    return lax.optimization_barrier((value, *others))[0]


def on_device_by_tokens(
    hidden,
    first_gain,
    first_bias,
    second_gain,
    second_bias,
    joined_frozen_weight,
    output_frozen_weight,
    expand_frozen_weight,
    shrink_frozen_weight,
    joined_a,
    joined_up_factor,
    output_a,
    output_up_factor,
    expand_a,
    expand_up_factor,
    shrink_a,
    shrink_up_factor,
    cotangent,
):
    x, c, q = lax.axis_index("x"), lax.axis_index("core"), lax.axis_index(("zn", "y"))
    f, far = 2 * x + c, lax.axis_index(("zf", "x"))
    seq, half = SEQ_LEN, SEQ_LEN // 2
    width = 4 * hidden.shape[1]
    rank = joined_a.shape[1]
    units = 4 * expand_frozen_weight.shape[1]
    ids = jnp.stack([f, q, far, 1 - x, 3 - q, 0 * f + 2]).astype(jnp.int32)
    to_core, to_x, to_diag = swap("core"), swap("x"), swap(("x", "core"))
    near = swap("y"), swap("zn"), swap(("zn", "y"))
    cross = to_x, swap("zf"), swap(("zf", "x"))

    piece = width // 4

    shard, part = joined_frozen_weight.shape[1], expand_frozen_weight.shape[1]
    (one_pack,) = pack(
        ids,
        (joined_frozen_weight, output_frozen_weight),
        (((piece, shard + piece), ((0, 1, piece, 0, piece, 0, 0), (1, 1, piece, 0, piece, 0, shard))),),
    )
    one_x = to_x(one_pack)
    own, shared = pack(
        after(ids, one_pack),
        (hidden, cotangent),
        tuple(((2 * seq, piece), ((0, at, seq, 0, seq, 0, 0), (1, at, seq, 0, seq, seq, 0))) for at in (3, 5)),
    )
    two_first, two_last = pack(
        after(ids, own),
        (expand_frozen_weight, shrink_frozen_weight),
        tuple(
            (
                (piece + BLOCK, part),
                ((0, at, piece, 0, piece, 0, 0),)
                + tuple((1, at, part, u, BLOCK, piece, u) for u in range(0, part, BLOCK)),
            )
            for at in (1, 4)
        ),
    )
    place = lax.broadcasted_iota(jnp.int32, (rank, rank), 0)
    half_order, order = (
        (lax.broadcasted_iota(jnp.int32, (rank, rank), 1) == (place ^ mask)).astype(BF) for mask in (c * 64, c * 64 + q * 16)
    )
    gain_one, bias_one, gain_two, bias_two, ja, oa, ea, sa, ju, ou, eu, su = order_params(
        after(ids, own),
        half_order,
        order,
        tuple(v[None, :] for v in (first_gain, first_bias, second_gain, second_bias))
        + (joined_a, output_a, expand_a, shrink_a)
        + (joined_up_factor, output_up_factor, expand_up_factor, shrink_up_factor),
        (6, 7, 10, 11),
    )
    position = np.arange(seq, dtype=np.float32)[None, :]
    frequency = np.float32(10000.0) ** (-(np.arange(ROTARY // 2, dtype=np.float32) * np.float32(2.0)) / np.float32(ROTARY))
    angles = frequency[:, None] * position
    cos, sin = jnp.asarray(np.cos(angles), F32), jnp.asarray(np.sin(angles), F32)
    h_mate, g_mate = (to_core(v) for v in after((hidden, cotangent), one_pack))
    one_x = after(one_x, own, two_first, gain_one, h_mate, g_mate)
    o_mate = to_core(output_frozen_weight)
    own_x = to_x(after(own, one_x))
    one_near = tuple(go(one_x) for go in near)
    own_x = after(own_x, one_near)
    own_mate = to_core(own_x)
    one_foreign = (one_x,) + one_near
    one_diag = tuple(to_core(p) for p in one_foreign)
    local = (hidden, h_mate, cotangent, g_mate)
    o_parts = (output_frozen_weight, o_mate) + one_foreign + one_diag
    params = (gain_one, bias_one, ju, ja, oa, ou, cos, sin)
    shared_x = to_x(after(shared, own_x))
    e_mate, s_mate, w_mate = (to_core(w) for w in (expand_frozen_weight, shrink_frozen_weight, joined_frozen_weight))
    two_x = to_x(after(two_first, own_x))
    keep_a, send_a = attention(
        (0, 2), False, ids, local + (own_x, own_mate), joined_frozen_weight, o_parts, *params
    )
    shared_x, two_x = after((shared_x, two_x), keep_a)
    e_mate, s_mate, w_mate = after((e_mate, s_mate, w_mate), shared_x, two_x)
    two_x = after(two_x, e_mate, s_mate, w_mate)
    shared_mate = to_core(shared_x)
    two_y, two_z, two_yz = near[0](two_x), near[1](two_x), to_x(after(two_last, two_x))
    b_parts = attention(
        (0,), True, ids, local + (shared_x, shared_mate), joined_frozen_weight, o_parts, *params
    )
    two_y, two_z, two_yz = after((two_y, two_z, two_yz), b_parts[0])
    foreign_two = (two_x, two_y, two_z, two_yz)
    diag_two = tuple(to_core(p) for p in foreign_two)
    tokens = local + (own_x, own_mate, shared_x, shared_mate)
    mlp_weights = (expand_frozen_weight, e_mate, shrink_frozen_weight, s_mate) + foreign_two + diag_two
    act, dup, ls, dle, keep_two, send_two = mlp_first(
        ids, tokens, mlp_weights, gain_two, bias_two, ea, eu, sa, su
    )
    b_moved = tuple(go(p) for go, p in zip((to_core, to_x, to_diag), b_parts[1:]))
    b_moved, a_mate = after((b_moved, to_core(send_a)), act)
    a_own, a_shared = (keep_a, a_mate), (b_parts[0],) + b_moved

    two = to_core(send_two)
    low_out, low_joined_grad, keep_one, send_one = grads_of_attention(
        ids, tokens, a_own, a_shared, gain_one, bias_one, ju, ja, oa, ou
    )
    two = split_rows(keep_two, after(two, low_out))
    dup = after(dup, two, send_one)
    two = (two[0],) + tuple(go(p) for go, p in zip(near, two[1:]))
    one = to_core(send_one)
    hidden_grad = input_grad_parts(
        ids, tokens, a_own, a_shared, (joined_frozen_weight, w_mate), (expand_frozen_weight, e_mate),
        one_foreign + one_diag, foreign_two + diag_two, dup, gain_one, gain_two, ja, ea, low_joined_grad, dle,
    )
    two, one = after((two, one), hidden_grad[4])
    sums = hidden_grad[4]
    hidden_grad = (hidden_grad[0], to_core(hidden_grad[1]), to_x(hidden_grad[2]), to_diag(hidden_grad[3]))

    def part_sum(parts):
        return reduce(jnp.add, [p.astype(F32) for p in parts]).astype(BF)

    two = part_sum(two)
    one = join_rows(keep_one, one, sums, to_core(sums))
    act = after(act, two, one, hidden_grad[1])
    two_other = cross[1](two)
    one = lax.all_to_all(one, ("zn", "y"), 0, 0, tiled=True)
    result = result_parts(
        ids, tokens, a_own, a_shared, (output_frozen_weight, o_mate), (shrink_frozen_weight, s_mate),
        one_foreign + one_diag, foreign_two + diag_two, act, low_out, ou, ls, su,
    )
    hidden_grad, two_other, one = after((hidden_grad, two_other, one), result)

    def all_of(part, ways):
        return (part,) + tuple(go(part) for go in ways)

    two = part_sum((two, two_other))
    two_other = cross[0](two)
    one = part_sum(after(one, two).reshape(4, -1, one.shape[1]))
    one_other = cross[1](one)
    hidden_grad = gather_rows(ids, hidden_grad, F32)
    two_other = after(two_other, hidden_grad)
    result = (result[0],) + tuple(go(p) for go, p in zip((to_core, to_x, to_diag), after(result[1:], two_other)))
    two = all_of(part_sum((two, two_other)), near)
    one = part_sum((one, one_other))
    one_other = cross[0](one)
    one = all_of(part_sum((one, one_other)), near)
    result = gather_rows(ids, result, BF)
    two = two + tuple(to_core(p) for p in after(two, result))
    one = one + tuple(to_core(p) for p in one)
    joined = ju.shape[1]
    expand_a_grad, expand_b_grad, shrink_a_grad, shrink_b_grad = adapters_out(
        ids, order, two,
        ((2 * units + width, width, True), (units, units, False), (0, units, True), (2 * units, width, False)),
    )
    joined_a_grad, joined_b_grad, output_a_grad, output_b_grad, sums = adapters_out(
        ids, order, one,
        ((2 * width + joined, width, True), (2 * width, joined, False), (width, width, True), (0, width, False)),
        3 * width + joined,
    )
    return (
        result,
        hidden_grad,
        sums[0],
        sums[1],
        sums[2],
        sums[3],
        joined_a_grad,
        joined_b_grad,
        output_a_grad,
        output_b_grad,
        expand_a_grad,
        expand_b_grad,
        shrink_a_grad,
        shrink_b_grad,
    )


def solution(mesh):
    step, rows, cols = on_device, "dp", "mp"
    if mesh.shape["dp"] == 8 and mesh.shape["mp"] == 4:
        step, rows, cols = on_device_by_tokens, ("zf", "zn", "y"), ("x", "core")
        mesh = Mesh(mesh.devices.reshape((2,) * 5), rows + cols)
    whole, split, tokens = P(), P(None, cols), P(rows, cols)
    return jax.shard_map(
        step,
        mesh=mesh,
        in_specs=(tokens,) + (whole,) * 4 + (split,) * 4 + (whole,) * 8 + (tokens,),
        out_specs=(tokens, tokens) + (whole,) * 12,
        check_vma=False,
    )
```

```python
from functools import partial, reduce

import jax
import jax.numpy as jnp
import numpy as np
from jax import lax
from jax.experimental import pallas as pl
from jax.experimental.pallas import tpu as pltpu
from jax.sharding import Mesh
from jax.sharding import PartitionSpec as P

ROTARY = 16
SEQ_LEN = 1024
HEAD_DIM = 64


ADAPTER_SCALE = 0.25
EPS = 1e-05


def matrix_product(left, right):
    return jnp.dot(left, right, preferred_element_type=jnp.float32)


def matrix_product_transposed_left(left, right):
    return lax.dot_general(
        left, right, (((0,), (0,)), ((), ())), preferred_element_type=jnp.float32
    )


def matrix_product_transposed_right(left, right):
    return lax.dot_general(
        left, right, (((1,), (1,)), ((), ())), preferred_element_type=jnp.float32
    )


def normalize(full, gain, bias):
    center = full - jnp.mean(full, -1, keepdims=True)
    factor = lax.rsqrt(jnp.mean(center * center, -1, keepdims=True) + EPS)
    unit = center * factor
    return (unit, factor, unit * gain + bias)


def tables():
    position = jnp.arange(SEQ_LEN, dtype=jnp.float32)[:, None]
    frequency = 10000.0 ** (-(jnp.arange(ROTARY // 2, dtype=jnp.float32) * 2.0) / ROTARY)
    angles = position * frequency[None, :]
    cosine = jnp.concatenate([jnp.cos(angles), jnp.cos(angles)], -1)[:, None, :]
    sine = jnp.concatenate([jnp.sin(angles), jnp.sin(angles)], -1)[:, None, :]
    return (cosine, sine)


def rotate(block, cosine, sine):
    half = ROTARY // 2
    part = block[..., :ROTARY]
    turned = jnp.concatenate([-part[..., half:], part[..., :half]], -1)
    return jnp.concatenate([part * cosine + turned * sine, block[..., ROTARY:]], -1)


def unrotate(grad, cosine, sine):
    half = ROTARY // 2
    part = grad[..., :ROTARY]
    scaled = part * sine
    untied = jnp.concatenate([scaled[..., half:], -scaled[..., :half]], -1)
    return jnp.concatenate([part * cosine + untied, grad[..., ROTARY:]], -1)


def attend(causal, block):
    query, keys, values = block
    scores = jnp.einsum(
        "qhe,khe->hqk", query, keys, preferred_element_type=jnp.float32
    ) * HEAD_DIM ** (-0.5)
    scores = jnp.where(causal, scores, -1e30)
    peak = jnp.max(scores, -1, keepdims=True)
    weights = jnp.exp(scores - peak)
    total = jnp.sum(weights, -1, keepdims=True)
    probs = (weights / total).astype(jnp.bfloat16)
    attended_context = jnp.einsum("hqk,khe->qhe", probs, values, preferred_element_type=jnp.float32)
    return (attended_context.astype(jnp.bfloat16), (peak + jnp.log(total))[..., 0])


def attend_back(causal, block):
    query, keys, values, grad_context, logsum = block
    scores = jnp.einsum(
        "qhe,khe->hqk", query, keys, preferred_element_type=jnp.float32
    ) * HEAD_DIM ** (-0.5)
    scores = jnp.where(causal, scores, -1e30)
    probs = jnp.exp(scores - logsum[..., None])
    grad_probs = jnp.einsum(
        "qhe,khe->hqk", grad_context, values, preferred_element_type=jnp.float32
    )
    inner = jnp.sum(probs * grad_probs, -1, keepdims=True)
    grad_scores = (probs * (grad_probs - inner)).astype(jnp.bfloat16)
    grad_query = jnp.einsum(
        "hqk,khe->qhe", grad_scores, keys, preferred_element_type=jnp.float32
    ) * HEAD_DIM ** (-0.5)
    grad_keys = jnp.einsum(
        "hqk,qhe->khe", grad_scores, query, preferred_element_type=jnp.float32
    ) * HEAD_DIM ** (-0.5)
    grad_values = jnp.einsum(
        "hqk,qhe->khe", probs.astype(jnp.bfloat16), grad_context, preferred_element_type=jnp.float32
    )
    return (grad_query, grad_keys, grad_values)


def fold_with(weight, adapter_a, carry, piece):
    span = piece.shape[1]
    weight_rows = lax.slice_in_dim(weight, 0, span, axis=0)
    adapter_rows = lax.slice_in_dim(adapter_a, 0, span, axis=0)
    return (
        carry[0] + matrix_product(piece, weight_rows),
        carry[1] + matrix_product(piece, adapter_rows),
    )


def finish(summed_result, low_sum, columns_up_factor):
    adapter_values = low_sum.astype(jnp.bfloat16)
    return (
        summed_result + ADAPTER_SCALE * matrix_product(adapter_values, columns_up_factor),
        adapter_values,
    )


def on_device(
    hidden,
    first_gain,
    first_bias,
    second_gain,
    second_bias,
    joined_frozen_weight,
    output_frozen_weight,
    expand_frozen_weight,
    shrink_frozen_weight,
    joined_a,
    joined_up_factor,
    output_a,
    output_up_factor,
    expand_a,
    expand_up_factor,
    shrink_a,
    shrink_up_factor,
    cotangent,
):
    rank = lax.axis_index("mp")
    rows = hidden.shape[0]
    cols = hidden.shape[1]
    width = cols * lax.axis_size("mp")
    count = rows // SEQ_LEN
    joined_cols = joined_frozen_weight.shape[1]
    expand_cols = expand_frozen_weight.shape[1]
    heads_here = joined_cols // (3 * HEAD_DIM)
    inner_out = joined_cols // 3
    full = lax.all_gather(hidden, "mp", axis=1, tiled=True).astype(jnp.float32)
    unit_one, factor_one, first_norm_output = normalize(full, first_gain, first_bias)
    unit_two, factor_two, second_norm_output = normalize(full, second_gain, second_bias)
    first_norm_output = first_norm_output.astype(jnp.bfloat16)
    second_norm_output = second_norm_output.astype(jnp.bfloat16)
    adapter_joined_hidden = matrix_product(first_norm_output, joined_a).astype(jnp.bfloat16)
    joined_weight_local = lax.dynamic_slice_in_dim(
        joined_up_factor, rank * joined_cols, joined_cols, 1
    )
    mixed_state = matrix_product(
        first_norm_output, joined_frozen_weight
    ) + ADAPTER_SCALE * matrix_product(adapter_joined_hidden, joined_weight_local)
    mixed_state = mixed_state.reshape(count, SEQ_LEN, heads_here, 3, HEAD_DIM)
    cosine, sine = tables()
    query = rotate(mixed_state[:, :, :, 0], cosine, sine).astype(jnp.bfloat16)
    keys = rotate(mixed_state[:, :, :, 1], cosine, sine).astype(jnp.bfloat16)
    values = mixed_state[:, :, :, 2].astype(jnp.bfloat16)
    causal = jnp.arange(SEQ_LEN)[:, None] >= jnp.arange(SEQ_LEN)[None, :]
    attended_context, logsum = lax.map(partial(attend, causal), (query, keys, values))
    attended_context = attended_context.reshape(rows, inner_out)
    adapter_expand_hidden = matrix_product(second_norm_output, expand_a).astype(jnp.bfloat16)
    expand_weight_local = lax.dynamic_slice_in_dim(
        expand_up_factor, rank * expand_cols, expand_cols, 1
    )
    upper_hidden = matrix_product(
        second_norm_output, expand_frozen_weight
    ) + ADAPTER_SCALE * matrix_product(adapter_expand_hidden, expand_weight_local)
    gelu_exact = partial(jax.nn.gelu, approximate=False)
    active_f, gelu_pull = jax.vjp(gelu_exact, upper_hidden)
    active_hidden = active_f.astype(jnp.bfloat16)
    out_rows_a = lax.dynamic_slice_in_dim(output_a, rank * inner_out, inner_out, 0)
    output_columns_up_factor = lax.dynamic_slice_in_dim(output_up_factor, rank * cols, cols, 1)
    shrink_rows_a = lax.dynamic_slice_in_dim(shrink_a, rank * expand_cols, expand_cols, 0)
    shrink_columns_up_factor = lax.dynamic_slice_in_dim(shrink_up_factor, rank * cols, cols, 1)
    zero_pair = (
        jnp.zeros((rows, cols), jnp.float32),
        jnp.zeros((rows, output_a.shape[1]), jnp.float32),
    )
    attn_summed, attn_low = fold_with(
        output_frozen_weight,
        output_a,
        zero_pair,
        lax.all_gather(attended_context, "mp", axis=1, tiled=True),
    )
    mlp_summed, mlp_low = fold_with(
        shrink_frozen_weight,
        shrink_a,
        zero_pair,
        jax.tree.map(lambda a: lax.all_gather(a, "mp", axis=1, tiled=True), active_hidden),
    )
    attention_branch, adapter_output_hidden = finish(
        attn_summed, attn_low, output_columns_up_factor
    )
    feedforward_branch, adapter_shrink_hidden = finish(
        mlp_summed, mlp_low, shrink_columns_up_factor
    )
    result = (hidden.astype(jnp.float32) + attention_branch + feedforward_branch).astype(
        jnp.bfloat16
    )
    back_out, back_shrink = (
        lax.psum_scatter(
            matrix_product_transposed_right(cotangent, output_frozen_weight),
            "mp",
            scatter_dimension=1,
            tiled=True,
        ),
        lax.psum_scatter(
            matrix_product_transposed_right(cotangent, shrink_frozen_weight),
            "mp",
            scatter_dimension=1,
            tiled=True,
        ),
    )
    rank_out, rank_shrink = lax.psum(
        (
            ADAPTER_SCALE * matrix_product_transposed_right(cotangent, output_columns_up_factor),
            ADAPTER_SCALE * matrix_product_transposed_right(cotangent, shrink_columns_up_factor),
        ),
        "mp",
    )
    low_out_grad = rank_out.astype(jnp.bfloat16)
    low_shrink_grad = rank_shrink.astype(jnp.bfloat16)
    output_up_factor_piece = ADAPTER_SCALE * matrix_product_transposed_left(
        adapter_output_hidden, cotangent
    )
    shrink_up_factor_piece = ADAPTER_SCALE * matrix_product_transposed_left(
        adapter_shrink_hidden, cotangent
    )
    grad_context = (back_out + matrix_product_transposed_right(low_out_grad, out_rows_a)).astype(
        jnp.bfloat16
    )
    output_a_piece = matrix_product_transposed_left(attended_context, low_out_grad)
    shrink_a_piece = matrix_product_transposed_left(active_hidden, low_shrink_grad)
    grad_active = back_shrink + matrix_product_transposed_right(low_shrink_grad, shrink_rows_a)
    upper_gradient = gelu_pull(grad_active)[0].astype(jnp.bfloat16)
    grad_context = grad_context.reshape(count, SEQ_LEN, heads_here, HEAD_DIM)
    grad_query, grad_keys, grad_values = lax.map(
        partial(attend_back, causal), (query, keys, values, grad_context, logsum)
    )
    mixed_gradient = jnp.stack(
        [unrotate(grad_query, cosine, sine), unrotate(grad_keys, cosine, sine), grad_values], 3
    )
    mixed_gradient = mixed_gradient.reshape(rows, joined_cols).astype(jnp.bfloat16)
    rank_joined, rank_expand = lax.psum(
        (
            ADAPTER_SCALE * matrix_product_transposed_right(mixed_gradient, joined_weight_local),
            ADAPTER_SCALE * matrix_product_transposed_right(upper_gradient, expand_weight_local),
        ),
        "mp",
    )
    low_joined_grad = rank_joined.astype(jnp.bfloat16)
    low_expand_grad = rank_expand.astype(jnp.bfloat16)
    joined_up_factor_piece = ADAPTER_SCALE * matrix_product_transposed_left(
        adapter_joined_hidden, mixed_gradient
    )
    expand_up_factor_piece = ADAPTER_SCALE * matrix_product_transposed_left(
        adapter_expand_hidden, upper_gradient
    )
    norm_one_cols = lax.dynamic_slice_in_dim(first_norm_output, rank * cols, cols, 1)
    norm_two_cols = lax.dynamic_slice_in_dim(second_norm_output, rank * cols, cols, 1)
    joined_a_piece = matrix_product_transposed_left(norm_one_cols, low_joined_grad)
    expand_a_piece = matrix_product_transposed_left(norm_two_cols, low_expand_grad)
    grad_one, grad_two = (
        lax.psum_scatter(
            matrix_product_transposed_right(mixed_gradient, joined_frozen_weight),
            "mp",
            scatter_dimension=1,
            tiled=True,
        ),
        lax.psum_scatter(
            matrix_product_transposed_right(upper_gradient, expand_frozen_weight),
            "mp",
            scatter_dimension=1,
            tiled=True,
        ),
    )
    joined_rows_a = lax.dynamic_slice_in_dim(joined_a, rank * cols, cols, 0)
    expand_rows_a = lax.dynamic_slice_in_dim(expand_a, rank * cols, cols, 0)
    grad_one = grad_one + matrix_product_transposed_right(low_joined_grad, joined_rows_a)
    grad_two = grad_two + matrix_product_transposed_right(low_expand_grad, expand_rows_a)
    unit_one_cols = lax.dynamic_slice_in_dim(unit_one, rank * cols, cols, 1)
    unit_two_cols = lax.dynamic_slice_in_dim(unit_two, rank * cols, cols, 1)
    gain_one_cols = lax.dynamic_slice_in_dim(first_gain, rank * cols, cols, 0)
    gain_two_cols = lax.dynamic_slice_in_dim(second_gain, rank * cols, cols, 0)
    first_gain_piece = jnp.sum(grad_one * unit_one_cols, 0)
    first_bias_piece = jnp.sum(grad_one, 0)
    second_gain_piece = jnp.sum(grad_two * unit_two_cols, 0)
    second_bias_piece = jnp.sum(grad_two, 0)
    scaled_one = grad_one * gain_one_cols
    scaled_two = grad_two * gain_two_cols
    plain_one, along_one, plain_two, along_two = (
        lax.psum(jnp.sum(scaled_one, -1).astype(jnp.bfloat16), "mp").astype(jnp.float32),
        lax.psum(jnp.sum(scaled_one * unit_one_cols, -1).astype(jnp.bfloat16), "mp").astype(
            jnp.float32
        ),
        lax.psum(jnp.sum(scaled_two, -1).astype(jnp.bfloat16), "mp").astype(jnp.float32),
        lax.psum(jnp.sum(scaled_two * unit_two_cols, -1).astype(jnp.bfloat16), "mp").astype(
            jnp.float32
        ),
    )
    back_one = factor_one * (
        scaled_one - plain_one[:, None] / width - unit_one_cols * along_one[:, None] / width
    )
    back_two = factor_two * (
        scaled_two - plain_two[:, None] / width - unit_two_cols * along_two[:, None] / width
    )
    hidden_grad = cotangent.astype(jnp.float32) + back_one + back_two
    pieces = (
        first_gain_piece,
        first_bias_piece,
        second_gain_piece,
        second_bias_piece,
        joined_a_piece,
        joined_up_factor_piece,
        output_a_piece,
        output_up_factor_piece,
        expand_a_piece,
        expand_up_factor_piece,
        shrink_a_piece,
        shrink_up_factor_piece,
    )
    shapes = (
        first_gain.shape,
        first_bias.shape,
        second_gain.shape,
        second_bias.shape,
        joined_a.shape,
        joined_up_factor.shape,
        output_a.shape,
        output_up_factor.shape,
        expand_a.shape,
        expand_up_factor.shape,
        shrink_a.shape,
        shrink_up_factor.shape,
    )
    along = (0, 0, 0, 0, 0, 1, 0, 1, 0, 1, 0, 1)
    padded = [
        lax.dynamic_update_slice_in_dim(
            jnp.zeros(shape, jnp.float32), piece, rank * piece.shape[axis_dim], axis_dim
        )
        for piece, shape, axis_dim in zip(pieces, shapes, along)
    ]
    grads = lax.psum(
        (
            padded[0],
            padded[1],
            padded[2],
            padded[3],
            padded[4],
            padded[5],
            padded[6],
            padded[7],
            padded[8],
            padded[9],
            padded[10],
            padded[11],
        ),
        ("dp", "mp"),
    )
    return (
        result,
        hidden_grad,
        grads[0],
        grads[1],
        grads[2],
        grads[3],
        grads[4],
        grads[5],
        grads[6],
        grads[7],
        grads[8],
        grads[9],
        grads[10],
        grads[11],
    )


BF = jnp.bfloat16
F32 = jnp.float32
BLOCK = 256
VMEM_LIMIT = 62 << 20


def nn(left, right):
    return lax.dot_general(left, right, (((1,), (0,)), ((), ())), preferred_element_type=F32)


def nt(left, right):
    return lax.dot_general(left, right, (((1,), (1,)), ((), ())), preferred_element_type=F32)


def tn(left, right):
    return lax.dot_general(left, right, (((0,), (0,)), ((), ())), preferred_element_type=F32)


def span(start, size, unit=128):
    return pl.ds(pl.multiple_of(start, unit), size)


def layer_norm(rows_f32):
    center = rows_f32 - jnp.mean(rows_f32, 1, keepdims=True)
    factor = lax.rsqrt(jnp.mean(center * center, 1, keepdims=True) + EPS)
    return center * factor, factor


def attention_kernel(slots, shared, ids, *refs):
    hg_refs, w_own = refs[0:6], refs[6]
    o_own, o_mate = refs[7:9]
    foreign, diag = refs[9:13], refs[13:17]
    gain, bias, up, ja, oa, ou, cos_ref, sin_ref = refs[17:25]
    n_out = 4 if shared else 2
    outs = refs[25 : 25 + n_out]
    (h_v, g_v, w_v, o_v, w_t, q_t, k_t, v_t, k_n, v_n, do_t, dm_t, ctx_t, dk, dv, both, tok_sem, w_sem) = refs[25 + n_out :]
    f, q = ids[0], ids[1]
    seq = h_v.shape[0]
    steps = seq // BLOCK
    heads = q_t.shape[0] // HEAD_DIM
    width = h_v.shape[1]
    piece = width // 4
    shard = w_v.shape[1] // len(slots)
    for i, slot in enumerate(slots):
        if slot == 0:
            for s in range(4):
                pltpu.make_async_copy(
                    w_own.at[span(lax.bitwise_xor(f, s) * piece, piece), :],
                    w_v.at[s * piece : (s + 1) * piece, i * shard : (i + 1) * shard],
                    w_sem.at[0],
                ).start()
        else:
            for k in range(4):
                row = lax.bitwise_xor(lax.bitwise_xor(q, k), f) * piece
                pltpu.make_async_copy(
                    foreign[k].at[:, :shard], w_v.at[span(row, piece), i * shard : (i + 1) * shard], w_sem.at[0]
                ).start()
        head_block = lax.bitwise_xor(f, slot)
        rows = slice(i * BLOCK, (i + 1) * BLOCK)
        for s, ref in ((0, o_own), (1, o_mate)):
            pltpu.make_async_copy(
                ref.at[span(head_block * BLOCK, BLOCK), :], o_v.at[rows, s * piece : (s + 1) * piece], w_sem.at[1]
            ).start()
        for s, pieces in ((2, foreign), (3, diag)):
            for k in range(4):

                @pl.when(lax.bitwise_xor(q, k) == head_block)
                def _():
                    pltpu.make_async_copy(
                        pieces[k].at[:, shard : shard + BLOCK], o_v.at[rows, s * piece : (s + 1) * piece], w_sem.at[1]
                    ).start()

    start = 2 * seq if shared else lax.shift_right_logical(f, 1) * seq
    for i, dst in enumerate((h_v, g_v)):
        for s in range(4):
            ref = hg_refs[2 * i + s] if s < 2 else hg_refs[2 + s]
            at = start if s < 2 else i * seq
            pltpu.make_async_copy(
                ref.at[span(at, seq), :], dst.at[:, s * piece : (s + 1) * piece], tok_sem.at[i]
            ).start()

    pltpu.make_async_copy(w_v, w_v, w_sem.at[0]).wait()
    w_t[...] = w_v[...].T
    pltpu.make_async_copy(o_v, o_v, w_sem.at[1]).wait()
    up_t = jnp.concatenate([up[:, s * shard : (s + 1) * shard] for s in slots], 1).T
    oa_rows = jnp.concatenate([oa[s * BLOCK : (s + 1) * BLOCK, :] for s in slots], 0)
    o_rows = o_v[...]

    def project(t):
        rows = slice(t * BLOCK, (t + 1) * BLOCK)
        unit, _ = layer_norm(h_v[rows, :].astype(F32))
        n = (unit * gain[...] + bias[...]).astype(BF)
        low = (nn(n, ja[...]).astype(BF) * ADAPTER_SCALE).astype(BF)
        mixed = nt(w_t[...], n) + nt(up_t, low)
        cos, sin = cos_ref[:, rows], sin_ref[:, rows]
        half = ROTARY // 2
        for h in range(heads):
            own = slice(h * HEAD_DIM, (h + 1) * HEAD_DIM)
            base = 3 * HEAD_DIM * h
            for part in range(2):
                block = mixed[base + part * HEAD_DIM : base + (part + 1) * HEAD_DIM]
                a, b = block[:half], block[half:ROTARY]
                block = jnp.concatenate([a * cos - b * sin, b * cos + a * sin, block[ROTARY:]], 0).astype(BF)
                if part == 0:
                    q_t[own, rows] = (block * HEAD_DIM ** (-0.5)).astype(BF)
                else:
                    k_t[own, rows] = block
                    k_n[rows, own] = block.T
            block = mixed[base + 2 * HEAD_DIM : base + 3 * HEAD_DIM].astype(BF)
            v_t[own, rows] = block
            v_n[rows, own] = block.T
        g = g_v[rows, :]
        low_grad = (nt(g, ou[...]) * ADAPTER_SCALE).astype(BF)
        do_t[:, rows] = (nt(o_rows, g) + nt(oa_rows, low_grad)).astype(BF)

    for i, dst in enumerate((h_v, g_v)):
        pltpu.make_async_copy(dst, dst, tok_sem.at[i]).wait()
    for t in range(steps):
        project(t)

    later = lax.broadcasted_iota(jnp.int32, (BLOCK, BLOCK), 0) > lax.broadcasted_iota(jnp.int32, (BLOCK, BLOCK), 1)
    state = {}

    def products(h, i):
        own, qs = slice(h * HEAD_DIM, (h + 1) * HEAD_DIM), slice(i * BLOCK, (i + 1) * BLOCK)
        state[h, i] = (
            [nn(k_n[j * BLOCK : (j + 1) * BLOCK, own], q_t[own, qs]) for j in range(i + 1)],
            [nn(v_n[j * BLOCK : (j + 1) * BLOCK, own], do_t[own, qs]) for j in range(i + 1)],
        )

    def soft(h, i):
        scores, d_probs = state[h, i]
        scores[-1] = jnp.where(later, -1e30, scores[-1])
        peak = reduce(jnp.maximum, [jnp.max(s, 0, keepdims=True) for s in scores])
        weights = [jnp.exp(s - peak) for s in scores]
        inverse = 1.0 / reduce(jnp.add, [jnp.sum(w, 0, keepdims=True) for w in weights])
        probs = [w * inverse for w in weights]
        inner = reduce(jnp.add, [jnp.sum(p * d, 0, keepdims=True) for p, d in zip(probs, d_probs)])
        state[h, i] = (
            [p.astype(BF) for p in probs],
            [(p * (d - inner)).astype(BF) for p, d in zip(probs, d_probs)],
        )

    def unturn(block, cos, sin):
        half = ROTARY // 2
        a, b = block[:half], block[half:ROTARY]
        return jnp.concatenate([a * cos + b * sin, b * cos - a * sin, block[ROTARY:]], 0).astype(BF)

    def finish_block(h, i):
        own, qs = slice(h * HEAD_DIM, (h + 1) * HEAD_DIM), slice(i * BLOCK, (i + 1) * BLOCK)
        base = 3 * HEAD_DIM * h
        probs, d_scores = state.pop((h, i))
        keys = slice(0, (i + 1) * BLOCK)
        ctx_t[own, qs] = nn(v_t[own, keys], jnp.concatenate(probs, 0)).astype(BF)
        d_query = nn(k_t[own, keys], jnp.concatenate(d_scores, 0)) * HEAD_DIM ** (-0.5)
        dm_t[base : base + HEAD_DIM, qs] = unturn(d_query, cos_ref[:, qs], sin_ref[:, qs])
        query, d_out = q_t[own, qs], do_t[own, qs]
        for j in range(i + 1):
            js = slice(j * BLOCK, (j + 1) * BLOCK)
            if j == i:
                dk[own, js] = nt(query, d_scores[j])
                dv[own, js] = nt(d_out, probs[j])
            else:
                dk[own, js] += nt(query, d_scores[j])
                dv[own, js] += nt(d_out, probs[j])
        if i == steps - 1:
            dm_t[base + HEAD_DIM : base + 2 * HEAD_DIM, :] = unturn(dk[own, :], cos_ref[...], sin_ref[...])
            dm_t[base + 2 * HEAD_DIM : base + 3 * HEAD_DIM, :] = dv[own, :].astype(BF)

    order = [(h, i) for h in range(heads) for i in range(steps)]
    for at in range(len(order) + 2):
        if at < len(order):
            products(*order[at])
        if at >= 2:
            finish_block(*order[at - 2])
        if 1 <= at <= len(order):
            soft(*order[at - 1])
    for i in range(len(slots)):
        at = i * (BLOCK + shard)
        both[:, at : at + BLOCK] = ctx_t[i * BLOCK : (i + 1) * BLOCK, :].T
        both[:, at + BLOCK : at + BLOCK + shard] = dm_t[i * shard : (i + 1) * shard, :].T
    if shared:
        for s in range(4):
            outs[s][...] = both[span(lax.bitwise_xor(f, s) * BLOCK, BLOCK), :]
    else:
        c = lax.bitwise_and(f, 1)
        half = seq // 2
        outs[0][...] = both[span(c * half, half), :]
        outs[1][...] = both[span((1 - c) * half, half), :]


def any_spec():
    return pl.BlockSpec(memory_space=pl.ANY)


def vmem_spec():
    return pl.BlockSpec(memory_space=pltpu.VMEM)


def smem_spec():
    return pl.BlockSpec(memory_space=pltpu.SMEM)


def attention(slots, shared, ids, hg, w_own, os, gain, bias, up, ja, oa, ou, cos, sin):
    seq, piece = SEQ_LEN, hg[0].shape[1]
    width = 4 * piece
    shard, own = up.shape[1] // 4, oa.shape[0] // 4
    joined, inner = shard * len(slots), own * len(slots)
    out_shape = [jax.ShapeDtypeStruct((BLOCK if shared else seq // 2, inner + joined), BF)] * (4 if shared else 2)

    return pl.pallas_call(
        partial(attention_kernel, slots, shared),
        in_specs=[smem_spec()] + [any_spec()] * 17 + [vmem_spec()] * 8,
        out_specs=[vmem_spec()] * len(out_shape),
        out_shape=out_shape,
        scratch_shapes=[
            pltpu.VMEM((seq, width), BF),
            pltpu.VMEM((seq, width), BF),
            pltpu.VMEM((width, joined), BF),
            pltpu.VMEM((inner, width), BF),
            pltpu.VMEM((joined, width), BF),
            pltpu.VMEM((inner, seq), BF),
            pltpu.VMEM((inner, seq), BF),
            pltpu.VMEM((inner, seq), BF),
            pltpu.VMEM((seq, inner), BF),
            pltpu.VMEM((seq, inner), BF),
            pltpu.VMEM((inner, seq), BF),
            pltpu.VMEM((joined, seq), BF),
            pltpu.VMEM((inner, seq), BF),
            pltpu.VMEM((inner, seq), F32),
            pltpu.VMEM((inner, seq), F32),
            pltpu.VMEM((seq, inner + joined), BF),
            pltpu.SemaphoreType.DMA((2,)),
            pltpu.SemaphoreType.DMA((2,)),
        ],
        compiler_params=pltpu.CompilerParams(vmem_limit_bytes=VMEM_LIMIT),
        cost_estimate=pl.CostEstimate(flops=100_000_000_000, bytes_accessed=100_000, transcendentals=0),
        name="attention",
    )(ids, *hg, w_own, *os, gain, bias, up, ja, oa, ou, cos, sin)


def token_copies(ids, tokens, which, dst, sem):
    f = ids[0]
    x, c = lax.shift_right_logical(f, 1), lax.bitwise_and(f, 1)
    seq = SEQ_LEN
    half = seq // 2
    piece = tokens[0].shape[1]
    for s in range(4):
        cols = slice(s * piece, (s + 1) * piece)
        if s < 2:
            own, shared = tokens[2 * which + s], tokens[2 * which + s]
            own_at, shared_at = x * seq, 2 * seq
        else:
            own, shared = tokens[2 + s], tokens[4 + s]
            own_at, shared_at = which * seq, which * seq
        pltpu.make_async_copy(own.at[span(own_at + c * half, half), :], dst.at[:half, cols], sem).start()
        pltpu.make_async_copy(
            shared.at[span(shared_at + f * BLOCK, BLOCK), :], dst.at[half : half + BLOCK, cols], sem
        ).start()


def attention_copies(own, shared, at, dst, sem):
    half = dst.shape[0] - BLOCK
    size = dst.shape[1] // 4
    pitch = shared[0].shape[1]
    for s in range(4):
        to = slice(s * size, (s + 1) * size)
        col = (s // 2) * pitch + at
        pltpu.make_async_copy(own[s % 2].at[:, col : col + size], dst.at[:half, to], sem).start()
        pltpu.make_async_copy(shared[s].at[:, at : at + size], dst.at[half : half + BLOCK, to], sem).start()


def arrived(dst, sem):
    pltpu.make_async_copy(dst, dst, sem).wait()


def grads_kernel(ids, *refs):
    tokens, a_own, a_sh = refs[0:8], refs[8:10], refs[10:14]
    gain, bias, up, ja, oa, ou = refs[14:20]
    low_out_ref, low_grad_ref, keep, send = refs[20:24]
    h_v, g_v, c_v, m_v, sem = refs[24:]
    f = ids[0]
    rows, width = h_v.shape
    piece = width // 4
    shard = m_v.shape[1] // 4
    token_copies(ids, tokens, 1, g_v, sem.at[1])
    attention_copies(a_own, a_sh, 0, c_v, sem.at[2])
    token_copies(ids, tokens, 0, h_v, sem.at[0])
    attention_copies(a_own, a_sh, BLOCK, m_v, sem.at[3])
    put = partial(put_blocks, f, keep, send)
    arrived(g_v, sem.at[1])
    arrived(c_v, sem.at[2])
    low_out = (nn(c_v[...], oa[...]).astype(BF) * ADAPTER_SCALE).astype(BF)
    low_out_ref[...] = low_out
    low_out_grad = (nt(g_v[...], ou[...]) * ADAPTER_SCALE).astype(BF)
    put(0, piece, low_out.T, g_v)
    put(width, piece, low_out_grad.T, c_v)
    arrived(h_v, sem.at[0])
    unit, _ = layer_norm(h_v[...].astype(F32))
    n = (unit * gain[...] + bias[...]).astype(BF)
    low = (nn(n, ja[...]).astype(BF) * ADAPTER_SCALE).astype(BF)
    arrived(m_v, sem.at[3])
    low_grad = (nt(m_v[...], up[...]) * ADAPTER_SCALE).astype(BF)
    low_grad_ref[...] = low_grad
    put(2 * width, shard, low.T, m_v)
    put(2 * width + 4 * shard, piece, low_grad.T, n)


def put_blocks(f, keep, send, base, size, left, right):
    half = keep.shape[0]
    for s in range(4):
        value = nn(left, right[:, s * size : (s + 1) * size])
        to = span(base + lax.bitwise_xor(f, s) * size, size)
        keep[:, to] = value[:half]
        send[:, to] = value[half:]


def grads_of_attention(ids, tokens, a_own, a_sh, gain, bias, up, ja, oa, ou):
    piece = tokens[0].shape[1]
    width = 4 * piece
    rows = SEQ_LEN // 2 + BLOCK
    shard = up.shape[1] // 4
    rank = ja.shape[1]
    total = 3 * width + 4 * shard
    return pl.pallas_call(
        grads_kernel,
        in_specs=[smem_spec()] + [any_spec()] * 14 + [vmem_spec()] * 6,
        out_specs=[vmem_spec()] * 4,
        out_shape=[
            jax.ShapeDtypeStruct((rows, rank), BF),
            jax.ShapeDtypeStruct((rows, rank), BF),
            jax.ShapeDtypeStruct((rank // 2, total), F32),
            jax.ShapeDtypeStruct((rank // 2, total), F32),
        ],
        scratch_shapes=[
            pltpu.VMEM((rows, width), BF),
            pltpu.VMEM((rows, width), BF),
            pltpu.VMEM((rows, width), BF),
            pltpu.VMEM((rows, 4 * shard), BF),
            pltpu.SemaphoreType.DMA((4,)),
        ],
        compiler_params=pltpu.CompilerParams(vmem_limit_bytes=VMEM_LIMIT),
        cost_estimate=pl.CostEstimate(flops=100_000_000_000, bytes_accessed=100_000, transcendentals=0),
        name="grads_of_attention",
    )(ids, *tokens, *a_own, *a_sh, gain, bias, up, ja, oa, ou)


def start_slot(slot, ids, weights, e_v, s_v, e_sem, s_sem):
    f, q = ids[0], ids[1]
    e_own, e_mate, s_own, s_mate = weights[:4]
    foreign, diag = weights[4:8], weights[8:12]
    width, hidden = e_v.shape
    piece, part = width // 4, hidden // 4
    cols = slice(slot * part, (slot + 1) * part)
    if slot < 2:
        for t in range(4):
            pltpu.make_async_copy(
                weights[slot].at[span(lax.bitwise_xor(f, t) * piece, piece), :],
                e_v.at[t * piece : (t + 1) * piece, cols],
                e_sem.at[slot],
            ).start()
    else:
        for k in range(4):
            rows = span(lax.bitwise_xor(lax.bitwise_xor(q, k), f) * piece, piece)
            pltpu.make_async_copy(
                weights[4 * slot - 4 + k].at[:piece, :], e_v.at[rows, cols], e_sem.at[slot]
            ).start()
    for s, ref in ((0, s_own), (1, s_mate)):
        pltpu.make_async_copy(
            ref.at[span(lax.bitwise_xor(f, slot) * part, part), :],
            s_v.at[cols, s * piece : (s + 1) * piece],
            s_sem.at[slot],
        ).start()
    for k in range(4):

        @pl.when(lax.bitwise_xor(lax.bitwise_xor(q, k), f) == slot)
        def _():
            for s, pieces in ((2, foreign), (3, diag)):
                shrink_copies(pieces[k], s_v, slot * part, s * piece, s_sem.at[slot])


def shrink_copies(pack, dst, row, col, sem):
    for u in range(pack.shape[1] // BLOCK):
        pltpu.make_async_copy(
            pack.at[BLOCK:, u * BLOCK : (u + 1) * BLOCK],
            dst.at[span(row + u * BLOCK, BLOCK), col : col + BLOCK],
            sem,
        ).start()


CHUNK = 512


def mlp_first_kernel(ids, *refs):
    tokens, weights = refs[0:8], refs[8:20]
    gain, bias, ea, eu, sa, su = refs[20:26]
    act_out, dup_out, ls_out, dle_out, keep, send = refs[26:32]
    h_v, g_v, n_v, e_v, s_v, act, dup, sem, e_sem, s_sem, o_sem = refs[32:]
    f = ids[0]
    rows, width = h_v.shape
    hidden = e_v.shape[1]
    token_copies(ids, tokens, 0, h_v, sem.at[0])
    token_copies(ids, tokens, 1, g_v, sem.at[1])
    load = lambda slot: start_slot(slot, ids, weights, e_v, s_v, e_sem, s_sem)
    load(0)
    arrived(h_v, sem.at[0])
    unit, _ = layer_norm(h_v[...].astype(F32))
    n_v[...] = (unit * gain[...] + bias[...]).astype(BF)
    low = (nn(n_v[...], ea[...]).astype(BF) * ADAPTER_SCALE).astype(BF)
    arrived(g_v, sem.at[1])
    low_grad = (nt(g_v[...], su[...]) * ADAPTER_SCALE).astype(BF)
    load(1)
    state = {}
    part, piece = hidden // 4, width // 4

    def products(b, t):
        ts, bs = slice(t * BLOCK, (t + 1) * BLOCK), slice(b * CHUNK, (b + 1) * CHUNK)
        if t == 0 and bs.start % part == 0:
            slot = bs.start // part
            whole = slice(slot * part, (slot + 1) * part)
            if 1 <= slot < 3:
                load(slot + 1)
            arrived(e_v.at[:, whole], e_sem.at[slot])
            arrived(s_v.at[whole, :], s_sem.at[slot])
        state[b, t] = (
            nn(n_v[ts, :], e_v[:, bs]) + nn(low[ts], eu[:, bs]),
            nt(g_v[ts, :], s_v[bs, :]) + nt(low_grad[ts], sa[bs, :]),
        )

    def bend(b, t):
        ts, bs = slice(t * BLOCK, (t + 1) * BLOCK), slice(b * CHUNK, (b + 1) * CHUNK)
        upper, d_active = state.pop((b, t))
        normal = 0.5 * (1.0 + lax.erf(upper * 0.7071067811865476))
        density = jnp.exp(-0.5 * upper * upper) * 0.3989422804014327
        act[ts, bs] = (upper * normal).astype(BF)
        dup[ts, bs] = (d_active * (normal + upper * density)).astype(BF)
        if t == rows // BLOCK - 1:
            pltpu.make_async_copy(act.at[:, bs], act_out.at[:, bs], o_sem.at[0]).start()
            pltpu.make_async_copy(dup.at[:, bs], dup_out.at[:, bs], o_sem.at[1]).start()

    order = [(b, t) for b in range(hidden // CHUNK) for t in range(rows // BLOCK)]
    for at in range(len(order) + 1):
        if at < len(order):
            products(*order[at])
        if at > 0:
            bend(*order[at - 1])

    put = partial(put_blocks, f, keep, send)
    put(0, part, low_grad.T, act)
    put(hidden, part, low.T, dup)
    low_shrink = (nn(act[...], sa[...]).astype(BF) * ADAPTER_SCALE).astype(BF)
    low_expand_grad = (nt(dup[...], eu[...]) * ADAPTER_SCALE).astype(BF)
    ls_out[...] = low_shrink
    dle_out[...] = low_expand_grad
    put(2 * hidden, piece, low_shrink.T, g_v)
    put(2 * hidden + width, piece, low_expand_grad.T, n_v)
    arrived(act, o_sem.at[0])
    arrived(dup, o_sem.at[1])


def mlp_first(ids, tokens, weights, gain, bias, ea, eu, sa, su):
    piece = tokens[0].shape[1]
    width = 4 * piece
    rows = SEQ_LEN // 2 + BLOCK
    hidden = eu.shape[1]
    rank = ea.shape[1]
    return pl.pallas_call(
        mlp_first_kernel,
        in_specs=[smem_spec()] + [any_spec()] * 20 + [vmem_spec()] * 6,
        out_specs=[any_spec()] * 2 + [vmem_spec()] * 4,
        out_shape=[
            jax.ShapeDtypeStruct((rows, hidden), BF),
            jax.ShapeDtypeStruct((rows, hidden), BF),
            jax.ShapeDtypeStruct((rows, rank), BF),
            jax.ShapeDtypeStruct((rows, rank), BF),
            jax.ShapeDtypeStruct((rank // 2, 2 * hidden + 2 * width), F32),
            jax.ShapeDtypeStruct((rank // 2, 2 * hidden + 2 * width), F32),
        ],
        scratch_shapes=[
            pltpu.VMEM((rows, width), BF),
            pltpu.VMEM((rows, width), BF),
            pltpu.VMEM((rows, width), BF),
            pltpu.VMEM((width, hidden), BF),
            pltpu.VMEM((hidden, width), BF),
            pltpu.VMEM((rows, hidden), BF),
            pltpu.VMEM((rows, hidden), BF),
            pltpu.SemaphoreType.DMA((2,)),
            pltpu.SemaphoreType.DMA((4,)),
            pltpu.SemaphoreType.DMA((4,)),
            pltpu.SemaphoreType.DMA((2,)),
        ],
        compiler_params=pltpu.CompilerParams(vmem_limit_bytes=VMEM_LIMIT),
        cost_estimate=pl.CostEstimate(flops=100_000_000_000, bytes_accessed=100_000, transcendentals=0),
        name="mlp_first",
    )(ids, *tokens, *weights, gain, bias, ea, eu, sa, su)


def rows_of_slot(s, ids, own, mate, foreign, diag, col, dst, sems):
    f, q = ids[0], ids[1]
    piece = own.shape[0] // 4
    cols = own.shape[1]
    to = slice(s * cols, (s + 1) * cols)
    for t in range(4):
        if s < 2:
            src = (own, mate)[s].at[span(lax.bitwise_xor(f, t) * piece, piece), :]
            place = t
        else:
            src = (foreign, diag)[s - 2][t].at[:piece, col : col + cols]
            place = lax.bitwise_xor(lax.bitwise_xor(q, t), f)
        pltpu.make_async_copy(src, dst.at[span(place * piece, piece), to], sems.at[place]).start()


def shrink_of_slot(s, ids, own, mate, foreign, diag, dst, sem):
    f, q = ids[0], ids[1]
    part, piece = dst.shape[0] // 4, dst.shape[1] // 4
    for t in range(4):
        if s < 2:
            src = (own, mate)[s].at[span(lax.bitwise_xor(f, t) * part, part), :]
            pltpu.make_async_copy(src, dst.at[t * part : (t + 1) * part, s * piece : (s + 1) * piece], sem).start()
        else:
            row = lax.bitwise_xor(lax.bitwise_xor(q, t), f) * part
            shrink_copies((foreign, diag)[s - 2][t], dst, row, s * piece, sem)


def result_kernel(ids, *refs):
    tokens, a_own, a_sh = refs[0:8], refs[8:10], refs[10:14]
    o_own, o_mate, s_own, s_mate = refs[14:18]
    one_f, one_d, two_f, two_d = refs[18:22], refs[22:26], refs[26:30], refs[30:34]
    act_ref = refs[34]
    low_out, ou, low_shrink, su = refs[35:39]
    out = refs[39]
    h_v, c_v, o_v, s_v, act, sem, o_sem, s_sem = refs[40:]
    f = ids[0]
    rows, width = h_v.shape
    piece = width // 4
    attention_copies(a_own, a_sh, 0, c_v, sem.at[1])
    for s in range(4):
        rows_of_slot(s, ids, o_own, o_mate, one_f, one_d, 3 * piece, o_v, o_sem)
    token_copies(ids, tokens, 0, h_v, sem.at[2])
    pltpu.make_async_copy(act_ref, act, sem.at[3]).start()
    arrived(c_v, sem.at[1])
    for t in range(4):
        arrived(o_v.at[t * piece : (t + 1) * piece, :], o_sem.at[t])
    arrived(h_v, sem.at[2])
    for s in range(4):
        shrink_of_slot(s, ids, s_own, s_mate, two_f, two_d, s_v, s_sem.at[s])
    blocks = [slice(t * BLOCK, (t + 1) * BLOCK) for t in range(rows // BLOCK)]
    sums = [
        h_v[ts, :].astype(F32)
        + (nn(c_v[ts, :], o_v[...]) + nn(low_out[ts, :], ou[...]))
        + nn(low_shrink[ts, :], su[...])
        for ts in blocks
    ]
    arrived(act, sem.at[3])
    for s in range(4):
        arrived(s_v.at[:, s * piece : (s + 1) * piece], s_sem.at[s])
    for total, ts in zip(sums, blocks):
        value = (total + nn(act[ts, :], s_v[...])).astype(BF)
        for s in range(4):
            out[lax.bitwise_xor(f, s), ts, :] = value[:, s * piece : (s + 1) * piece]


def result_parts(ids, tokens, a_own, a_sh, o_parts, s_parts, one, two, act, low_out, ou, low_shrink, su):
    piece = tokens[0].shape[1]
    width = 4 * piece
    rows = SEQ_LEN // 2 + BLOCK
    hidden = act.shape[1]
    return pl.pallas_call(
        result_kernel,
        in_specs=[smem_spec()] + [any_spec()] * 35 + [vmem_spec()] * 4,
        out_specs=vmem_spec(),
        out_shape=jax.ShapeDtypeStruct((4, rows, piece), BF),
        scratch_shapes=[
            pltpu.VMEM((rows, width), BF),
            pltpu.VMEM((rows, width), BF),
            pltpu.VMEM((width, width), BF),
            pltpu.VMEM((hidden, width), BF),
            pltpu.VMEM((rows, hidden), BF),
            pltpu.SemaphoreType.DMA((4,)),
            pltpu.SemaphoreType.DMA((4,)),
            pltpu.SemaphoreType.DMA((4,)),
        ],
        compiler_params=pltpu.CompilerParams(vmem_limit_bytes=VMEM_LIMIT),
        cost_estimate=pl.CostEstimate(flops=100_000_000_000, bytes_accessed=100_000, transcendentals=0),
        name="result_parts",
    )(ids, *tokens, *a_own, *a_sh, *o_parts, *s_parts, *one, *two, act, low_out, ou, low_shrink, su)


def input_grad_kernel(ids, *refs):
    tokens, a_own, a_sh = refs[0:8], refs[8:10], refs[10:14]
    w_own, w_mate, e_own, e_mate = refs[14:18]
    one_f, one_d, two_f, two_d = refs[18:22], refs[22:26], refs[26:30], refs[30:34]
    dup_ref = refs[34]
    gain_one, gain_two, ja, ea, low_joined_grad, low_expand_grad = refs[35:41]
    outs, sums = refs[41:45], refs[45]
    h_v, g_v, m_v, w_v, e_v, dup, one_v, sem, w_sem, e_sem = refs[46:]
    f = ids[0]
    rows, width = h_v.shape
    piece = width // 4
    shard = m_v.shape[1] // 4
    attention_copies(a_own, a_sh, BLOCK, m_v, sem.at[0])
    for s in range(4):
        rows_of_slot(s, ids, w_own, w_mate, one_f, one_d, 0, w_v, w_sem)
    arrived(m_v, sem.at[0])
    blocks = [slice(t * BLOCK, (t + 1) * BLOCK) for t in range(rows // BLOCK)]
    for t in range(4):
        arrived(w_v.at[t * piece : (t + 1) * piece, :], w_sem.at[t])
    pltpu.make_async_copy(dup_ref, dup, sem.at[3]).start()
    for s in range(4):
        rows_of_slot(s, ids, e_own, e_mate, two_f, two_d, 0, e_v, e_sem)
    token_copies(ids, tokens, 0, h_v, sem.at[1])
    token_copies(ids, tokens, 1, g_v, sem.at[2])
    for ts in blocks:
        one_v[ts, :] = nt(m_v[ts, :], w_v[...]) + nt(low_joined_grad[ts, :], ja[...])
    arrived(dup, sem.at[3])
    for t in range(4):
        arrived(e_v.at[t * piece : (t + 1) * piece, :], e_sem.at[t])
    arrived(h_v, sem.at[1])
    arrived(g_v, sem.at[2])
    total = None
    for ts in blocks:
        one = one_v[ts, :]
        two = nt(dup[ts, :], e_v[...]) + nt(low_expand_grad[ts, :], ea[...])
        unit, factor = layer_norm(h_v[ts, :].astype(F32))
        here = [jnp.sum(v, 0, keepdims=True) for v in (one * unit, one, two * unit, two)]
        total = here if total is None else [a + b for a, b in zip(total, here)]
        e = one * gain_one[...] + two * gain_two[...]
        plain = jnp.mean(e, 1, keepdims=True)
        along = jnp.mean(e * unit, 1, keepdims=True)
        value = g_v[ts, :].astype(F32) + factor * (e - plain - unit * along)
        for s in range(4):
            outs[s][ts, :] = value[:, s * piece : (s + 1) * piece].astype(outs[s].dtype)
    value = jnp.concatenate(total + [jnp.zeros((4, width), F32)], 0)
    for s in range(4):
        sums[:, span(lax.bitwise_xor(f, s) * piece, piece)] = value[:, s * piece : (s + 1) * piece]


def input_grad_parts(
    ids, tokens, a_own, a_sh, w_parts, e_parts, one, two, dup, gain_one, gain_two, ja, ea, low_joined_grad, low_expand_grad
):
    piece = tokens[0].shape[1]
    width = 4 * piece
    rows = SEQ_LEN // 2 + BLOCK
    hidden = dup.shape[1]
    joined = 4 * w_parts[0].shape[1]
    return pl.pallas_call(
        input_grad_kernel,
        in_specs=[smem_spec()] + [any_spec()] * 35 + [vmem_spec()] * 6,
        out_specs=[vmem_spec()] * 5,
        out_shape=[jax.ShapeDtypeStruct((rows, piece), t) for t in (F32, F32, BF, BF)]
        + [jax.ShapeDtypeStruct((8, width), F32)],
        scratch_shapes=[
            pltpu.VMEM((rows, width), BF),
            pltpu.VMEM((rows, width), BF),
            pltpu.VMEM((rows, joined), BF),
            pltpu.VMEM((width, joined), BF),
            pltpu.VMEM((width, hidden), BF),
            pltpu.VMEM((rows, hidden), BF),
            pltpu.VMEM((rows, width), F32),
            pltpu.SemaphoreType.DMA((4,)),
            pltpu.SemaphoreType.DMA((4,)),
            pltpu.SemaphoreType.DMA((4,)),
        ],
        compiler_params=pltpu.CompilerParams(vmem_limit_bytes=VMEM_LIMIT),
        cost_estimate=pl.CostEstimate(flops=100_000_000_000, bytes_accessed=100_000, transcendentals=0),
        name="input_grad_parts",
    )(
        ids, *tokens, *a_own, *a_sh, *w_parts, *e_parts, *one, *two, dup,
        gain_one, gain_two, ja, ea, low_joined_grad, low_expand_grad,
    )


def gather_rows_kernel(widen, ids, *refs):
    parts, out = refs[:4], refs[4]
    scratch = refs[5:]
    f = ids[0]
    sem = scratch[-1]
    rows = parts[0].shape[0]
    half = rows - BLOCK
    seq = 2 * half
    copies = []
    for s in range(4):
        src = parts[s]
        if src.dtype != out.dtype:
            scratch[s - 2][...] = src[...].astype(out.dtype)
            src = scratch[s - 2]
        at = lax.bitwise_xor(f, s)
        copies.append(pltpu.make_async_copy(src.at[:half, :], out.at[span(at * half, half), :], sem.at[2 * s]))
        copies.append(
            pltpu.make_async_copy(src.at[half:, :], out.at[span(2 * seq + at * BLOCK, BLOCK), :], sem.at[2 * s + 1])
        )
        copies[-2].start()
        copies[-1].start()
    for copy in copies:
        copy.wait()


def gather_rows(ids, parts, dtype):
    rows, piece = parts[0].shape
    narrow = [p for p in parts if p.dtype != dtype]
    return pl.pallas_call(
        partial(gather_rows_kernel, dtype),
        in_specs=[smem_spec()] + [vmem_spec()] * 4,
        out_specs=any_spec(),
        out_shape=jax.ShapeDtypeStruct((4 * rows, piece), dtype),
        scratch_shapes=[pltpu.VMEM((rows, piece), dtype)] * len(narrow) + [pltpu.SemaphoreType.DMA((8,))],
        compiler_params=pltpu.CompilerParams(vmem_limit_bytes=VMEM_LIMIT),
        name="gather_rows",
    )(ids, *parts)


def adapters_kernel(cuts, sums_at, ids, order_ref, *refs):
    order = order_ref[...]
    pieces, outs = refs[:8], refs[8:]
    for (at, size, turned), out in zip(cuts, outs):
        value = jnp.concatenate([p[:, at : at + size] for p in pieces], 0)
        out[...] = tn(value, order) if turned else tn(order, value)
    if sums_at is not None:
        sums, lanes = outs[-5:-1], outs[-1]
        for k in range(4):
            lanes[span(lax.bitwise_xor(ids[1], k) * 16, 16, 16), :] = pieces[k][:, sums_at : sums_at + 128].astype(F32)
        for i, out in enumerate(sums):
            for j in range(8):
                out[:, j * 128 : (j + 1) * 128] = lanes[8 * j + i : 8 * j + i + 1, :]


def adapters_out(ids, order, pieces, cuts, sums_at=None):
    rank = order.shape[0]
    out_shape = [jax.ShapeDtypeStruct((size, rank) if turned else (rank, size), F32) for at, size, turned in cuts]
    scratch = []
    if sums_at is not None:
        out_shape += [jax.ShapeDtypeStruct((1, 1024), F32)] * 4
        scratch.append(pltpu.VMEM((64, 128), F32))
    return pl.pallas_call(
        partial(adapters_kernel, cuts, sums_at),
        in_specs=[smem_spec()] + [vmem_spec()] * 9,
        out_specs=[vmem_spec()] * len(out_shape),
        out_shape=out_shape,
        scratch_shapes=scratch,
        compiler_params=pltpu.CompilerParams(vmem_limit_bytes=VMEM_LIMIT),
        name="adapters_out",
    )(ids, order, *pieces)


def join_rows_kernel(keep, received, sums, other, out):
    cols = keep.shape[1]
    out[:, :cols] = (keep[...] + received[...]).astype(BF)
    total = sums[...] + other[...]
    out[:, cols:] = jnp.concatenate([total[:, i * 128 : (i + 1) * 128] for i in range(8)], 0).astype(BF)


def join_rows(keep, received, sums, other):
    rows, cols = keep.shape
    return pl.pallas_call(
        join_rows_kernel,
        in_specs=[vmem_spec()] * 4,
        out_specs=vmem_spec(),
        out_shape=jax.ShapeDtypeStruct((rows, cols + 128), BF),
        compiler_params=pltpu.CompilerParams(vmem_limit_bytes=VMEM_LIMIT),
        name="join_rows",
    )(keep, received, sums, other)


def split_rows_kernel(keep, received, own, *outs):
    size = own.shape[0]
    own[...] = keep[:size, :] + received[:size, :]
    for k, out in enumerate(outs):
        rows = slice((k + 1) * size, (k + 2) * size)
        out[...] = (keep[rows, :] + received[rows, :]).astype(BF)


def split_rows(keep, received):
    rows, cols = keep.shape
    return pl.pallas_call(
        split_rows_kernel,
        in_specs=[vmem_spec()] * 2,
        out_specs=[vmem_spec()] * 4,
        out_shape=[jax.ShapeDtypeStruct((rows // 4, cols), t) for t in (F32, BF, BF, BF)],
        compiler_params=pltpu.CompilerParams(vmem_limit_bytes=VMEM_LIMIT),
        name="split_rows",
    )(keep, received)


def pack_kernel(plan, ids, *refs):
    n_in = len(refs) - 1 - len(plan)
    srcs, outs, sem = refs[:n_in], refs[n_in:-1], refs[-1]
    for out, (shape, blocks) in zip(outs, plan):
        for src, which, size, sub, rows, to_row, to_col in blocks:
            cols = srcs[src].shape[1]
            pltpu.make_async_copy(
                srcs[src].at[span(ids[which] * size + sub, rows), :],
                out.at[to_row : to_row + rows, to_col : to_col + cols],
                sem,
            ).start()
    for out in outs:
        pltpu.make_async_copy(out, out, sem).wait()


def pack(ids, arrays, plan):
    return pl.pallas_call(
        partial(pack_kernel, plan),
        in_specs=[smem_spec()] + [any_spec()] * len(arrays),
        out_specs=[vmem_spec()] * len(plan),
        out_shape=[jax.ShapeDtypeStruct(shape, arrays[0].dtype) for shape, _ in plan],
        scratch_shapes=[pltpu.SemaphoreType.DMA],
        compiler_params=pltpu.CompilerParams(vmem_limit_bytes=VMEM_LIMIT),
        name="pack",
    )(ids, *arrays)


def order_kernel(late, ids, order_ref, other_ref, *refs):
    n = len(refs) // 2
    f = ids[0]
    for i, (src, out) in enumerate(zip(refs[:n], refs[n:])):
        order = (other_ref if i in late else order_ref)[...]
        axis = 0 if src.shape[0] > src.shape[1] else 1
        size = src.shape[axis] // 4
        for s in range(4):
            at, to = span(lax.bitwise_xor(f, s) * size, size), slice(s * size, (s + 1) * size)
            if src.dtype == F32:
                out[:, to] = src[:, at]
            elif axis == 0:
                out[to, :] = nt(src[at, :], order).astype(BF)
            else:
                out[:, to] = nn(order, src[:, at]).astype(BF)


def order_params(ids, order, other, params, late):
    return pl.pallas_call(
        partial(order_kernel, late),
        in_specs=[smem_spec()] + [vmem_spec()] * (2 + len(params)),
        out_specs=[vmem_spec()] * len(params),
        out_shape=[jax.ShapeDtypeStruct(p.shape, p.dtype) for p in params],
        compiler_params=pltpu.CompilerParams(vmem_limit_bytes=VMEM_LIMIT),
        name="order_params",
    )(ids, order, other, *params)


def swap(axes):
    def run(value):
        size = lax.axis_size(axes)
        return lax.ppermute(value, axes, [(i, size - 1 - i) for i in range(size)])

    return run


def after(value, *others):
    return lax.optimization_barrier((value, *others))[0]


def on_device_by_tokens(
    hidden,
    first_gain,
    first_bias,
    second_gain,
    second_bias,
    joined_frozen_weight,
    output_frozen_weight,
    expand_frozen_weight,
    shrink_frozen_weight,
    joined_a,
    joined_up_factor,
    output_a,
    output_up_factor,
    expand_a,
    expand_up_factor,
    shrink_a,
    shrink_up_factor,
    cotangent,
):
    x, c, q = lax.axis_index("x"), lax.axis_index("core"), lax.axis_index(("zn", "y"))
    f, far = 2 * x + c, lax.axis_index(("zf", "x"))
    seq, half = SEQ_LEN, SEQ_LEN // 2
    width = 4 * hidden.shape[1]
    rank = joined_a.shape[1]
    units = 4 * expand_frozen_weight.shape[1]
    ids = jnp.stack([f, q, far, 1 - x, 3 - q, 0 * f + 2]).astype(jnp.int32)
    to_core, to_x, to_diag = swap("core"), swap("x"), swap(("x", "core"))
    near = swap("y"), swap("zn"), swap(("zn", "y"))
    cross = to_x, swap("zf"), swap(("zf", "x"))

    piece = width // 4

    shard, part = joined_frozen_weight.shape[1], expand_frozen_weight.shape[1]
    (one_pack,) = pack(
        ids,
        (joined_frozen_weight, output_frozen_weight),
        (((piece, shard + piece), ((0, 1, piece, 0, piece, 0, 0), (1, 1, piece, 0, piece, 0, shard))),),
    )
    one_x = to_x(one_pack)
    own, shared = pack(
        after(ids, one_pack),
        (hidden, cotangent),
        tuple(((2 * seq, piece), ((0, at, seq, 0, seq, 0, 0), (1, at, seq, 0, seq, seq, 0))) for at in (3, 5)),
    )
    two_first, two_last = pack(
        after(ids, own),
        (expand_frozen_weight, shrink_frozen_weight),
        tuple(
            (
                (piece + BLOCK, part),
                ((0, at, piece, 0, piece, 0, 0),)
                + tuple((1, at, part, u, BLOCK, piece, u) for u in range(0, part, BLOCK)),
            )
            for at in (1, 4)
        ),
    )
    place = lax.broadcasted_iota(jnp.int32, (rank, rank), 0)
    half_order, order = (
        (lax.broadcasted_iota(jnp.int32, (rank, rank), 1) == (place ^ mask)).astype(BF) for mask in (c * 64, c * 64 + q * 16)
    )
    gain_one, bias_one, gain_two, bias_two, ja, oa, ea, sa, ju, ou, eu, su = order_params(
        after(ids, own),
        half_order,
        order,
        tuple(v[None, :] for v in (first_gain, first_bias, second_gain, second_bias))
        + (joined_a, output_a, expand_a, shrink_a)
        + (joined_up_factor, output_up_factor, expand_up_factor, shrink_up_factor),
        (6, 7, 10, 11),
    )
    position = np.arange(seq, dtype=np.float32)[None, :]
    frequency = np.float32(10000.0) ** (-(np.arange(ROTARY // 2, dtype=np.float32) * np.float32(2.0)) / np.float32(ROTARY))
    angles = frequency[:, None] * position
    cos, sin = jnp.asarray(np.cos(angles), F32), jnp.asarray(np.sin(angles), F32)
    h_mate, g_mate = (to_core(v) for v in after((hidden, cotangent), one_pack))
    one_x = after(one_x, own, two_first, gain_one, h_mate, g_mate)
    o_mate = to_core(output_frozen_weight)
    own_x = to_x(after(own, one_x))
    one_near = tuple(go(one_x) for go in near)
    own_x = after(own_x, one_near)
    own_mate = to_core(own_x)
    one_foreign = (one_x,) + one_near
    one_diag = tuple(to_core(p) for p in one_foreign)
    local = (hidden, h_mate, cotangent, g_mate)
    o_parts = (output_frozen_weight, o_mate) + one_foreign + one_diag
    params = (gain_one, bias_one, ju, ja, oa, ou, cos, sin)
    shared_x = to_x(after(shared, own_x))
    e_mate, s_mate, w_mate = (to_core(w) for w in (expand_frozen_weight, shrink_frozen_weight, joined_frozen_weight))
    two_x = to_x(after(two_first, own_x))
    keep_a, send_a = attention(
        (0, 2), False, ids, local + (own_x, own_mate), joined_frozen_weight, o_parts, *params
    )
    shared_x, two_x = after((shared_x, two_x), keep_a)
    e_mate, s_mate, w_mate = after((e_mate, s_mate, w_mate), shared_x, two_x)
    two_x = after(two_x, e_mate, s_mate, w_mate)
    shared_mate = to_core(shared_x)
    two_y, two_z, two_yz = near[0](two_x), near[1](two_x), to_x(after(two_last, two_x))
    b_parts = attention(
        (0,), True, ids, local + (shared_x, shared_mate), joined_frozen_weight, o_parts, *params
    )
    two_y, two_z, two_yz = after((two_y, two_z, two_yz), b_parts[0])
    foreign_two = (two_x, two_y, two_z, two_yz)
    diag_two = tuple(to_core(p) for p in foreign_two)
    tokens = local + (own_x, own_mate, shared_x, shared_mate)
    mlp_weights = (expand_frozen_weight, e_mate, shrink_frozen_weight, s_mate) + foreign_two + diag_two
    act, dup, ls, dle, keep_two, send_two = mlp_first(
        ids, tokens, mlp_weights, gain_two, bias_two, ea, eu, sa, su
    )
    b_moved = tuple(go(p) for go, p in zip((to_core, to_x, to_diag), b_parts[1:]))
    b_moved, a_mate = after((b_moved, to_core(send_a)), act)
    a_own, a_shared = (keep_a, a_mate), (b_parts[0],) + b_moved

    two = to_core(send_two)
    low_out, low_joined_grad, keep_one, send_one = grads_of_attention(
        ids, tokens, a_own, a_shared, gain_one, bias_one, ju, ja, oa, ou
    )
    two = split_rows(keep_two, after(two, low_out))
    dup = after(dup, two, send_one)
    two = (two[0],) + tuple(go(p) for go, p in zip(near, two[1:]))
    one = to_core(send_one)
    hidden_grad = input_grad_parts(
        ids, tokens, a_own, a_shared, (joined_frozen_weight, w_mate), (expand_frozen_weight, e_mate),
        one_foreign + one_diag, foreign_two + diag_two, dup, gain_one, gain_two, ja, ea, low_joined_grad, dle,
    )
    two, one = after((two, one), hidden_grad[4])
    sums = hidden_grad[4]
    hidden_grad = (hidden_grad[0], to_core(hidden_grad[1]), to_x(hidden_grad[2]), to_diag(hidden_grad[3]))

    def part_sum(parts):
        return reduce(jnp.add, [p.astype(F32) for p in parts]).astype(BF)

    two = part_sum(two)
    one = join_rows(keep_one, one, sums, to_core(sums))
    act = after(act, two, one, hidden_grad[1])
    two_other = cross[1](two)
    one = lax.all_to_all(one, ("zn", "y"), 0, 0, tiled=True)
    result = result_parts(
        ids, tokens, a_own, a_shared, (output_frozen_weight, o_mate), (shrink_frozen_weight, s_mate),
        one_foreign + one_diag, foreign_two + diag_two, act, low_out, ou, ls, su,
    )
    hidden_grad, two_other, one = after((hidden_grad, two_other, one), result)

    two = part_sum((two, two_other))
    two_other = cross[0](two)
    one = part_sum(after(one, two).reshape(4, -1, one.shape[1]))
    one_other = cross[1](one)
    hidden_grad = gather_rows(ids, hidden_grad, F32)
    two_other = after(two_other, hidden_grad)
    result = lax.all_to_all(after(result, two_other).reshape(-1, piece), ("x", "core"), 0, 0, tiled=True)
    two = part_sum((two, two_other))
    two = (two,) + tuple(go(two) for go in near)
    one = part_sum((one, one_other))
    one_other = cross[0](one)
    one = part_sum((one, one_other))
    one_y, one_z, one_yz = near[0](one), near[1](one), near[2](after(one, two))
    two = two + tuple(to_core(p) for p in two)
    joined = ju.shape[1]
    expand_a_grad, expand_b_grad, shrink_a_grad, shrink_b_grad = adapters_out(
        ids, order, two,
        ((2 * units + width, width, True), (units, units, False), (0, units, True), (2 * units, width, False)),
    )
    one = (one, one_y, one_z) + after((one_yz,), expand_a_grad)
    one = one + tuple(to_core(p) for p in one)
    result = after(result, expand_a_grad).reshape(4, -1, piece)
    result = jnp.concatenate([result[:, : seq // 2].reshape(-1, piece), result[:, seq // 2 :].reshape(-1, piece)], 0)
    joined_a_grad, joined_b_grad, output_a_grad, output_b_grad, *sums = adapters_out(
        ids, order, one,
        ((2 * width + joined, width, True), (2 * width, joined, False), (width, width, True), (0, width, False)),
        3 * width + joined,
    )
    return (
        result,
        hidden_grad,
        sums[0].reshape(-1),
        sums[1].reshape(-1),
        sums[2].reshape(-1),
        sums[3].reshape(-1),
        joined_a_grad,
        joined_b_grad,
        output_a_grad,
        output_b_grad,
        expand_a_grad,
        expand_b_grad,
        shrink_a_grad,
        shrink_b_grad,
    )


def solution(mesh):
    step, rows, cols = on_device, "dp", "mp"
    if mesh.shape["dp"] == 8 and mesh.shape["mp"] == 4:
        step, rows, cols = on_device_by_tokens, ("zf", "zn", "y"), ("x", "core")
        mesh = Mesh(mesh.devices.reshape((2,) * 5), rows + cols)
    whole, split, tokens = P(), P(None, cols), P(rows, cols)
    return jax.shard_map(
        step,
        mesh=mesh,
        in_specs=(tokens,) + (whole,) * 4 + (split,) * 4 + (whole,) * 8 + (tokens,),
        out_specs=(tokens, tokens) + (whole,) * 12,
        check_vma=False,
    )
```

```python
from functools import partial, reduce

import jax
import jax.numpy as jnp
import numpy as np
from jax import lax
from jax.experimental import pallas as pl
from jax.experimental.pallas import tpu as pltpu
from jax.sharding import Mesh
from jax.sharding import PartitionSpec as P

ROTARY = 16
SEQ_LEN = 1024
HEAD_DIM = 64


ADAPTER_SCALE = 0.25
EPS = 1e-05


def matrix_product(left, right):
    return jnp.dot(left, right, preferred_element_type=jnp.float32)


def matrix_product_transposed_left(left, right):
    return lax.dot_general(
        left, right, (((0,), (0,)), ((), ())), preferred_element_type=jnp.float32
    )


def matrix_product_transposed_right(left, right):
    return lax.dot_general(
        left, right, (((1,), (1,)), ((), ())), preferred_element_type=jnp.float32
    )


def normalize(full, gain, bias):
    center = full - jnp.mean(full, -1, keepdims=True)
    factor = lax.rsqrt(jnp.mean(center * center, -1, keepdims=True) + EPS)
    unit = center * factor
    return (unit, factor, unit * gain + bias)


def tables():
    position = jnp.arange(SEQ_LEN, dtype=jnp.float32)[:, None]
    frequency = 10000.0 ** (-(jnp.arange(ROTARY // 2, dtype=jnp.float32) * 2.0) / ROTARY)
    angles = position * frequency[None, :]
    cosine = jnp.concatenate([jnp.cos(angles), jnp.cos(angles)], -1)[:, None, :]
    sine = jnp.concatenate([jnp.sin(angles), jnp.sin(angles)], -1)[:, None, :]
    return (cosine, sine)


def rotate(block, cosine, sine):
    half = ROTARY // 2
    part = block[..., :ROTARY]
    turned = jnp.concatenate([-part[..., half:], part[..., :half]], -1)
    return jnp.concatenate([part * cosine + turned * sine, block[..., ROTARY:]], -1)


def unrotate(grad, cosine, sine):
    half = ROTARY // 2
    part = grad[..., :ROTARY]
    scaled = part * sine
    untied = jnp.concatenate([scaled[..., half:], -scaled[..., :half]], -1)
    return jnp.concatenate([part * cosine + untied, grad[..., ROTARY:]], -1)


def attend(causal, block):
    query, keys, values = block
    scores = jnp.einsum(
        "qhe,khe->hqk", query, keys, preferred_element_type=jnp.float32
    ) * HEAD_DIM ** (-0.5)
    scores = jnp.where(causal, scores, -1e30)
    peak = jnp.max(scores, -1, keepdims=True)
    weights = jnp.exp(scores - peak)
    total = jnp.sum(weights, -1, keepdims=True)
    probs = (weights / total).astype(jnp.bfloat16)
    attended_context = jnp.einsum("hqk,khe->qhe", probs, values, preferred_element_type=jnp.float32)
    return (attended_context.astype(jnp.bfloat16), (peak + jnp.log(total))[..., 0])


def attend_back(causal, block):
    query, keys, values, grad_context, logsum = block
    scores = jnp.einsum(
        "qhe,khe->hqk", query, keys, preferred_element_type=jnp.float32
    ) * HEAD_DIM ** (-0.5)
    scores = jnp.where(causal, scores, -1e30)
    probs = jnp.exp(scores - logsum[..., None])
    grad_probs = jnp.einsum(
        "qhe,khe->hqk", grad_context, values, preferred_element_type=jnp.float32
    )
    inner = jnp.sum(probs * grad_probs, -1, keepdims=True)
    grad_scores = (probs * (grad_probs - inner)).astype(jnp.bfloat16)
    grad_query = jnp.einsum(
        "hqk,khe->qhe", grad_scores, keys, preferred_element_type=jnp.float32
    ) * HEAD_DIM ** (-0.5)
    grad_keys = jnp.einsum(
        "hqk,qhe->khe", grad_scores, query, preferred_element_type=jnp.float32
    ) * HEAD_DIM ** (-0.5)
    grad_values = jnp.einsum(
        "hqk,qhe->khe", probs.astype(jnp.bfloat16), grad_context, preferred_element_type=jnp.float32
    )
    return (grad_query, grad_keys, grad_values)


def fold_with(weight, adapter_a, carry, piece):
    span = piece.shape[1]
    weight_rows = lax.slice_in_dim(weight, 0, span, axis=0)
    adapter_rows = lax.slice_in_dim(adapter_a, 0, span, axis=0)
    return (
        carry[0] + matrix_product(piece, weight_rows),
        carry[1] + matrix_product(piece, adapter_rows),
    )


def finish(summed_result, low_sum, columns_up_factor):
    adapter_values = low_sum.astype(jnp.bfloat16)
    return (
        summed_result + ADAPTER_SCALE * matrix_product(adapter_values, columns_up_factor),
        adapter_values,
    )


def on_device(
    hidden,
    first_gain,
    first_bias,
    second_gain,
    second_bias,
    joined_frozen_weight,
    output_frozen_weight,
    expand_frozen_weight,
    shrink_frozen_weight,
    joined_a,
    joined_up_factor,
    output_a,
    output_up_factor,
    expand_a,
    expand_up_factor,
    shrink_a,
    shrink_up_factor,
    cotangent,
):
    rank = lax.axis_index("mp")
    rows = hidden.shape[0]
    cols = hidden.shape[1]
    width = cols * lax.axis_size("mp")
    count = rows // SEQ_LEN
    joined_cols = joined_frozen_weight.shape[1]
    expand_cols = expand_frozen_weight.shape[1]
    heads_here = joined_cols // (3 * HEAD_DIM)
    inner_out = joined_cols // 3
    full = lax.all_gather(hidden, "mp", axis=1, tiled=True).astype(jnp.float32)
    unit_one, factor_one, first_norm_output = normalize(full, first_gain, first_bias)
    unit_two, factor_two, second_norm_output = normalize(full, second_gain, second_bias)
    first_norm_output = first_norm_output.astype(jnp.bfloat16)
    second_norm_output = second_norm_output.astype(jnp.bfloat16)
    adapter_joined_hidden = matrix_product(first_norm_output, joined_a).astype(jnp.bfloat16)
    joined_weight_local = lax.dynamic_slice_in_dim(
        joined_up_factor, rank * joined_cols, joined_cols, 1
    )
    mixed_state = matrix_product(
        first_norm_output, joined_frozen_weight
    ) + ADAPTER_SCALE * matrix_product(adapter_joined_hidden, joined_weight_local)
    mixed_state = mixed_state.reshape(count, SEQ_LEN, heads_here, 3, HEAD_DIM)
    cosine, sine = tables()
    query = rotate(mixed_state[:, :, :, 0], cosine, sine).astype(jnp.bfloat16)
    keys = rotate(mixed_state[:, :, :, 1], cosine, sine).astype(jnp.bfloat16)
    values = mixed_state[:, :, :, 2].astype(jnp.bfloat16)
    causal = jnp.arange(SEQ_LEN)[:, None] >= jnp.arange(SEQ_LEN)[None, :]
    attended_context, logsum = lax.map(partial(attend, causal), (query, keys, values))
    attended_context = attended_context.reshape(rows, inner_out)
    adapter_expand_hidden = matrix_product(second_norm_output, expand_a).astype(jnp.bfloat16)
    expand_weight_local = lax.dynamic_slice_in_dim(
        expand_up_factor, rank * expand_cols, expand_cols, 1
    )
    upper_hidden = matrix_product(
        second_norm_output, expand_frozen_weight
    ) + ADAPTER_SCALE * matrix_product(adapter_expand_hidden, expand_weight_local)
    gelu_exact = partial(jax.nn.gelu, approximate=False)
    active_f, gelu_pull = jax.vjp(gelu_exact, upper_hidden)
    active_hidden = active_f.astype(jnp.bfloat16)
    out_rows_a = lax.dynamic_slice_in_dim(output_a, rank * inner_out, inner_out, 0)
    output_columns_up_factor = lax.dynamic_slice_in_dim(output_up_factor, rank * cols, cols, 1)
    shrink_rows_a = lax.dynamic_slice_in_dim(shrink_a, rank * expand_cols, expand_cols, 0)
    shrink_columns_up_factor = lax.dynamic_slice_in_dim(shrink_up_factor, rank * cols, cols, 1)
    zero_pair = (
        jnp.zeros((rows, cols), jnp.float32),
        jnp.zeros((rows, output_a.shape[1]), jnp.float32),
    )
    attn_summed, attn_low = fold_with(
        output_frozen_weight,
        output_a,
        zero_pair,
        lax.all_gather(attended_context, "mp", axis=1, tiled=True),
    )
    mlp_summed, mlp_low = fold_with(
        shrink_frozen_weight,
        shrink_a,
        zero_pair,
        jax.tree.map(lambda a: lax.all_gather(a, "mp", axis=1, tiled=True), active_hidden),
    )
    attention_branch, adapter_output_hidden = finish(
        attn_summed, attn_low, output_columns_up_factor
    )
    feedforward_branch, adapter_shrink_hidden = finish(
        mlp_summed, mlp_low, shrink_columns_up_factor
    )
    result = (hidden.astype(jnp.float32) + attention_branch + feedforward_branch).astype(
        jnp.bfloat16
    )
    back_out, back_shrink = (
        lax.psum_scatter(
            matrix_product_transposed_right(cotangent, output_frozen_weight),
            "mp",
            scatter_dimension=1,
            tiled=True,
        ),
        lax.psum_scatter(
            matrix_product_transposed_right(cotangent, shrink_frozen_weight),
            "mp",
            scatter_dimension=1,
            tiled=True,
        ),
    )
    rank_out, rank_shrink = lax.psum(
        (
            ADAPTER_SCALE * matrix_product_transposed_right(cotangent, output_columns_up_factor),
            ADAPTER_SCALE * matrix_product_transposed_right(cotangent, shrink_columns_up_factor),
        ),
        "mp",
    )
    low_out_grad = rank_out.astype(jnp.bfloat16)
    low_shrink_grad = rank_shrink.astype(jnp.bfloat16)
    output_up_factor_piece = ADAPTER_SCALE * matrix_product_transposed_left(
        adapter_output_hidden, cotangent
    )
    shrink_up_factor_piece = ADAPTER_SCALE * matrix_product_transposed_left(
        adapter_shrink_hidden, cotangent
    )
    grad_context = (back_out + matrix_product_transposed_right(low_out_grad, out_rows_a)).astype(
        jnp.bfloat16
    )
    output_a_piece = matrix_product_transposed_left(attended_context, low_out_grad)
    shrink_a_piece = matrix_product_transposed_left(active_hidden, low_shrink_grad)
    grad_active = back_shrink + matrix_product_transposed_right(low_shrink_grad, shrink_rows_a)
    upper_gradient = gelu_pull(grad_active)[0].astype(jnp.bfloat16)
    grad_context = grad_context.reshape(count, SEQ_LEN, heads_here, HEAD_DIM)
    grad_query, grad_keys, grad_values = lax.map(
        partial(attend_back, causal), (query, keys, values, grad_context, logsum)
    )
    mixed_gradient = jnp.stack(
        [unrotate(grad_query, cosine, sine), unrotate(grad_keys, cosine, sine), grad_values], 3
    )
    mixed_gradient = mixed_gradient.reshape(rows, joined_cols).astype(jnp.bfloat16)
    rank_joined, rank_expand = lax.psum(
        (
            ADAPTER_SCALE * matrix_product_transposed_right(mixed_gradient, joined_weight_local),
            ADAPTER_SCALE * matrix_product_transposed_right(upper_gradient, expand_weight_local),
        ),
        "mp",
    )
    low_joined_grad = rank_joined.astype(jnp.bfloat16)
    low_expand_grad = rank_expand.astype(jnp.bfloat16)
    joined_up_factor_piece = ADAPTER_SCALE * matrix_product_transposed_left(
        adapter_joined_hidden, mixed_gradient
    )
    expand_up_factor_piece = ADAPTER_SCALE * matrix_product_transposed_left(
        adapter_expand_hidden, upper_gradient
    )
    norm_one_cols = lax.dynamic_slice_in_dim(first_norm_output, rank * cols, cols, 1)
    norm_two_cols = lax.dynamic_slice_in_dim(second_norm_output, rank * cols, cols, 1)
    joined_a_piece = matrix_product_transposed_left(norm_one_cols, low_joined_grad)
    expand_a_piece = matrix_product_transposed_left(norm_two_cols, low_expand_grad)
    grad_one, grad_two = (
        lax.psum_scatter(
            matrix_product_transposed_right(mixed_gradient, joined_frozen_weight),
            "mp",
            scatter_dimension=1,
            tiled=True,
        ),
        lax.psum_scatter(
            matrix_product_transposed_right(upper_gradient, expand_frozen_weight),
            "mp",
            scatter_dimension=1,
            tiled=True,
        ),
    )
    joined_rows_a = lax.dynamic_slice_in_dim(joined_a, rank * cols, cols, 0)
    expand_rows_a = lax.dynamic_slice_in_dim(expand_a, rank * cols, cols, 0)
    grad_one = grad_one + matrix_product_transposed_right(low_joined_grad, joined_rows_a)
    grad_two = grad_two + matrix_product_transposed_right(low_expand_grad, expand_rows_a)
    unit_one_cols = lax.dynamic_slice_in_dim(unit_one, rank * cols, cols, 1)
    unit_two_cols = lax.dynamic_slice_in_dim(unit_two, rank * cols, cols, 1)
    gain_one_cols = lax.dynamic_slice_in_dim(first_gain, rank * cols, cols, 0)
    gain_two_cols = lax.dynamic_slice_in_dim(second_gain, rank * cols, cols, 0)
    first_gain_piece = jnp.sum(grad_one * unit_one_cols, 0)
    first_bias_piece = jnp.sum(grad_one, 0)
    second_gain_piece = jnp.sum(grad_two * unit_two_cols, 0)
    second_bias_piece = jnp.sum(grad_two, 0)
    scaled_one = grad_one * gain_one_cols
    scaled_two = grad_two * gain_two_cols
    plain_one, along_one, plain_two, along_two = (
        lax.psum(jnp.sum(scaled_one, -1).astype(jnp.bfloat16), "mp").astype(jnp.float32),
        lax.psum(jnp.sum(scaled_one * unit_one_cols, -1).astype(jnp.bfloat16), "mp").astype(
            jnp.float32
        ),
        lax.psum(jnp.sum(scaled_two, -1).astype(jnp.bfloat16), "mp").astype(jnp.float32),
        lax.psum(jnp.sum(scaled_two * unit_two_cols, -1).astype(jnp.bfloat16), "mp").astype(
            jnp.float32
        ),
    )
    back_one = factor_one * (
        scaled_one - plain_one[:, None] / width - unit_one_cols * along_one[:, None] / width
    )
    back_two = factor_two * (
        scaled_two - plain_two[:, None] / width - unit_two_cols * along_two[:, None] / width
    )
    hidden_grad = cotangent.astype(jnp.float32) + back_one + back_two
    pieces = (
        first_gain_piece,
        first_bias_piece,
        second_gain_piece,
        second_bias_piece,
        joined_a_piece,
        joined_up_factor_piece,
        output_a_piece,
        output_up_factor_piece,
        expand_a_piece,
        expand_up_factor_piece,
        shrink_a_piece,
        shrink_up_factor_piece,
    )
    shapes = (
        first_gain.shape,
        first_bias.shape,
        second_gain.shape,
        second_bias.shape,
        joined_a.shape,
        joined_up_factor.shape,
        output_a.shape,
        output_up_factor.shape,
        expand_a.shape,
        expand_up_factor.shape,
        shrink_a.shape,
        shrink_up_factor.shape,
    )
    along = (0, 0, 0, 0, 0, 1, 0, 1, 0, 1, 0, 1)
    padded = [
        lax.dynamic_update_slice_in_dim(
            jnp.zeros(shape, jnp.float32), piece, rank * piece.shape[axis_dim], axis_dim
        )
        for piece, shape, axis_dim in zip(pieces, shapes, along)
    ]
    grads = lax.psum(
        (
            padded[0],
            padded[1],
            padded[2],
            padded[3],
            padded[4],
            padded[5],
            padded[6],
            padded[7],
            padded[8],
            padded[9],
            padded[10],
            padded[11],
        ),
        ("dp", "mp"),
    )
    return (
        result,
        hidden_grad,
        grads[0],
        grads[1],
        grads[2],
        grads[3],
        grads[4],
        grads[5],
        grads[6],
        grads[7],
        grads[8],
        grads[9],
        grads[10],
        grads[11],
    )


BF = jnp.bfloat16
F32 = jnp.float32
BLOCK = 256
VMEM_LIMIT = 62 << 20


def nn(left, right):
    return lax.dot_general(left, right, (((1,), (0,)), ((), ())), preferred_element_type=F32)


def nt(left, right):
    return lax.dot_general(left, right, (((1,), (1,)), ((), ())), preferred_element_type=F32)


def tn(left, right):
    return lax.dot_general(left, right, (((0,), (0,)), ((), ())), preferred_element_type=F32)


def span(start, size, unit=128):
    return pl.ds(pl.multiple_of(start, unit), size)


def layer_norm(rows_f32):
    center = rows_f32 - jnp.mean(rows_f32, 1, keepdims=True)
    factor = lax.rsqrt(jnp.mean(center * center, 1, keepdims=True) + EPS)
    return center * factor, factor


def attention_kernel(slots, shared, ids, *refs):
    hg_refs, w_own = refs[0:6], refs[6]
    o_own, o_mate = refs[7:9]
    foreign, diag = refs[9:13], refs[13:17]
    gain, bias, up, ja, oa, ou, cos_ref, sin_ref = refs[17:25]
    n_out = 4 if shared else 2
    outs = refs[25 : 25 + n_out]
    (h_v, g_v, w_v, o_v, w_t, q_t, k_t, v_t, k_n, v_n, do_t, dm_t, ctx_t, dk, dv, both, tok_sem, w_sem) = refs[25 + n_out :]
    f, q = ids[0], ids[1]
    seq = h_v.shape[0]
    steps = seq // BLOCK
    heads = q_t.shape[0] // HEAD_DIM
    width = h_v.shape[1]
    piece = width // 4
    shard = w_v.shape[1] // len(slots)
    for i, slot in enumerate(slots):
        if slot == 0:
            for s in range(4):
                pltpu.make_async_copy(
                    w_own.at[span(lax.bitwise_xor(f, s) * piece, piece), :],
                    w_v.at[s * piece : (s + 1) * piece, i * shard : (i + 1) * shard],
                    w_sem.at[0],
                ).start()
        else:
            for k in range(4):
                row = lax.bitwise_xor(lax.bitwise_xor(q, k), f) * piece
                pltpu.make_async_copy(
                    foreign[k].at[:, :shard], w_v.at[span(row, piece), i * shard : (i + 1) * shard], w_sem.at[0]
                ).start()
        head_block = lax.bitwise_xor(f, slot)
        rows = slice(i * BLOCK, (i + 1) * BLOCK)
        for s, ref in ((0, o_own), (1, o_mate)):
            pltpu.make_async_copy(
                ref.at[span(head_block * BLOCK, BLOCK), :], o_v.at[rows, s * piece : (s + 1) * piece], w_sem.at[1]
            ).start()
        for s, pieces in ((2, foreign), (3, diag)):
            for k in range(4):

                @pl.when(lax.bitwise_xor(q, k) == head_block)
                def _():
                    pltpu.make_async_copy(
                        pieces[k].at[:, shard : shard + BLOCK], o_v.at[rows, s * piece : (s + 1) * piece], w_sem.at[1]
                    ).start()

    start = 2 * seq if shared else lax.shift_right_logical(f, 1) * seq
    for i, dst in enumerate((h_v, g_v)):
        for s in range(4):
            ref = hg_refs[2 * i + s] if s < 2 else hg_refs[2 + s]
            at = start if s < 2 else i * seq
            pltpu.make_async_copy(
                ref.at[span(at, seq), :], dst.at[:, s * piece : (s + 1) * piece], tok_sem.at[i]
            ).start()

    pltpu.make_async_copy(w_v, w_v, w_sem.at[0]).wait()
    w_t[...] = w_v[...].T
    pltpu.make_async_copy(o_v, o_v, w_sem.at[1]).wait()
    up_t = jnp.concatenate([up[:, s * shard : (s + 1) * shard] for s in slots], 1).T
    oa_rows = jnp.concatenate([oa[s * BLOCK : (s + 1) * BLOCK, :] for s in slots], 0)
    o_rows = o_v[...]

    def project(t):
        rows = slice(t * BLOCK, (t + 1) * BLOCK)
        unit, _ = layer_norm(h_v[rows, :].astype(F32))
        n = (unit * gain[...] + bias[...]).astype(BF)
        low = (nn(n, ja[...]).astype(BF) * ADAPTER_SCALE).astype(BF)
        mixed = nt(w_t[...], n) + nt(up_t, low)
        cos, sin = cos_ref[:, rows], sin_ref[:, rows]
        half = ROTARY // 2
        for h in range(heads):
            own = slice(h * HEAD_DIM, (h + 1) * HEAD_DIM)
            base = 3 * HEAD_DIM * h
            for part in range(2):
                block = mixed[base + part * HEAD_DIM : base + (part + 1) * HEAD_DIM]
                a, b = block[:half], block[half:ROTARY]
                block = jnp.concatenate([a * cos - b * sin, b * cos + a * sin, block[ROTARY:]], 0).astype(BF)
                if part == 0:
                    q_t[own, rows] = (block * HEAD_DIM ** (-0.5)).astype(BF)
                else:
                    k_t[own, rows] = block
                    k_n[rows, own] = block.T
            block = mixed[base + 2 * HEAD_DIM : base + 3 * HEAD_DIM].astype(BF)
            v_t[own, rows] = block
            v_n[rows, own] = block.T
        g = g_v[rows, :]
        low_grad = (nt(g, ou[...]) * ADAPTER_SCALE).astype(BF)
        do_t[:, rows] = (nt(o_rows, g) + nt(oa_rows, low_grad)).astype(BF)

    for i, dst in enumerate((h_v, g_v)):
        pltpu.make_async_copy(dst, dst, tok_sem.at[i]).wait()
    for t in range(steps):
        project(t)

    later = lax.broadcasted_iota(jnp.int32, (BLOCK, BLOCK), 0) > lax.broadcasted_iota(jnp.int32, (BLOCK, BLOCK), 1)
    state = {}

    def products(h, i):
        own, qs = slice(h * HEAD_DIM, (h + 1) * HEAD_DIM), slice(i * BLOCK, (i + 1) * BLOCK)
        state[h, i] = (
            [nn(k_n[j * BLOCK : (j + 1) * BLOCK, own], q_t[own, qs]) for j in range(i + 1)],
            [nn(v_n[j * BLOCK : (j + 1) * BLOCK, own], do_t[own, qs]) for j in range(i + 1)],
        )

    def soft(h, i):
        scores, d_probs = state[h, i]
        scores[-1] = jnp.where(later, -1e30, scores[-1])
        peak = reduce(jnp.maximum, [jnp.max(s, 0, keepdims=True) for s in scores])
        weights = [jnp.exp(s - peak) for s in scores]
        inverse = 1.0 / reduce(jnp.add, [jnp.sum(w, 0, keepdims=True) for w in weights])
        probs = [w * inverse for w in weights]
        inner = reduce(jnp.add, [jnp.sum(p * d, 0, keepdims=True) for p, d in zip(probs, d_probs)])
        state[h, i] = (
            [p.astype(BF) for p in probs],
            [(p * (d - inner)).astype(BF) for p, d in zip(probs, d_probs)],
        )

    def unturn(block, cos, sin):
        half = ROTARY // 2
        a, b = block[:half], block[half:ROTARY]
        return jnp.concatenate([a * cos + b * sin, b * cos - a * sin, block[ROTARY:]], 0).astype(BF)

    def finish_block(h, i):
        own, qs = slice(h * HEAD_DIM, (h + 1) * HEAD_DIM), slice(i * BLOCK, (i + 1) * BLOCK)
        base = 3 * HEAD_DIM * h
        probs, d_scores = state.pop((h, i))
        keys = slice(0, (i + 1) * BLOCK)
        ctx_t[own, qs] = nn(v_t[own, keys], jnp.concatenate(probs, 0)).astype(BF)
        d_query = nn(k_t[own, keys], jnp.concatenate(d_scores, 0)) * HEAD_DIM ** (-0.5)
        dm_t[base : base + HEAD_DIM, qs] = unturn(d_query, cos_ref[:, qs], sin_ref[:, qs])
        query, d_out = q_t[own, qs], do_t[own, qs]
        for j in range(i + 1):
            js = slice(j * BLOCK, (j + 1) * BLOCK)
            if j == i:
                dk[own, js] = nt(query, d_scores[j])
                dv[own, js] = nt(d_out, probs[j])
            else:
                dk[own, js] += nt(query, d_scores[j])
                dv[own, js] += nt(d_out, probs[j])
        if i == steps - 1:
            dm_t[base + HEAD_DIM : base + 2 * HEAD_DIM, :] = unturn(dk[own, :], cos_ref[...], sin_ref[...])
            dm_t[base + 2 * HEAD_DIM : base + 3 * HEAD_DIM, :] = dv[own, :].astype(BF)

    order = [(h, i) for h in range(heads) for i in range(steps)]
    for at in range(len(order) + 2):
        if at < len(order):
            products(*order[at])
        if at >= 2:
            finish_block(*order[at - 2])
        if 1 <= at <= len(order):
            soft(*order[at - 1])
    for i in range(len(slots)):
        at = i * (BLOCK + shard)
        both[:, at : at + BLOCK] = ctx_t[i * BLOCK : (i + 1) * BLOCK, :].T
        both[:, at + BLOCK : at + BLOCK + shard] = dm_t[i * shard : (i + 1) * shard, :].T
    if shared:
        for s in range(4):
            outs[s][...] = both[span(lax.bitwise_xor(f, s) * BLOCK, BLOCK), :]
    else:
        c = lax.bitwise_and(f, 1)
        half = seq // 2
        outs[0][...] = both[span(c * half, half), :]
        outs[1][...] = both[span((1 - c) * half, half), :]


def any_spec():
    return pl.BlockSpec(memory_space=pl.ANY)


def vmem_spec():
    return pl.BlockSpec(memory_space=pltpu.VMEM)


def smem_spec():
    return pl.BlockSpec(memory_space=pltpu.SMEM)


def attention(slots, shared, ids, hg, w_own, os, gain, bias, up, ja, oa, ou, cos, sin):
    seq, piece = SEQ_LEN, hg[0].shape[1]
    width = 4 * piece
    shard, own = up.shape[1] // 4, oa.shape[0] // 4
    joined, inner = shard * len(slots), own * len(slots)
    out_shape = [jax.ShapeDtypeStruct((BLOCK if shared else seq // 2, inner + joined), BF)] * (4 if shared else 2)

    return pl.pallas_call(
        partial(attention_kernel, slots, shared),
        in_specs=[smem_spec()] + [any_spec()] * 17 + [vmem_spec()] * 8,
        out_specs=[vmem_spec()] * len(out_shape),
        out_shape=out_shape,
        scratch_shapes=[
            pltpu.VMEM((seq, width), BF),
            pltpu.VMEM((seq, width), BF),
            pltpu.VMEM((width, joined), BF),
            pltpu.VMEM((inner, width), BF),
            pltpu.VMEM((joined, width), BF),
            pltpu.VMEM((inner, seq), BF),
            pltpu.VMEM((inner, seq), BF),
            pltpu.VMEM((inner, seq), BF),
            pltpu.VMEM((seq, inner), BF),
            pltpu.VMEM((seq, inner), BF),
            pltpu.VMEM((inner, seq), BF),
            pltpu.VMEM((joined, seq), BF),
            pltpu.VMEM((inner, seq), BF),
            pltpu.VMEM((inner, seq), F32),
            pltpu.VMEM((inner, seq), F32),
            pltpu.VMEM((seq, inner + joined), BF),
            pltpu.SemaphoreType.DMA((2,)),
            pltpu.SemaphoreType.DMA((2,)),
        ],
        compiler_params=pltpu.CompilerParams(vmem_limit_bytes=VMEM_LIMIT),
        cost_estimate=pl.CostEstimate(
            flops=100_000_000_000 if shared else 1_000_000, bytes_accessed=100_000, transcendentals=0
        ),
        name="attention",
    )(ids, *hg, w_own, *os, gain, bias, up, ja, oa, ou, cos, sin)


def token_copies(ids, tokens, which, dst, sem):
    f = ids[0]
    x, c = lax.shift_right_logical(f, 1), lax.bitwise_and(f, 1)
    seq = SEQ_LEN
    half = seq // 2
    piece = tokens[0].shape[1]
    for s in range(4):
        cols = slice(s * piece, (s + 1) * piece)
        if s < 2:
            own, shared = tokens[2 * which + s], tokens[2 * which + s]
            own_at, shared_at = x * seq, 2 * seq
        else:
            own, shared = tokens[2 + s], tokens[4 + s]
            own_at, shared_at = which * seq, which * seq
        pltpu.make_async_copy(own.at[span(own_at + c * half, half), :], dst.at[:half, cols], sem).start()
        pltpu.make_async_copy(
            shared.at[span(shared_at + f * BLOCK, BLOCK), :], dst.at[half : half + BLOCK, cols], sem
        ).start()


def attention_copies(own, shared, at, dst, sem):
    half = dst.shape[0] - BLOCK
    size = dst.shape[1] // 4
    pitch = shared[0].shape[1]
    for s in range(4):
        to = slice(s * size, (s + 1) * size)
        col = (s // 2) * pitch + at
        pltpu.make_async_copy(own[s % 2].at[:, col : col + size], dst.at[:half, to], sem).start()
        pltpu.make_async_copy(shared[s].at[:, at : at + size], dst.at[half : half + BLOCK, to], sem).start()


def arrived(dst, sem):
    pltpu.make_async_copy(dst, dst, sem).wait()


def grads_kernel(ids, *refs):
    tokens, a_own, a_sh = refs[0:8], refs[8:10], refs[10:14]
    gain, bias, up, ja, oa, ou = refs[14:20]
    low_out_ref, low_grad_ref, keep, send = refs[20:24]
    h_v, g_v, c_v, m_v, sem = refs[24:]
    f = ids[0]
    rows, width = h_v.shape
    piece = width // 4
    shard = m_v.shape[1] // 4
    token_copies(ids, tokens, 1, g_v, sem.at[1])
    attention_copies(a_own, a_sh, 0, c_v, sem.at[2])
    token_copies(ids, tokens, 0, h_v, sem.at[0])
    attention_copies(a_own, a_sh, BLOCK, m_v, sem.at[3])
    put = partial(put_blocks, f, keep, send)
    arrived(g_v, sem.at[1])
    arrived(c_v, sem.at[2])
    low_out = (nn(c_v[...], oa[...]).astype(BF) * ADAPTER_SCALE).astype(BF)
    low_out_ref[...] = low_out
    low_out_grad = (nt(g_v[...], ou[...]) * ADAPTER_SCALE).astype(BF)
    put(0, piece, low_out.T, g_v)
    put(width, piece, low_out_grad.T, c_v)
    arrived(h_v, sem.at[0])
    unit, _ = layer_norm(h_v[...].astype(F32))
    n = (unit * gain[...] + bias[...]).astype(BF)
    low = (nn(n, ja[...]).astype(BF) * ADAPTER_SCALE).astype(BF)
    arrived(m_v, sem.at[3])
    low_grad = (nt(m_v[...], up[...]) * ADAPTER_SCALE).astype(BF)
    low_grad_ref[...] = low_grad
    put(2 * width, shard, low.T, m_v)
    put(2 * width + 4 * shard, piece, low_grad.T, n)


def put_blocks(f, keep, send, base, size, left, right):
    half = keep.shape[0]
    for s in range(4):
        value = nn(left, right[:, s * size : (s + 1) * size])
        to = span(base + lax.bitwise_xor(f, s) * size, size)
        keep[:, to] = value[:half]
        send[:, to] = value[half:]


def grads_of_attention(ids, tokens, a_own, a_sh, gain, bias, up, ja, oa, ou):
    piece = tokens[0].shape[1]
    width = 4 * piece
    rows = SEQ_LEN // 2 + BLOCK
    shard = up.shape[1] // 4
    rank = ja.shape[1]
    total = 3 * width + 4 * shard
    return pl.pallas_call(
        grads_kernel,
        in_specs=[smem_spec()] + [any_spec()] * 14 + [vmem_spec()] * 6,
        out_specs=[vmem_spec()] * 4,
        out_shape=[
            jax.ShapeDtypeStruct((rows, rank), BF),
            jax.ShapeDtypeStruct((rows, rank), BF),
            jax.ShapeDtypeStruct((rank // 2, total), F32),
            jax.ShapeDtypeStruct((rank // 2, total), F32),
        ],
        scratch_shapes=[
            pltpu.VMEM((rows, width), BF),
            pltpu.VMEM((rows, width), BF),
            pltpu.VMEM((rows, width), BF),
            pltpu.VMEM((rows, 4 * shard), BF),
            pltpu.SemaphoreType.DMA((4,)),
        ],
        compiler_params=pltpu.CompilerParams(vmem_limit_bytes=VMEM_LIMIT),
        cost_estimate=pl.CostEstimate(flops=100_000_000_000, bytes_accessed=100_000, transcendentals=0),
        name="grads_of_attention",
    )(ids, *tokens, *a_own, *a_sh, gain, bias, up, ja, oa, ou)


def start_slot(slot, ids, weights, e_v, s_v, e_sem, s_sem):
    f, q = ids[0], ids[1]
    e_own, e_mate, s_own, s_mate = weights[:4]
    foreign, diag = weights[4:8], weights[8:12]
    width, hidden = e_v.shape
    piece, part = width // 4, hidden // 4
    cols = slice(slot * part, (slot + 1) * part)
    if slot < 2:
        for t in range(4):
            pltpu.make_async_copy(
                weights[slot].at[span(lax.bitwise_xor(f, t) * piece, piece), :],
                e_v.at[t * piece : (t + 1) * piece, cols],
                e_sem.at[slot],
            ).start()
    else:
        for k in range(4):
            rows = span(lax.bitwise_xor(lax.bitwise_xor(q, k), f) * piece, piece)
            pltpu.make_async_copy(
                weights[4 * slot - 4 + k].at[:piece, :], e_v.at[rows, cols], e_sem.at[slot]
            ).start()
    for s, ref in ((0, s_own), (1, s_mate)):
        pltpu.make_async_copy(
            ref.at[span(lax.bitwise_xor(f, slot) * part, part), :],
            s_v.at[cols, s * piece : (s + 1) * piece],
            s_sem.at[slot],
        ).start()
    for k in range(4):

        @pl.when(lax.bitwise_xor(lax.bitwise_xor(q, k), f) == slot)
        def _():
            for s, pieces in ((2, foreign), (3, diag)):
                shrink_copies(pieces[k], s_v, slot * part, s * piece, s_sem.at[slot])


def shrink_copies(pack, dst, row, col, sem):
    for u in range(pack.shape[1] // BLOCK):
        pltpu.make_async_copy(
            pack.at[BLOCK:, u * BLOCK : (u + 1) * BLOCK],
            dst.at[span(row + u * BLOCK, BLOCK), col : col + BLOCK],
            sem,
        ).start()


CHUNK = 512


def mlp_first_kernel(ids, *refs):
    tokens, weights = refs[0:8], refs[8:20]
    gain, bias, ea, eu, sa, su = refs[20:26]
    act_out, dup_out, ls_out, dle_out, keep, send = refs[26:32]
    h_v, g_v, n_v, e_v, s_v, act, dup, sem, e_sem, s_sem, o_sem = refs[32:]
    f = ids[0]
    rows, width = h_v.shape
    hidden = e_v.shape[1]
    token_copies(ids, tokens, 0, h_v, sem.at[0])
    token_copies(ids, tokens, 1, g_v, sem.at[1])
    load = lambda slot: start_slot(slot, ids, weights, e_v, s_v, e_sem, s_sem)
    load(0)
    arrived(h_v, sem.at[0])
    unit, _ = layer_norm(h_v[...].astype(F32))
    n_v[...] = (unit * gain[...] + bias[...]).astype(BF)
    low = (nn(n_v[...], ea[...]).astype(BF) * ADAPTER_SCALE).astype(BF)
    arrived(g_v, sem.at[1])
    low_grad = (nt(g_v[...], su[...]) * ADAPTER_SCALE).astype(BF)
    load(1)
    state = {}
    part, piece = hidden // 4, width // 4

    def products(b, t):
        ts, bs = slice(t * BLOCK, (t + 1) * BLOCK), slice(b * CHUNK, (b + 1) * CHUNK)
        if t == 0 and bs.start % part == 0:
            slot = bs.start // part
            whole = slice(slot * part, (slot + 1) * part)
            if 1 <= slot < 3:
                load(slot + 1)
            arrived(e_v.at[:, whole], e_sem.at[slot])
            arrived(s_v.at[whole, :], s_sem.at[slot])
        state[b, t] = (
            nn(n_v[ts, :], e_v[:, bs]) + nn(low[ts], eu[:, bs]),
            nt(g_v[ts, :], s_v[bs, :]) + nt(low_grad[ts], sa[bs, :]),
        )

    def bend(b, t):
        ts, bs = slice(t * BLOCK, (t + 1) * BLOCK), slice(b * CHUNK, (b + 1) * CHUNK)
        upper, d_active = state.pop((b, t))
        normal = 0.5 * (1.0 + lax.erf(upper * 0.7071067811865476))
        density = jnp.exp(-0.5 * upper * upper) * 0.3989422804014327
        act[ts, bs] = (upper * normal).astype(BF)
        dup[ts, bs] = (d_active * (normal + upper * density)).astype(BF)
        if t == rows // BLOCK - 1:
            pltpu.make_async_copy(act.at[:, bs], act_out.at[:, bs], o_sem.at[0]).start()
            pltpu.make_async_copy(dup.at[:, bs], dup_out.at[:, bs], o_sem.at[1]).start()

    order = [(b, t) for b in range(hidden // CHUNK) for t in range(rows // BLOCK)]
    for at in range(len(order) + 1):
        if at < len(order):
            products(*order[at])
        if at > 0:
            bend(*order[at - 1])

    put = partial(put_blocks, f, keep, send)
    put(0, part, low_grad.T, act)
    put(hidden, part, low.T, dup)
    low_shrink = (nn(act[...], sa[...]).astype(BF) * ADAPTER_SCALE).astype(BF)
    low_expand_grad = (nt(dup[...], eu[...]) * ADAPTER_SCALE).astype(BF)
    ls_out[...] = low_shrink
    dle_out[...] = low_expand_grad
    put(2 * hidden, piece, low_shrink.T, g_v)
    put(2 * hidden + width, piece, low_expand_grad.T, n_v)
    arrived(act, o_sem.at[0])
    arrived(dup, o_sem.at[1])


def mlp_first(ids, tokens, weights, gain, bias, ea, eu, sa, su):
    piece = tokens[0].shape[1]
    width = 4 * piece
    rows = SEQ_LEN // 2 + BLOCK
    hidden = eu.shape[1]
    rank = ea.shape[1]
    return pl.pallas_call(
        mlp_first_kernel,
        in_specs=[smem_spec()] + [any_spec()] * 20 + [vmem_spec()] * 6,
        out_specs=[any_spec()] * 2 + [vmem_spec()] * 4,
        out_shape=[
            jax.ShapeDtypeStruct((rows, hidden), BF),
            jax.ShapeDtypeStruct((rows, hidden), BF),
            jax.ShapeDtypeStruct((rows, rank), BF),
            jax.ShapeDtypeStruct((rows, rank), BF),
            jax.ShapeDtypeStruct((rank // 2, 2 * hidden + 2 * width), F32),
            jax.ShapeDtypeStruct((rank // 2, 2 * hidden + 2 * width), F32),
        ],
        scratch_shapes=[
            pltpu.VMEM((rows, width), BF),
            pltpu.VMEM((rows, width), BF),
            pltpu.VMEM((rows, width), BF),
            pltpu.VMEM((width, hidden), BF),
            pltpu.VMEM((hidden, width), BF),
            pltpu.VMEM((rows, hidden), BF),
            pltpu.VMEM((rows, hidden), BF),
            pltpu.SemaphoreType.DMA((2,)),
            pltpu.SemaphoreType.DMA((4,)),
            pltpu.SemaphoreType.DMA((4,)),
            pltpu.SemaphoreType.DMA((2,)),
        ],
        compiler_params=pltpu.CompilerParams(vmem_limit_bytes=VMEM_LIMIT),
        cost_estimate=pl.CostEstimate(flops=100_000_000_000, bytes_accessed=100_000, transcendentals=0),
        name="mlp_first",
    )(ids, *tokens, *weights, gain, bias, ea, eu, sa, su)


def rows_of_slot(s, ids, own, mate, foreign, diag, col, dst, sems):
    f, q = ids[0], ids[1]
    piece = own.shape[0] // 4
    cols = own.shape[1]
    to = slice(s * cols, (s + 1) * cols)
    for t in range(4):
        if s < 2:
            src = (own, mate)[s].at[span(lax.bitwise_xor(f, t) * piece, piece), :]
            place = t
        else:
            src = (foreign, diag)[s - 2][t].at[:piece, col : col + cols]
            place = lax.bitwise_xor(lax.bitwise_xor(q, t), f)
        pltpu.make_async_copy(src, dst.at[span(place * piece, piece), to], sems.at[place]).start()


def shrink_of_slot(s, ids, own, mate, foreign, diag, dst, sem):
    f, q = ids[0], ids[1]
    part, piece = dst.shape[0] // 4, dst.shape[1] // 4
    for t in range(4):
        if s < 2:
            src = (own, mate)[s].at[span(lax.bitwise_xor(f, t) * part, part), :]
            pltpu.make_async_copy(src, dst.at[t * part : (t + 1) * part, s * piece : (s + 1) * piece], sem).start()
        else:
            row = lax.bitwise_xor(lax.bitwise_xor(q, t), f) * part
            shrink_copies((foreign, diag)[s - 2][t], dst, row, s * piece, sem)


def result_kernel(ids, *refs):
    tokens, a_own, a_sh = refs[0:8], refs[8:10], refs[10:14]
    o_own, o_mate, s_own, s_mate = refs[14:18]
    one_f, one_d, two_f, two_d = refs[18:22], refs[22:26], refs[26:30], refs[30:34]
    act_ref = refs[34]
    low_out, ou, low_shrink, su = refs[35:39]
    out = refs[39]
    h_v, c_v, o_v, s_v, act, sem, o_sem, s_sem = refs[40:]
    f = ids[0]
    rows, width = h_v.shape
    piece = width // 4
    attention_copies(a_own, a_sh, 0, c_v, sem.at[1])
    for s in range(4):
        rows_of_slot(s, ids, o_own, o_mate, one_f, one_d, 3 * piece, o_v, o_sem)
    token_copies(ids, tokens, 0, h_v, sem.at[2])
    pltpu.make_async_copy(act_ref, act, sem.at[3]).start()
    arrived(c_v, sem.at[1])
    for t in range(4):
        arrived(o_v.at[t * piece : (t + 1) * piece, :], o_sem.at[t])
    arrived(h_v, sem.at[2])
    for s in range(4):
        shrink_of_slot(s, ids, s_own, s_mate, two_f, two_d, s_v, s_sem.at[s])
    blocks = [slice(t * BLOCK, (t + 1) * BLOCK) for t in range(rows // BLOCK)]
    sums = [
        h_v[ts, :].astype(F32)
        + (nn(c_v[ts, :], o_v[...]) + nn(low_out[ts, :], ou[...]))
        + nn(low_shrink[ts, :], su[...])
        for ts in blocks
    ]
    arrived(act, sem.at[3])
    for s in range(4):
        arrived(s_v.at[:, s * piece : (s + 1) * piece], s_sem.at[s])
    for total, ts in zip(sums, blocks):
        value = (total + nn(act[ts, :], s_v[...])).astype(BF)
        for s in range(4):
            out[lax.bitwise_xor(f, s), ts, :] = value[:, s * piece : (s + 1) * piece]


def result_parts(ids, tokens, a_own, a_sh, o_parts, s_parts, one, two, act, low_out, ou, low_shrink, su):
    piece = tokens[0].shape[1]
    width = 4 * piece
    rows = SEQ_LEN // 2 + BLOCK
    hidden = act.shape[1]
    return pl.pallas_call(
        result_kernel,
        in_specs=[smem_spec()] + [any_spec()] * 35 + [vmem_spec()] * 4,
        out_specs=vmem_spec(),
        out_shape=jax.ShapeDtypeStruct((4, rows, piece), BF),
        scratch_shapes=[
            pltpu.VMEM((rows, width), BF),
            pltpu.VMEM((rows, width), BF),
            pltpu.VMEM((width, width), BF),
            pltpu.VMEM((hidden, width), BF),
            pltpu.VMEM((rows, hidden), BF),
            pltpu.SemaphoreType.DMA((4,)),
            pltpu.SemaphoreType.DMA((4,)),
            pltpu.SemaphoreType.DMA((4,)),
        ],
        compiler_params=pltpu.CompilerParams(vmem_limit_bytes=VMEM_LIMIT),
        cost_estimate=pl.CostEstimate(flops=100_000_000_000, bytes_accessed=100_000, transcendentals=0),
        name="result_parts",
    )(ids, *tokens, *a_own, *a_sh, *o_parts, *s_parts, *one, *two, act, low_out, ou, low_shrink, su)


def input_grad_kernel(ids, *refs):
    tokens, a_own, a_sh = refs[0:8], refs[8:10], refs[10:14]
    w_own, w_mate, e_own, e_mate = refs[14:18]
    one_f, one_d, two_f, two_d = refs[18:22], refs[22:26], refs[26:30], refs[30:34]
    dup_ref = refs[34]
    gain_one, gain_two, ja, ea, low_joined_grad, low_expand_grad = refs[35:41]
    outs, sums = refs[41:45], refs[45]
    h_v, g_v, m_v, w_v, e_v, dup, one_v, sem, w_sem, e_sem = refs[46:]
    f = ids[0]
    rows, width = h_v.shape
    piece = width // 4
    shard = m_v.shape[1] // 4
    attention_copies(a_own, a_sh, BLOCK, m_v, sem.at[0])
    for s in range(4):
        rows_of_slot(s, ids, w_own, w_mate, one_f, one_d, 0, w_v, w_sem)
    arrived(m_v, sem.at[0])
    blocks = [slice(t * BLOCK, (t + 1) * BLOCK) for t in range(rows // BLOCK)]
    for t in range(4):
        arrived(w_v.at[t * piece : (t + 1) * piece, :], w_sem.at[t])
    pltpu.make_async_copy(dup_ref, dup, sem.at[3]).start()
    for s in range(4):
        rows_of_slot(s, ids, e_own, e_mate, two_f, two_d, 0, e_v, e_sem)
    token_copies(ids, tokens, 0, h_v, sem.at[1])
    token_copies(ids, tokens, 1, g_v, sem.at[2])
    for ts in blocks:
        one_v[ts, :] = nt(m_v[ts, :], w_v[...]) + nt(low_joined_grad[ts, :], ja[...])
    arrived(dup, sem.at[3])
    for t in range(4):
        arrived(e_v.at[t * piece : (t + 1) * piece, :], e_sem.at[t])
    arrived(h_v, sem.at[1])
    arrived(g_v, sem.at[2])
    total = None
    for ts in blocks:
        one = one_v[ts, :]
        two = nt(dup[ts, :], e_v[...]) + nt(low_expand_grad[ts, :], ea[...])
        unit, factor = layer_norm(h_v[ts, :].astype(F32))
        here = [jnp.sum(v, 0, keepdims=True) for v in (one * unit, one, two * unit, two)]
        total = here if total is None else [a + b for a, b in zip(total, here)]
        e = one * gain_one[...] + two * gain_two[...]
        plain = jnp.mean(e, 1, keepdims=True)
        along = jnp.mean(e * unit, 1, keepdims=True)
        value = g_v[ts, :].astype(F32) + factor * (e - plain - unit * along)
        for s in range(4):
            outs[s][ts, :] = value[:, s * piece : (s + 1) * piece].astype(outs[s].dtype)
    value = jnp.concatenate(total + [jnp.zeros((4, width), F32)], 0)
    for s in range(4):
        sums[:, span(lax.bitwise_xor(f, s) * piece, piece)] = value[:, s * piece : (s + 1) * piece]


def input_grad_parts(
    ids, tokens, a_own, a_sh, w_parts, e_parts, one, two, dup, gain_one, gain_two, ja, ea, low_joined_grad, low_expand_grad
):
    piece = tokens[0].shape[1]
    width = 4 * piece
    rows = SEQ_LEN // 2 + BLOCK
    hidden = dup.shape[1]
    joined = 4 * w_parts[0].shape[1]
    return pl.pallas_call(
        input_grad_kernel,
        in_specs=[smem_spec()] + [any_spec()] * 35 + [vmem_spec()] * 6,
        out_specs=[vmem_spec()] * 5,
        out_shape=[jax.ShapeDtypeStruct((rows, piece), t) for t in (F32, F32, BF, BF)]
        + [jax.ShapeDtypeStruct((8, width), F32)],
        scratch_shapes=[
            pltpu.VMEM((rows, width), BF),
            pltpu.VMEM((rows, width), BF),
            pltpu.VMEM((rows, joined), BF),
            pltpu.VMEM((width, joined), BF),
            pltpu.VMEM((width, hidden), BF),
            pltpu.VMEM((rows, hidden), BF),
            pltpu.VMEM((rows, width), F32),
            pltpu.SemaphoreType.DMA((4,)),
            pltpu.SemaphoreType.DMA((4,)),
            pltpu.SemaphoreType.DMA((4,)),
        ],
        compiler_params=pltpu.CompilerParams(vmem_limit_bytes=VMEM_LIMIT),
        cost_estimate=pl.CostEstimate(flops=100_000_000_000, bytes_accessed=100_000, transcendentals=0),
        name="input_grad_parts",
    )(
        ids, *tokens, *a_own, *a_sh, *w_parts, *e_parts, *one, *two, dup,
        gain_one, gain_two, ja, ea, low_joined_grad, low_expand_grad,
    )


def gather_rows_kernel(widen, ids, *refs):
    parts, out = refs[:4], refs[4]
    scratch = refs[5:]
    f = ids[0]
    sem = scratch[-1]
    rows = parts[0].shape[0]
    half = rows - BLOCK
    seq = 2 * half
    copies = []
    for s in range(4):
        src = parts[s]
        if src.dtype != out.dtype:
            scratch[s - 2][...] = src[...].astype(out.dtype)
            src = scratch[s - 2]
        at = lax.bitwise_xor(f, s)
        copies.append(pltpu.make_async_copy(src.at[:half, :], out.at[span(at * half, half), :], sem.at[2 * s]))
        copies.append(
            pltpu.make_async_copy(src.at[half:, :], out.at[span(2 * seq + at * BLOCK, BLOCK), :], sem.at[2 * s + 1])
        )
        copies[-2].start()
        copies[-1].start()
    for copy in copies:
        copy.wait()


def gather_rows(ids, parts, dtype):
    rows, piece = parts[0].shape
    narrow = [p for p in parts if p.dtype != dtype]
    return pl.pallas_call(
        partial(gather_rows_kernel, dtype),
        in_specs=[smem_spec()] + [vmem_spec()] * 4,
        out_specs=any_spec(),
        out_shape=jax.ShapeDtypeStruct((4 * rows, piece), dtype),
        scratch_shapes=[pltpu.VMEM((rows, piece), dtype)] * len(narrow) + [pltpu.SemaphoreType.DMA((8,))],
        compiler_params=pltpu.CompilerParams(vmem_limit_bytes=VMEM_LIMIT),
        name="gather_rows",
    )(ids, *parts)


def adapters_kernel(cuts, sums_at, ids, order_ref, *refs):
    order = order_ref[...]
    pieces, outs = refs[:8], refs[8:]
    for (at, size, turned), out in zip(cuts, outs):
        value = jnp.concatenate([p[:, at : at + size] for p in pieces], 0)
        out[...] = tn(value, order) if turned else tn(order, value)
    if sums_at is not None:
        sums, lanes = outs[-5:-1], outs[-1]
        for k in range(4):
            lanes[span(lax.bitwise_xor(ids[1], k) * 16, 16, 16), :] = pieces[k][:, sums_at : sums_at + 128].astype(F32)
        for i, out in enumerate(sums):
            for j in range(8):
                out[:, j * 128 : (j + 1) * 128] = lanes[8 * j + i : 8 * j + i + 1, :]


def adapters_out(ids, order, pieces, cuts, sums_at=None):
    rank = order.shape[0]
    out_shape = [jax.ShapeDtypeStruct((size, rank) if turned else (rank, size), F32) for at, size, turned in cuts]
    scratch = []
    if sums_at is not None:
        out_shape += [jax.ShapeDtypeStruct((1, 1024), F32)] * 4
        scratch.append(pltpu.VMEM((64, 128), F32))
    return pl.pallas_call(
        partial(adapters_kernel, cuts, sums_at),
        in_specs=[smem_spec()] + [vmem_spec()] * 9,
        out_specs=[vmem_spec()] * len(out_shape),
        out_shape=out_shape,
        scratch_shapes=scratch,
        compiler_params=pltpu.CompilerParams(vmem_limit_bytes=VMEM_LIMIT),
        name="adapters_out",
    )(ids, order, *pieces)


def join_rows_kernel(keep, received, sums, other, out):
    cols = keep.shape[1]
    out[:, :cols] = (keep[...] + received[...]).astype(BF)
    total = sums[...] + other[...]
    out[:, cols:] = jnp.concatenate([total[:, i * 128 : (i + 1) * 128] for i in range(8)], 0).astype(BF)


def join_rows(keep, received, sums, other):
    rows, cols = keep.shape
    return pl.pallas_call(
        join_rows_kernel,
        in_specs=[vmem_spec()] * 4,
        out_specs=vmem_spec(),
        out_shape=jax.ShapeDtypeStruct((rows, cols + 128), BF),
        compiler_params=pltpu.CompilerParams(vmem_limit_bytes=VMEM_LIMIT),
        name="join_rows",
    )(keep, received, sums, other)


def split_rows_kernel(keep, received, own, *outs):
    size = own.shape[0]
    own[...] = keep[:size, :] + received[:size, :]
    for k, out in enumerate(outs):
        rows = slice((k + 1) * size, (k + 2) * size)
        out[...] = (keep[rows, :] + received[rows, :]).astype(BF)


def split_rows(keep, received):
    rows, cols = keep.shape
    return pl.pallas_call(
        split_rows_kernel,
        in_specs=[vmem_spec()] * 2,
        out_specs=[vmem_spec()] * 4,
        out_shape=[jax.ShapeDtypeStruct((rows // 4, cols), t) for t in (F32, BF, BF, BF)],
        compiler_params=pltpu.CompilerParams(vmem_limit_bytes=VMEM_LIMIT),
        name="split_rows",
    )(keep, received)


def pack_kernel(plan, ids, *refs):
    n_in = len(refs) - 1 - len(plan)
    srcs, outs, sem = refs[:n_in], refs[n_in:-1], refs[-1]
    for out, (shape, blocks) in zip(outs, plan):
        for src, which, size, sub, rows, to_row, to_col in blocks:
            cols = srcs[src].shape[1]
            pltpu.make_async_copy(
                srcs[src].at[span(ids[which] * size + sub, rows), :],
                out.at[to_row : to_row + rows, to_col : to_col + cols],
                sem,
            ).start()
    for out in outs:
        pltpu.make_async_copy(out, out, sem).wait()


def pack(ids, arrays, plan):
    return pl.pallas_call(
        partial(pack_kernel, plan),
        in_specs=[smem_spec()] + [any_spec()] * len(arrays),
        out_specs=[vmem_spec()] * len(plan),
        out_shape=[jax.ShapeDtypeStruct(shape, arrays[0].dtype) for shape, _ in plan],
        scratch_shapes=[pltpu.SemaphoreType.DMA],
        compiler_params=pltpu.CompilerParams(vmem_limit_bytes=VMEM_LIMIT),
        name="pack",
    )(ids, *arrays)


def order_kernel(late, ids, order_ref, other_ref, *refs):
    n = len(refs) // 2
    f = ids[0]
    for i, (src, out) in enumerate(zip(refs[:n], refs[n:])):
        order = (other_ref if i in late else order_ref)[...]
        axis = 0 if src.shape[0] > src.shape[1] else 1
        size = src.shape[axis] // 4
        for s in range(4):
            at, to = span(lax.bitwise_xor(f, s) * size, size), slice(s * size, (s + 1) * size)
            if src.dtype == F32:
                out[:, to] = src[:, at]
            elif axis == 0:
                out[to, :] = nt(src[at, :], order).astype(BF)
            else:
                out[:, to] = nn(order, src[:, at]).astype(BF)


def order_params(ids, order, other, params, late):
    return pl.pallas_call(
        partial(order_kernel, late),
        in_specs=[smem_spec()] + [vmem_spec()] * (2 + len(params)),
        out_specs=[vmem_spec()] * len(params),
        out_shape=[jax.ShapeDtypeStruct(p.shape, p.dtype) for p in params],
        compiler_params=pltpu.CompilerParams(vmem_limit_bytes=VMEM_LIMIT),
        name="order_params",
    )(ids, order, other, *params)


def turn_kernel(ids, out):
    for i in range(ids.shape[0]):
        out[i] = ids[i]


def turn(ids):
    return pl.pallas_call(
        turn_kernel,
        in_specs=[smem_spec()],
        out_specs=smem_spec(),
        out_shape=jax.ShapeDtypeStruct(ids.shape, ids.dtype),
        cost_estimate=pl.CostEstimate(flops=100_000_000_000, bytes_accessed=100_000, transcendentals=0),
        name="turn",
    )(ids)


def swap(axes):
    def run(value):
        size = lax.axis_size(axes)
        return lax.ppermute(value, axes, [(i, size - 1 - i) for i in range(size)])

    return run


def after(value, *others):
    return lax.optimization_barrier((value, *others))[0]


def on_device_by_tokens(
    hidden,
    first_gain,
    first_bias,
    second_gain,
    second_bias,
    joined_frozen_weight,
    output_frozen_weight,
    expand_frozen_weight,
    shrink_frozen_weight,
    joined_a,
    joined_up_factor,
    output_a,
    output_up_factor,
    expand_a,
    expand_up_factor,
    shrink_a,
    shrink_up_factor,
    cotangent,
):
    x, c, q = lax.axis_index("x"), lax.axis_index("core"), lax.axis_index(("zn", "y"))
    f, far = 2 * x + c, lax.axis_index(("zf", "x"))
    seq, half = SEQ_LEN, SEQ_LEN // 2
    width = 4 * hidden.shape[1]
    rank = joined_a.shape[1]
    units = 4 * expand_frozen_weight.shape[1]
    ids = jnp.stack([f, q, far, 1 - x, 3 - q, 0 * f + 2]).astype(jnp.int32)
    to_core, to_x, to_diag = swap("core"), swap("x"), swap(("x", "core"))
    near = swap("y"), swap("zn"), swap(("zn", "y"))
    cross = to_x, swap("zf"), swap(("zf", "x"))

    piece = width // 4

    shard, part = joined_frozen_weight.shape[1], expand_frozen_weight.shape[1]
    (one_pack,) = pack(
        ids,
        (joined_frozen_weight, output_frozen_weight),
        (((piece, shard + piece), ((0, 1, piece, 0, piece, 0, 0), (1, 1, piece, 0, piece, 0, shard))),),
    )
    one_x = to_x(one_pack)
    own, shared = pack(
        after(ids, one_pack),
        (hidden, cotangent),
        tuple(((2 * seq, piece), ((0, at, seq, 0, seq, 0, 0), (1, at, seq, 0, seq, seq, 0))) for at in (3, 5)),
    )
    two_first, two_last = pack(
        after(ids, own),
        (expand_frozen_weight, shrink_frozen_weight),
        tuple(
            (
                (piece + BLOCK, part),
                ((0, at, piece, 0, piece, 0, 0),)
                + tuple((1, at, part, u, BLOCK, piece, u) for u in range(0, part, BLOCK)),
            )
            for at in (1, 4)
        ),
    )
    place = lax.broadcasted_iota(jnp.int32, (rank, rank), 0)
    half_order, order = (
        (lax.broadcasted_iota(jnp.int32, (rank, rank), 1) == (place ^ mask)).astype(BF) for mask in (c * 64, c * 64 + q * 16)
    )
    gain_one, bias_one, gain_two, bias_two, ja, oa, ea, sa, ju, ou, eu, su = order_params(
        after(ids, own),
        half_order,
        order,
        tuple(v[None, :] for v in (first_gain, first_bias, second_gain, second_bias))
        + (joined_a, output_a, expand_a, shrink_a)
        + (joined_up_factor, output_up_factor, expand_up_factor, shrink_up_factor),
        (6, 7, 10, 11),
    )
    position = np.arange(seq, dtype=np.float32)[None, :]
    frequency = np.float32(10000.0) ** (-(np.arange(ROTARY // 2, dtype=np.float32) * np.float32(2.0)) / np.float32(ROTARY))
    angles = frequency[:, None] * position
    cos, sin = jnp.asarray(np.cos(angles), F32), jnp.asarray(np.sin(angles), F32)
    h_mate, g_mate, e_mate, s_mate = (
        to_core(v) for v in after((hidden, cotangent, expand_frozen_weight, shrink_frozen_weight), one_pack)
    )
    one_x = after(one_x, own, two_first, gain_one, h_mate, g_mate, e_mate, s_mate)
    own_x = to_x(after(own, one_x))
    one_near = tuple(go(one_x) for go in near)
    own_x = after(own_x, one_near)
    ids = turn(after(ids, own_x))
    own_mate = to_core(after(own_x, ids))
    one_foreign = (one_x,) + one_near
    o_mate, *one_diag = (to_core(p) for p in after((output_frozen_weight,) + one_foreign, ids))
    one_diag = tuple(one_diag)
    local = (hidden, h_mate, cotangent, g_mate)
    o_parts = (output_frozen_weight, o_mate) + one_foreign + one_diag
    params = (gain_one, bias_one, ju, ja, oa, ou, cos, sin)
    shared_x = to_x(after(shared, own_x))
    two_x = to_x(after(two_first, own_x))
    keep_a, send_a = attention(
        (0, 2), False, ids, local + (own_x, own_mate), joined_frozen_weight, o_parts, *params
    )
    shared_x, two_x = after((shared_x, two_x), keep_a)
    shared_mate = to_core(shared_x)
    two_y, two_z, two_yz = near[0](two_x), near[1](two_x), to_x(after(two_last, two_x))
    b_parts = attention(
        (0,), True, ids, local + (shared_x, shared_mate), joined_frozen_weight, o_parts, *params
    )
    two_y, two_z, two_yz = after((two_y, two_z, two_yz), b_parts[0])
    foreign_two = (two_x, two_y, two_z, two_yz)
    diag_two = tuple(to_core(p) for p in foreign_two)
    tokens = local + (own_x, own_mate, shared_x, shared_mate)
    mlp_weights = (expand_frozen_weight, e_mate, shrink_frozen_weight, s_mate) + foreign_two + diag_two
    act, dup, ls, dle, keep_two, send_two = mlp_first(
        ids, tokens, mlp_weights, gain_two, bias_two, ea, eu, sa, su
    )
    b_moved = tuple(go(p) for go, p in zip((to_core, to_x, to_diag), b_parts[1:]))
    w_mate = to_core(joined_frozen_weight)
    b_moved, a_mate, w_mate = after((b_moved, to_core(send_a), w_mate), act)
    a_own, a_shared = (keep_a, a_mate), (b_parts[0],) + b_moved

    two = to_core(send_two)
    low_out, low_joined_grad, keep_one, send_one = grads_of_attention(
        ids, tokens, a_own, a_shared, gain_one, bias_one, ju, ja, oa, ou
    )
    two = split_rows(keep_two, after(two, low_out))
    dup = after(dup, two, send_one)
    two = (two[0],) + tuple(go(p) for go, p in zip(near, two[1:]))
    one = to_core(send_one)
    hidden_grad = input_grad_parts(
        ids, tokens, a_own, a_shared, (joined_frozen_weight, w_mate), (expand_frozen_weight, e_mate),
        one_foreign + one_diag, foreign_two + diag_two, dup, gain_one, gain_two, ja, ea, low_joined_grad, dle,
    )
    two, one = after((two, one), hidden_grad[4])
    sums = hidden_grad[4]
    hidden_grad = (hidden_grad[0], to_core(hidden_grad[1]), to_x(hidden_grad[2]), to_diag(hidden_grad[3]))

    def part_sum(parts):
        return reduce(jnp.add, [p.astype(F32) for p in parts]).astype(BF)

    two = part_sum(two)
    one = join_rows(keep_one, one, sums, to_core(sums))
    act = after(act, two, one, hidden_grad[1])
    two_other = cross[1](two)
    one = lax.all_to_all(one, ("zn", "y"), 0, 0, tiled=True)
    result = result_parts(
        ids, tokens, a_own, a_shared, (output_frozen_weight, o_mate), (shrink_frozen_weight, s_mate),
        one_foreign + one_diag, foreign_two + diag_two, act, low_out, ou, ls, su,
    )
    hidden_grad, two_other, one = after((hidden_grad, two_other, one), result)

    two = part_sum((two, two_other))
    two_other = cross[0](two)
    one = part_sum(after(one, two).reshape(4, -1, one.shape[1]))
    one_other = cross[1](one)
    hidden_grad = gather_rows(ids, hidden_grad, F32)
    two_other = after(two_other, hidden_grad)
    result = lax.all_to_all(after(result, two_other).reshape(-1, piece), ("x", "core"), 0, 0, tiled=True)
    two = part_sum((two, two_other))
    two = (two,) + tuple(go(two) for go in near)
    one = part_sum((one, one_other))
    one_other = cross[0](one)
    one = part_sum((one, one_other))
    one_y, one_z, one_yz = near[0](one), near[1](one), near[2](after(one, two))
    two = two + tuple(to_core(p) for p in two)
    joined = ju.shape[1]
    expand_a_grad, expand_b_grad, shrink_a_grad, shrink_b_grad = adapters_out(
        ids, order, two,
        ((2 * units + width, width, True), (units, units, False), (0, units, True), (2 * units, width, False)),
    )
    one = (one, one_y, one_z) + after((one_yz,), expand_a_grad)
    one = one + tuple(to_core(p) for p in one)
    result = after(result, expand_a_grad).reshape(4, -1, piece)
    result = jnp.concatenate([result[:, : seq // 2].reshape(-1, piece), result[:, seq // 2 :].reshape(-1, piece)], 0)
    joined_a_grad, joined_b_grad, output_a_grad, output_b_grad, *sums = adapters_out(
        ids, order, one,
        ((2 * width + joined, width, True), (2 * width, joined, False), (width, width, True), (0, width, False)),
        3 * width + joined,
    )
    return (
        result,
        hidden_grad,
        sums[0].reshape(-1),
        sums[1].reshape(-1),
        sums[2].reshape(-1),
        sums[3].reshape(-1),
        joined_a_grad,
        joined_b_grad,
        output_a_grad,
        output_b_grad,
        expand_a_grad,
        expand_b_grad,
        shrink_a_grad,
        shrink_b_grad,
    )


def solution(mesh):
    step, rows, cols = on_device, "dp", "mp"
    if mesh.shape["dp"] == 8 and mesh.shape["mp"] == 4:
        step, rows, cols = on_device_by_tokens, ("zf", "zn", "y"), ("x", "core")
        mesh = Mesh(mesh.devices.reshape((2,) * 5), rows + cols)
    whole, split, tokens = P(), P(None, cols), P(rows, cols)
    return jax.shard_map(
        step,
        mesh=mesh,
        in_specs=(tokens,) + (whole,) * 4 + (split,) * 4 + (whole,) * 8 + (tokens,),
        out_specs=(tokens, tokens) + (whole,) * 12,
        check_vma=False,
    )
```

```python
from functools import partial, reduce

import jax
import jax.numpy as jnp
import numpy as np
from jax import lax
from jax.experimental import pallas as pl
from jax.experimental.pallas import tpu as pltpu
from jax.sharding import Mesh
from jax.sharding import PartitionSpec as P

ROTARY = 16
SEQ_LEN = 1024
HEAD_DIM = 64


ADAPTER_SCALE = 0.25
EPS = 1e-05


def matrix_product(left, right):
    return jnp.dot(left, right, preferred_element_type=jnp.float32)


def matrix_product_transposed_left(left, right):
    return lax.dot_general(
        left, right, (((0,), (0,)), ((), ())), preferred_element_type=jnp.float32
    )


def matrix_product_transposed_right(left, right):
    return lax.dot_general(
        left, right, (((1,), (1,)), ((), ())), preferred_element_type=jnp.float32
    )


def normalize(full, gain, bias):
    center = full - jnp.mean(full, -1, keepdims=True)
    factor = lax.rsqrt(jnp.mean(center * center, -1, keepdims=True) + EPS)
    unit = center * factor
    return (unit, factor, unit * gain + bias)


def tables():
    position = jnp.arange(SEQ_LEN, dtype=jnp.float32)[:, None]
    frequency = 10000.0 ** (-(jnp.arange(ROTARY // 2, dtype=jnp.float32) * 2.0) / ROTARY)
    angles = position * frequency[None, :]
    cosine = jnp.concatenate([jnp.cos(angles), jnp.cos(angles)], -1)[:, None, :]
    sine = jnp.concatenate([jnp.sin(angles), jnp.sin(angles)], -1)[:, None, :]
    return (cosine, sine)


def rotate(block, cosine, sine):
    half = ROTARY // 2
    part = block[..., :ROTARY]
    turned = jnp.concatenate([-part[..., half:], part[..., :half]], -1)
    return jnp.concatenate([part * cosine + turned * sine, block[..., ROTARY:]], -1)


def unrotate(grad, cosine, sine):
    half = ROTARY // 2
    part = grad[..., :ROTARY]
    scaled = part * sine
    untied = jnp.concatenate([scaled[..., half:], -scaled[..., :half]], -1)
    return jnp.concatenate([part * cosine + untied, grad[..., ROTARY:]], -1)


def attend(causal, block):
    query, keys, values = block
    scores = jnp.einsum(
        "qhe,khe->hqk", query, keys, preferred_element_type=jnp.float32
    ) * HEAD_DIM ** (-0.5)
    scores = jnp.where(causal, scores, -1e30)
    peak = jnp.max(scores, -1, keepdims=True)
    weights = jnp.exp(scores - peak)
    total = jnp.sum(weights, -1, keepdims=True)
    probs = (weights / total).astype(jnp.bfloat16)
    attended_context = jnp.einsum("hqk,khe->qhe", probs, values, preferred_element_type=jnp.float32)
    return (attended_context.astype(jnp.bfloat16), (peak + jnp.log(total))[..., 0])


def attend_back(causal, block):
    query, keys, values, grad_context, logsum = block
    scores = jnp.einsum(
        "qhe,khe->hqk", query, keys, preferred_element_type=jnp.float32
    ) * HEAD_DIM ** (-0.5)
    scores = jnp.where(causal, scores, -1e30)
    probs = jnp.exp(scores - logsum[..., None])
    grad_probs = jnp.einsum(
        "qhe,khe->hqk", grad_context, values, preferred_element_type=jnp.float32
    )
    inner = jnp.sum(probs * grad_probs, -1, keepdims=True)
    grad_scores = (probs * (grad_probs - inner)).astype(jnp.bfloat16)
    grad_query = jnp.einsum(
        "hqk,khe->qhe", grad_scores, keys, preferred_element_type=jnp.float32
    ) * HEAD_DIM ** (-0.5)
    grad_keys = jnp.einsum(
        "hqk,qhe->khe", grad_scores, query, preferred_element_type=jnp.float32
    ) * HEAD_DIM ** (-0.5)
    grad_values = jnp.einsum(
        "hqk,qhe->khe", probs.astype(jnp.bfloat16), grad_context, preferred_element_type=jnp.float32
    )
    return (grad_query, grad_keys, grad_values)


def fold_with(weight, adapter_a, carry, piece):
    span = piece.shape[1]
    weight_rows = lax.slice_in_dim(weight, 0, span, axis=0)
    adapter_rows = lax.slice_in_dim(adapter_a, 0, span, axis=0)
    return (
        carry[0] + matrix_product(piece, weight_rows),
        carry[1] + matrix_product(piece, adapter_rows),
    )


def finish(summed_result, low_sum, columns_up_factor):
    adapter_values = low_sum.astype(jnp.bfloat16)
    return (
        summed_result + ADAPTER_SCALE * matrix_product(adapter_values, columns_up_factor),
        adapter_values,
    )


def on_device(
    hidden,
    first_gain,
    first_bias,
    second_gain,
    second_bias,
    joined_frozen_weight,
    output_frozen_weight,
    expand_frozen_weight,
    shrink_frozen_weight,
    joined_a,
    joined_up_factor,
    output_a,
    output_up_factor,
    expand_a,
    expand_up_factor,
    shrink_a,
    shrink_up_factor,
    cotangent,
):
    rank = lax.axis_index("mp")
    rows = hidden.shape[0]
    cols = hidden.shape[1]
    width = cols * lax.axis_size("mp")
    count = rows // SEQ_LEN
    joined_cols = joined_frozen_weight.shape[1]
    expand_cols = expand_frozen_weight.shape[1]
    heads_here = joined_cols // (3 * HEAD_DIM)
    inner_out = joined_cols // 3
    full = lax.all_gather(hidden, "mp", axis=1, tiled=True).astype(jnp.float32)
    unit_one, factor_one, first_norm_output = normalize(full, first_gain, first_bias)
    unit_two, factor_two, second_norm_output = normalize(full, second_gain, second_bias)
    first_norm_output = first_norm_output.astype(jnp.bfloat16)
    second_norm_output = second_norm_output.astype(jnp.bfloat16)
    adapter_joined_hidden = matrix_product(first_norm_output, joined_a).astype(jnp.bfloat16)
    joined_weight_local = lax.dynamic_slice_in_dim(
        joined_up_factor, rank * joined_cols, joined_cols, 1
    )
    mixed_state = matrix_product(
        first_norm_output, joined_frozen_weight
    ) + ADAPTER_SCALE * matrix_product(adapter_joined_hidden, joined_weight_local)
    mixed_state = mixed_state.reshape(count, SEQ_LEN, heads_here, 3, HEAD_DIM)
    cosine, sine = tables()
    query = rotate(mixed_state[:, :, :, 0], cosine, sine).astype(jnp.bfloat16)
    keys = rotate(mixed_state[:, :, :, 1], cosine, sine).astype(jnp.bfloat16)
    values = mixed_state[:, :, :, 2].astype(jnp.bfloat16)
    causal = jnp.arange(SEQ_LEN)[:, None] >= jnp.arange(SEQ_LEN)[None, :]
    attended_context, logsum = lax.map(partial(attend, causal), (query, keys, values))
    attended_context = attended_context.reshape(rows, inner_out)
    adapter_expand_hidden = matrix_product(second_norm_output, expand_a).astype(jnp.bfloat16)
    expand_weight_local = lax.dynamic_slice_in_dim(
        expand_up_factor, rank * expand_cols, expand_cols, 1
    )
    upper_hidden = matrix_product(
        second_norm_output, expand_frozen_weight
    ) + ADAPTER_SCALE * matrix_product(adapter_expand_hidden, expand_weight_local)
    gelu_exact = partial(jax.nn.gelu, approximate=False)
    active_f, gelu_pull = jax.vjp(gelu_exact, upper_hidden)
    active_hidden = active_f.astype(jnp.bfloat16)
    out_rows_a = lax.dynamic_slice_in_dim(output_a, rank * inner_out, inner_out, 0)
    output_columns_up_factor = lax.dynamic_slice_in_dim(output_up_factor, rank * cols, cols, 1)
    shrink_rows_a = lax.dynamic_slice_in_dim(shrink_a, rank * expand_cols, expand_cols, 0)
    shrink_columns_up_factor = lax.dynamic_slice_in_dim(shrink_up_factor, rank * cols, cols, 1)
    zero_pair = (
        jnp.zeros((rows, cols), jnp.float32),
        jnp.zeros((rows, output_a.shape[1]), jnp.float32),
    )
    attn_summed, attn_low = fold_with(
        output_frozen_weight,
        output_a,
        zero_pair,
        lax.all_gather(attended_context, "mp", axis=1, tiled=True),
    )
    mlp_summed, mlp_low = fold_with(
        shrink_frozen_weight,
        shrink_a,
        zero_pair,
        jax.tree.map(lambda a: lax.all_gather(a, "mp", axis=1, tiled=True), active_hidden),
    )
    attention_branch, adapter_output_hidden = finish(
        attn_summed, attn_low, output_columns_up_factor
    )
    feedforward_branch, adapter_shrink_hidden = finish(
        mlp_summed, mlp_low, shrink_columns_up_factor
    )
    result = (hidden.astype(jnp.float32) + attention_branch + feedforward_branch).astype(
        jnp.bfloat16
    )
    back_out, back_shrink = (
        lax.psum_scatter(
            matrix_product_transposed_right(cotangent, output_frozen_weight),
            "mp",
            scatter_dimension=1,
            tiled=True,
        ),
        lax.psum_scatter(
            matrix_product_transposed_right(cotangent, shrink_frozen_weight),
            "mp",
            scatter_dimension=1,
            tiled=True,
        ),
    )
    rank_out, rank_shrink = lax.psum(
        (
            ADAPTER_SCALE * matrix_product_transposed_right(cotangent, output_columns_up_factor),
            ADAPTER_SCALE * matrix_product_transposed_right(cotangent, shrink_columns_up_factor),
        ),
        "mp",
    )
    low_out_grad = rank_out.astype(jnp.bfloat16)
    low_shrink_grad = rank_shrink.astype(jnp.bfloat16)
    output_up_factor_piece = ADAPTER_SCALE * matrix_product_transposed_left(
        adapter_output_hidden, cotangent
    )
    shrink_up_factor_piece = ADAPTER_SCALE * matrix_product_transposed_left(
        adapter_shrink_hidden, cotangent
    )
    grad_context = (back_out + matrix_product_transposed_right(low_out_grad, out_rows_a)).astype(
        jnp.bfloat16
    )
    output_a_piece = matrix_product_transposed_left(attended_context, low_out_grad)
    shrink_a_piece = matrix_product_transposed_left(active_hidden, low_shrink_grad)
    grad_active = back_shrink + matrix_product_transposed_right(low_shrink_grad, shrink_rows_a)
    upper_gradient = gelu_pull(grad_active)[0].astype(jnp.bfloat16)
    grad_context = grad_context.reshape(count, SEQ_LEN, heads_here, HEAD_DIM)
    grad_query, grad_keys, grad_values = lax.map(
        partial(attend_back, causal), (query, keys, values, grad_context, logsum)
    )
    mixed_gradient = jnp.stack(
        [unrotate(grad_query, cosine, sine), unrotate(grad_keys, cosine, sine), grad_values], 3
    )
    mixed_gradient = mixed_gradient.reshape(rows, joined_cols).astype(jnp.bfloat16)
    rank_joined, rank_expand = lax.psum(
        (
            ADAPTER_SCALE * matrix_product_transposed_right(mixed_gradient, joined_weight_local),
            ADAPTER_SCALE * matrix_product_transposed_right(upper_gradient, expand_weight_local),
        ),
        "mp",
    )
    low_joined_grad = rank_joined.astype(jnp.bfloat16)
    low_expand_grad = rank_expand.astype(jnp.bfloat16)
    joined_up_factor_piece = ADAPTER_SCALE * matrix_product_transposed_left(
        adapter_joined_hidden, mixed_gradient
    )
    expand_up_factor_piece = ADAPTER_SCALE * matrix_product_transposed_left(
        adapter_expand_hidden, upper_gradient
    )
    norm_one_cols = lax.dynamic_slice_in_dim(first_norm_output, rank * cols, cols, 1)
    norm_two_cols = lax.dynamic_slice_in_dim(second_norm_output, rank * cols, cols, 1)
    joined_a_piece = matrix_product_transposed_left(norm_one_cols, low_joined_grad)
    expand_a_piece = matrix_product_transposed_left(norm_two_cols, low_expand_grad)
    grad_one, grad_two = (
        lax.psum_scatter(
            matrix_product_transposed_right(mixed_gradient, joined_frozen_weight),
            "mp",
            scatter_dimension=1,
            tiled=True,
        ),
        lax.psum_scatter(
            matrix_product_transposed_right(upper_gradient, expand_frozen_weight),
            "mp",
            scatter_dimension=1,
            tiled=True,
        ),
    )
    joined_rows_a = lax.dynamic_slice_in_dim(joined_a, rank * cols, cols, 0)
    expand_rows_a = lax.dynamic_slice_in_dim(expand_a, rank * cols, cols, 0)
    grad_one = grad_one + matrix_product_transposed_right(low_joined_grad, joined_rows_a)
    grad_two = grad_two + matrix_product_transposed_right(low_expand_grad, expand_rows_a)
    unit_one_cols = lax.dynamic_slice_in_dim(unit_one, rank * cols, cols, 1)
    unit_two_cols = lax.dynamic_slice_in_dim(unit_two, rank * cols, cols, 1)
    gain_one_cols = lax.dynamic_slice_in_dim(first_gain, rank * cols, cols, 0)
    gain_two_cols = lax.dynamic_slice_in_dim(second_gain, rank * cols, cols, 0)
    first_gain_piece = jnp.sum(grad_one * unit_one_cols, 0)
    first_bias_piece = jnp.sum(grad_one, 0)
    second_gain_piece = jnp.sum(grad_two * unit_two_cols, 0)
    second_bias_piece = jnp.sum(grad_two, 0)
    scaled_one = grad_one * gain_one_cols
    scaled_two = grad_two * gain_two_cols
    plain_one, along_one, plain_two, along_two = (
        lax.psum(jnp.sum(scaled_one, -1).astype(jnp.bfloat16), "mp").astype(jnp.float32),
        lax.psum(jnp.sum(scaled_one * unit_one_cols, -1).astype(jnp.bfloat16), "mp").astype(
            jnp.float32
        ),
        lax.psum(jnp.sum(scaled_two, -1).astype(jnp.bfloat16), "mp").astype(jnp.float32),
        lax.psum(jnp.sum(scaled_two * unit_two_cols, -1).astype(jnp.bfloat16), "mp").astype(
            jnp.float32
        ),
    )
    back_one = factor_one * (
        scaled_one - plain_one[:, None] / width - unit_one_cols * along_one[:, None] / width
    )
    back_two = factor_two * (
        scaled_two - plain_two[:, None] / width - unit_two_cols * along_two[:, None] / width
    )
    hidden_grad = cotangent.astype(jnp.float32) + back_one + back_two
    pieces = (
        first_gain_piece,
        first_bias_piece,
        second_gain_piece,
        second_bias_piece,
        joined_a_piece,
        joined_up_factor_piece,
        output_a_piece,
        output_up_factor_piece,
        expand_a_piece,
        expand_up_factor_piece,
        shrink_a_piece,
        shrink_up_factor_piece,
    )
    shapes = (
        first_gain.shape,
        first_bias.shape,
        second_gain.shape,
        second_bias.shape,
        joined_a.shape,
        joined_up_factor.shape,
        output_a.shape,
        output_up_factor.shape,
        expand_a.shape,
        expand_up_factor.shape,
        shrink_a.shape,
        shrink_up_factor.shape,
    )
    along = (0, 0, 0, 0, 0, 1, 0, 1, 0, 1, 0, 1)
    padded = [
        lax.dynamic_update_slice_in_dim(
            jnp.zeros(shape, jnp.float32), piece, rank * piece.shape[axis_dim], axis_dim
        )
        for piece, shape, axis_dim in zip(pieces, shapes, along)
    ]
    grads = lax.psum(
        (
            padded[0],
            padded[1],
            padded[2],
            padded[3],
            padded[4],
            padded[5],
            padded[6],
            padded[7],
            padded[8],
            padded[9],
            padded[10],
            padded[11],
        ),
        ("dp", "mp"),
    )
    return (
        result,
        hidden_grad,
        grads[0],
        grads[1],
        grads[2],
        grads[3],
        grads[4],
        grads[5],
        grads[6],
        grads[7],
        grads[8],
        grads[9],
        grads[10],
        grads[11],
    )


BF = jnp.bfloat16
F32 = jnp.float32
BLOCK = 256
VMEM_LIMIT = 62 << 20


def nn(left, right):
    return lax.dot_general(left, right, (((1,), (0,)), ((), ())), preferred_element_type=F32)


def nt(left, right):
    return lax.dot_general(left, right, (((1,), (1,)), ((), ())), preferred_element_type=F32)


def tn(left, right):
    return lax.dot_general(left, right, (((0,), (0,)), ((), ())), preferred_element_type=F32)


def span(start, size, unit=128):
    return pl.ds(pl.multiple_of(start, unit), size)


def layer_norm(rows_f32):
    center = rows_f32 - jnp.mean(rows_f32, 1, keepdims=True)
    factor = lax.rsqrt(jnp.mean(center * center, 1, keepdims=True) + EPS)
    return center * factor, factor


def attention_kernel(slots, shared, ids, *refs):
    hg_refs, w_own = refs[0:6], refs[6]
    o_own, o_mate = refs[7:9]
    foreign, diag = refs[9:13], refs[13:17]
    gain, bias, up, ja, oa, ou, cos_ref, sin_ref = refs[17:25]
    n_out = 4 if shared else 2
    outs = refs[25 : 25 + n_out]
    (h_v, g_v, w_v, o_v, w_t, q_t, k_t, v_t, k_n, v_n, do_t, dm_t, ctx_t, dk, dv, both, tok_sem, w_sem) = refs[25 + n_out :]
    f, q = ids[0], ids[1]
    seq = h_v.shape[0]
    steps = seq // BLOCK
    heads = q_t.shape[0] // HEAD_DIM
    width = h_v.shape[1]
    piece = width // 4
    shard = w_v.shape[1] // len(slots)
    for i, slot in enumerate(slots):
        if slot == 0:
            for s in range(4):
                pltpu.make_async_copy(
                    w_own.at[span(lax.bitwise_xor(f, s) * piece, piece), :],
                    w_v.at[s * piece : (s + 1) * piece, i * shard : (i + 1) * shard],
                    w_sem.at[0],
                ).start()
        else:
            for k in range(4):
                row = lax.bitwise_xor(lax.bitwise_xor(q, k), f) * piece
                pltpu.make_async_copy(
                    foreign[k].at[:, :shard], w_v.at[span(row, piece), i * shard : (i + 1) * shard], w_sem.at[0]
                ).start()
        head_block = lax.bitwise_xor(f, slot)
        rows = slice(i * BLOCK, (i + 1) * BLOCK)
        for s, ref in ((0, o_own), (1, o_mate)):
            pltpu.make_async_copy(
                ref.at[span(head_block * BLOCK, BLOCK), :], o_v.at[rows, s * piece : (s + 1) * piece], w_sem.at[1]
            ).start()
        for s, pieces in ((2, foreign), (3, diag)):
            for k in range(4):

                @pl.when(lax.bitwise_xor(q, k) == head_block)
                def _():
                    pltpu.make_async_copy(
                        pieces[k].at[:, shard : shard + BLOCK], o_v.at[rows, s * piece : (s + 1) * piece], w_sem.at[1]
                    ).start()

    start = 2 * seq if shared else lax.shift_right_logical(f, 1) * seq
    for i, dst in enumerate((h_v, g_v)):
        for s in range(4):
            ref = hg_refs[2 * i + s] if s < 2 else hg_refs[2 + s]
            at = start if s < 2 else i * seq
            pltpu.make_async_copy(
                ref.at[span(at, seq), :], dst.at[:, s * piece : (s + 1) * piece], tok_sem.at[i]
            ).start()

    pltpu.make_async_copy(w_v, w_v, w_sem.at[0]).wait()
    w_t[...] = w_v[...].T
    pltpu.make_async_copy(o_v, o_v, w_sem.at[1]).wait()
    up_t = jnp.concatenate([up[:, s * shard : (s + 1) * shard] for s in slots], 1).T
    oa_rows = jnp.concatenate([oa[s * BLOCK : (s + 1) * BLOCK, :] for s in slots], 0)
    o_rows = o_v[...]

    def project(t):
        rows = slice(t * BLOCK, (t + 1) * BLOCK)
        unit, _ = layer_norm(h_v[rows, :].astype(F32))
        n = (unit * gain[...] + bias[...]).astype(BF)
        low = (nn(n, ja[...]).astype(BF) * ADAPTER_SCALE).astype(BF)
        mixed = nt(w_t[...], n) + nt(up_t, low)
        cos, sin = cos_ref[:, rows], sin_ref[:, rows]
        half = ROTARY // 2
        for h in range(heads):
            own = slice(h * HEAD_DIM, (h + 1) * HEAD_DIM)
            base = 3 * HEAD_DIM * h
            for part in range(2):
                block = mixed[base + part * HEAD_DIM : base + (part + 1) * HEAD_DIM]
                a, b = block[:half], block[half:ROTARY]
                block = jnp.concatenate([a * cos - b * sin, b * cos + a * sin, block[ROTARY:]], 0).astype(BF)
                if part == 0:
                    q_t[own, rows] = (block * HEAD_DIM ** (-0.5)).astype(BF)
                else:
                    k_t[own, rows] = block
                    k_n[rows, own] = block.T
            block = mixed[base + 2 * HEAD_DIM : base + 3 * HEAD_DIM].astype(BF)
            v_t[own, rows] = block
            v_n[rows, own] = block.T
        g = g_v[rows, :]
        low_grad = (nt(g, ou[...]) * ADAPTER_SCALE).astype(BF)
        do_t[:, rows] = (nt(o_rows, g) + nt(oa_rows, low_grad)).astype(BF)

    for i, dst in enumerate((h_v, g_v)):
        pltpu.make_async_copy(dst, dst, tok_sem.at[i]).wait()
    for t in range(steps):
        project(t)

    later = lax.broadcasted_iota(jnp.int32, (BLOCK, BLOCK), 0) > lax.broadcasted_iota(jnp.int32, (BLOCK, BLOCK), 1)
    state = {}

    def products(h, i):
        own, qs = slice(h * HEAD_DIM, (h + 1) * HEAD_DIM), slice(i * BLOCK, (i + 1) * BLOCK)
        state[h, i] = (
            [nn(k_n[j * BLOCK : (j + 1) * BLOCK, own], q_t[own, qs]) for j in range(i + 1)],
            [nn(v_n[j * BLOCK : (j + 1) * BLOCK, own], do_t[own, qs]) for j in range(i + 1)],
        )

    def soft(h, i):
        scores, d_probs = state[h, i]
        scores[-1] = jnp.where(later, -1e30, scores[-1])
        peak = reduce(jnp.maximum, [jnp.max(s, 0, keepdims=True) for s in scores])
        weights = [jnp.exp(s - peak) for s in scores]
        inverse = 1.0 / reduce(jnp.add, [jnp.sum(w, 0, keepdims=True) for w in weights])
        probs = [w * inverse for w in weights]
        inner = reduce(jnp.add, [jnp.sum(p * d, 0, keepdims=True) for p, d in zip(probs, d_probs)])
        state[h, i] = (
            [p.astype(BF) for p in probs],
            [(p * (d - inner)).astype(BF) for p, d in zip(probs, d_probs)],
        )

    def unturn(block, cos, sin):
        half = ROTARY // 2
        a, b = block[:half], block[half:ROTARY]
        return jnp.concatenate([a * cos + b * sin, b * cos - a * sin, block[ROTARY:]], 0).astype(BF)

    def finish_block(h, i):
        own, qs = slice(h * HEAD_DIM, (h + 1) * HEAD_DIM), slice(i * BLOCK, (i + 1) * BLOCK)
        base = 3 * HEAD_DIM * h
        probs, d_scores = state.pop((h, i))
        keys = slice(0, (i + 1) * BLOCK)
        ctx_t[own, qs] = nn(v_t[own, keys], jnp.concatenate(probs, 0)).astype(BF)
        d_query = nn(k_t[own, keys], jnp.concatenate(d_scores, 0)) * HEAD_DIM ** (-0.5)
        dm_t[base : base + HEAD_DIM, qs] = unturn(d_query, cos_ref[:, qs], sin_ref[:, qs])
        query, d_out = q_t[own, qs], do_t[own, qs]
        for j in range(i + 1):
            js = slice(j * BLOCK, (j + 1) * BLOCK)
            if j == i:
                dk[own, js] = nt(query, d_scores[j])
                dv[own, js] = nt(d_out, probs[j])
            else:
                dk[own, js] += nt(query, d_scores[j])
                dv[own, js] += nt(d_out, probs[j])
        if i == steps - 1:
            dm_t[base + HEAD_DIM : base + 2 * HEAD_DIM, :] = unturn(dk[own, :], cos_ref[...], sin_ref[...])
            dm_t[base + 2 * HEAD_DIM : base + 3 * HEAD_DIM, :] = dv[own, :].astype(BF)

    order = [(h, i) for h in range(heads) for i in range(steps)]
    for at in range(len(order) + 2):
        if at < len(order):
            products(*order[at])
        if at >= 2:
            finish_block(*order[at - 2])
        if 1 <= at <= len(order):
            soft(*order[at - 1])
    for i in range(len(slots)):
        at = i * (BLOCK + shard)
        both[:, at : at + BLOCK] = ctx_t[i * BLOCK : (i + 1) * BLOCK, :].T
        both[:, at + BLOCK : at + BLOCK + shard] = dm_t[i * shard : (i + 1) * shard, :].T
    if shared:
        for s in range(4):
            outs[s][...] = both[span(lax.bitwise_xor(f, s) * BLOCK, BLOCK), :]
    else:
        c = lax.bitwise_and(f, 1)
        half = seq // 2
        outs[0][...] = both[span(c * half, half), :]
        outs[1][...] = both[span((1 - c) * half, half), :]


def any_spec():
    return pl.BlockSpec(memory_space=pl.ANY)


def vmem_spec():
    return pl.BlockSpec(memory_space=pltpu.VMEM)


def smem_spec():
    return pl.BlockSpec(memory_space=pltpu.SMEM)


def attention(slots, shared, ids, hg, w_own, os, gain, bias, up, ja, oa, ou, cos, sin):
    seq, piece = SEQ_LEN, hg[0].shape[1]
    width = 4 * piece
    shard, own = up.shape[1] // 4, oa.shape[0] // 4
    joined, inner = shard * len(slots), own * len(slots)
    out_shape = [jax.ShapeDtypeStruct((BLOCK if shared else seq // 2, inner + joined), BF)] * (4 if shared else 2)

    return pl.pallas_call(
        partial(attention_kernel, slots, shared),
        in_specs=[smem_spec()] + [any_spec()] * 17 + [vmem_spec()] * 8,
        out_specs=[vmem_spec()] * len(out_shape),
        out_shape=out_shape,
        scratch_shapes=[
            pltpu.VMEM((seq, width), BF),
            pltpu.VMEM((seq, width), BF),
            pltpu.VMEM((width, joined), BF),
            pltpu.VMEM((inner, width), BF),
            pltpu.VMEM((joined, width), BF),
            pltpu.VMEM((inner, seq), BF),
            pltpu.VMEM((inner, seq), BF),
            pltpu.VMEM((inner, seq), BF),
            pltpu.VMEM((seq, inner), BF),
            pltpu.VMEM((seq, inner), BF),
            pltpu.VMEM((inner, seq), BF),
            pltpu.VMEM((joined, seq), BF),
            pltpu.VMEM((inner, seq), BF),
            pltpu.VMEM((inner, seq), F32),
            pltpu.VMEM((inner, seq), F32),
            pltpu.VMEM((seq, inner + joined), BF),
            pltpu.SemaphoreType.DMA((2,)),
            pltpu.SemaphoreType.DMA((2,)),
        ],
        compiler_params=pltpu.CompilerParams(vmem_limit_bytes=VMEM_LIMIT),
        cost_estimate=pl.CostEstimate(
            flops=100_000_000_000 if shared else 1_000_000, bytes_accessed=100_000, transcendentals=0
        ),
        name="attention",
    )(ids, *hg, w_own, *os, gain, bias, up, ja, oa, ou, cos, sin)


def token_copies(ids, tokens, which, dst, sem):
    f = ids[0]
    x, c = lax.shift_right_logical(f, 1), lax.bitwise_and(f, 1)
    seq = SEQ_LEN
    half = seq // 2
    piece = tokens[0].shape[1]
    for s in range(4):
        cols = slice(s * piece, (s + 1) * piece)
        if s < 2:
            own, shared = tokens[2 * which + s], tokens[2 * which + s]
            own_at, shared_at = x * seq, 2 * seq
        else:
            own, shared = tokens[2 + s], tokens[4 + s]
            own_at, shared_at = which * seq, which * seq
        pltpu.make_async_copy(own.at[span(own_at + c * half, half), :], dst.at[:half, cols], sem).start()
        pltpu.make_async_copy(
            shared.at[span(shared_at + f * BLOCK, BLOCK), :], dst.at[half : half + BLOCK, cols], sem
        ).start()


def attention_copies(own, shared, at, dst, sem):
    half = dst.shape[0] - BLOCK
    size = dst.shape[1] // 4
    pitch = shared[0].shape[1]
    for s in range(4):
        to = slice(s * size, (s + 1) * size)
        col = (s // 2) * pitch + at
        pltpu.make_async_copy(own[s % 2].at[:, col : col + size], dst.at[:half, to], sem).start()
        pltpu.make_async_copy(shared[s].at[:, at : at + size], dst.at[half : half + BLOCK, to], sem).start()


def arrived(dst, sem):
    pltpu.make_async_copy(dst, dst, sem).wait()


def grads_kernel(ids, *refs):
    tokens, a_own, a_sh = refs[0:8], refs[8:10], refs[10:14]
    gain, bias, up, ja, oa, ou = refs[14:20]
    low_out_ref, low_grad_ref, keep, send = refs[20:24]
    h_v, g_v, c_v, m_v, sem = refs[24:]
    f = ids[0]
    rows, width = h_v.shape
    piece = width // 4
    shard = m_v.shape[1] // 4
    token_copies(ids, tokens, 1, g_v, sem.at[1])
    attention_copies(a_own, a_sh, 0, c_v, sem.at[2])
    token_copies(ids, tokens, 0, h_v, sem.at[0])
    attention_copies(a_own, a_sh, BLOCK, m_v, sem.at[3])
    put = partial(put_blocks, f, keep, send)
    arrived(g_v, sem.at[1])
    arrived(c_v, sem.at[2])
    low_out = (nn(c_v[...], oa[...]).astype(BF) * ADAPTER_SCALE).astype(BF)
    low_out_ref[...] = low_out
    low_out_grad = (nt(g_v[...], ou[...]) * ADAPTER_SCALE).astype(BF)
    put(0, piece, low_out.T, g_v)
    put(width, piece, low_out_grad.T, c_v)
    arrived(h_v, sem.at[0])
    unit, _ = layer_norm(h_v[...].astype(F32))
    n = (unit * gain[...] + bias[...]).astype(BF)
    low = (nn(n, ja[...]).astype(BF) * ADAPTER_SCALE).astype(BF)
    arrived(m_v, sem.at[3])
    low_grad = (nt(m_v[...], up[...]) * ADAPTER_SCALE).astype(BF)
    low_grad_ref[...] = low_grad
    put(2 * width, shard, low.T, m_v)
    put(2 * width + 4 * shard, piece, low_grad.T, n)


def put_blocks(f, keep, send, base, size, left, right):
    half = keep.shape[0]
    for s in range(4):
        value = nn(left, right[:, s * size : (s + 1) * size])
        to = span(base + lax.bitwise_xor(f, s) * size, size)
        keep[:, to] = value[:half]
        send[:, to] = value[half:]


def grads_of_attention(ids, tokens, a_own, a_sh, gain, bias, up, ja, oa, ou):
    piece = tokens[0].shape[1]
    width = 4 * piece
    rows = SEQ_LEN // 2 + BLOCK
    shard = up.shape[1] // 4
    rank = ja.shape[1]
    total = 3 * width + 4 * shard
    return pl.pallas_call(
        grads_kernel,
        in_specs=[smem_spec()] + [any_spec()] * 14 + [vmem_spec()] * 6,
        out_specs=[vmem_spec()] * 4,
        out_shape=[
            jax.ShapeDtypeStruct((rows, rank), BF),
            jax.ShapeDtypeStruct((rows, rank), BF),
            jax.ShapeDtypeStruct((rank // 2, total), F32),
            jax.ShapeDtypeStruct((rank // 2, total), F32),
        ],
        scratch_shapes=[
            pltpu.VMEM((rows, width), BF),
            pltpu.VMEM((rows, width), BF),
            pltpu.VMEM((rows, width), BF),
            pltpu.VMEM((rows, 4 * shard), BF),
            pltpu.SemaphoreType.DMA((4,)),
        ],
        compiler_params=pltpu.CompilerParams(vmem_limit_bytes=VMEM_LIMIT),
        cost_estimate=pl.CostEstimate(flops=100_000_000_000, bytes_accessed=100_000, transcendentals=0),
        name="grads_of_attention",
    )(ids, *tokens, *a_own, *a_sh, gain, bias, up, ja, oa, ou)


def start_slot(slot, ids, weights, e_v, s_v, e_sem, s_sem):
    f, q = ids[0], ids[1]
    e_own, e_mate, s_own, s_mate = weights[:4]
    foreign, diag = weights[4:8], weights[8:12]
    width, hidden = e_v.shape
    piece, part = width // 4, hidden // 4
    cols = slice(slot * part, (slot + 1) * part)
    if slot < 2:
        for t in range(4):
            pltpu.make_async_copy(
                weights[slot].at[span(lax.bitwise_xor(f, t) * piece, piece), :],
                e_v.at[t * piece : (t + 1) * piece, cols],
                e_sem.at[slot],
            ).start()
    else:
        for k in range(4):
            rows = span(lax.bitwise_xor(lax.bitwise_xor(q, k), f) * piece, piece)
            pltpu.make_async_copy(
                weights[4 * slot - 4 + k].at[:piece, :], e_v.at[rows, cols], e_sem.at[slot]
            ).start()
    for s, ref in ((0, s_own), (1, s_mate)):
        pltpu.make_async_copy(
            ref.at[span(lax.bitwise_xor(f, slot) * part, part), :],
            s_v.at[cols, s * piece : (s + 1) * piece],
            s_sem.at[slot],
        ).start()
    for k in range(4):

        @pl.when(lax.bitwise_xor(lax.bitwise_xor(q, k), f) == slot)
        def _():
            for s, pieces in ((2, foreign), (3, diag)):
                shrink_copies(pieces[k], s_v, slot * part, s * piece, s_sem.at[slot])


def shrink_copies(pack, dst, row, col, sem):
    for u in range(pack.shape[1] // BLOCK):
        pltpu.make_async_copy(
            pack.at[BLOCK:, u * BLOCK : (u + 1) * BLOCK],
            dst.at[span(row + u * BLOCK, BLOCK), col : col + BLOCK],
            sem,
        ).start()


CHUNK = 512


def mlp_first_kernel(ids, *refs):
    tokens, weights = refs[0:8], refs[8:20]
    gain, bias, ea, eu, sa, su = refs[20:26]
    act_out, dup_out, ls_out, dle_out, keep, send = refs[26:32]
    h_v, g_v, n_v, e_v, s_v, act, dup, sem, e_sem, s_sem, o_sem = refs[32:]
    f = ids[0]
    rows, width = h_v.shape
    hidden = e_v.shape[1]
    token_copies(ids, tokens, 0, h_v, sem.at[0])
    token_copies(ids, tokens, 1, g_v, sem.at[1])
    load = lambda slot: start_slot(slot, ids, weights, e_v, s_v, e_sem, s_sem)
    load(0)
    arrived(h_v, sem.at[0])
    unit, _ = layer_norm(h_v[...].astype(F32))
    n_v[...] = (unit * gain[...] + bias[...]).astype(BF)
    low = (nn(n_v[...], ea[...]).astype(BF) * ADAPTER_SCALE).astype(BF)
    arrived(g_v, sem.at[1])
    low_grad = (nt(g_v[...], su[...]) * ADAPTER_SCALE).astype(BF)
    load(1)
    state = {}
    part, piece = hidden // 4, width // 4

    def products(b, t):
        ts, bs = slice(t * BLOCK, (t + 1) * BLOCK), slice(b * CHUNK, (b + 1) * CHUNK)
        if t == 0 and bs.start % part == 0:
            slot = bs.start // part
            whole = slice(slot * part, (slot + 1) * part)
            if 1 <= slot < 3:
                load(slot + 1)
            arrived(e_v.at[:, whole], e_sem.at[slot])
            arrived(s_v.at[whole, :], s_sem.at[slot])
        state[b, t] = (
            nn(n_v[ts, :], e_v[:, bs]) + nn(low[ts], eu[:, bs]),
            nt(g_v[ts, :], s_v[bs, :]) + nt(low_grad[ts], sa[bs, :]),
        )

    def bend(b, t):
        ts, bs = slice(t * BLOCK, (t + 1) * BLOCK), slice(b * CHUNK, (b + 1) * CHUNK)
        upper, d_active = state.pop((b, t))
        normal = 0.5 * (1.0 + lax.erf(upper * 0.7071067811865476))
        density = jnp.exp(-0.5 * upper * upper) * 0.3989422804014327
        act[ts, bs] = (upper * normal).astype(BF)
        dup[ts, bs] = (d_active * (normal + upper * density)).astype(BF)
        if t == rows // BLOCK - 1:
            pltpu.make_async_copy(act.at[:, bs], act_out.at[:, bs], o_sem.at[0]).start()
            pltpu.make_async_copy(dup.at[:, bs], dup_out.at[:, bs], o_sem.at[1]).start()

    order = [(b, t) for b in range(hidden // CHUNK) for t in range(rows // BLOCK)]
    for at in range(len(order) + 1):
        if at < len(order):
            products(*order[at])
        if at > 0:
            bend(*order[at - 1])

    put = partial(put_blocks, f, keep, send)
    put(0, part, low_grad.T, act)
    put(hidden, part, low.T, dup)
    low_shrink = (nn(act[...], sa[...]).astype(BF) * ADAPTER_SCALE).astype(BF)
    low_expand_grad = (nt(dup[...], eu[...]) * ADAPTER_SCALE).astype(BF)
    ls_out[...] = low_shrink
    dle_out[...] = low_expand_grad
    put(2 * hidden, piece, low_shrink.T, g_v)
    put(2 * hidden + width, piece, low_expand_grad.T, n_v)
    arrived(act, o_sem.at[0])
    arrived(dup, o_sem.at[1])


def mlp_first(ids, tokens, weights, gain, bias, ea, eu, sa, su):
    piece = tokens[0].shape[1]
    width = 4 * piece
    rows = SEQ_LEN // 2 + BLOCK
    hidden = eu.shape[1]
    rank = ea.shape[1]
    return pl.pallas_call(
        mlp_first_kernel,
        in_specs=[smem_spec()] + [any_spec()] * 20 + [vmem_spec()] * 6,
        out_specs=[any_spec()] * 2 + [vmem_spec()] * 4,
        out_shape=[
            jax.ShapeDtypeStruct((rows, hidden), BF),
            jax.ShapeDtypeStruct((rows, hidden), BF),
            jax.ShapeDtypeStruct((rows, rank), BF),
            jax.ShapeDtypeStruct((rows, rank), BF),
            jax.ShapeDtypeStruct((rank // 2, 2 * hidden + 2 * width), F32),
            jax.ShapeDtypeStruct((rank // 2, 2 * hidden + 2 * width), F32),
        ],
        scratch_shapes=[
            pltpu.VMEM((rows, width), BF),
            pltpu.VMEM((rows, width), BF),
            pltpu.VMEM((rows, width), BF),
            pltpu.VMEM((width, hidden), BF),
            pltpu.VMEM((hidden, width), BF),
            pltpu.VMEM((rows, hidden), BF),
            pltpu.VMEM((rows, hidden), BF),
            pltpu.SemaphoreType.DMA((2,)),
            pltpu.SemaphoreType.DMA((4,)),
            pltpu.SemaphoreType.DMA((4,)),
            pltpu.SemaphoreType.DMA((2,)),
        ],
        compiler_params=pltpu.CompilerParams(vmem_limit_bytes=VMEM_LIMIT),
        cost_estimate=pl.CostEstimate(flops=100_000_000_000, bytes_accessed=100_000, transcendentals=0),
        name="mlp_first",
    )(ids, *tokens, *weights, gain, bias, ea, eu, sa, su)


def rows_of_slot(s, ids, own, mate, foreign, diag, col, dst, sems):
    f, q = ids[0], ids[1]
    piece = own.shape[0] // 4
    cols = own.shape[1]
    to = slice(s * cols, (s + 1) * cols)
    for t in range(4):
        if s < 2:
            src = (own, mate)[s].at[span(lax.bitwise_xor(f, t) * piece, piece), :]
            place = t
        else:
            src = (foreign, diag)[s - 2][t].at[:piece, col : col + cols]
            place = lax.bitwise_xor(lax.bitwise_xor(q, t), f)
        pltpu.make_async_copy(src, dst.at[span(place * piece, piece), to], sems.at[place]).start()


def shrink_of_slot(s, ids, own, mate, foreign, diag, dst, sem):
    f, q = ids[0], ids[1]
    part, piece = dst.shape[0] // 4, dst.shape[1] // 4
    for t in range(4):
        if s < 2:
            src = (own, mate)[s].at[span(lax.bitwise_xor(f, t) * part, part), :]
            pltpu.make_async_copy(src, dst.at[t * part : (t + 1) * part, s * piece : (s + 1) * piece], sem).start()
        else:
            row = lax.bitwise_xor(lax.bitwise_xor(q, t), f) * part
            shrink_copies((foreign, diag)[s - 2][t], dst, row, s * piece, sem)


def result_kernel(ids, *refs):
    tokens, a_own, a_sh = refs[0:8], refs[8:10], refs[10:14]
    o_own, o_mate, s_own, s_mate = refs[14:18]
    one_f, one_d, two_f, two_d = refs[18:22], refs[22:26], refs[26:30], refs[30:34]
    act_ref = refs[34]
    low_out, ou, low_shrink, su = refs[35:39]
    out = refs[39]
    h_v, c_v, o_v, s_v, act, sem, o_sem, s_sem = refs[40:]
    f = ids[0]
    rows, width = h_v.shape
    piece = width // 4
    attention_copies(a_own, a_sh, 0, c_v, sem.at[1])
    for s in range(4):
        rows_of_slot(s, ids, o_own, o_mate, one_f, one_d, 3 * piece, o_v, o_sem)
    token_copies(ids, tokens, 0, h_v, sem.at[2])
    pltpu.make_async_copy(act_ref, act, sem.at[3]).start()
    arrived(c_v, sem.at[1])
    for t in range(4):
        arrived(o_v.at[t * piece : (t + 1) * piece, :], o_sem.at[t])
    arrived(h_v, sem.at[2])
    for s in range(4):
        shrink_of_slot(s, ids, s_own, s_mate, two_f, two_d, s_v, s_sem.at[s])
    blocks = [slice(t * BLOCK, (t + 1) * BLOCK) for t in range(rows // BLOCK)]
    sums = [
        h_v[ts, :].astype(F32)
        + (nn(c_v[ts, :], o_v[...]) + nn(low_out[ts, :], ou[...]))
        + nn(low_shrink[ts, :], su[...])
        for ts in blocks
    ]
    arrived(act, sem.at[3])
    for s in range(4):
        arrived(s_v.at[:, s * piece : (s + 1) * piece], s_sem.at[s])
    for total, ts in zip(sums, blocks):
        value = (total + nn(act[ts, :], s_v[...])).astype(BF)
        for s in range(4):
            out[lax.bitwise_xor(f, s), ts, :] = value[:, s * piece : (s + 1) * piece]


def result_parts(ids, tokens, a_own, a_sh, o_parts, s_parts, one, two, act, low_out, ou, low_shrink, su):
    piece = tokens[0].shape[1]
    width = 4 * piece
    rows = SEQ_LEN // 2 + BLOCK
    hidden = act.shape[1]
    return pl.pallas_call(
        result_kernel,
        in_specs=[smem_spec()] + [any_spec()] * 35 + [vmem_spec()] * 4,
        out_specs=vmem_spec(),
        out_shape=jax.ShapeDtypeStruct((4, rows, piece), BF),
        scratch_shapes=[
            pltpu.VMEM((rows, width), BF),
            pltpu.VMEM((rows, width), BF),
            pltpu.VMEM((width, width), BF),
            pltpu.VMEM((hidden, width), BF),
            pltpu.VMEM((rows, hidden), BF),
            pltpu.SemaphoreType.DMA((4,)),
            pltpu.SemaphoreType.DMA((4,)),
            pltpu.SemaphoreType.DMA((4,)),
        ],
        compiler_params=pltpu.CompilerParams(vmem_limit_bytes=VMEM_LIMIT),
        cost_estimate=pl.CostEstimate(flops=100_000_000_000, bytes_accessed=100_000, transcendentals=0),
        name="result_parts",
    )(ids, *tokens, *a_own, *a_sh, *o_parts, *s_parts, *one, *two, act, low_out, ou, low_shrink, su)


def input_grad_kernel(ids, *refs):
    tokens, a_own, a_sh = refs[0:8], refs[8:10], refs[10:14]
    w_own, w_mate, e_own, e_mate = refs[14:18]
    one_f, one_d, two_f, two_d = refs[18:22], refs[22:26], refs[26:30], refs[30:34]
    dup_ref = refs[34]
    gain_one, gain_two, ja, ea, low_joined_grad, low_expand_grad = refs[35:41]
    outs, sums = refs[41:45], refs[45]
    h_v, g_v, m_v, w_v, e_v, dup, one_v, sem, w_sem, e_sem = refs[46:]
    f = ids[0]
    rows, width = h_v.shape
    piece = width // 4
    shard = m_v.shape[1] // 4
    attention_copies(a_own, a_sh, BLOCK, m_v, sem.at[0])
    for s in range(4):
        rows_of_slot(s, ids, w_own, w_mate, one_f, one_d, 0, w_v, w_sem)
    arrived(m_v, sem.at[0])
    blocks = [slice(t * BLOCK, (t + 1) * BLOCK) for t in range(rows // BLOCK)]
    for t in range(4):
        arrived(w_v.at[t * piece : (t + 1) * piece, :], w_sem.at[t])
    pltpu.make_async_copy(dup_ref, dup, sem.at[3]).start()
    for s in range(4):
        rows_of_slot(s, ids, e_own, e_mate, two_f, two_d, 0, e_v, e_sem)
    token_copies(ids, tokens, 0, h_v, sem.at[1])
    token_copies(ids, tokens, 1, g_v, sem.at[2])
    for ts in blocks:
        one_v[ts, :] = nt(m_v[ts, :], w_v[...]) + nt(low_joined_grad[ts, :], ja[...])
    arrived(dup, sem.at[3])
    for t in range(4):
        arrived(e_v.at[t * piece : (t + 1) * piece, :], e_sem.at[t])
    arrived(h_v, sem.at[1])
    arrived(g_v, sem.at[2])
    total = None
    for ts in blocks:
        one = one_v[ts, :]
        two = nt(dup[ts, :], e_v[...]) + nt(low_expand_grad[ts, :], ea[...])
        unit, factor = layer_norm(h_v[ts, :].astype(F32))
        here = [jnp.sum(v, 0, keepdims=True) for v in (one * unit, one, two * unit, two)]
        total = here if total is None else [a + b for a, b in zip(total, here)]
        e = one * gain_one[...] + two * gain_two[...]
        plain = jnp.mean(e, 1, keepdims=True)
        along = jnp.mean(e * unit, 1, keepdims=True)
        value = g_v[ts, :].astype(F32) + factor * (e - plain - unit * along)
        for s in range(4):
            outs[s][ts, :] = value[:, s * piece : (s + 1) * piece].astype(outs[s].dtype)
    value = jnp.concatenate(total + [jnp.zeros((4, width), F32)], 0)
    for s in range(4):
        sums[:, span(lax.bitwise_xor(f, s) * piece, piece)] = value[:, s * piece : (s + 1) * piece]


def input_grad_parts(
    ids, tokens, a_own, a_sh, w_parts, e_parts, one, two, dup, gain_one, gain_two, ja, ea, low_joined_grad, low_expand_grad
):
    piece = tokens[0].shape[1]
    width = 4 * piece
    rows = SEQ_LEN // 2 + BLOCK
    hidden = dup.shape[1]
    joined = 4 * w_parts[0].shape[1]
    return pl.pallas_call(
        input_grad_kernel,
        in_specs=[smem_spec()] + [any_spec()] * 35 + [vmem_spec()] * 6,
        out_specs=[vmem_spec()] * 5,
        out_shape=[jax.ShapeDtypeStruct((rows, piece), t) for t in (F32, F32, BF, BF)]
        + [jax.ShapeDtypeStruct((8, width), F32)],
        scratch_shapes=[
            pltpu.VMEM((rows, width), BF),
            pltpu.VMEM((rows, width), BF),
            pltpu.VMEM((rows, joined), BF),
            pltpu.VMEM((width, joined), BF),
            pltpu.VMEM((width, hidden), BF),
            pltpu.VMEM((rows, hidden), BF),
            pltpu.VMEM((rows, width), F32),
            pltpu.SemaphoreType.DMA((4,)),
            pltpu.SemaphoreType.DMA((4,)),
            pltpu.SemaphoreType.DMA((4,)),
        ],
        compiler_params=pltpu.CompilerParams(vmem_limit_bytes=VMEM_LIMIT),
        cost_estimate=pl.CostEstimate(flops=100_000_000_000, bytes_accessed=100_000, transcendentals=0),
        name="input_grad_parts",
    )(
        ids, *tokens, *a_own, *a_sh, *w_parts, *e_parts, *one, *two, dup,
        gain_one, gain_two, ja, ea, low_joined_grad, low_expand_grad,
    )


def gather_rows_kernel(widen, ids, *refs):
    parts, out = refs[:4], refs[4]
    scratch = refs[5:]
    f = ids[0]
    sem = scratch[-1]
    rows = parts[0].shape[0]
    half = rows - BLOCK
    seq = 2 * half
    copies = []
    for s in range(4):
        src = parts[s]
        if src.dtype != out.dtype:
            scratch[s - 2][...] = src[...].astype(out.dtype)
            src = scratch[s - 2]
        at = lax.bitwise_xor(f, s)
        copies.append(pltpu.make_async_copy(src.at[:half, :], out.at[span(at * half, half), :], sem.at[2 * s]))
        copies.append(
            pltpu.make_async_copy(src.at[half:, :], out.at[span(2 * seq + at * BLOCK, BLOCK), :], sem.at[2 * s + 1])
        )
        copies[-2].start()
        copies[-1].start()
    for copy in copies:
        copy.wait()


def gather_rows(ids, parts, dtype):
    rows, piece = parts[0].shape
    narrow = [p for p in parts if p.dtype != dtype]
    return pl.pallas_call(
        partial(gather_rows_kernel, dtype),
        in_specs=[smem_spec()] + [vmem_spec()] * 4,
        out_specs=any_spec(),
        out_shape=jax.ShapeDtypeStruct((4 * rows, piece), dtype),
        scratch_shapes=[pltpu.VMEM((rows, piece), dtype)] * len(narrow) + [pltpu.SemaphoreType.DMA((8,))],
        compiler_params=pltpu.CompilerParams(vmem_limit_bytes=VMEM_LIMIT),
        name="gather_rows",
    )(ids, *parts)


def adapters_kernel(cuts, sums_at, ids, order_ref, *refs):
    order = order_ref[...]
    pieces, outs = refs[:8], refs[8:]
    for (at, size, turned), out in zip(cuts, outs):
        value = jnp.concatenate([p[:, at : at + size] for p in pieces], 0)
        out[...] = tn(value, order) if turned else tn(order, value)
    if sums_at is not None:
        sums, lanes = outs[-5:-1], outs[-1]
        for k in range(4):
            lanes[span(lax.bitwise_xor(ids[1], k) * 16, 16, 16), :] = pieces[k][:, sums_at : sums_at + 128].astype(F32)
        for i, out in enumerate(sums):
            for j in range(8):
                out[:, j * 128 : (j + 1) * 128] = lanes[8 * j + i : 8 * j + i + 1, :]


def adapters_out(ids, order, pieces, cuts, sums_at=None):
    rank = order.shape[0]
    out_shape = [jax.ShapeDtypeStruct((size, rank) if turned else (rank, size), F32) for at, size, turned in cuts]
    scratch = []
    if sums_at is not None:
        out_shape += [jax.ShapeDtypeStruct((1, 1024), F32)] * 4
        scratch.append(pltpu.VMEM((64, 128), F32))
    return pl.pallas_call(
        partial(adapters_kernel, cuts, sums_at),
        in_specs=[smem_spec()] + [vmem_spec()] * 9,
        out_specs=[vmem_spec()] * len(out_shape),
        out_shape=out_shape,
        scratch_shapes=scratch,
        compiler_params=pltpu.CompilerParams(vmem_limit_bytes=VMEM_LIMIT),
        name="adapters_out",
    )(ids, order, *pieces)


def join_rows_kernel(keep, received, sums, other, out):
    cols = keep.shape[1]
    out[:, :cols] = (keep[...] + received[...]).astype(BF)
    total = sums[...] + other[...]
    out[:, cols:] = jnp.concatenate([total[:, i * 128 : (i + 1) * 128] for i in range(8)], 0).astype(BF)


def join_rows(keep, received, sums, other):
    rows, cols = keep.shape
    return pl.pallas_call(
        join_rows_kernel,
        in_specs=[vmem_spec()] * 4,
        out_specs=vmem_spec(),
        out_shape=jax.ShapeDtypeStruct((rows, cols + 128), BF),
        compiler_params=pltpu.CompilerParams(vmem_limit_bytes=VMEM_LIMIT),
        name="join_rows",
    )(keep, received, sums, other)


def split_rows_kernel(keep, received, own, *outs):
    size = own.shape[0]
    own[...] = keep[:size, :] + received[:size, :]
    for k, out in enumerate(outs):
        rows = slice((k + 1) * size, (k + 2) * size)
        out[...] = (keep[rows, :] + received[rows, :]).astype(BF)


def split_rows(keep, received):
    rows, cols = keep.shape
    return pl.pallas_call(
        split_rows_kernel,
        in_specs=[vmem_spec()] * 2,
        out_specs=[vmem_spec()] * 4,
        out_shape=[jax.ShapeDtypeStruct((rows // 4, cols), t) for t in (F32, BF, BF, BF)],
        compiler_params=pltpu.CompilerParams(vmem_limit_bytes=VMEM_LIMIT),
        name="split_rows",
    )(keep, received)


def pack_kernel(plan, ids, *refs):
    n_in = len(refs) - 1 - len(plan)
    srcs, outs, sem = refs[:n_in], refs[n_in:-1], refs[-1]
    for out, (shape, blocks) in zip(outs, plan):
        for src, which, size, sub, rows, to_row, to_col in blocks:
            cols = srcs[src].shape[1]
            pltpu.make_async_copy(
                srcs[src].at[span(ids[which] * size + sub, rows), :],
                out.at[to_row : to_row + rows, to_col : to_col + cols],
                sem,
            ).start()
    for out in outs:
        pltpu.make_async_copy(out, out, sem).wait()


def pack(ids, arrays, plan):
    return pl.pallas_call(
        partial(pack_kernel, plan),
        in_specs=[smem_spec()] + [any_spec()] * len(arrays),
        out_specs=[vmem_spec()] * len(plan),
        out_shape=[jax.ShapeDtypeStruct(shape, arrays[0].dtype) for shape, _ in plan],
        scratch_shapes=[pltpu.SemaphoreType.DMA],
        compiler_params=pltpu.CompilerParams(vmem_limit_bytes=VMEM_LIMIT),
        name="pack",
    )(ids, *arrays)


def order_kernel(late, ids, order_ref, other_ref, *refs):
    n = len(refs) // 2
    f = ids[0]
    for i, (src, out) in enumerate(zip(refs[:n], refs[n:])):
        order = (other_ref if i in late else order_ref)[...]
        axis = 0 if src.shape[0] > src.shape[1] else 1
        size = src.shape[axis] // 4
        for s in range(4):
            at, to = span(lax.bitwise_xor(f, s) * size, size), slice(s * size, (s + 1) * size)
            if src.dtype == F32:
                out[:, to] = src[:, at]
            elif axis == 0:
                out[to, :] = nt(src[at, :], order).astype(BF)
            else:
                out[:, to] = nn(order, src[:, at]).astype(BF)


def order_params(ids, order, other, params, late):
    return pl.pallas_call(
        partial(order_kernel, late),
        in_specs=[smem_spec()] + [vmem_spec()] * (2 + len(params)),
        out_specs=[vmem_spec()] * len(params),
        out_shape=[jax.ShapeDtypeStruct(p.shape, p.dtype) for p in params],
        compiler_params=pltpu.CompilerParams(vmem_limit_bytes=VMEM_LIMIT),
        name="order_params",
    )(ids, order, other, *params)


def turn_kernel(ids, out):
    for i in range(ids.shape[0]):
        out[i] = ids[i]


def turn(ids):
    return pl.pallas_call(
        turn_kernel,
        in_specs=[smem_spec()],
        out_specs=smem_spec(),
        out_shape=jax.ShapeDtypeStruct(ids.shape, ids.dtype),
        cost_estimate=pl.CostEstimate(flops=100_000_000_000, bytes_accessed=100_000, transcendentals=0),
        name="turn",
    )(ids)


def swap(axes):
    def run(value):
        size = lax.axis_size(axes)
        return lax.ppermute(value, axes, [(i, size - 1 - i) for i in range(size)])

    return run


def after(value, *others):
    return lax.optimization_barrier((value, *others))[0]


def on_device_by_tokens(
    hidden,
    first_gain,
    first_bias,
    second_gain,
    second_bias,
    joined_frozen_weight,
    output_frozen_weight,
    expand_frozen_weight,
    shrink_frozen_weight,
    joined_a,
    joined_up_factor,
    output_a,
    output_up_factor,
    expand_a,
    expand_up_factor,
    shrink_a,
    shrink_up_factor,
    cotangent,
):
    x, c, q = lax.axis_index("x"), lax.axis_index("core"), lax.axis_index(("zn", "y"))
    f, far = 2 * x + c, lax.axis_index(("zf", "x"))
    seq, half = SEQ_LEN, SEQ_LEN // 2
    width = 4 * hidden.shape[1]
    rank = joined_a.shape[1]
    units = 4 * expand_frozen_weight.shape[1]
    ids = jnp.stack([f, q, far, 1 - x, 3 - q, 0 * f + 2]).astype(jnp.int32)
    to_core, to_x, to_diag = swap("core"), swap("x"), swap(("x", "core"))
    near = swap("y"), swap("zn"), swap(("zn", "y"))
    cross = to_x, swap("zf"), swap(("zf", "x"))

    piece = width // 4

    shard, part = joined_frozen_weight.shape[1], expand_frozen_weight.shape[1]
    (one_pack,) = pack(
        ids,
        (joined_frozen_weight, output_frozen_weight),
        (((piece, shard + piece), ((0, 1, piece, 0, piece, 0, 0), (1, 1, piece, 0, piece, 0, shard))),),
    )
    one_x = to_x(one_pack)
    own, shared = pack(
        after(ids, one_pack),
        (hidden, cotangent),
        tuple(((2 * seq, piece), ((0, at, seq, 0, seq, 0, 0), (1, at, seq, 0, seq, seq, 0))) for at in (3, 5)),
    )
    two_first, two_last = pack(
        after(ids, own),
        (expand_frozen_weight, shrink_frozen_weight),
        tuple(
            (
                (piece + BLOCK, part),
                ((0, at, piece, 0, piece, 0, 0),)
                + tuple((1, at, part, u, BLOCK, piece, u) for u in range(0, part, BLOCK)),
            )
            for at in (1, 4)
        ),
    )
    place = lax.broadcasted_iota(jnp.int32, (rank, rank), 0)
    half_order, order = (
        (lax.broadcasted_iota(jnp.int32, (rank, rank), 1) == (place ^ mask)).astype(BF) for mask in (c * 64, c * 64 + q * 16)
    )
    gain_one, bias_one, gain_two, bias_two, ja, oa, ea, sa, ju, ou, eu, su = order_params(
        after(ids, own),
        half_order,
        order,
        tuple(v[None, :] for v in (first_gain, first_bias, second_gain, second_bias))
        + (joined_a, output_a, expand_a, shrink_a)
        + (joined_up_factor, output_up_factor, expand_up_factor, shrink_up_factor),
        (6, 7, 10, 11),
    )
    position = np.arange(seq, dtype=np.float32)[None, :]
    frequency = np.float32(10000.0) ** (-(np.arange(ROTARY // 2, dtype=np.float32) * np.float32(2.0)) / np.float32(ROTARY))
    angles = frequency[:, None] * position
    cos, sin = jnp.asarray(np.cos(angles), F32), jnp.asarray(np.sin(angles), F32)
    h_mate, g_mate, e_mate, s_mate = (
        to_core(v) for v in after((hidden, cotangent, expand_frozen_weight, shrink_frozen_weight), one_pack)
    )
    one_x = after(one_x, own, two_first, gain_one, h_mate, g_mate, e_mate, s_mate)
    own_x = to_x(after(own, one_x))
    one_near = tuple(go(one_x) for go in near)
    own_x = after(own_x, one_near)
    ids = turn(after(ids, own_x))
    own_mate = to_core(after(own_x, ids))
    one_foreign = (one_x,) + one_near
    o_mate, *one_diag = (to_core(p) for p in after((output_frozen_weight,) + one_foreign, ids))
    one_diag = tuple(one_diag)
    local = (hidden, h_mate, cotangent, g_mate)
    o_parts = (output_frozen_weight, o_mate) + one_foreign + one_diag
    params = (gain_one, bias_one, ju, ja, oa, ou, cos, sin)
    shared_x = to_x(after(shared, own_x))
    two_x = to_x(after(two_first, own_x))
    keep_a, send_a = attention(
        (0, 2), False, ids, local + (own_x, own_mate), joined_frozen_weight, o_parts, *params
    )
    shared_x, two_x = after((shared_x, two_x), keep_a)
    shared_mate = to_core(shared_x)
    two_y, two_z, two_yz = near[0](two_x), near[1](two_x), to_x(after(two_last, two_x))
    b_parts = attention(
        (0,), True, ids, local + (shared_x, shared_mate), joined_frozen_weight, o_parts, *params
    )
    two_y, two_z, two_yz = (after(p, b_parts[0]) for p in (two_y, two_z, two_yz))
    foreign_two = (two_x, two_y, two_z, two_yz)
    diag_two = tuple(to_core(p) for p in foreign_two)
    tokens = local + (own_x, own_mate, shared_x, shared_mate)
    mlp_weights = (expand_frozen_weight, e_mate, shrink_frozen_weight, s_mate) + foreign_two + diag_two
    act, dup, ls, dle, keep_two, send_two = mlp_first(
        ids, tokens, mlp_weights, gain_two, bias_two, ea, eu, sa, su
    )
    b_moved = tuple(go(p) for go, p in zip((to_core, to_x, to_diag), b_parts[1:]))
    w_mate = to_core(joined_frozen_weight)
    b_moved, a_mate, w_mate = after((b_moved, to_core(send_a), w_mate), act)
    a_own, a_shared = (keep_a, a_mate), (b_parts[0],) + b_moved

    two = to_core(send_two)
    low_out, low_joined_grad, keep_one, send_one = grads_of_attention(
        ids, tokens, a_own, a_shared, gain_one, bias_one, ju, ja, oa, ou
    )
    two = split_rows(keep_two, after(two, low_out))
    dup = after(dup, two, send_one)
    two = (two[0],) + tuple(go(p) for go, p in zip(near, two[1:]))
    one = to_core(send_one)
    hidden_grad = input_grad_parts(
        ids, tokens, a_own, a_shared, (joined_frozen_weight, w_mate), (expand_frozen_weight, e_mate),
        one_foreign + one_diag, foreign_two + diag_two, dup, gain_one, gain_two, ja, ea, low_joined_grad, dle,
    )
    two, one = after((two, one), hidden_grad[4])
    sums = hidden_grad[4]
    hidden_grad = (hidden_grad[0], to_core(hidden_grad[1]), to_x(hidden_grad[2]), to_diag(hidden_grad[3]))

    def part_sum(parts):
        return reduce(jnp.add, [p.astype(F32) for p in parts]).astype(BF)

    two = part_sum(two)
    one = join_rows(keep_one, one, sums, to_core(sums))
    act = after(act, two, one, hidden_grad[1])
    two_other = cross[1](two)
    one = lax.all_to_all(one, ("zn", "y"), 0, 0, tiled=True)
    result = result_parts(
        ids, tokens, a_own, a_shared, (output_frozen_weight, o_mate), (shrink_frozen_weight, s_mate),
        one_foreign + one_diag, foreign_two + diag_two, act, low_out, ou, ls, su,
    )
    hidden_grad, two_other, one = after((hidden_grad, two_other, one), result)

    two = part_sum((two, two_other))
    two_other = cross[0](two)
    one = part_sum(after(one, two).reshape(4, -1, one.shape[1]))
    one_other = cross[1](one)
    hidden_grad = gather_rows(ids, hidden_grad, F32)
    two_other = after(two_other, hidden_grad)
    result = lax.all_to_all(after(result, two_other).reshape(-1, piece), ("x", "core"), 0, 0, tiled=True)
    two = part_sum((two, two_other))
    two = (two,) + tuple(go(two) for go in near)
    one = part_sum((one, one_other))
    one_other = cross[0](one)
    one = part_sum((one, one_other))
    one_y, one_z, one_yz = near[0](one), near[1](one), near[2](after(one, two))
    two = two + tuple(to_core(p) for p in two)
    joined = ju.shape[1]
    expand_a_grad, expand_b_grad, shrink_a_grad, shrink_b_grad = adapters_out(
        ids, order, two,
        ((2 * units + width, width, True), (units, units, False), (0, units, True), (2 * units, width, False)),
    )
    one = (one, one_y, one_z) + after((one_yz,), expand_a_grad)
    one = one + tuple(to_core(p) for p in one)
    result = after(result, expand_a_grad).reshape(4, -1, piece)
    result = jnp.concatenate([result[:, : seq // 2].reshape(-1, piece), result[:, seq // 2 :].reshape(-1, piece)], 0)
    joined_a_grad, joined_b_grad, output_a_grad, output_b_grad, *sums = adapters_out(
        ids, order, one,
        ((2 * width + joined, width, True), (2 * width, joined, False), (width, width, True), (0, width, False)),
        3 * width + joined,
    )
    return (
        result,
        hidden_grad,
        sums[0].reshape(-1),
        sums[1].reshape(-1),
        sums[2].reshape(-1),
        sums[3].reshape(-1),
        joined_a_grad,
        joined_b_grad,
        output_a_grad,
        output_b_grad,
        expand_a_grad,
        expand_b_grad,
        shrink_a_grad,
        shrink_b_grad,
    )


def solution(mesh):
    step, rows, cols = on_device, "dp", "mp"
    if mesh.shape["dp"] == 8 and mesh.shape["mp"] == 4:
        step, rows, cols = on_device_by_tokens, ("zf", "zn", "y"), ("x", "core")
        mesh = Mesh(mesh.devices.reshape((2,) * 5), rows + cols)
    whole, split, tokens = P(), P(None, cols), P(rows, cols)
    return jax.shard_map(
        step,
        mesh=mesh,
        in_specs=(tokens,) + (whole,) * 4 + (split,) * 4 + (whole,) * 8 + (tokens,),
        out_specs=(tokens, tokens) + (whole,) * 12,
        check_vma=False,
    )
```
